32 devices in a mesh: ctx: 8 (over y, x, core), tp: 4 (over z).
Axes of the slice: x: 2, y: 2, z: 4, core: 2. Of those that a mesh axis runs over, the one named last changes fastest.
Arguments:
- tokens: bfloat16 [6144, 2048], P('ctx', 'tp'), may hold values from -6 to 6
- segment_ids: int32 [6144], P('ctx'), may hold values from 0 to 6143, as said below
- in_weight: bfloat16 [2048, 3, 2048], P(None, None, 'tp'), may hold values from -0.125 to 0.125
- out_weight: bfloat16 [2048, 2048], P('tp'), may hold values from -2 to 2
- gate_up_weight: bfloat16 [2048, 2, 8192], P(None, None, 'tp'), may hold values from -0.125 to 0.125
- down_weight: bfloat16 [8192, 2048], P('tp'), may hold values from -0.0625 to 0.0625
- cotangent: bfloat16 [6144, 2048], P('ctx', 'tp'), may hold values from -6 to 6
Outputs:
- layer_out: bfloat16 [6144, 2048], P('ctx', 'tp')
- tokens_grad: float32 [6144, 2048], P('ctx', 'tp')
- in_weight_grad: float32 [2048, 3, 2048], P(None, None, 'tp')
- out_weight_grad: float32 [2048, 2048], P('tp')
- gate_up_weight_grad: float32 [2048, 2, 8192], P(None, None, 'tp')
- down_weight_grad: float32 [8192, 2048], P('tp')
The draws below stay inside these ranges and needn't reach their ends.
Inputs may be any that keep to these rules, and one draw needn't show every extreme that they name: `segment_ids`: document numbers never fall along the sequence; the first token's number is 0 and the last token's is 6143.
All inputs are finite; a program needn't handle non-finite values.
Results may differ from the reference program's by a relative error of at most 0.024.
Values may be sent and summed in bfloat16 or wider, within the bound.
A program may use at most 256 MiB of HBM per device.

```python
import jax
import jax.numpy as jnp
from jax import lax

D = 2048
H = 16
HD = 128
FF = 8192
TOK_DEV = 768
DOC = 512
TOKENS = 6144
QBLOCK = 512


def draw_segment_ids(key, part):
    key = jax.random.fold_in(key, 11)
    first, second, third = jax.random.split(key, 3)
    begin = jax.random.randint(first, (), 1, TOK_DEV)
    finish = TOKENS - jax.random.randint(second, (), 1, TOK_DEV)
    place = jnp.arange(TOKENS, dtype=jnp.int32)
    starts = jax.random.randint(third, (TOKENS,), 0, DOC) == 0
    starts = starts & ((place < begin) | (place > finish)) | (place == begin) | (place == finish) | (place == 0)
    counted = jnp.cumsum(starts.astype(jnp.int32)) - 1
    lift = TOKENS - 1 - counted[TOKENS - 1]
    return counted + jnp.where(place >= finish, lift, 0).astype(jnp.int32)


def shard_levels(own_key, dims, shards, least, high):
    factor_of = 1.0
    for dim, shards_of in shards:
        heights = jax.random.uniform(jax.random.fold_in(jax.random.fold_in(own_key, 6), dim), (shards_of,), jnp.float32, least / len(shards), high / len(shards))
        factor_of = factor_of * jnp.repeat(jnp.exp(heights), dims[dim] // shards_of).reshape((-1,) + (1,) * (len(dims) - 1 - dim))
    return factor_of


def normal_values(stream_key, dims, width, bound, cuts=(), kind=jnp.bfloat16):
    array = jax.random.normal(stream_key, dims, jnp.float32) * width
    if len(cuts) > 0:
        array = shard_levels(stream_key, dims, cuts, -0.22, 0.18) * array
    return jnp.clip(array, min=-bound, max=bound).astype(kind)


def setup_inputs(seed: int = 0) -> dict:
    keys = jax.random.split(jax.random.key(seed), 8)
    return {
        "tokens": normal_values(keys[0], (TOKENS, D), 1.0, 6.0, ((0, 8), (1, 4))),
        "segment_ids": draw_segment_ids(jax.random.fold_in(keys[7], 71), 0),
        "in_weight": normal_values(keys[2], (D, 3, D), D ** -0.5, 0.125, ((2, 4),)),
        "out_weight": normal_values(keys[3], (D, D), (max(D // 256, 2)) ** -0.5, 2.0, ((0, 4),)),
        "gate_up_weight": normal_values(keys[4], (D, 2, FF), D ** -0.5, 0.125, ((2, 4),)),
        "down_weight": normal_values(keys[5], (FF, D), FF ** -0.5, 0.0625, ((0, 4),)),
        "cotangent": normal_values(keys[6], (TOKENS, D), 1.0, 6.0, ((0, 8), (1, 4))),
    }


EPS = 1e-05
NEG = -1e+30
HIGH = lax.Precision.HIGHEST

@jax.custom_vjp
def low(v):
    return lax.optimization_barrier(v.astype(jnp.bfloat16)).astype(jnp.float32)

@jax.custom_vjp
def low_back(v):
    return v

def low_keep(v):
    return (low(v), None)

def low_pass(kept, grad):
    return (grad,)

def back_keep(v):
    return (v, None)

def back_low(kept, grad):
    return (low(grad),)
low.defvjp(low_keep, low_pass)
low_back.defvjp(back_keep, back_low)

def norm_rows(values):
    center = values - lax.optimization_barrier(jnp.mean(values, axis=1, keepdims=True))
    spread = lax.optimization_barrier(jnp.mean(center * center, axis=1, keepdims=True))
    return center * lax.rsqrt(spread + EPS)

def rope_tables(count):
    half = HD // 2
    freq = 10000.0 ** (-jnp.arange(half, dtype=jnp.float32) * 2.0 / HD)
    angle = jnp.arange(count, dtype=jnp.float32)[:, None] * freq[None, :]
    angle = jnp.concatenate([angle, angle], axis=1)[:, None, :]
    return (jnp.cos(angle), jnp.sin(angle))

def rotate(values, cosine, sine):
    half = values.shape[-1] // 2
    swapped = jnp.concatenate([-values[..., half:], values[..., :half]], axis=-1)
    return values * cosine + swapped * sine

def attend(query, key, value, segment_ids):
    count = query.shape[0]
    blocks = count // QBLOCK
    scale = HD ** (-0.5)
    key_place = jnp.arange(count, dtype=jnp.int32)

    def one_block(inputs):
        query_block, index = inputs
        start = index * QBLOCK
        query_place = start + jnp.arange(QBLOCK, dtype=jnp.int32)
        query_seg = lax.dynamic_slice_in_dim(segment_ids, start, QBLOCK)
        allowed = ((query_seg[:, None] == segment_ids[None, :]) & (query_place[:, None] >= key_place[None, :]))[None]
        scores = low_back(jnp.einsum('qhd,khd->hqk', query_block, key, precision=HIGH) * scale)
        scores = jnp.where(allowed, scores, NEG)
        highest = lax.optimization_barrier(jnp.max(scores, axis=2, keepdims=True))
        weights = jnp.where(allowed, jnp.exp(scores - highest), 0.0)
        probs = weights / lax.optimization_barrier(jnp.sum(weights, axis=2, keepdims=True))
        return jnp.einsum('hqk,khd->qhd', low(probs), value, precision=HIGH)
    blocked = query.reshape(blocks, QBLOCK, H, HD)
    result = lax.map(jax.checkpoint(one_block), (blocked, jnp.arange(blocks, dtype=jnp.int32)))
    return result.reshape(count, H * HD)

def layer(resid, in_weight, out_weight, gate_up_weight, down_weight, segment_ids):
    count = resid.shape[0]
    inner1 = low(norm_rows(resid))
    projected = low_back(jnp.dot(inner1, in_weight.reshape(D, 3 * D), precision=HIGH)).reshape(count, 3, H, HD)
    cosine, sine = rope_tables(count)
    query = low(rotate(projected[:, 0], cosine, sine))
    key = low(rotate(projected[:, 1], cosine, sine))
    value = low(projected[:, 2])
    mixed = low_back(low(attend(query, key, value, segment_ids)))
    resid1 = resid + low_back(jnp.dot(mixed, out_weight, precision=HIGH))
    inner2 = low(norm_rows(resid1))
    gate_up = low_back(jnp.dot(inner2, gate_up_weight.reshape(D, 2 * FF), precision=HIGH))
    hidden = low(jax.nn.silu(gate_up[:, :FF]) * gate_up[:, FF:])
    return resid1 + low_back(jnp.dot(hidden, down_weight, precision=HIGH))

def reference(tokens, segment_ids, in_weight, out_weight, gate_up_weight, down_weight, cotangent):

    def forward(resid, first, second, third, fourth):
        return layer(resid, first, second, third, fourth, segment_ids)
    result, pullback = jax.vjp(forward, tokens.astype(jnp.float32), in_weight.astype(jnp.float32), out_weight.astype(jnp.float32), gate_up_weight.astype(jnp.float32), down_weight.astype(jnp.float32))
    grads = pullback(cotangent.astype(jnp.float32))
    return (result.astype(jnp.bfloat16), grads[0], grads[1], grads[2], grads[3], grads[4])
```

```python
import functools

import jax
import jax.numpy as jnp
from jax import lax
from jax.experimental import pallas as pl
from jax.experimental.pallas import tpu as pltpu
from jax.sharding import PartitionSpec as P

HD = 128
EPS = 1e-05
NEG = -1e30
SCALE = HD ** (-0.5)
LOG2E = 1.4426950408889634
C2 = SCALE * LOG2E
F32 = jnp.float32
BF16 = jnp.bfloat16
NT = (((1,), (1,)), ((), ()))
TN = (((0,), (0,)), ((), ()))


def params(mib, **more):
    return pltpu.CompilerParams(vmem_limit_bytes=mib << 20, **more)


def cost(flops, nbytes, trans=0):
    return pl.CostEstimate(flops=int(flops), bytes_accessed=int(nbytes), transcendentals=int(trans))


def rope_tables(places):
    half = HD // 2
    freq = 10000.0 ** (-jnp.arange(half, dtype=F32) * 2.0 / HD)
    angle = places.astype(F32)[:, None] * freq[None, :]
    cosine, sine = jnp.cos(angle), jnp.sin(angle)
    return jnp.concatenate([cosine, cosine], axis=1), jnp.concatenate([-sine, sine], axis=1)


def project_kernel(heads, tok_ref, w_ref, cos_ref, sin_ref, inner_ref, stat_ref, q_ref, kv_ref):
    x = tok_ref[...].astype(F32)
    center = x - jnp.mean(x, axis=1, keepdims=True)
    inverse = lax.rsqrt(jnp.mean(center * center, axis=1, keepdims=True) + EPS)
    inner = (center * inverse).astype(BF16)
    inner_ref[...] = inner
    stat_ref[...] = jnp.concatenate(
        [jnp.mean(x, axis=1, keepdims=True), inverse], axis=1
    )
    cosine, sine = cos_ref[...], sin_ref[...]
    span = heads * HD
    for part in range(3):
        out = jnp.dot(inner, w_ref[part], preferred_element_type=F32)
        if part == 2:
            kv_ref[:, span:] = out.astype(BF16)
            continue
        for h in range(heads):
            piece = out[:, h * HD : (h + 1) * HD]
            turned = (piece * cosine + pltpu.roll(piece, HD // 2, 1) * sine).astype(BF16)
            if part == 0:
                q_ref[:, h * HD : (h + 1) * HD] = turned
            else:
                kv_ref[:, h * HD : (h + 1) * HD] = turned


def project(tok_full, weight, cosine, sine, heads):
    rows, width = tok_full.shape
    span = heads * HD
    block = 256
    row = lambda n: pl.BlockSpec((block, n), lambda i: (i, 0))
    return pl.pallas_call(
        functools.partial(project_kernel, heads),
        grid=(rows // block,),
        in_specs=[
            row(width),
            pl.BlockSpec((3, width, span), lambda i: (0, 0, 0)),
            row(HD),
            row(HD),
        ],
        out_specs=[row(width), row(2), row(span), row(2 * span)],
        out_shape=[
            jax.ShapeDtypeStruct((rows, width), BF16),
            jax.ShapeDtypeStruct((rows, 2), F32),
            jax.ShapeDtypeStruct((rows, span), BF16),
            jax.ShapeDtypeStruct((rows, 2 * span), BF16),
        ],
        compiler_params=params(56),
        cost_estimate=cost(6 * rows * width * span, 6 * width * span + 6 * rows * width),
        name="project",
    )(tok_full, weight, cosine, sine)


def masked(scores, j, me, rows, begin):
    key_place = lax.broadcasted_iota(jnp.int32, scores.shape, 0) + j * rows
    query_place = lax.broadcasted_iota(jnp.int32, scores.shape, 1) + me * rows
    return jnp.where((key_place <= query_place) & (key_place >= begin), scores, NEG)


def attend_kernel(
    heads, info, q_ref, k_ref, v_ref, begin_ref, raw_ref, mixed_ref, lse_ref,
    high_ref, total_ref, acc_ref, s_ref,
):
    me, first, clear = info[0], info[1], info[2]
    j = pl.program_id(0)
    rows = q_ref.shape[0]

    @pl.when(j == 0)
    def _():
        high_ref[...] = jnp.full_like(high_ref, NEG)
        total_ref[...] = jnp.zeros_like(total_ref)
        acc_ref[...] = jnp.zeros_like(acc_ref)

    def block(hide):
        def score(h):
            hs = slice(h * HD, (h + 1) * HD)
            s = lax.dot_general(k_ref[:, hs], q_ref[:, hs], NT, preferred_element_type=F32)
            if hide:
                s = masked(s, j, me, rows, begin_ref[...])
            s_ref[h % 2] = s

        def spread(h):
            hs = slice(h * HD, (h + 1) * HD)
            s = s_ref[h % 2]
            old = high_ref[h : h + 1, :]
            new = jnp.maximum(old, jnp.max(s, axis=0, keepdims=True))
            high_ref[h : h + 1, :] = new
            p = jnp.exp2(s * C2 - new * C2)
            decay = jnp.exp2((old - new) * C2)
            total_ref[h : h + 1, :] = total_ref[h : h + 1, :] * decay + jnp.sum(
                p, axis=0, keepdims=True
            )
            acc_ref[h] = acc_ref[h] * decay + lax.dot_general(
                v_ref[:, hs], p.astype(BF16), TN, preferred_element_type=F32
            )

        score(0)
        for h in range(heads):
            if h + 1 < heads:
                score(h + 1)
            spread(h)

    @pl.when((j >= clear) & (j < me))
    def _():
        block(False)

    @pl.when(((j >= first) & (j < clear) & (j < me)) | (j == me))
    def _():
        block(True)

    @pl.when(j == me)
    def _():
        for h in range(heads):
            hs = slice(h * HD, (h + 1) * HD)
            out = (acc_ref[h] / total_ref[h : h + 1, :]).T
            raw_ref[:, hs] = out
            mixed_ref[:, hs] = out.astype(BF16)
        lse_ref[...] = high_ref[...] * C2 + jnp.log2(total_ref[...])


def attend(info, query, pairs, begin, heads):
    rows = query.shape[0]
    total = pairs.shape[0]
    span = heads * HD
    full = lambda shape: pl.BlockSpec(shape, lambda j, s: (0, 0))
    key = pl.BlockSpec((rows, span), lambda j, s: (jnp.clip(j, s[1], s[0]), 0))
    value = pl.BlockSpec((rows, span), lambda j, s: (jnp.clip(j, s[1], s[0]), 1))
    return pl.pallas_call(
        functools.partial(attend_kernel, heads),
        grid_spec=pltpu.PrefetchScalarGridSpec(
            num_scalar_prefetch=1,
            grid=(total // rows,),
            in_specs=[full((rows, span)), key, value, full((1, rows))],
            out_specs=[full((rows, span)), full((rows, span)), full((heads, rows))],
            scratch_shapes=[
                pltpu.VMEM((heads, rows), F32),
                pltpu.VMEM((heads, rows), F32),
                pltpu.VMEM((heads, HD, rows), F32),
                pltpu.VMEM((2, rows, rows), F32),
            ],
        ),
        out_shape=[
            jax.ShapeDtypeStruct((rows, span), F32),
            jax.ShapeDtypeStruct((rows, span), BF16),
            jax.ShapeDtypeStruct((heads, rows), F32),
        ],
        compiler_params=params(56),
        cost_estimate=cost(4 * rows * total * span, 4 * total * span, rows * total * heads),
        name="attend",
    )(info, query, pairs, pairs, begin)


def attend_back_kernel(
    heads, info, q_ref, do_ref, raw_ref, lse_ref, k_ref, v_ref, begin_ref,
    dq_ref, dpair_ref, acc_ref, delta_ref, s_ref, g_ref,
):
    me, first, clear = info[0], info[1], info[2]
    j = pl.program_id(0)
    rows = q_ref.shape[0]
    span = heads * HD

    @pl.when(j == 0)
    def _():
        acc_ref[...] = jnp.zeros_like(acc_ref)
        for h in range(heads):
            hs = slice(h * HD, (h + 1) * HD)
            both = do_ref[:, hs].astype(F32) * raw_ref[:, hs]
            delta_ref[h : h + 1, :] = jnp.sum(both.T, axis=0, keepdims=True)

    def block(hide):
        def score(h):
            hs = slice(h * HD, (h + 1) * HD)
            s = lax.dot_general(k_ref[:, hs], q_ref[:, hs], NT, preferred_element_type=F32)
            if hide:
                s = masked(s, j, me, rows, begin_ref[...])
            s_ref[h % 2] = s
            g_ref[h % 2] = lax.dot_general(
                v_ref[:, hs], do_ref[:, hs], NT, preferred_element_type=F32
            )

        def spread(h):
            hs = slice(h * HD, (h + 1) * HD)
            p = jnp.exp2(s_ref[h % 2] * C2 - lse_ref[h : h + 1, :])
            ds = (p * (g_ref[h % 2] - delta_ref[h : h + 1, :])).astype(BF16)
            dv = jnp.dot(p.astype(BF16), do_ref[:, hs], preferred_element_type=F32)
            dk = jnp.dot(ds, q_ref[:, hs], preferred_element_type=F32)
            dpair_ref[:, hs] = (dk * SCALE).astype(BF16)
            dpair_ref[:, span + h * HD : span + (h + 1) * HD] = dv.astype(BF16)
            acc_ref[h] = acc_ref[h] + lax.dot_general(
                k_ref[:, hs], ds, TN, preferred_element_type=F32
            )

        score(0)
        for h in range(heads):
            if h + 1 < heads:
                score(h + 1)
            spread(h)

    @pl.when((j >= clear) & (j < me))
    def _():
        block(False)

    @pl.when(((j >= first) & (j < clear) & (j < me)) | (j == me))
    def _():
        block(True)

    @pl.when((j < first) | (j > me))
    def _():
        dpair_ref[...] = jnp.zeros_like(dpair_ref)

    @pl.when(j == me)
    def _():
        for h in range(heads):
            dq_ref[:, h * HD : (h + 1) * HD] = (acc_ref[h] * SCALE).T


def attend_back(info, query, grad_mixed, raw, lse, pairs, begin, heads):
    rows = query.shape[0]
    total = pairs.shape[0]
    span = heads * HD
    full = lambda shape: pl.BlockSpec(shape, lambda j, s: (0, 0))
    key = pl.BlockSpec((rows, span), lambda j, s: (jnp.clip(j, s[1], s[0]), 0))
    value = pl.BlockSpec((rows, span), lambda j, s: (jnp.clip(j, s[1], s[0]), 1))
    wide = full((rows, span))
    return pl.pallas_call(
        functools.partial(attend_back_kernel, heads),
        grid_spec=pltpu.PrefetchScalarGridSpec(
            num_scalar_prefetch=1,
            grid=(total // rows,),
            in_specs=[wide, wide, wide, full((heads, rows)), key, value, full((1, rows))],
            out_specs=[wide, pl.BlockSpec((rows, 2 * span), lambda j, s: (j, 0))],
            scratch_shapes=[
                pltpu.VMEM((heads, HD, rows), F32),
                pltpu.VMEM((heads, rows), F32),
                pltpu.VMEM((2, rows, rows), F32),
                pltpu.VMEM((2, rows, rows), F32),
            ],
        ),
        out_shape=[
            jax.ShapeDtypeStruct((rows, span), F32),
            jax.ShapeDtypeStruct((total, 2 * span), BF16),
        ],
        compiler_params=params(58),
        cost_estimate=cost(10 * rows * total * span, 8 * total * span, rows * total * heads),
        name="attend_back",
    )(info, query, grad_mixed, raw, lse, pairs, pairs, begin)


def merge_kernel(mixed_ref, w_ref, tok_ref, resid_ref, stat_ref, inner_ref):
    out = jnp.dot(mixed_ref[...], w_ref[...], preferred_element_type=F32)
    x = tok_ref[...].astype(F32) + out
    resid_ref[...] = x
    mean = jnp.mean(x, axis=1, keepdims=True)
    center = x - mean
    inverse = lax.rsqrt(jnp.mean(center * center, axis=1, keepdims=True) + EPS)
    stat_ref[...] = jnp.concatenate([mean, inverse], axis=1)
    inner_ref[...] = (center * inverse).astype(BF16)


def merge(mixed_full, weight, tok_full):
    rows, width = tok_full.shape
    block = 256
    row = lambda n: pl.BlockSpec((block, n), lambda i: (i, 0))
    return pl.pallas_call(
        merge_kernel,
        grid=(rows // block,),
        in_specs=[row(width), pl.BlockSpec((width, width), lambda i: (0, 0)), row(width)],
        out_specs=[row(width), row(2), row(width)],
        out_shape=[
            jax.ShapeDtypeStruct((rows, width), F32),
            jax.ShapeDtypeStruct((rows, 2), F32),
            jax.ShapeDtypeStruct((rows, width), BF16),
        ],
        compiler_params=params(56),
        cost_estimate=cost(2 * rows * width * width, 2 * width * width + 10 * rows * width),
        name="merge",
    )(mixed_full, weight, tok_full)


def unproject_kernel(
    heads, dq_ref, dpair_ref, cos_ref, sin_ref, tok_ref, stat_ref, w_ref,
    dproj_ref, part_ref, sums_ref,
):
    cosine, sine = cos_ref[...], sin_ref[...]
    span = heads * HD

    def back(piece):
        return piece * cosine - pltpu.roll(piece, HD // 2, 1) * sine

    for h in range(heads):
        hs = slice(h * HD, (h + 1) * HD)
        dproj_ref[:, hs] = back(dq_ref[:, hs]).astype(BF16)
        dproj_ref[:, span + h * HD : span + (h + 1) * HD] = back(
            dpair_ref[:, hs].astype(F32)
        ).astype(BF16)
    dproj_ref[:, 2 * span :] = dpair_ref[:, span:]
    total = None
    for part in range(3):
        term = lax.dot_general(
            dproj_ref[:, part * span : (part + 1) * span], w_ref[part], NT,
            preferred_element_type=F32,
        )
        total = term if total is None else total + term
    part_ref[...] = total.astype(BF16)
    normed = (tok_ref[...].astype(F32) - stat_ref[:, 0:1]) * stat_ref[:, 1:2]
    sums_ref[...] = jnp.concatenate(
        [
            jnp.sum(total, axis=1, keepdims=True),
            jnp.sum(total * normed, axis=1, keepdims=True),
        ],
        axis=1,
    )


def unproject(dq, own_pairs, cosine, sine, tok_full, stat, weight, heads):
    rows, width = tok_full.shape
    span = heads * HD
    block = 256
    row = lambda n: pl.BlockSpec((block, n), lambda i: (i, 0))
    return pl.pallas_call(
        functools.partial(unproject_kernel, heads),
        grid=(rows // block,),
        in_specs=[
            row(span), row(2 * span), row(HD), row(HD), row(width), row(2),
            pl.BlockSpec((3, width, span), lambda i: (0, 0, 0)),
        ],
        out_specs=[row(3 * span), row(width), row(2)],
        out_shape=[
            jax.ShapeDtypeStruct((rows, 3 * span), BF16),
            jax.ShapeDtypeStruct((rows, width), BF16),
            jax.ShapeDtypeStruct((rows, 2), F32),
        ],
        compiler_params=params(56),
        cost_estimate=cost(6 * rows * width * span, 6 * width * span + 6 * rows * width),
        name="unproject",
    )(dq, own_pairs, cosine, sine, tok_full, stat, weight)


def per_device(tokens, segment_ids, in_weight, out_weight, gate_up_weight, down_weight, cotangent):
    rows, shard = tokens.shape
    width = in_weight.shape[0]
    span = in_weight.shape[2]
    heads = span // HD
    hidden_local = down_weight.shape[0]
    me = lax.axis_index("ctx")
    tp_at = lax.axis_index("tp")

    def own(whole):
        return lax.dynamic_slice_in_dim(whole, tp_at * shard, shard, axis=1)

    def gather(local, axis=1):
        return lax.all_gather(local, "tp", axis=axis, tiled=True)

    places = me * rows + jnp.arange(rows, dtype=jnp.int32)
    cosine, sine = rope_tables(places)
    in_w = jnp.transpose(in_weight, (1, 0, 2))
    gate_w, up_w = lax.optimization_barrier((gate_up_weight[:, 0, :], gate_up_weight[:, 1, :]))

    all_seg = lax.all_gather(segment_ids, "ctx", axis=0, tiled=True)
    before = jnp.sum((all_seg < segment_ids[0]).astype(jnp.int32))
    own_begin = me * rows + jnp.sum(
        (segment_ids[None, :] < segment_ids[:, None]).astype(jnp.int32), axis=1
    )
    begin = jnp.where(segment_ids == segment_ids[0], before, own_begin).astype(jnp.int32)
    last = jnp.max(begin)
    info = jnp.stack([me, before // rows, (last + rows - 1) // rows]).astype(jnp.int32)
    begin = begin[None, :]

    tok_full = gather(tokens)
    inner1, stat1, query, pairs = project(tok_full, in_w, cosine, sine, heads)
    all_pairs = lax.all_gather(pairs, "ctx", axis=0, tiled=True)
    out_full = gather(out_weight, 0)
    cot_full = gather(cotangent)
    raw, mixed, lse = attend(info, query, all_pairs, begin, heads)
    resid1, stat2, inner2 = merge(gather(mixed), out_full, tok_full)

    gate = jnp.dot(inner2, gate_w, preferred_element_type=F32)
    up = jnp.dot(inner2, up_w, preferred_element_type=F32)
    sigma = jax.nn.sigmoid(gate)
    active = gate * sigma
    hidden = (active * up).astype(BF16)
    branch = jnp.dot(hidden, down_weight, preferred_element_type=F32).astype(BF16)
    branch = lax.psum_scatter(branch, "tp", scatter_dimension=1, tiled=True)
    layer_out = (own(resid1) + branch.astype(F32)).astype(BF16)

    grad_hidden = lax.dot_general(cot_full, down_weight, NT, preferred_element_type=F32)
    grad_gate = (grad_hidden * up * sigma * (1.0 + gate * (1.0 - sigma))).astype(BF16)
    grad_up = (grad_hidden * active).astype(BF16)
    grad_normed2 = lax.dot_general(
        grad_gate, gate_w, NT, preferred_element_type=F32
    ) + lax.dot_general(grad_up, up_w, NT, preferred_element_type=F32)
    grad_normed2 = lax.psum(grad_normed2.astype(BF16), "tp").astype(F32)

    down_grad = lax.dot_general(hidden, cot_full, TN, preferred_element_type=F32)
    gate_grad = lax.dot_general(inner2, grad_gate, TN, preferred_element_type=F32)
    up_grad = lax.dot_general(inner2, grad_up, TN, preferred_element_type=F32)
    down_grad, gate_grad, up_grad = lax.optimization_barrier(
        lax.psum(
            lax.optimization_barrier(
                (down_grad.astype(BF16), gate_grad.astype(BF16), up_grad.astype(BF16))
            ),
            "ctx",
        )
    )

    normed2 = (resid1 - stat2[:, 0:1]) * stat2[:, 1:2]
    mean_g = jnp.mean(grad_normed2, axis=1, keepdims=True)
    mean_gn = jnp.mean(grad_normed2 * normed2, axis=1, keepdims=True)
    resid1_grad = cot_full.astype(F32) + stat2[:, 1:2] * (
        grad_normed2 - mean_g - normed2 * mean_gn
    )
    branch_grad = resid1_grad.astype(BF16)
    grad_mixed = lax.dot_general(
        branch_grad, out_weight, NT, preferred_element_type=F32
    ).astype(BF16)
    out_grad = lax.dot_general(mixed, branch_grad, TN, preferred_element_type=F32).astype(BF16)

    dq, dpairs = attend_back(info, query, grad_mixed, raw, lse, all_pairs, begin, heads)
    own_pairs = lax.psum_scatter(dpairs, "ctx", scatter_dimension=0, tiled=True)
    dproj, part, sums = unproject(dq, own_pairs, cosine, sine, tok_full, stat1, in_w, heads)
    grad_normed1 = lax.psum_scatter(part, "tp", scatter_dimension=1, tiled=True).astype(F32)
    sums = lax.psum(sums, "tp") / width
    in_grad = jnp.stack(
        [
            lax.dot_general(
                inner1, dproj[:, i * span : (i + 1) * span], TN, preferred_element_type=F32
            ).astype(BF16)
            for i in range(3)
        ]
    )
    in_grad, out_grad, down_grad = lax.optimization_barrier((in_grad, out_grad, down_grad))
    in_grad, out_grad = lax.psum((in_grad, out_grad), "ctx")

    normed1 = (tokens.astype(F32) - stat1[:, 0:1]) * stat1[:, 1:2]
    tokens_grad = own(resid1_grad) + stat1[:, 1:2] * (
        grad_normed1 - sums[:, 0:1] - normed1 * sums[:, 1:2]
    )
    return (
        layer_out,
        tokens_grad,
        jnp.transpose(in_grad, (1, 0, 2)).astype(F32),
        out_grad.astype(F32),
        jnp.stack([gate_grad.astype(F32), up_grad.astype(F32)], axis=1),
        down_grad.astype(F32),
    )


def solution(mesh):
    placed = (
        P("ctx", "tp"),
        P("ctx"),
        P(None, None, "tp"),
        P("tp", None),
        P(None, None, "tp"),
        P("tp", None),
        P("ctx", "tp"),
    )
    return jax.shard_map(
        per_device,
        mesh=mesh,
        in_specs=placed,
        out_specs=(
            P("ctx", "tp"),
            P("ctx", "tp"),
            P(None, None, "tp"),
            P("tp", None),
            P(None, None, "tp"),
            P("tp", None),
        ),
        check_vma=False,
    )
```

```python
import functools

import jax
import jax.numpy as jnp
from jax import lax
from jax.experimental import pallas as pl
from jax.experimental.pallas import tpu as pltpu
from jax.sharding import PartitionSpec as P

HD = 128
EPS = 1e-05
NEG = -1e30
SCALE = HD ** (-0.5)
LOG2E = 1.4426950408889634
C2 = SCALE * LOG2E
F32 = jnp.float32
BF16 = jnp.bfloat16
NT = (((1,), (1,)), ((), ()))
TN = (((0,), (0,)), ((), ()))
MESH = pl.DeviceIdType.MESH
BLOCK = 512


def params(mib, **more):
    return pltpu.CompilerParams(vmem_limit_bytes=mib << 20, **more)


def cost(flops, nbytes, trans=0):
    return pl.CostEstimate(flops=int(flops), bytes_accessed=int(nbytes), transcendentals=int(trans))


def rope_tables(places):
    half = HD // 2
    freq = 10000.0 ** (-jnp.arange(half, dtype=F32) * 2.0 / HD)
    angle = places.astype(F32)[:, None] * freq[None, :]
    cosine, sine = jnp.cos(angle), jnp.sin(angle)
    return jnp.concatenate([cosine, cosine], axis=1), jnp.concatenate([-sine, sine], axis=1)


def project_kernel(heads, tok_ref, w_ref, cos_ref, sin_ref, inner_ref, stat_ref, q_ref, kv_ref):
    x = tok_ref[...].astype(F32)
    center = x - jnp.mean(x, axis=1, keepdims=True)
    inverse = lax.rsqrt(jnp.mean(center * center, axis=1, keepdims=True) + EPS)
    inner = (center * inverse).astype(BF16)
    inner_ref[...] = inner
    stat_ref[...] = jnp.concatenate(
        [jnp.mean(x, axis=1, keepdims=True), inverse], axis=1
    )
    cosine, sine = cos_ref[...], sin_ref[...]
    span = heads * HD
    for part in range(3):
        out = jnp.dot(inner, w_ref[part], preferred_element_type=F32)
        if part == 2:
            kv_ref[:, span:] = out.astype(BF16)
            continue
        for h in range(heads):
            piece = out[:, h * HD : (h + 1) * HD]
            turned = (piece * cosine + pltpu.roll(piece, HD // 2, 1) * sine).astype(BF16)
            if part == 0:
                q_ref[:, h * HD : (h + 1) * HD] = turned
            else:
                kv_ref[:, h * HD : (h + 1) * HD] = turned


def project(tok_full, weight, cosine, sine, heads):
    rows, width = tok_full.shape
    span = heads * HD
    block = 256
    row = lambda n: pl.BlockSpec((block, n), lambda i: (i, 0))
    return pl.pallas_call(
        functools.partial(project_kernel, heads),
        grid=(rows // block,),
        in_specs=[
            row(width),
            pl.BlockSpec((3, width, span), lambda i: (0, 0, 0)),
            row(HD),
            row(HD),
        ],
        out_specs=[row(width), row(2), row(span), row(2 * span)],
        out_shape=[
            jax.ShapeDtypeStruct((rows, width), BF16),
            jax.ShapeDtypeStruct((rows, 2), F32),
            jax.ShapeDtypeStruct((rows, span), BF16),
            jax.ShapeDtypeStruct((rows, 2 * span), BF16),
        ],
        compiler_params=params(56),
        cost_estimate=cost(6 * rows * width * span, 6 * width * span + 6 * rows * width),
        name="project",
    )(tok_full, weight, cosine, sine)


def masked(scores, j, me, rows, begin):
    key_place = lax.broadcasted_iota(jnp.int32, scores.shape, 0) + j * rows
    query_place = lax.broadcasted_iota(jnp.int32, scores.shape, 1) + me * rows
    return jnp.where((key_place <= query_place) & (key_place >= begin), scores, NEG)


def attend_kernel(
    heads, info, q_ref, k_ref, v_ref, begin_ref, raw_ref, mixed_ref, lse_ref,
    high_ref, total_ref, acc_ref, s_ref,
):
    me, first, clear = info[0], info[1], info[2]
    j = pl.program_id(0)
    rows = q_ref.shape[0]

    @pl.when(j == 0)
    def _():
        high_ref[...] = jnp.full_like(high_ref, NEG)
        total_ref[...] = jnp.zeros_like(total_ref)
        acc_ref[...] = jnp.zeros_like(acc_ref)

    def block(hide):
        def score(h):
            hs = slice(h * HD, (h + 1) * HD)
            s = lax.dot_general(k_ref[:, hs], q_ref[:, hs], NT, preferred_element_type=F32)
            if hide:
                s = masked(s, j, me, rows, begin_ref[...])
            s_ref[h % 2] = s

        def spread(h):
            hs = slice(h * HD, (h + 1) * HD)
            s = s_ref[h % 2]
            old = high_ref[h : h + 1, :]
            new = jnp.maximum(old, jnp.max(s, axis=0, keepdims=True))
            high_ref[h : h + 1, :] = new
            p = jnp.exp2(s * C2 - new * C2)
            decay = jnp.exp2((old - new) * C2)
            total_ref[h : h + 1, :] = total_ref[h : h + 1, :] * decay + jnp.sum(
                p, axis=0, keepdims=True
            )
            acc_ref[h] = acc_ref[h] * decay + lax.dot_general(
                v_ref[:, hs], p.astype(BF16), TN, preferred_element_type=F32
            )

        score(0)
        for h in range(heads):
            if h + 1 < heads:
                score(h + 1)
            spread(h)

    @pl.when((j >= clear) & (j < me))
    def _():
        block(False)

    @pl.when(((j >= first) & (j < clear) & (j < me)) | (j == me))
    def _():
        block(True)

    @pl.when(j == me)
    def _():
        for h in range(heads):
            hs = slice(h * HD, (h + 1) * HD)
            out = (acc_ref[h] / total_ref[h : h + 1, :]).T
            raw_ref[:, hs] = out
            mixed_ref[:, hs] = out.astype(BF16)
        lse_ref[...] = high_ref[...] * C2 + jnp.log2(total_ref[...])


def attend(info, query, pairs, begin, heads):
    rows = query.shape[0]
    total = pairs.shape[0]
    span = heads * HD
    full = lambda shape: pl.BlockSpec(shape, lambda j, s: (0, 0))
    key = pl.BlockSpec((rows, span), lambda j, s: (jnp.clip(j, s[1], s[0]), 0))
    value = pl.BlockSpec((rows, span), lambda j, s: (jnp.clip(j, s[1], s[0]), 1))
    return pl.pallas_call(
        functools.partial(attend_kernel, heads),
        grid_spec=pltpu.PrefetchScalarGridSpec(
            num_scalar_prefetch=1,
            grid=(total // rows,),
            in_specs=[full((rows, span)), key, value, full((1, rows))],
            out_specs=[full((rows, span)), full((rows, span)), full((heads, rows))],
            scratch_shapes=[
                pltpu.VMEM((heads, rows), F32),
                pltpu.VMEM((heads, rows), F32),
                pltpu.VMEM((heads, HD, rows), F32),
                pltpu.VMEM((2, rows, rows), F32),
            ],
        ),
        out_shape=[
            jax.ShapeDtypeStruct((rows, span), F32),
            jax.ShapeDtypeStruct((rows, span), BF16),
            jax.ShapeDtypeStruct((heads, rows), F32),
        ],
        compiler_params=params(56),
        cost_estimate=cost(4 * rows * total * span, 4 * total * span, rows * total * heads),
        name="attend",
    )(info, query, pairs, pairs, begin)


def query_grad_kernel(
    heads, info, q_ref, do_ref, lse_ref, delta_ref, k_ref, v_ref, begin_ref,
    dq_ref, acc_ref, s_ref, g_ref,
):
    me, first, clear = info[0], info[1], info[2]
    j = pl.program_id(0)
    rows = q_ref.shape[0]

    @pl.when(j == 0)
    def _():
        acc_ref[...] = jnp.zeros_like(acc_ref)

    def block(hide):
        def score(h):
            hs = slice(h * HD, (h + 1) * HD)
            s = lax.dot_general(k_ref[:, hs], q_ref[:, hs], NT, preferred_element_type=F32)
            if hide:
                s = masked(s, j, me, rows, begin_ref[...])
            s_ref[h % 2] = s
            g_ref[h % 2] = lax.dot_general(
                v_ref[:, hs], do_ref[:, hs], NT, preferred_element_type=F32
            )

        def spread(h):
            hs = slice(h * HD, (h + 1) * HD)
            p = jnp.exp2(s_ref[h % 2] * C2 - lse_ref[h : h + 1, :])
            ds = (p * (g_ref[h % 2] - delta_ref[h : h + 1, :])).astype(BF16)
            acc_ref[h] = acc_ref[h] + lax.dot_general(
                k_ref[:, hs], ds, TN, preferred_element_type=F32
            )

        score(0)
        for h in range(heads):
            if h + 1 < heads:
                score(h + 1)
            spread(h)

    @pl.when((j >= clear) & (j < me))
    def _():
        block(False)

    @pl.when(((j >= first) & (j < clear) & (j < me)) | (j == me))
    def _():
        block(True)

    @pl.when(j == me)
    def _():
        for h in range(heads):
            dq_ref[:, h * HD : (h + 1) * HD] = (acc_ref[h] * SCALE).T


def query_grad(info, query, grad_mixed, lse, delta, pairs, begin, heads):
    rows = query.shape[0]
    total = pairs.shape[0]
    span = heads * HD
    full = lambda shape: pl.BlockSpec(shape, lambda j, s: (0, 0))
    key = pl.BlockSpec((rows, span), lambda j, s: (jnp.clip(j, s[1], s[0]), 0))
    value = pl.BlockSpec((rows, span), lambda j, s: (jnp.clip(j, s[1], s[0]), 1))
    wide = full((rows, span))
    thin = full((heads, rows))
    return pl.pallas_call(
        functools.partial(query_grad_kernel, heads),
        grid_spec=pltpu.PrefetchScalarGridSpec(
            num_scalar_prefetch=1,
            grid=(total // rows,),
            in_specs=[wide, wide, thin, thin, key, value, full((1, rows))],
            out_specs=wide,
            scratch_shapes=[
                pltpu.VMEM((heads, HD, rows), F32),
                pltpu.VMEM((2, rows, rows), F32),
                pltpu.VMEM((2, rows, rows), F32),
            ],
        ),
        out_shape=jax.ShapeDtypeStruct((rows, span), F32),
        compiler_params=params(58),
        cost_estimate=cost(6 * rows * total * span, 4 * total * span, rows * total * heads),
        name="query_grad",
    )(info, query, grad_mixed, lse, delta, pairs, pairs, begin)


def key_grad_kernel(
    heads, info, k_ref, v_ref, q_ref, g_ref, begin_ref, dk_ref, dv_ref,
    rows_ref, s_ref, p_ref,
):
    me, last, clear = info[0], info[1], info[2]
    j = pl.program_id(0)
    rows = k_ref.shape[0]
    span = heads * HD

    @pl.when(j == me)
    def _():
        dk_ref[...] = jnp.zeros_like(dk_ref)
        dv_ref[...] = jnp.zeros_like(dv_ref)

    def block(hide):
        coded = g_ref[:, span:].astype(F32).T
        for n in range(2 * heads):
            rows_ref[n : n + 1, :] = (
                coded[3 * n : 3 * n + 1] + coded[3 * n + 1 : 3 * n + 2] + coded[3 * n + 2 : 3 * n + 3]
            )

        def score(h):
            hs = slice(h * HD, (h + 1) * HD)
            s = lax.dot_general(k_ref[:, hs], q_ref[:, hs], NT, preferred_element_type=F32)
            if hide:
                key_place = lax.broadcasted_iota(jnp.int32, s.shape, 0) + me * rows
                query_place = lax.broadcasted_iota(jnp.int32, s.shape, 1) + j * rows
                s = jnp.where(
                    (key_place <= query_place) & (key_place >= begin_ref[...]), s, NEG
                )
            s_ref[h % 2] = s
            p_ref[h % 2] = lax.dot_general(
                v_ref[:, hs], g_ref[:, hs], NT, preferred_element_type=F32
            )

        def spread(h):
            hs = slice(h * HD, (h + 1) * HD)
            p = jnp.exp2(s_ref[h % 2] * C2 - rows_ref[h : h + 1, :])
            ds = (p * (p_ref[h % 2] - rows_ref[heads + h : heads + h + 1, :])).astype(BF16)
            dv_ref[:, hs] += jnp.dot(p.astype(BF16), g_ref[:, hs], preferred_element_type=F32)
            dk_ref[:, hs] += jnp.dot(ds, q_ref[:, hs], preferred_element_type=F32)

        score(0)
        for h in range(heads):
            if h + 1 < heads:
                score(h + 1)
            spread(h)

    @pl.when((j > me) & (j <= clear))
    def _():
        block(False)

    @pl.when((j == me) | ((j > me) & (j > clear) & (j <= last)))
    def _():
        block(True)

    @pl.when(j == pl.num_programs(0) - 1)
    def _():
        dk_ref[...] = dk_ref[...] * SCALE


def key_grad(info, pairs, all_query, all_grad, all_begin, heads):
    rows = pairs.shape[0]
    total = all_query.shape[0]
    span = heads * HD
    full = lambda shape, at=0: pl.BlockSpec(shape, lambda j, s: (0, at))
    near = lambda j, s: (jnp.clip(j, s[0], s[1]), 0)
    wide = full((rows, span))
    return pl.pallas_call(
        functools.partial(key_grad_kernel, heads),
        grid_spec=pltpu.PrefetchScalarGridSpec(
            num_scalar_prefetch=1,
            grid=(total // rows,),
            in_specs=[
                wide, full((rows, span), 1),
                pl.BlockSpec((rows, span), near),
                pl.BlockSpec((rows, span + HD), near),
                pl.BlockSpec((1, rows), lambda j, s: (0, jnp.clip(j, s[0], s[1]))),
            ],
            out_specs=[wide, wide],
            scratch_shapes=[
                pltpu.VMEM((2 * heads, rows), F32),
                pltpu.VMEM((2, rows, rows), F32),
                pltpu.VMEM((2, rows, rows), F32),
            ],
        ),
        out_shape=[jax.ShapeDtypeStruct((rows, span), F32)] * 2,
        compiler_params=params(58),
        cost_estimate=cost(8 * rows * total * span, 4 * total * span, rows * total * heads),
        name="key_grad",
    )(info, pairs, pairs, all_query, all_grad, all_begin)


def mixed_grad_kernel(heads, branch_ref, w_ref, raw_ref, lse_ref, out_ref, delta_ref):
    span = heads * HD
    low = lax.dot_general(
        branch_ref[...], w_ref[...], NT, preferred_element_type=F32
    ).astype(BF16)
    out_ref[:, :span] = low
    count = low.shape[0]
    both = low.astype(F32) * raw_ref[...]
    for h in range(heads):
        delta_ref[h : h + 1, :] = jnp.sum(both[:, h * HD : (h + 1) * HD].T, axis=0, keepdims=True)
    lines = []
    for n in range(2 * heads):
        value = lse_ref[n : n + 1, :] if n < heads else delta_ref[n - heads : n - heads + 1, :]
        for _ in range(3):
            piece = value.astype(BF16).astype(F32)
            lines.append(piece)
            value = value - piece
    lines.append(jnp.zeros((HD - len(lines), count), F32))
    out_ref[:, span:] = jnp.concatenate(lines, axis=0).T.astype(BF16)


def mixed_grad(branch, weight, raw, lse, heads):
    rows, width = branch.shape
    span = heads * HD
    block = 256
    row = lambda n: pl.BlockSpec((block, n), lambda i: (i, 0))
    line = pl.BlockSpec((heads, block), lambda i: (0, i))
    return pl.pallas_call(
        functools.partial(mixed_grad_kernel, heads),
        grid=(rows // block,),
        in_specs=[row(width), pl.BlockSpec((span, width), lambda i: (0, 0)), row(span), line],
        out_specs=[row(span + HD), line],
        out_shape=[
            jax.ShapeDtypeStruct((rows, span + HD), BF16),
            jax.ShapeDtypeStruct((heads, rows), F32),
        ],
        compiler_params=params(56),
        cost_estimate=cost(2 * rows * width * span, 2 * width * span + 4 * rows * width),
        name="mixed_grad",
    )(branch, weight, raw, lse)


def merge_kernel(mixed_ref, w_ref, tok_ref, resid_ref, stat_ref, inner_ref):
    out = jnp.dot(mixed_ref[...], w_ref[...], preferred_element_type=F32)
    x = tok_ref[...].astype(F32) + out
    resid_ref[...] = x
    mean = jnp.mean(x, axis=1, keepdims=True)
    center = x - mean
    inverse = lax.rsqrt(jnp.mean(center * center, axis=1, keepdims=True) + EPS)
    stat_ref[...] = jnp.concatenate([mean, inverse], axis=1)
    inner_ref[...] = (center * inverse).astype(BF16)


def merge(mixed_full, weight, tok_full):
    rows, width = tok_full.shape
    block = 256
    row = lambda n: pl.BlockSpec((block, n), lambda i: (i, 0))
    return pl.pallas_call(
        merge_kernel,
        grid=(rows // block,),
        in_specs=[row(width), pl.BlockSpec((width, width), lambda i: (0, 0)), row(width)],
        out_specs=[row(width), row(2), row(width)],
        out_shape=[
            jax.ShapeDtypeStruct((rows, width), F32),
            jax.ShapeDtypeStruct((rows, 2), F32),
            jax.ShapeDtypeStruct((rows, width), BF16),
        ],
        compiler_params=params(56),
        cost_estimate=cost(2 * rows * width * width, 2 * width * width + 10 * rows * width),
        name="merge",
    )(mixed_full, weight, tok_full)


def feed_kernel(inner_ref, cot_ref, w_ref, down_ref, hidden_ref, dgu_ref):
    block = down_ref.shape[0]
    both = jnp.dot(inner_ref[...], w_ref[...], preferred_element_type=F32)
    grad = lax.dot_general(cot_ref[...], down_ref[...], NT, preferred_element_type=F32)
    gate, up = both[:, :block], both[:, block:]
    sigma = 1.0 / (1.0 + jnp.exp(-gate))
    active = gate * sigma
    hidden_ref[...] = (active * up).astype(BF16)
    dgu_ref[:, :block] = (grad * up * sigma * (1.0 + gate * (1.0 - sigma))).astype(BF16)
    dgu_ref[:, block:] = (grad * active).astype(BF16)


def feed(inner, cot, weight, down, block):
    rows, width = inner.shape
    units = down.shape[0]
    whole = pl.BlockSpec((rows, width), lambda j: (0, 0))
    return pl.pallas_call(
        feed_kernel,
        grid=(units // block,),
        in_specs=[
            whole, whole,
            pl.BlockSpec((width, 2 * block), lambda j: (0, j)),
            pl.BlockSpec((block, width), lambda j: (j, 0)),
        ],
        out_specs=[
            pl.BlockSpec((rows, block), lambda j: (0, j)),
            pl.BlockSpec((rows, 2 * block), lambda j: (0, j)),
        ],
        out_shape=[
            jax.ShapeDtypeStruct((rows, units), BF16),
            jax.ShapeDtypeStruct((rows, 2 * units), BF16),
        ],
        compiler_params=params(56),
        cost_estimate=cost(
            6 * rows * width * units, 6 * width * units + 4 * rows * width, rows * units
        ),
        name="feed",
    )(inner, cot, weight, down)


def weave_kernel(block, sum_ref, out_ref):
    for j in range(sum_ref.shape[1] // (2 * block)):
        for k in range(2):
            at = (2 * j + k) * block
            out_ref[:, k, j * block : (j + 1) * block] = sum_ref[:, at : at + block].astype(F32)


def weave(summed, block):
    width, both = summed.shape
    rows = 256
    return pl.pallas_call(
        functools.partial(weave_kernel, block),
        grid=(width // rows,),
        in_specs=[pl.BlockSpec((rows, both), lambda i: (i, 0))],
        out_specs=pl.BlockSpec((rows, 2, both // 2), lambda i: (i, 0, 0)),
        out_shape=jax.ShapeDtypeStruct((width, 2, both // 2), F32),
        compiler_params=params(56),
        cost_estimate=cost(width * both, 6 * width * both),
        name="weave",
    )(summed)


def line_barrier(at, n):
    barrier = pltpu.get_barrier_semaphore()

    @pl.when(at > 0)
    def _():
        pl.semaphore_signal(barrier, inc=1, device_id={"tp": at - 1}, device_id_type=MESH)

    @pl.when(at < n - 1)
    def _():
        pl.semaphore_signal(barrier, inc=1, device_id={"tp": at + 1}, device_id_type=MESH)

    pl.semaphore_wait(barrier, jnp.where((at > 0) & (at < n - 1), 2, 1))


def sum_rows(n, sub, part_ref, out_ref, row_fn, from_left, from_right, send, recv):
    at = lax.axis_index("tp")
    chunks = part_ref.shape[0] // sub
    middle = (n // 2 - 1, n // 2)

    def link(kind, right, src, dst, c):
        which = (kind * 2 + (1 if right else 0), c)
        return pltpu.make_async_remote_copy(
            src_ref=src.at[pl.ds(c * sub, sub)],
            dst_ref=dst.at[pl.ds(c * sub, sub)],
            send_sem=send.at[which],
            recv_sem=recv.at[which],
            device_id={"tp": at + 1 if right else at - 1},
            device_id_type=MESH,
        )

    def came(right):
        return from_left if right else from_right

    def first(right, c):
        return link(0, right, part_ref, came(right), c)

    def onward(right, c):
        return link(0, right, came(right), came(right), c)

    def hand(right, c):
        return link(1, right, out_ref, out_ref, c)

    def reduce_step(c):
        owner = middle[c % 2]
        rows = slice(c * sub, (c + 1) * sub)
        for right in (True, False):
            edge = 0 if right else n - 1
            held = came(right)

            @pl.when(at == edge)
            def _():
                first(right, c).start()

            @pl.when(((at < owner) if right else (at > owner)) & (at != edge))
            def _():
                copy = onward(right, c)
                copy.wait_recv()
                held[rows, :] = (
                    held[rows, :].astype(F32) + part_ref[rows, :].astype(F32)
                ).astype(BF16)
                copy.start()

    def final_step(c):
        owner = middle[c % 2]
        rows = slice(c * sub, (c + 1) * sub)

        @pl.when(at == owner)
        def _():
            total = part_ref[rows, :].astype(F32)
            onward(True, c).wait_recv()
            total = total + from_left[rows, :].astype(F32)
            onward(False, c).wait_recv()
            total = total + from_right[rows, :].astype(F32)
            row_fn(total, rows)
            hand(True, c).start()
            hand(False, c).start()

    def hand_step(c):
        owner = middle[c % 2]
        for right in (True, False):
            edge = n - 1 if right else 0

            @pl.when((at > owner) if right else (at < owner))
            def _():
                copy = hand(right, c)
                copy.wait_recv()

                @pl.when(at != edge)
                def _():
                    copy.start()

    for c in range(chunks + 4):
        if c < chunks:
            reduce_step(c)
        if 2 <= c < chunks + 2:
            final_step(c - 2)
        if c >= 4:
            hand_step(c - 4)
    for c in range(chunks):
        owner = middle[c % 2]

        @pl.when(at < owner)
        def _():
            first(True, c).wait_send()

        @pl.when(at > owner)
        def _():
            first(False, c).wait_send()

        @pl.when((at >= owner) & (at < n - 1))
        def _():
            hand(True, c).wait_send()

        @pl.when((at <= owner) & (at > 0))
        def _():
            hand(False, c).wait_send()


def norm_back_kernel(
    n, sub, part_ref, cot_ref, resid_ref, stat_ref, out_ref, from_left, from_right, send, recv
):
    line_barrier(lax.axis_index("tp"), n)

    def row_fn(total, rows):
        inverse = stat_ref[rows, 1:2]
        normed = (resid_ref[rows, :] - stat_ref[rows, 0:1]) * inverse
        mean = jnp.mean(total, axis=1, keepdims=True)
        inner = jnp.mean(total * normed, axis=1, keepdims=True)
        out = cot_ref[rows, :].astype(F32) + inverse * (total - mean - normed * inner)
        out_ref[rows, :] = out.astype(BF16)

    sum_rows(n, sub, part_ref, out_ref, row_fn, from_left, from_right, send, recv)


def norm_back(part, cot, resid, stat, n):
    rows, width = part.shape
    sub = 48
    vmem = pl.BlockSpec(memory_space=pltpu.VMEM)
    return pl.pallas_call(
        functools.partial(norm_back_kernel, n, sub),
        in_specs=[vmem] * 4,
        out_specs=vmem,
        out_shape=jax.ShapeDtypeStruct((rows, width), BF16),
        scratch_shapes=[pltpu.VMEM((rows, width), BF16)] * 2
        + [pltpu.SemaphoreType.DMA((4, rows // sub))] * 2,
        compiler_params=params(56, collective_id=1, has_side_effects=True),
        cost_estimate=cost(100e9, 12 * rows * width),
        name="norm_back",
    )(part, cot, resid, stat)


def unproject_kernel(
    heads, dq_ref, dk_ref, dv_ref, cos_ref, sin_ref, tok_ref, stat_ref, w_ref,
    dproj_ref, part_ref, sums_ref,
):
    cosine, sine = cos_ref[...], sin_ref[...]
    span = heads * HD

    def back(piece):
        return piece * cosine - pltpu.roll(piece, HD // 2, 1) * sine

    for h in range(heads):
        hs = slice(h * HD, (h + 1) * HD)
        dproj_ref[:, hs] = back(dq_ref[:, hs]).astype(BF16)
        dproj_ref[:, span + h * HD : span + (h + 1) * HD] = back(dk_ref[:, hs]).astype(BF16)
    dproj_ref[:, 2 * span :] = dv_ref[...].astype(BF16)
    total = None
    for part in range(3):
        term = lax.dot_general(
            dproj_ref[:, part * span : (part + 1) * span], w_ref[part], NT,
            preferred_element_type=F32,
        )
        total = term if total is None else total + term
    part_ref[...] = total.astype(BF16)
    normed = (tok_ref[...].astype(F32) - stat_ref[:, 0:1]) * stat_ref[:, 1:2]
    sums_ref[...] = jnp.concatenate(
        [
            jnp.sum(total, axis=1, keepdims=True),
            jnp.sum(total * normed, axis=1, keepdims=True),
        ],
        axis=1,
    )


def unproject(dq, dk, dv, cosine, sine, tok_full, stat, weight, heads):
    rows, width = tok_full.shape
    span = heads * HD
    block = 256
    row = lambda n: pl.BlockSpec((block, n), lambda i: (i, 0))
    return pl.pallas_call(
        functools.partial(unproject_kernel, heads),
        grid=(rows // block,),
        in_specs=[
            row(span), row(span), row(span), row(HD), row(HD), row(width), row(2),
            pl.BlockSpec((3, width, span), lambda i: (0, 0, 0)),
        ],
        out_specs=[row(3 * span), row(width), row(2)],
        out_shape=[
            jax.ShapeDtypeStruct((rows, 3 * span), BF16),
            jax.ShapeDtypeStruct((rows, width), BF16),
            jax.ShapeDtypeStruct((rows, 2), F32),
        ],
        compiler_params=params(56),
        cost_estimate=cost(6 * rows * width * span, 6 * width * span + 6 * rows * width),
        name="unproject",
    )(dq, dk, dv, cosine, sine, tok_full, stat, weight)


def per_device(tokens, segment_ids, in_weight, out_weight, gate_up_weight, down_weight, cotangent):
    rows, shard = tokens.shape
    width = in_weight.shape[0]
    span = in_weight.shape[2]
    heads = span // HD
    hidden_local = down_weight.shape[0]
    me = lax.axis_index("ctx")
    tp_at = lax.axis_index("tp")

    def own(whole):
        return lax.dynamic_slice_in_dim(whole, tp_at * shard, shard, axis=1)

    def gather(local, axis=1):
        return lax.all_gather(local, "tp", axis=axis, tiled=True)

    places = me * rows + jnp.arange(rows, dtype=jnp.int32)
    cosine, sine = rope_tables(places)
    in_w = jnp.transpose(in_weight, (1, 0, 2))
    gu_w = jnp.transpose(
        gate_up_weight.reshape(width, 2, hidden_local // BLOCK, BLOCK), (0, 2, 1, 3)
    )
    gu_w = lax.optimization_barrier(gu_w.reshape(width, 2 * hidden_local))

    all_seg = lax.all_gather(segment_ids, "ctx", axis=0, tiled=True)
    count = all_seg.shape[0]
    every = jnp.arange(count, dtype=jnp.int32)
    opens = jnp.concatenate([jnp.ones((1,), jnp.bool_), all_seg[1:] != all_seg[:-1]])
    all_begin = lax.cummax(jnp.where(opens, every, 0))
    begin = lax.dynamic_slice_in_dim(all_begin, me * rows, rows, 0)
    blocks = all_begin.reshape(count // rows, rows)
    key_info = jnp.stack(
        [me, blocks[me, 0] // rows, (blocks[me, rows - 1] + rows - 1) // rows]
    ).astype(jnp.int32)
    query_info = jnp.stack(
        [
            me,
            jnp.sum((blocks[:, 0] < (me + 1) * rows).astype(jnp.int32)) - 1,
            jnp.sum((blocks[:, rows - 1] <= me * rows).astype(jnp.int32)) - 1,
        ]
    ).astype(jnp.int32)
    begin, all_begin = begin[None, :], all_begin[None, :]

    tok_full = gather(tokens)
    inner1, stat1, query, pairs = project(tok_full, in_w, cosine, sine, heads)
    all_pairs = lax.all_gather(pairs, "ctx", axis=0, tiled=True)
    share = width // lax.axis_size("ctx")
    out_full = gather(lax.dynamic_slice_in_dim(out_weight, me * share, share, axis=1), 0)
    out_full = lax.all_gather(out_full, "ctx", axis=1, tiled=True)
    all_query = lax.all_gather(query, "ctx", axis=0, tiled=True)
    cot_full = gather(cotangent)
    raw, mixed, lse = attend(key_info, query, all_pairs, begin, heads)
    resid1, stat2, inner2 = merge(gather(mixed), out_full, tok_full)

    hidden, grad_gu = feed(inner2, cot_full, gu_w, down_weight, BLOCK)
    grad_part = lax.dot_general(grad_gu, gu_w, NT, preferred_element_type=F32).astype(BF16)
    down_grad = lax.dot_general(hidden, cot_full, TN, preferred_element_type=F32)
    gu_grad = lax.dot_general(inner2, grad_gu, TN, preferred_element_type=F32)
    grad_part, down_grad, gu_grad = lax.optimization_barrier(
        (grad_part, down_grad.astype(BF16), gu_grad.astype(BF16))
    )
    down_grad, gu_grad = lax.optimization_barrier(lax.psum((down_grad, gu_grad), "ctx"))
    branch_grad = norm_back(grad_part, cot_full, resid1, stat2, lax.axis_size("tp"))

    branch = jnp.dot(hidden, down_weight, preferred_element_type=F32).astype(BF16)
    branch = lax.psum_scatter(branch, "tp", scatter_dimension=1, tiled=True)
    layer_out = (own(resid1) + branch.astype(F32)).astype(BF16)

    out_grad = lax.dot_general(mixed, branch_grad, TN, preferred_element_type=F32).astype(BF16)
    grad_mixed, delta = mixed_grad(branch_grad, out_weight, raw, lse, heads)
    all_grad = lax.all_gather(grad_mixed, "ctx", axis=0, tiled=True)
    dq = query_grad(key_info, query, grad_mixed, lse, delta, all_pairs, begin, heads)
    dk, dv = key_grad(query_info, pairs, all_query, all_grad, all_begin, heads)
    dproj, part, sums = unproject(dq, dk, dv, cosine, sine, tok_full, stat1, in_w, heads)
    grad_normed1 = lax.psum_scatter(part, "tp", scatter_dimension=1, tiled=True).astype(F32)
    sums = lax.psum(sums, "tp") / width
    in_grad = jnp.stack(
        [
            lax.dot_general(
                inner1, dproj[:, i * span : (i + 1) * span], TN, preferred_element_type=F32
            ).astype(BF16)
            for i in range(3)
        ]
    )
    in_grad, out_grad, down_grad, gu_grad = lax.optimization_barrier(
        (in_grad, out_grad, down_grad, gu_grad)
    )
    in_grad, out_grad = lax.psum((in_grad, out_grad), "ctx")

    normed1 = (tokens.astype(F32) - stat1[:, 0:1]) * stat1[:, 1:2]
    tokens_grad = own(branch_grad).astype(F32) + stat1[:, 1:2] * (
        grad_normed1 - sums[:, 0:1] - normed1 * sums[:, 1:2]
    )
    return (
        layer_out,
        tokens_grad,
        jnp.transpose(in_grad, (1, 0, 2)).astype(F32),
        out_grad.astype(F32),
        weave(gu_grad, BLOCK),
        down_grad.astype(F32),
    )


def solution(mesh):
    placed = (
        P("ctx", "tp"),
        P("ctx"),
        P(None, None, "tp"),
        P("tp", None),
        P(None, None, "tp"),
        P("tp", None),
        P("ctx", "tp"),
    )
    return jax.shard_map(
        per_device,
        mesh=mesh,
        in_specs=placed,
        out_specs=(
            P("ctx", "tp"),
            P("ctx", "tp"),
            P(None, None, "tp"),
            P("tp", None),
            P(None, None, "tp"),
            P("tp", None),
        ),
        check_vma=False,
    )
```

```python
import functools

import jax
import jax.numpy as jnp
from jax import lax
from jax.experimental import pallas as pl
from jax.experimental.pallas import tpu as pltpu
from jax.sharding import PartitionSpec as P

HD = 128
EPS = 1e-05
NEG = -1e30
SCALE = HD ** (-0.5)
LOG2E = 1.4426950408889634
C2 = SCALE * LOG2E
F32 = jnp.float32
BF16 = jnp.bfloat16
NT = (((1,), (1,)), ((), ()))
TN = (((0,), (0,)), ((), ()))
MESH = pl.DeviceIdType.MESH
BLOCK = 512


def params(mib, **more):
    return pltpu.CompilerParams(vmem_limit_bytes=mib << 20, **more)


def cost(flops, nbytes, trans=0):
    return pl.CostEstimate(flops=int(flops), bytes_accessed=int(nbytes), transcendentals=int(trans))


def rope_tables(places):
    half = HD // 2
    freq = 10000.0 ** (-jnp.arange(half, dtype=F32) * 2.0 / HD)
    angle = places.astype(F32)[:, None] * freq[None, :]
    cosine, sine = jnp.cos(angle), jnp.sin(angle)
    return jnp.concatenate([cosine, cosine], axis=1), jnp.concatenate([-sine, sine], axis=1)


def project_kernel(heads, tok_ref, w_ref, cos_ref, sin_ref, inner_ref, stat_ref, q_ref, kv_ref):
    x = tok_ref[...].astype(F32)
    center = x - jnp.mean(x, axis=1, keepdims=True)
    inverse = lax.rsqrt(jnp.mean(center * center, axis=1, keepdims=True) + EPS)
    inner = (center * inverse).astype(BF16)
    inner_ref[...] = inner
    stat_ref[...] = jnp.concatenate(
        [jnp.mean(x, axis=1, keepdims=True), inverse], axis=1
    )
    cosine, sine = cos_ref[...], sin_ref[...]
    span = heads * HD
    for part in range(3):
        out = jnp.dot(inner, w_ref[part], preferred_element_type=F32)
        if part == 2:
            kv_ref[:, span:] = out.astype(BF16)
            continue
        for h in range(heads):
            piece = out[:, h * HD : (h + 1) * HD]
            turned = (piece * cosine + pltpu.roll(piece, HD // 2, 1) * sine).astype(BF16)
            if part == 0:
                q_ref[:, h * HD : (h + 1) * HD] = turned
            else:
                kv_ref[:, h * HD : (h + 1) * HD] = turned


def project(tok_full, weight, cosine, sine, heads):
    rows, width = tok_full.shape
    span = heads * HD
    block = 256
    row = lambda n: pl.BlockSpec((block, n), lambda i: (i, 0))
    return pl.pallas_call(
        functools.partial(project_kernel, heads),
        grid=(rows // block,),
        in_specs=[
            row(width),
            pl.BlockSpec((3, width, span), lambda i: (0, 0, 0)),
            row(HD),
            row(HD),
        ],
        out_specs=[row(width), row(2), row(span), row(2 * span)],
        out_shape=[
            jax.ShapeDtypeStruct((rows, width), BF16),
            jax.ShapeDtypeStruct((rows, 2), F32),
            jax.ShapeDtypeStruct((rows, span), BF16),
            jax.ShapeDtypeStruct((rows, 2 * span), BF16),
        ],
        compiler_params=params(56),
        cost_estimate=cost(6 * rows * width * span, 6 * width * span + 6 * rows * width),
        name="project",
    )(tok_full, weight, cosine, sine)


def masked(scores, j, me, rows, begin):
    key_place = lax.broadcasted_iota(jnp.int32, scores.shape, 0) + j * rows
    query_place = lax.broadcasted_iota(jnp.int32, scores.shape, 1) + me * rows
    return jnp.where((key_place <= query_place) & (key_place >= begin), scores, NEG)


def attend_kernel(
    heads, info, q_ref, k_ref, v_ref, begin_ref, raw_ref, mixed_ref, lse_ref,
    high_ref, total_ref, acc_ref, s_ref,
):
    me, first, clear = info[0], info[1], info[2]
    j = pl.program_id(0)
    rows = q_ref.shape[0]

    @pl.when(j == 0)
    def _():
        high_ref[...] = jnp.full_like(high_ref, NEG)
        total_ref[...] = jnp.zeros_like(total_ref)
        acc_ref[...] = jnp.zeros_like(acc_ref)

    def block(hide):
        def score(h):
            hs = slice(h * HD, (h + 1) * HD)
            s = lax.dot_general(k_ref[:, hs], q_ref[:, hs], NT, preferred_element_type=F32)
            if hide:
                s = masked(s, j, me, rows, begin_ref[...])
            s_ref[h % 2] = s

        def spread(h):
            hs = slice(h * HD, (h + 1) * HD)
            s = s_ref[h % 2]
            old = high_ref[h : h + 1, :]
            new = jnp.maximum(old, jnp.max(s, axis=0, keepdims=True))
            high_ref[h : h + 1, :] = new
            p = jnp.exp2(s * C2 - new * C2)
            decay = jnp.exp2((old - new) * C2)
            total_ref[h : h + 1, :] = total_ref[h : h + 1, :] * decay + jnp.sum(
                p, axis=0, keepdims=True
            )
            acc_ref[h] = acc_ref[h] * decay + lax.dot_general(
                v_ref[:, hs], p.astype(BF16), TN, preferred_element_type=F32
            )

        score(0)
        for h in range(heads):
            if h + 1 < heads:
                score(h + 1)
            spread(h)

    @pl.when((j >= clear) & (j < me))
    def _():
        block(False)

    @pl.when(((j >= first) & (j < clear) & (j < me)) | (j == me))
    def _():
        block(True)

    @pl.when(j == me)
    def _():
        for h in range(heads):
            hs = slice(h * HD, (h + 1) * HD)
            out = (acc_ref[h] / total_ref[h : h + 1, :]).T
            raw_ref[:, hs] = out
            mixed_ref[:, hs] = out.astype(BF16)
        lse_ref[...] = high_ref[...] * C2 + jnp.log2(total_ref[...])


def attend(info, query, pairs, begin, heads):
    rows = query.shape[0]
    total = pairs.shape[0]
    span = heads * HD
    full = lambda shape: pl.BlockSpec(shape, lambda j, s: (0, 0))
    key = pl.BlockSpec((rows, span), lambda j, s: (jnp.clip(j, s[1], s[0]), 0))
    value = pl.BlockSpec((rows, span), lambda j, s: (jnp.clip(j, s[1], s[0]), 1))
    return pl.pallas_call(
        functools.partial(attend_kernel, heads),
        grid_spec=pltpu.PrefetchScalarGridSpec(
            num_scalar_prefetch=1,
            grid=(total // rows,),
            in_specs=[full((rows, span)), key, value, full((1, rows))],
            out_specs=[full((rows, span)), full((rows, span)), full((heads, rows))],
            scratch_shapes=[
                pltpu.VMEM((heads, rows), F32),
                pltpu.VMEM((heads, rows), F32),
                pltpu.VMEM((heads, HD, rows), F32),
                pltpu.VMEM((2, rows, rows), F32),
            ],
        ),
        out_shape=[
            jax.ShapeDtypeStruct((rows, span), F32),
            jax.ShapeDtypeStruct((rows, span), BF16),
            jax.ShapeDtypeStruct((heads, rows), F32),
        ],
        compiler_params=params(56),
        cost_estimate=cost(4 * rows * total * span, 4 * total * span, rows * total * heads),
        name="attend",
    )(info, query, pairs, pairs, begin)


CUBE = 8
CUBE_SENDS = 10


class Cube:
    def __init__(self, buf, send, recv):
        me = lax.axis_index("ctx")
        flip = (1 - 2 * (me % 2), 2 - 4 * ((me // 2) % 2), 4 - 8 * (me // 4))
        self.me, self.flip, self.buf, self.send, self.recv = me, flip, buf, send, recv
        self.rows = buf.shape[0] // CUBE

    def copy(self, n):
        core, x, y = self.flip
        half = self.rows // 2
        block, part, target = (
            (0, None, core),
            (0, 0, x), (0, 1, x), (0, 1, y), (0, 0, y),
            (x, 0, y), (y, 1, x),
            (x, None, core), (y, None, core), (x + y, None, core),
        )[n]
        start = (self.me + block) * self.rows
        size = self.rows
        if part is not None:
            start, size = start + part * half, half
        place = self.buf.at[pl.ds(pl.multiple_of(start, 16), size)]
        return pltpu.make_async_remote_copy(
            src_ref=place, dst_ref=place, send_sem=self.send.at[n], recv_sem=self.recv.at[n],
            device_id={"ctx": self.me + target}, device_id_type=MESH,
        )

    def arrived(self, n):
        self.copy(n).wait_recv()

    def start(self, *which):
        for n in which:
            self.copy(n).start()

    def signal(self, barrier):
        for target in self.flip:
            pl.semaphore_signal(
                barrier, inc=1, device_id={"ctx": self.me + target}, device_id_type=MESH
            )

    def block(self, step):
        core, x, y = self.flip
        on = lambda *steps: sum((step == n).astype(jnp.int32) for n in steps)
        return self.me + on(1, 4, 5, 7) * core + on(2, 4, 6, 7) * x + on(3, 5, 6, 7) * y

    def advance(self, step):
        @pl.when(step == 0)
        def _():
            self.start(0, 1, 3, 2, 4)

        @pl.when(step == 1)
        def _():
            self.arrived(0)

        @pl.when(step == 2)
        def _():
            self.arrived(1)
            self.start(5)
            self.arrived(3)
            self.start(6)
            self.arrived(2)
            self.start(7)

        @pl.when(step == 3)
        def _():
            self.arrived(4)
            self.start(8)

        @pl.when(step == 4)
        def _():
            self.arrived(7)

        @pl.when(step == 5)
        def _():
            self.arrived(8)

        @pl.when(step == 6)
        def _():
            self.arrived(5)
            self.arrived(6)
            self.start(9)

        @pl.when(step == 7)
        def _():
            self.arrived(9)

    def finish(self):
        for n in range(CUBE_SENDS):
            self.copy(n).wait_send()


def hidden_scores(scores, key_block, query_block, rows, begin):
    key_place = lax.broadcasted_iota(jnp.int32, scores.shape, 0) + key_block * rows
    query_place = lax.broadcasted_iota(jnp.int32, scores.shape, 1) + query_block * rows
    return jnp.where((key_place <= query_place) & (key_place >= begin), scores, NEG)


def attend_far_kernel(
    heads, n, q_ref, own_ref, begin_ref, cot_ref,
    raw_ref, mixed_ref, lse_ref, pair_ref, full_ref,
    high_ref, total_ref, acc_ref, s_ref, send, recv, zsend, zrecv,
):
    rows = q_ref.shape[0]
    span = heads * HD
    shard = cot_ref.shape[1]
    at = lax.axis_index("tp")
    cube = Cube(pair_ref, send, recv)
    me = cube.me
    barrier = pltpu.get_barrier_semaphore()
    cube.signal(barrier)

    @pl.when(at > 0)
    def _():
        pl.semaphore_signal(barrier, inc=1, device_id={"tp": at - 1}, device_id_type=MESH)

    @pl.when(at < n - 1)
    def _():
        pl.semaphore_signal(barrier, inc=1, device_id={"tp": at + 1}, device_id_type=MESH)

    pair_ref[pl.ds(pl.multiple_of(me * rows, 16), rows), :] = own_ref[...]
    full_ref[:, pl.ds(pl.multiple_of(at * shard, 128), shard)] = cot_ref[...]
    high_ref[...] = jnp.full_like(high_ref, NEG)
    total_ref[...] = jnp.zeros_like(total_ref)
    acc_ref[...] = jnp.zeros_like(acc_ref)
    pl.semaphore_wait(barrier, jnp.where((at > 0) & (at < n - 1), 5, 4))

    def pass_on(right, s, k):
        place = full_ref.at[:, pl.ds(pl.multiple_of(s * shard, 128), shard)]
        which = (1 if right else 0, k)
        return pltpu.make_async_remote_copy(
            src_ref=place, dst_ref=place, send_sem=zsend.at[which], recv_sem=zrecv.at[which],
            device_id={"tp": at + 1 if right else at - 1}, device_id_type=MESH,
        )

    def line_step(k):
        @pl.when(at >= k)
        def _():
            if k > 0:
                pass_on(True, at - k, k - 1).wait_recv()

            @pl.when(at < n - 1)
            def _():
                pass_on(True, at - k, k).start()

        @pl.when(at + k < n)
        def _():
            if k > 0:
                pass_on(False, at + k, k - 1).wait_recv()

            @pl.when(at > 0)
            def _():
                pass_on(False, at + k, k).start()

    def turn(step, carry):
        cube.advance(step)
        for k in range(n):
            @pl.when(step == min(k * 2, CUBE - 1 - (n - 1 - k)) if n <= CUBE else k)
            def _():
                line_step(k)
        block = cube.block(step)

        @pl.when(block <= me)
        def _():
            place = pl.ds(pl.multiple_of(block * rows, 16), rows)

            def score(h):
                hs = slice(h * HD, (h + 1) * HD)
                s = lax.dot_general(
                    pair_ref[place, hs], q_ref[:, hs], NT, preferred_element_type=F32
                )
                s_ref[h % 2] = hidden_scores(s, block, me, rows, begin_ref[...])

            def spread(h):
                s = s_ref[h % 2]
                old = high_ref[h : h + 1, :]
                new = jnp.maximum(old, jnp.max(s, axis=0, keepdims=True))
                high_ref[h : h + 1, :] = new
                p = jnp.exp2(s * C2 - new * C2)
                decay = jnp.exp2((old - new) * C2)
                total_ref[h : h + 1, :] = total_ref[h : h + 1, :] * decay + jnp.sum(
                    p, axis=0, keepdims=True
                )
                acc_ref[h] = acc_ref[h] * decay + lax.dot_general(
                    pair_ref[place, span + h * HD : span + (h + 1) * HD], p.astype(BF16), TN,
                    preferred_element_type=F32,
                )

            score(0)
            for h in range(heads):
                if h + 1 < heads:
                    score(h + 1)
                spread(h)

        return carry

    lax.fori_loop(0, CUBE, turn, 0)
    for h in range(heads):
        hs = slice(h * HD, (h + 1) * HD)
        out = (acc_ref[h] / total_ref[h : h + 1, :]).T
        raw_ref[:, hs] = out
        mixed_ref[:, hs] = out.astype(BF16)
    lse_ref[...] = high_ref[...] * C2 + jnp.log2(total_ref[...])
    cube.finish()
    for k in range(n):
        @pl.when((at >= k) & (at < n - 1))
        def _():
            pass_on(True, at - k, k).wait_send()

        @pl.when((at + k < n) & (at > 0))
        def _():
            pass_on(False, at + k, k).wait_send()


def attend_far(query, pairs, begin, cot, heads, n):
    rows = query.shape[0]
    span = heads * HD
    vmem = pl.BlockSpec(memory_space=pltpu.VMEM)
    return pl.pallas_call(
        functools.partial(attend_far_kernel, heads, n),
        in_specs=[vmem] * 4,
        out_specs=[vmem] * 5,
        out_shape=[
            jax.ShapeDtypeStruct((rows, span), F32),
            jax.ShapeDtypeStruct((rows, span), BF16),
            jax.ShapeDtypeStruct((heads, rows), F32),
            jax.ShapeDtypeStruct((CUBE * rows, 2 * span), BF16),
            jax.ShapeDtypeStruct((rows, n * cot.shape[1]), BF16),
        ],
        scratch_shapes=[
            pltpu.VMEM((heads, rows), F32),
            pltpu.VMEM((heads, rows), F32),
            pltpu.VMEM((heads, HD, rows), F32),
            pltpu.VMEM((2, rows, rows), F32),
            pltpu.SemaphoreType.DMA((CUBE_SENDS,)),
            pltpu.SemaphoreType.DMA((CUBE_SENDS,)),
            pltpu.SemaphoreType.DMA((2, n)),
            pltpu.SemaphoreType.DMA((2, n)),
        ],
        compiler_params=params(58, collective_id=2, has_side_effects=True),
        cost_estimate=cost(1e6, 1e6),
        name="attend_far",
    )(query, pairs, begin, cot)


def attend_back_far_kernel(
    heads, n, g_ref, q_ref, pair_ref, begin_ref, part_ref,
    dq_ref, dk_ref, dv_ref, layer_ref,
    all_ref, acc_ref, rows_ref, s_ref, p_ref, land_ref, send, recv, zsend, zrecv,
):
    rows = g_ref.shape[0]
    span = heads * HD
    shard = layer_ref.shape[1]
    at = lax.axis_index("tp")
    cube = Cube(all_ref, send, recv)
    me = cube.me
    barrier = pltpu.get_barrier_semaphore()
    cube.signal(barrier)
    for o in range(1, n):
        pl.semaphore_signal(
            barrier, inc=1, device_id={"tp": lax.rem(at + o, n)}, device_id_type=MESH
        )
    all_ref[pl.ds(pl.multiple_of(me * rows, 16), rows), :] = g_ref[...]
    acc_ref[...] = jnp.zeros_like(acc_ref)
    dk_ref[...] = jnp.zeros_like(dk_ref)
    dv_ref[...] = jnp.zeros_like(dv_ref)
    pl.semaphore_wait(barrier, 3 + n - 1)

    def term(o):
        target = lax.rem(at + o, n)
        return pltpu.make_async_remote_copy(
            src_ref=part_ref.at[:, pl.ds(pl.multiple_of(target * shard, 128), shard)],
            dst_ref=land_ref.at[o - 1],
            send_sem=zsend.at[o - 1], recv_sem=zrecv.at[o - 1],
            device_id={"tp": target}, device_id_type=MESH,
        )

    own = pl.ds(pl.multiple_of(me * rows, 16), rows)

    def turn(step, carry):
        cube.advance(step)

        @pl.when(step == 0)
        def _():
            for o in range(1, n):
                term(o).start()

        block = cube.block(step)
        place = pl.ds(pl.multiple_of(block * rows, 16), rows)

        def scores(h, key_block, key_place, query_block, query_place):
            hs = slice(h * HD, (h + 1) * HD)
            vs = slice(span + h * HD, span + (h + 1) * HD)
            s = lax.dot_general(
                pair_ref[key_place, hs], q_ref[query_place, hs], NT, preferred_element_type=F32
            )
            begin = begin_ref[pl.ds(query_block, 1), :]
            s_ref[h % 2] = hidden_scores(s, key_block, query_block, rows, begin)
            p_ref[h % 2] = lax.dot_general(
                pair_ref[key_place, vs], all_ref[query_place, hs], NT, preferred_element_type=F32
            )

        def read_rows(query_place):
            coded = all_ref[query_place, span:].astype(F32).T
            for k in range(2 * heads):
                rows_ref[k : k + 1, :] = (
                    coded[3 * k : 3 * k + 1]
                    + coded[3 * k + 1 : 3 * k + 2]
                    + coded[3 * k + 2 : 3 * k + 3]
                )

        def weights(h):
            p = jnp.exp2(s_ref[h % 2] * C2 - rows_ref[h : h + 1, :])
            ds = p * (p_ref[h % 2] - rows_ref[heads + h : heads + h + 1, :])
            return p.astype(BF16), ds.astype(BF16)

        @pl.when(block <= me)
        def _():
            read_rows(own)
            scores(0, block, place, me, own)
            for h in range(heads):
                if h + 1 < heads:
                    scores(h + 1, block, place, me, own)
                _, ds = weights(h)
                acc_ref[h] = acc_ref[h] + lax.dot_general(
                    pair_ref[place, h * HD : (h + 1) * HD], ds, TN, preferred_element_type=F32
                )

        @pl.when(block >= me)
        def _():
            read_rows(place)
            scores(0, me, own, block, place)
            for h in range(heads):
                hs = slice(h * HD, (h + 1) * HD)
                if h + 1 < heads:
                    scores(h + 1, me, own, block, place)
                p, ds = weights(h)
                dv_ref[:, hs] += jnp.dot(p, all_ref[place, hs], preferred_element_type=F32)
                dk_ref[:, hs] += jnp.dot(ds, q_ref[place, hs], preferred_element_type=F32)

        return carry

    lax.fori_loop(0, CUBE, turn, 0)
    for h in range(heads):
        dq_ref[:, h * HD : (h + 1) * HD] = (acc_ref[h] * SCALE).T
    dk_ref[...] = dk_ref[...] * SCALE
    total = part_ref[:, pl.ds(pl.multiple_of(at * shard, 128), shard)].astype(F32)
    for o in range(1, n):
        term(o).wait_recv()
        total = total + land_ref[o - 1].astype(F32)
    layer_ref[...] = total.astype(BF16)
    cube.finish()
    for o in range(1, n):
        term(o).wait_send()


def attend_back_far(grad, all_query, all_pairs, all_begin, part, heads, n):
    rows = grad.shape[0]
    span = heads * HD
    shard = part.shape[1] // n
    vmem = pl.BlockSpec(memory_space=pltpu.VMEM)
    wide = jax.ShapeDtypeStruct((rows, span), F32)
    return pl.pallas_call(
        functools.partial(attend_back_far_kernel, heads, n),
        in_specs=[vmem] * 5,
        out_specs=[vmem] * 4,
        out_shape=[wide, wide, wide, jax.ShapeDtypeStruct((rows, shard), BF16)],
        scratch_shapes=[
            pltpu.VMEM((CUBE * rows, span + HD), BF16),
            pltpu.VMEM((heads, HD, rows), F32),
            pltpu.VMEM((2 * heads, rows), F32),
            pltpu.VMEM((2, rows, rows), F32),
            pltpu.VMEM((2, rows, rows), F32),
            pltpu.VMEM((n - 1, rows, shard), BF16),
            pltpu.SemaphoreType.DMA((CUBE_SENDS,)),
            pltpu.SemaphoreType.DMA((CUBE_SENDS,)),
            pltpu.SemaphoreType.DMA((n - 1,)),
            pltpu.SemaphoreType.DMA((n - 1,)),
        ],
        compiler_params=params(60, collective_id=3, has_side_effects=True),
        cost_estimate=cost(1e6, 1e6),
        name="attend_back_far",
    )(grad, all_query, all_pairs, all_begin, part)


def query_grad_kernel(
    heads, info, q_ref, do_ref, lse_ref, delta_ref, k_ref, v_ref, begin_ref,
    dq_ref, acc_ref, s_ref, g_ref,
):
    me, first, clear = info[0], info[1], info[2]
    j = pl.program_id(0)
    rows = q_ref.shape[0]

    @pl.when(j == 0)
    def _():
        acc_ref[...] = jnp.zeros_like(acc_ref)

    def block(hide):
        def score(h):
            hs = slice(h * HD, (h + 1) * HD)
            s = lax.dot_general(k_ref[:, hs], q_ref[:, hs], NT, preferred_element_type=F32)
            if hide:
                s = masked(s, j, me, rows, begin_ref[...])
            s_ref[h % 2] = s
            g_ref[h % 2] = lax.dot_general(
                v_ref[:, hs], do_ref[:, hs], NT, preferred_element_type=F32
            )

        def spread(h):
            hs = slice(h * HD, (h + 1) * HD)
            p = jnp.exp2(s_ref[h % 2] * C2 - lse_ref[h : h + 1, :])
            ds = (p * (g_ref[h % 2] - delta_ref[h : h + 1, :])).astype(BF16)
            acc_ref[h] = acc_ref[h] + lax.dot_general(
                k_ref[:, hs], ds, TN, preferred_element_type=F32
            )

        score(0)
        for h in range(heads):
            if h + 1 < heads:
                score(h + 1)
            spread(h)

    @pl.when((j >= clear) & (j < me))
    def _():
        block(False)

    @pl.when(((j >= first) & (j < clear) & (j < me)) | (j == me))
    def _():
        block(True)

    @pl.when(j == me)
    def _():
        for h in range(heads):
            dq_ref[:, h * HD : (h + 1) * HD] = (acc_ref[h] * SCALE).T


def query_grad(info, query, grad_mixed, lse, delta, pairs, begin, heads):
    rows = query.shape[0]
    total = pairs.shape[0]
    span = heads * HD
    full = lambda shape: pl.BlockSpec(shape, lambda j, s: (0, 0))
    key = pl.BlockSpec((rows, span), lambda j, s: (jnp.clip(j, s[1], s[0]), 0))
    value = pl.BlockSpec((rows, span), lambda j, s: (jnp.clip(j, s[1], s[0]), 1))
    wide = full((rows, span))
    thin = full((heads, rows))
    return pl.pallas_call(
        functools.partial(query_grad_kernel, heads),
        grid_spec=pltpu.PrefetchScalarGridSpec(
            num_scalar_prefetch=1,
            grid=(total // rows,),
            in_specs=[wide, wide, thin, thin, key, value, full((1, rows))],
            out_specs=wide,
            scratch_shapes=[
                pltpu.VMEM((heads, HD, rows), F32),
                pltpu.VMEM((2, rows, rows), F32),
                pltpu.VMEM((2, rows, rows), F32),
            ],
        ),
        out_shape=jax.ShapeDtypeStruct((rows, span), F32),
        compiler_params=params(58),
        cost_estimate=cost(6 * rows * total * span, 4 * total * span, rows * total * heads),
        name="query_grad",
    )(info, query, grad_mixed, lse, delta, pairs, pairs, begin)


def key_grad_kernel(
    heads, info, k_ref, v_ref, q_ref, g_ref, begin_ref, dk_ref, dv_ref,
    rows_ref, s_ref, p_ref,
):
    me, last, clear = info[0], info[1], info[2]
    j = pl.program_id(0)
    rows = k_ref.shape[0]
    span = heads * HD

    @pl.when(j == me)
    def _():
        dk_ref[...] = jnp.zeros_like(dk_ref)
        dv_ref[...] = jnp.zeros_like(dv_ref)

    def block(hide):
        coded = g_ref[:, span:].astype(F32).T
        for n in range(2 * heads):
            rows_ref[n : n + 1, :] = (
                coded[3 * n : 3 * n + 1] + coded[3 * n + 1 : 3 * n + 2] + coded[3 * n + 2 : 3 * n + 3]
            )

        def score(h):
            hs = slice(h * HD, (h + 1) * HD)
            s = lax.dot_general(k_ref[:, hs], q_ref[:, hs], NT, preferred_element_type=F32)
            if hide:
                key_place = lax.broadcasted_iota(jnp.int32, s.shape, 0) + me * rows
                query_place = lax.broadcasted_iota(jnp.int32, s.shape, 1) + j * rows
                s = jnp.where(
                    (key_place <= query_place) & (key_place >= begin_ref[...]), s, NEG
                )
            s_ref[h % 2] = s
            p_ref[h % 2] = lax.dot_general(
                v_ref[:, hs], g_ref[:, hs], NT, preferred_element_type=F32
            )

        def spread(h):
            hs = slice(h * HD, (h + 1) * HD)
            p = jnp.exp2(s_ref[h % 2] * C2 - rows_ref[h : h + 1, :])
            ds = (p * (p_ref[h % 2] - rows_ref[heads + h : heads + h + 1, :])).astype(BF16)
            dv_ref[:, hs] += jnp.dot(p.astype(BF16), g_ref[:, hs], preferred_element_type=F32)
            dk_ref[:, hs] += jnp.dot(ds, q_ref[:, hs], preferred_element_type=F32)

        score(0)
        for h in range(heads):
            if h + 1 < heads:
                score(h + 1)
            spread(h)

    @pl.when((j > me) & (j <= clear))
    def _():
        block(False)

    @pl.when((j == me) | ((j > me) & (j > clear) & (j <= last)))
    def _():
        block(True)

    @pl.when(j == pl.num_programs(0) - 1)
    def _():
        dk_ref[...] = dk_ref[...] * SCALE


def key_grad(info, pairs, all_query, all_grad, all_begin, heads):
    rows = pairs.shape[0]
    total = all_query.shape[0]
    span = heads * HD
    full = lambda shape, at=0: pl.BlockSpec(shape, lambda j, s: (0, at))
    near = lambda j, s: (jnp.clip(j, s[0], s[1]), 0)
    wide = full((rows, span))
    return pl.pallas_call(
        functools.partial(key_grad_kernel, heads),
        grid_spec=pltpu.PrefetchScalarGridSpec(
            num_scalar_prefetch=1,
            grid=(total // rows,),
            in_specs=[
                wide, full((rows, span), 1),
                pl.BlockSpec((rows, span), near),
                pl.BlockSpec((rows, span + HD), near),
                pl.BlockSpec((1, rows), lambda j, s: (0, jnp.clip(j, s[0], s[1]))),
            ],
            out_specs=[wide, wide],
            scratch_shapes=[
                pltpu.VMEM((2 * heads, rows), F32),
                pltpu.VMEM((2, rows, rows), F32),
                pltpu.VMEM((2, rows, rows), F32),
            ],
        ),
        out_shape=[jax.ShapeDtypeStruct((rows, span), F32)] * 2,
        compiler_params=params(58),
        cost_estimate=cost(8 * rows * total * span, 4 * total * span, rows * total * heads),
        name="key_grad",
    )(info, pairs, pairs, all_query, all_grad, all_begin)


def mixed_grad_kernel(heads, branch_ref, w_ref, raw_ref, lse_ref, out_ref, delta_ref):
    span = heads * HD
    low = lax.dot_general(
        branch_ref[...], w_ref[...], NT, preferred_element_type=F32
    ).astype(BF16)
    out_ref[:, :span] = low
    count = low.shape[0]
    both = low.astype(F32) * raw_ref[...]
    for h in range(heads):
        delta_ref[h : h + 1, :] = jnp.sum(both[:, h * HD : (h + 1) * HD].T, axis=0, keepdims=True)
    lines = []
    for n in range(2 * heads):
        value = lse_ref[n : n + 1, :] if n < heads else delta_ref[n - heads : n - heads + 1, :]
        for _ in range(3):
            piece = value.astype(BF16).astype(F32)
            lines.append(piece)
            value = value - piece
    lines.append(jnp.zeros((HD - len(lines), count), F32))
    out_ref[:, span:] = jnp.concatenate(lines, axis=0).T.astype(BF16)


def mixed_grad(branch, weight, raw, lse, heads):
    rows, width = branch.shape
    span = heads * HD
    block = 256
    row = lambda n: pl.BlockSpec((block, n), lambda i: (i, 0))
    line = pl.BlockSpec((heads, block), lambda i: (0, i))
    return pl.pallas_call(
        functools.partial(mixed_grad_kernel, heads),
        grid=(rows // block,),
        in_specs=[row(width), pl.BlockSpec((span, width), lambda i: (0, 0)), row(span), line],
        out_specs=[row(span + HD), line],
        out_shape=[
            jax.ShapeDtypeStruct((rows, span + HD), BF16),
            jax.ShapeDtypeStruct((heads, rows), F32),
        ],
        compiler_params=params(56),
        cost_estimate=cost(2 * rows * width * span, 2 * width * span + 4 * rows * width),
        name="mixed_grad",
    )(branch, weight, raw, lse)


def feed_kernel(inner_ref, cot_ref, w_ref, down_ref, hidden_ref, dgu_ref):
    block = down_ref.shape[0]
    both = jnp.dot(inner_ref[...], w_ref[...], preferred_element_type=F32)
    grad = lax.dot_general(cot_ref[...], down_ref[...], NT, preferred_element_type=F32)
    gate, up = both[:, :block], both[:, block:]
    sigma = 1.0 / (1.0 + jnp.exp(-gate))
    active = gate * sigma
    hidden_ref[...] = (active * up).astype(BF16)
    dgu_ref[:, :block] = (grad * up * sigma * (1.0 + gate * (1.0 - sigma))).astype(BF16)
    dgu_ref[:, block:] = (grad * active).astype(BF16)


def feed(inner, cot, weight, down, block):
    rows, width = inner.shape
    units = down.shape[0]
    whole = pl.BlockSpec((rows, width), lambda j: (0, 0))
    return pl.pallas_call(
        feed_kernel,
        grid=(units // block,),
        in_specs=[
            whole, whole,
            pl.BlockSpec((width, 2 * block), lambda j: (0, j)),
            pl.BlockSpec((block, width), lambda j: (j, 0)),
        ],
        out_specs=[
            pl.BlockSpec((rows, block), lambda j: (0, j)),
            pl.BlockSpec((rows, 2 * block), lambda j: (0, j)),
        ],
        out_shape=[
            jax.ShapeDtypeStruct((rows, units), BF16),
            jax.ShapeDtypeStruct((rows, 2 * units), BF16),
        ],
        compiler_params=params(56),
        cost_estimate=cost(
            6 * rows * width * units, 6 * width * units + 4 * rows * width, rows * units
        ),
        name="feed",
    )(inner, cot, weight, down)


def weave_kernel(block, sum_ref, out_ref):
    for j in range(sum_ref.shape[1] // (2 * block)):
        for k in range(2):
            at = (2 * j + k) * block
            out_ref[:, k, j * block : (j + 1) * block] = sum_ref[:, at : at + block].astype(F32)


def weave(summed, block):
    width, both = summed.shape
    rows = 256
    return pl.pallas_call(
        functools.partial(weave_kernel, block),
        grid=(width // rows,),
        in_specs=[pl.BlockSpec((rows, both), lambda i: (i, 0))],
        out_specs=pl.BlockSpec((rows, 2, both // 2), lambda i: (i, 0, 0)),
        out_shape=jax.ShapeDtypeStruct((width, 2, both // 2), F32),
        compiler_params=params(56),
        cost_estimate=cost(width * both, 6 * width * both),
        name="weave",
    )(summed)


def line_barrier(at, n):
    barrier = pltpu.get_barrier_semaphore()

    @pl.when(at > 0)
    def _():
        pl.semaphore_signal(barrier, inc=1, device_id={"tp": at - 1}, device_id_type=MESH)

    @pl.when(at < n - 1)
    def _():
        pl.semaphore_signal(barrier, inc=1, device_id={"tp": at + 1}, device_id_type=MESH)

    pl.semaphore_wait(barrier, jnp.where((at > 0) & (at < n - 1), 2, 1))


def sum_rows(n, sub, part_ref, out_ref, row_fn, from_left, from_right, send, recv):
    at = lax.axis_index("tp")
    chunks = part_ref.shape[0] // sub
    middle = (n // 2 - 1, n // 2)

    def link(kind, right, src, dst, c):
        which = (kind * 2 + (1 if right else 0), c)
        return pltpu.make_async_remote_copy(
            src_ref=src.at[pl.ds(c * sub, sub)],
            dst_ref=dst.at[pl.ds(c * sub, sub)],
            send_sem=send.at[which],
            recv_sem=recv.at[which],
            device_id={"tp": at + 1 if right else at - 1},
            device_id_type=MESH,
        )

    def came(right):
        return from_left if right else from_right

    def first(right, c):
        return link(0, right, part_ref, came(right), c)

    def onward(right, c):
        return link(0, right, came(right), came(right), c)

    def hand(right, c):
        return link(1, right, out_ref, out_ref, c)

    def reduce_step(c):
        owner = middle[c % 2]
        rows = slice(c * sub, (c + 1) * sub)
        for right in (True, False):
            edge = 0 if right else n - 1
            held = came(right)

            @pl.when(at == edge)
            def _():
                first(right, c).start()

            @pl.when(((at < owner) if right else (at > owner)) & (at != edge))
            def _():
                copy = onward(right, c)
                copy.wait_recv()
                held[rows, :] = (
                    held[rows, :].astype(F32) + part_ref[rows, :].astype(F32)
                ).astype(BF16)
                copy.start()

    def final_step(c):
        owner = middle[c % 2]
        rows = slice(c * sub, (c + 1) * sub)

        @pl.when(at == owner)
        def _():
            total = part_ref[rows, :].astype(F32)
            onward(True, c).wait_recv()
            total = total + from_left[rows, :].astype(F32)
            onward(False, c).wait_recv()
            total = total + from_right[rows, :].astype(F32)
            row_fn(total, rows)
            hand(True, c).start()
            hand(False, c).start()

    def hand_step(c):
        owner = middle[c % 2]
        for right in (True, False):
            edge = n - 1 if right else 0

            @pl.when((at > owner) if right else (at < owner))
            def _():
                copy = hand(right, c)
                copy.wait_recv()

                @pl.when(at != edge)
                def _():
                    copy.start()

    for c in range(chunks + 4):
        if c < chunks:
            reduce_step(c)
        if 2 <= c < chunks + 2:
            final_step(c - 2)
        if c >= 4:
            hand_step(c - 4)
    for c in range(chunks):
        owner = middle[c % 2]

        @pl.when(at < owner)
        def _():
            first(True, c).wait_send()

        @pl.when(at > owner)
        def _():
            first(False, c).wait_send()

        @pl.when((at >= owner) & (at < n - 1))
        def _():
            hand(True, c).wait_send()

        @pl.when((at <= owner) & (at > 0))
        def _():
            hand(False, c).wait_send()


def merge_kernel(
    n, sub, part_ref, tok_ref, inner_ref, resid_ref, stat_ref, from_left, from_right, send, recv
):
    line_barrier(lax.axis_index("tp"), n)
    resid_ref[...] = jnp.zeros_like(resid_ref)
    stat_ref[...] = jnp.zeros_like(stat_ref)

    def row_fn(total, rows):
        x = tok_ref[rows, :].astype(F32) + total
        mean = jnp.mean(x, axis=1, keepdims=True)
        center = x - mean
        inverse = lax.rsqrt(jnp.mean(center * center, axis=1, keepdims=True) + EPS)
        resid_ref[rows, :] = x
        stat_ref[rows, :] = jnp.concatenate([mean, inverse], axis=1)
        inner_ref[rows, :] = (center * inverse).astype(BF16)

    sum_rows(n, sub, part_ref, inner_ref, row_fn, from_left, from_right, send, recv)


def merge(part, tok_full, n):
    rows, width = part.shape
    sub = 48
    vmem = pl.BlockSpec(memory_space=pltpu.VMEM)
    return pl.pallas_call(
        functools.partial(merge_kernel, n, sub),
        in_specs=[vmem] * 2,
        out_specs=[vmem] * 3,
        out_shape=[
            jax.ShapeDtypeStruct((rows, width), BF16),
            jax.ShapeDtypeStruct((rows, width), F32),
            jax.ShapeDtypeStruct((rows, 2), F32),
        ],
        scratch_shapes=[pltpu.VMEM((rows, width), BF16)] * 2
        + [pltpu.SemaphoreType.DMA((4, rows // sub))] * 2,
        compiler_params=params(56, collective_id=5, has_side_effects=True),
        cost_estimate=cost(1e6, 1e6),
        name="merge",
    )(part, tok_full)


def norm_back_kernel(
    n, sub, part_ref, cot_ref, resid_ref, stat_ref, out_ref, from_left, from_right, send, recv
):
    line_barrier(lax.axis_index("tp"), n)

    def row_fn(total, rows):
        inverse = stat_ref[rows, 1:2]
        normed = (resid_ref[rows, :] - stat_ref[rows, 0:1]) * inverse
        mean = jnp.mean(total, axis=1, keepdims=True)
        inner = jnp.mean(total * normed, axis=1, keepdims=True)
        out = cot_ref[rows, :].astype(F32) + inverse * (total - mean - normed * inner)
        out_ref[rows, :] = out.astype(BF16)

    sum_rows(n, sub, part_ref, out_ref, row_fn, from_left, from_right, send, recv)


def norm_back(part, cot, resid, stat, n):
    rows, width = part.shape
    sub = 48
    vmem = pl.BlockSpec(memory_space=pltpu.VMEM)
    return pl.pallas_call(
        functools.partial(norm_back_kernel, n, sub),
        in_specs=[vmem] * 4,
        out_specs=vmem,
        out_shape=jax.ShapeDtypeStruct((rows, width), BF16),
        scratch_shapes=[pltpu.VMEM((rows, width), BF16)] * 2
        + [pltpu.SemaphoreType.DMA((4, rows // sub))] * 2,
        compiler_params=params(56, collective_id=1, has_side_effects=True),
        cost_estimate=cost(1e6, 1e6),
        name="norm_back",
    )(part, cot, resid, stat)


def unrotate_kernel(heads, dq_ref, dk_ref, dv_ref, cos_ref, sin_ref, dproj_ref):
    cosine, sine = cos_ref[...], sin_ref[...]
    span = heads * HD

    def back(piece):
        return (piece * cosine - pltpu.roll(piece, HD // 2, 1) * sine).astype(BF16)

    for h in range(heads):
        hs = slice(h * HD, (h + 1) * HD)
        dproj_ref[:, hs] = back(dq_ref[:, hs])
        dproj_ref[:, span + h * HD : span + (h + 1) * HD] = back(dk_ref[:, hs])
    dproj_ref[:, 2 * span :] = dv_ref[...].astype(BF16)


def unrotate(dq, dk, dv, cosine, sine, heads):
    rows, span = dq.shape
    block = 256
    row = lambda n: pl.BlockSpec((block, n), lambda i: (i, 0))
    return pl.pallas_call(
        functools.partial(unrotate_kernel, heads),
        grid=(rows // block,),
        in_specs=[row(span), row(span), row(span), row(HD), row(HD)],
        out_specs=row(3 * span),
        out_shape=jax.ShapeDtypeStruct((rows, 3 * span), BF16),
        compiler_params=params(56),
        cost_estimate=cost(1e6, 18 * rows * span),
        name="unrotate",
    )(dq, dk, dv, cosine, sine)


def unproject_kernel(
    heads, n, dproj_ref, tok_ref, stat_ref, w_ref, branch_ref, out_ref,
    part_ref, mine_ref, land_ref, sums_ref, far_ref, send, recv, ssend, srecv,
):
    rows, width = tok_ref.shape
    shard = width // n
    span = heads * HD
    at = lax.axis_index("tp")
    barrier = pltpu.get_barrier_semaphore()
    for o in range(1, n):
        pl.semaphore_signal(
            barrier, inc=1, device_id={"tp": lax.rem(at + o, n)}, device_id_type=MESH
        )
    pl.semaphore_wait(barrier, n - 1)
    block = 256
    count = rows // block

    def term(o, i):
        target = lax.rem(at + o, n)
        place = pl.ds(i * block, block)
        return pltpu.make_async_remote_copy(
            src_ref=part_ref.at[place, pl.ds(pl.multiple_of(target * shard, 128), shard)],
            dst_ref=land_ref.at[o - 1, place],
            send_sem=send.at[o - 1, i], recv_sem=recv.at[o - 1, i],
            device_id={"tp": target}, device_id_type=MESH,
        )

    def sums(o):
        return pltpu.make_async_remote_copy(
            src_ref=sums_ref, dst_ref=far_ref.at[o - 1],
            send_sem=ssend.at[o - 1], recv_sem=srecv.at[o - 1],
            device_id={"tp": lax.rem(at + o, n)}, device_id_type=MESH,
        )

    own = pl.ds(pl.multiple_of(at * shard, 128), shard)
    for i in range(count):
        place = pl.ds(i * block, block)
        total = None
        for part in range(3):
            piece = lax.dot_general(
                dproj_ref[place, part * span : (part + 1) * span], w_ref[part], NT,
                preferred_element_type=F32,
            )
            total = piece if total is None else total + piece
        part_ref[place, :] = total.astype(BF16)
        for o in range(1, n):
            term(o, i).start()
        normed = (tok_ref[place, :].astype(F32) - stat_ref[place, 0:1]) * stat_ref[place, 1:2]
        first = jnp.sum(total, axis=1, keepdims=True)
        second = jnp.sum(total * normed, axis=1, keepdims=True)
        lane = lax.broadcasted_iota(jnp.int32, (block, HD), 1)
        both = jnp.where(lane == 0, first, jnp.where(lane == 1, second, 0.0))
        sums_ref[:, i * block : (i + 1) * block] = both.T[:8]
    for o in range(1, n):
        sums(o).start()
    total = sums_ref[...]
    for o in range(1, n):
        sums(o).wait_recv()
        total = total + far_ref[o - 1]
    mine_ref[...] = total
    for i in range(count):
        place = pl.ds(i * block, block)
        spread = jnp.concatenate(
            [mine_ref[:, i * block : (i + 1) * block], jnp.zeros((HD - 8, block), F32)], axis=0
        ).T / width
        total = part_ref[place, own].astype(F32)
        for o in range(1, n):
            term(o, i).wait_recv()
            total = total + land_ref[o - 1, place].astype(F32)
        inverse = stat_ref[place, 1:2]
        normed = (tok_ref[place, own].astype(F32) - stat_ref[place, 0:1]) * inverse
        out_ref[place, :] = branch_ref[place, own].astype(F32) + inverse * (
            total - spread[:, 0:1] - normed * spread[:, 1:2]
        )
    for o in range(1, n):
        sums(o).wait_send()
        for i in range(count):
            term(o, i).wait_send()


def unproject(dproj, tok_full, stat, weight, branch, heads, n):
    rows, width = tok_full.shape
    shard = width // n
    vmem = pl.BlockSpec(memory_space=pltpu.VMEM)
    return pl.pallas_call(
        functools.partial(unproject_kernel, heads, n),
        in_specs=[vmem] * 5,
        out_specs=vmem,
        out_shape=jax.ShapeDtypeStruct((rows, shard), F32),
        scratch_shapes=[
            pltpu.VMEM((rows, width), BF16),
            pltpu.VMEM((8, rows), F32),
            pltpu.VMEM((n - 1, rows, shard), BF16),
            pltpu.VMEM((8, rows), F32),
            pltpu.VMEM((n - 1, 8, rows), F32),
            pltpu.SemaphoreType.DMA((n - 1, rows // 256)),
            pltpu.SemaphoreType.DMA((n - 1, rows // 256)),
            pltpu.SemaphoreType.DMA((n - 1,)),
            pltpu.SemaphoreType.DMA((n - 1,)),
        ],
        compiler_params=params(56, collective_id=4, has_side_effects=True),
        cost_estimate=cost(1e6, 1e6),
        name="unproject",
    )(dproj, tok_full, stat, weight, branch)


def per_device(tokens, segment_ids, in_weight, out_weight, gate_up_weight, down_weight, cotangent):
    rows = tokens.shape[0]
    width = in_weight.shape[0]
    span = in_weight.shape[2]
    heads = span // HD
    hidden_local = down_weight.shape[0]
    me = lax.axis_index("ctx")
    tp_size = lax.axis_size("tp")
    cube = lax.axis_size("ctx") == CUBE

    def gather(local, axis=1):
        return lax.all_gather(local, "tp", axis=axis, tiled=True)

    places = me * rows + jnp.arange(rows, dtype=jnp.int32)
    cosine, sine = rope_tables(places)
    in_w = jnp.transpose(in_weight, (1, 0, 2))
    gu_w = jnp.transpose(
        gate_up_weight.reshape(width, 2, hidden_local // BLOCK, BLOCK), (0, 2, 1, 3)
    )
    gu_w = gu_w.reshape(width, 2 * hidden_local)

    all_seg = lax.all_gather(segment_ids, "ctx", axis=0, tiled=True)
    count = all_seg.shape[0]
    every = jnp.arange(count, dtype=jnp.int32)
    opens = jnp.concatenate([jnp.ones((1,), jnp.bool_), all_seg[1:] != all_seg[:-1]])
    all_begin = lax.cummax(jnp.where(opens, every, 0))
    begin = lax.dynamic_slice_in_dim(all_begin, me * rows, rows, 0)
    blocks = all_begin.reshape(count // rows, rows)
    key_info = jnp.stack(
        [me, blocks[me, 0] // rows, (blocks[me, rows - 1] + rows - 1) // rows]
    ).astype(jnp.int32)
    query_info = jnp.stack(
        [
            me,
            jnp.sum((blocks[:, 0] < (me + 1) * rows).astype(jnp.int32)) - 1,
            jnp.sum((blocks[:, rows - 1] <= me * rows).astype(jnp.int32)) - 1,
        ]
    ).astype(jnp.int32)
    begin, all_begin = begin[None, :], all_begin[None, :]

    tok_full, gu_w = lax.optimization_barrier((gather(tokens), gu_w))
    inner1, stat1, query, pairs = project(tok_full, in_w, cosine, sine, heads)
    if cube:
        raw, mixed, lse, all_pairs, cot_full = attend_far(
            query, pairs, begin, cotangent, heads, tp_size
        )
    else:
        all_pairs = lax.all_gather(pairs, "ctx", axis=0, tiled=True)
        cot_full = gather(cotangent)
        raw, mixed, lse = attend(key_info, query, all_pairs, begin, heads)
    out_part = jnp.dot(mixed, out_weight, preferred_element_type=F32).astype(BF16)
    inner2, resid1, stat2 = merge(out_part, tok_full, tp_size)
    all_query = lax.all_gather(query, "ctx", axis=0, tiled=True)

    hidden, grad_gu = feed(inner2, cot_full, gu_w, down_weight, BLOCK)
    down_grad = lax.dot_general(hidden, cot_full, TN, preferred_element_type=F32).astype(BF16)
    gu_grad = lax.dot_general(inner2, grad_gu, TN, preferred_element_type=F32).astype(BF16)
    down_grad, gu_grad, all_query, grad_gu, hidden = lax.optimization_barrier(
        (down_grad, gu_grad, all_query, grad_gu, hidden)
    )
    down_grad, gu_grad = lax.optimization_barrier(lax.psum((down_grad, gu_grad), "ctx"))

    grad_part = lax.dot_general(grad_gu, gu_w, NT, preferred_element_type=F32).astype(BF16)
    branch_grad = norm_back(grad_part, cot_full, resid1, stat2, tp_size)
    out_grad = lax.dot_general(mixed, branch_grad, TN, preferred_element_type=F32).astype(BF16)
    grad_mixed, delta = mixed_grad(branch_grad, out_weight, raw, lse, heads)
    branch = (resid1 + jnp.dot(hidden, down_weight, preferred_element_type=F32)).astype(BF16)
    if cube:
        dq, dk, dv, layer_out = attend_back_far(
            grad_mixed, all_query, all_pairs, blocks, branch, heads, tp_size
        )
    else:
        branch = lax.psum_scatter(branch, "tp", scatter_dimension=1, tiled=True)
        layer_out = branch
        all_grad = lax.all_gather(grad_mixed, "ctx", axis=0, tiled=True)
        dq = query_grad(key_info, query, grad_mixed, lse, delta, all_pairs, begin, heads)
        dk, dv = key_grad(query_info, pairs, all_query, all_grad, all_begin, heads)

    dproj = unrotate(dq, dk, dv, cosine, sine, heads)
    in_grad = jnp.stack(
        [
            lax.dot_general(
                inner1, dproj[:, i * span : (i + 1) * span], TN, preferred_element_type=F32
            ).astype(BF16)
            for i in range(3)
        ]
    )
    in_grad, out_grad, dproj, down_grad, gu_grad = lax.optimization_barrier(
        (in_grad, out_grad, dproj, down_grad, gu_grad)
    )
    in_grad, out_grad = lax.psum((in_grad, out_grad), "ctx")
    tokens_grad = unproject(dproj, tok_full, stat1, in_w, branch_grad, heads, tp_size)
    return (
        layer_out,
        tokens_grad,
        jnp.transpose(in_grad, (1, 0, 2)).astype(F32),
        out_grad.astype(F32),
        weave(gu_grad, BLOCK),
        down_grad.astype(F32),
    )


def solution(mesh):
    placed = (
        P("ctx", "tp"),
        P("ctx"),
        P(None, None, "tp"),
        P("tp", None),
        P(None, None, "tp"),
        P("tp", None),
        P("ctx", "tp"),
    )
    return jax.shard_map(
        per_device,
        mesh=mesh,
        in_specs=placed,
        out_specs=(
            P("ctx", "tp"),
            P("ctx", "tp"),
            P(None, None, "tp"),
            P("tp", None),
            P(None, None, "tp"),
            P("tp", None),
        ),
        check_vma=False,
    )
```

```python
import functools

import jax
import jax.numpy as jnp
from jax import lax
from jax.experimental import pallas as pl
from jax.experimental.pallas import tpu as pltpu
from jax.sharding import PartitionSpec as P

HD = 128
EPS = 1e-05
NEG = -1e30
SCALE = HD ** (-0.5)
LOG2E = 1.4426950408889634
C2 = SCALE * LOG2E
F32 = jnp.float32
BF16 = jnp.bfloat16
NT = (((1,), (1,)), ((), ()))
TN = (((0,), (0,)), ((), ()))
MESH = pl.DeviceIdType.MESH
BLOCK = 512


def params(mib, **more):
    return pltpu.CompilerParams(vmem_limit_bytes=mib << 20, **more)


def cost(flops, nbytes, trans=0):
    return pl.CostEstimate(flops=int(flops), bytes_accessed=int(nbytes), transcendentals=int(trans))


def rope_tables(places):
    half = HD // 2
    freq = 10000.0 ** (-jnp.arange(half, dtype=F32) * 2.0 / HD)
    angle = places.astype(F32)[:, None] * freq[None, :]
    cosine, sine = jnp.cos(angle), jnp.sin(angle)
    return jnp.concatenate([cosine, cosine], axis=1), jnp.concatenate([-sine, sine], axis=1)


def project_kernel(heads, tok_ref, w_ref, cos_ref, sin_ref, inner_ref, stat_ref, q_ref, kv_ref):
    x = tok_ref[...].astype(F32)
    center = x - jnp.mean(x, axis=1, keepdims=True)
    inverse = lax.rsqrt(jnp.mean(center * center, axis=1, keepdims=True) + EPS)
    inner = (center * inverse).astype(BF16)
    inner_ref[...] = inner
    stat_ref[...] = jnp.concatenate(
        [jnp.mean(x, axis=1, keepdims=True), inverse], axis=1
    )
    cosine, sine = cos_ref[...], sin_ref[...]
    span = heads * HD
    for part in range(3):
        out = jnp.dot(inner, w_ref[part], preferred_element_type=F32)
        if part == 2:
            kv_ref[:, span:] = out.astype(BF16)
            continue
        for h in range(heads):
            piece = out[:, h * HD : (h + 1) * HD]
            turned = (piece * cosine + pltpu.roll(piece, HD // 2, 1) * sine).astype(BF16)
            if part == 0:
                q_ref[:, h * HD : (h + 1) * HD] = turned
            else:
                kv_ref[:, h * HD : (h + 1) * HD] = turned


def project(tok_full, weight, cosine, sine, heads):
    rows, width = tok_full.shape
    span = heads * HD
    block = 256
    row = lambda n: pl.BlockSpec((block, n), lambda i: (i, 0))
    return pl.pallas_call(
        functools.partial(project_kernel, heads),
        grid=(rows // block,),
        in_specs=[
            row(width),
            pl.BlockSpec((3, width, span), lambda i: (0, 0, 0)),
            row(HD),
            row(HD),
        ],
        out_specs=[row(width), row(2), row(span), row(2 * span)],
        out_shape=[
            jax.ShapeDtypeStruct((rows, width), BF16),
            jax.ShapeDtypeStruct((rows, 2), F32),
            jax.ShapeDtypeStruct((rows, span), BF16),
            jax.ShapeDtypeStruct((rows, 2 * span), BF16),
        ],
        compiler_params=params(56),
        cost_estimate=cost(6 * rows * width * span, 6 * width * span + 6 * rows * width),
        name="project",
    )(tok_full, weight, cosine, sine)


def masked(scores, j, me, rows, begin):
    key_place = lax.broadcasted_iota(jnp.int32, scores.shape, 0) + j * rows
    query_place = lax.broadcasted_iota(jnp.int32, scores.shape, 1) + me * rows
    return jnp.where((key_place <= query_place) & (key_place >= begin), scores, NEG)


def attend_kernel(
    heads, info, q_ref, k_ref, v_ref, begin_ref, raw_ref, mixed_ref, lse_ref,
    high_ref, total_ref, acc_ref, s_ref,
):
    me, first, clear = info[0], info[1], info[2]
    j = pl.program_id(0)
    rows = q_ref.shape[0]

    @pl.when(j == 0)
    def _():
        high_ref[...] = jnp.full_like(high_ref, NEG)
        total_ref[...] = jnp.zeros_like(total_ref)
        acc_ref[...] = jnp.zeros_like(acc_ref)

    def block(hide):
        def score(h):
            hs = slice(h * HD, (h + 1) * HD)
            s = lax.dot_general(k_ref[:, hs], q_ref[:, hs], NT, preferred_element_type=F32)
            if hide:
                s = masked(s, j, me, rows, begin_ref[...])
            s_ref[h % 2] = s

        def spread(h):
            hs = slice(h * HD, (h + 1) * HD)
            s = s_ref[h % 2]
            old = high_ref[h : h + 1, :]
            new = jnp.maximum(old, jnp.max(s, axis=0, keepdims=True))
            high_ref[h : h + 1, :] = new
            p = jnp.exp2(s * C2 - new * C2)
            decay = jnp.exp2((old - new) * C2)
            total_ref[h : h + 1, :] = total_ref[h : h + 1, :] * decay + jnp.sum(
                p, axis=0, keepdims=True
            )
            acc_ref[h] = acc_ref[h] * decay + lax.dot_general(
                v_ref[:, hs], p.astype(BF16), TN, preferred_element_type=F32
            )

        score(0)
        for h in range(heads):
            if h + 1 < heads:
                score(h + 1)
            spread(h)

    @pl.when((j >= clear) & (j < me))
    def _():
        block(False)

    @pl.when(((j >= first) & (j < clear) & (j < me)) | (j == me))
    def _():
        block(True)

    @pl.when(j == me)
    def _():
        for h in range(heads):
            hs = slice(h * HD, (h + 1) * HD)
            out = (acc_ref[h] / total_ref[h : h + 1, :]).T
            raw_ref[:, hs] = out
            mixed_ref[:, hs] = out.astype(BF16)
        lse_ref[...] = high_ref[...] * C2 + jnp.log2(total_ref[...])


def attend(info, query, pairs, begin, heads):
    rows = query.shape[0]
    total = pairs.shape[0]
    span = heads * HD
    full = lambda shape: pl.BlockSpec(shape, lambda j, s: (0, 0))
    key = pl.BlockSpec((rows, span), lambda j, s: (jnp.clip(j, s[1], s[0]), 0))
    value = pl.BlockSpec((rows, span), lambda j, s: (jnp.clip(j, s[1], s[0]), 1))
    return pl.pallas_call(
        functools.partial(attend_kernel, heads),
        grid_spec=pltpu.PrefetchScalarGridSpec(
            num_scalar_prefetch=1,
            grid=(total // rows,),
            in_specs=[full((rows, span)), key, value, full((1, rows))],
            out_specs=[full((rows, span)), full((rows, span)), full((heads, rows))],
            scratch_shapes=[
                pltpu.VMEM((heads, rows), F32),
                pltpu.VMEM((heads, rows), F32),
                pltpu.VMEM((heads, HD, rows), F32),
                pltpu.VMEM((2, rows, rows), F32),
            ],
        ),
        out_shape=[
            jax.ShapeDtypeStruct((rows, span), F32),
            jax.ShapeDtypeStruct((rows, span), BF16),
            jax.ShapeDtypeStruct((heads, rows), F32),
        ],
        compiler_params=params(56),
        cost_estimate=cost(4 * rows * total * span, 4 * total * span, rows * total * heads),
        name="attend",
    )(info, query, pairs, pairs, begin)


CUBE = 8
CUBE_SENDS = 10


class Cube:
    def __init__(self, buf, send, recv):
        me = lax.axis_index("ctx")
        flip = (1 - 2 * (me % 2), 2 - 4 * ((me // 2) % 2), 4 - 8 * (me // 4))
        self.me, self.flip, self.buf, self.send, self.recv = me, flip, buf, send, recv
        self.rows = buf.shape[0] // CUBE

    def copy(self, n):
        core, x, y = self.flip
        half = self.rows // 2
        block, part, target = (
            (0, None, core),
            (0, 0, x), (0, 1, x), (0, 1, y), (0, 0, y),
            (x, 0, y), (y, 1, x),
            (x, None, core), (y, None, core), (x + y, None, core),
        )[n]
        start = (self.me + block) * self.rows
        size = self.rows
        if part is not None:
            start, size = start + part * half, half
        place = self.buf.at[pl.ds(pl.multiple_of(start, 16), size)]
        return pltpu.make_async_remote_copy(
            src_ref=place, dst_ref=place, send_sem=self.send.at[n], recv_sem=self.recv.at[n],
            device_id={"ctx": self.me + target}, device_id_type=MESH,
        )

    def arrived(self, n):
        self.copy(n).wait_recv()

    def start(self, *which):
        for n in which:
            self.copy(n).start()

    def signal(self, barrier):
        for target in self.flip:
            pl.semaphore_signal(
                barrier, inc=1, device_id={"ctx": self.me + target}, device_id_type=MESH
            )

    def block(self, step):
        core, x, y = self.flip
        on = lambda *steps: sum((step == n).astype(jnp.int32) for n in steps)
        return self.me + on(1, 4, 5, 7) * core + on(2, 4, 6, 7) * x + on(3, 5, 6, 7) * y

    def advance(self, step):
        @pl.when(step == 0)
        def _():
            self.start(0, 1, 3, 2, 4)

        @pl.when(step == 1)
        def _():
            self.arrived(0)

        @pl.when(step == 2)
        def _():
            self.arrived(1)
            self.start(5)
            self.arrived(3)
            self.start(6)
            self.arrived(2)
            self.start(7)

        @pl.when(step == 3)
        def _():
            self.arrived(4)
            self.start(8)

        @pl.when(step == 4)
        def _():
            self.arrived(7)

        @pl.when(step == 5)
        def _():
            self.arrived(8)

        @pl.when(step == 6)
        def _():
            self.arrived(5)
            self.arrived(6)
            self.start(9)

        @pl.when(step == 7)
        def _():
            self.arrived(9)

    def finish(self):
        for n in range(CUBE_SENDS):
            self.copy(n).wait_send()


SUM_SENDS = 11


class CubeSum:
    def __init__(self, own, out, land, send, recv):
        me = lax.axis_index("ctx")
        core, x, y = me % 2, (me // 2) % 2, me // 4
        self.me, self.own, self.out, self.land = me, own, out, land
        self.send, self.recv = send, recv
        rows = own.shape[0]
        self.half, self.quarter = rows // 2, rows // 4
        self.eighth, self.last = rows // 8, rows // 16
        mine = core * self.half
        first, second = mine, mine + self.quarter
        self.to = (1 - 2 * core, 2 - 4 * x, 4 - 8 * y)
        self.mine, self.other = mine, (1 - core) * self.half
        self.keep1 = (first + x * self.eighth, second + y * self.eighth)
        self.give1 = (first + (1 - x) * self.eighth, second + (1 - y) * self.eighth)
        self.keep2 = (self.keep1[0] + y * self.last, self.keep1[1] + x * self.last)
        self.give2 = (self.keep1[0] + (1 - y) * self.last, self.keep1[1] + (1 - x) * self.last)

    def place(self, ref, start, size):
        return ref.at[pl.ds(pl.multiple_of(start, 16), size)]

    def copy(self, n):
        core, x, y = self.to
        half, eighth, last, out, land = self.half, self.eighth, self.last, self.out, self.land
        landing = (0, half, half + eighth, half + 2 * eighth, half + 2 * eighth + last)
        mine = self.mine
        source, start, size, target = (
            (self.own, self.other, half, core),
            (land, self.give1[0] - mine, eighth, x), (land, self.give1[1] - mine, eighth, y),
            (land, self.give2[0] - mine, last, y), (land, self.give2[1] - mine, last, x),
            (out, self.keep2[0], last, y), (out, self.keep2[1], last, x),
            (out, self.keep1[0], eighth, x), (out, self.keep1[1], eighth, y),
            (out, mine, self.quarter, core),
            (out, mine + self.quarter, self.quarter, core),
        )[n]
        src = self.place(source, start, size)
        dst = land.at[pl.ds(landing[n], size)] if n < 5 else src
        return pltpu.make_async_remote_copy(
            src_ref=src, dst_ref=dst, send_sem=self.send.at[n], recv_sem=self.recv.at[n],
            device_id={"ctx": self.me + target}, device_id_type=MESH,
        )

    def add(self, target, to, source, at, landed, size):
        step = size
        while step * self.own.shape[1] > 256 * 1024 and step % 32 == 0:
            step = step // 2

        def part(i, carry):
            rows = lambda begin: pl.ds(pl.multiple_of(begin + i * step, 16), step)
            total = source[rows(at), :].astype(F32) + self.land[rows(landed), :].astype(F32)
            target[rows(to), :] = total.astype(BF16)
            return carry

        lax.fori_loop(0, size // step, part, 0)

    def step(self, k):
        half, eighth, last, land, mine = self.half, self.eighth, self.last, self.land, self.mine
        if k == 0:
            self.copy(0).start()
        if k == 1:
            self.copy(0).wait_recv()
            for i in range(2):
                at = self.give1[i]
                self.add(land, at - mine, self.own, at, at - mine, eighth)
                self.copy(1 + i).start()
            for i in range(2):
                at = self.keep1[i]
                self.add(land, at - mine, self.own, at, at - mine, eighth)
        if k == 2:
            for i in range(2):
                self.copy(1 + i).wait_recv()
                landed = half + i * eighth - self.keep1[i]
                at = self.give2[i]
                self.add(land, at - mine, land, at - mine, landed + at, last)
                self.copy(3 + i).start()
                at = self.keep2[i]
                self.add(land, at - mine, land, at - mine, landed + at, last)
        if k == 3:
            for i in range(2):
                self.copy(3 + i).wait_recv()
                at = self.keep2[i]
                self.add(self.out, at, land, at - mine, half + 2 * eighth + i * last, last)
                self.copy(5 + i).start()
        if k == 4:
            for i in range(2):
                self.copy(5 + i).wait_recv()
                self.copy(7 + i).start()
        if k == 5:
            for i in range(2):
                self.copy(7 + i).wait_recv()
                self.copy(9 + i).start()
        if k == 6:
            for i in range(2):
                self.copy(9 + i).wait_recv()
            for n in range(SUM_SENDS):
                self.copy(n).wait_send()

    def signal(self, barrier):
        for target in self.to:
            pl.semaphore_signal(
                barrier, inc=1, device_id={"ctx": self.me + target}, device_id_type=MESH
            )


def sum_scratch(shape):
    return [
        pltpu.VMEM((shape[0] // 2 + 3 * (shape[0] // 8), shape[1]), BF16),
        pltpu.SemaphoreType.DMA((SUM_SENDS,)),
        pltpu.SemaphoreType.DMA((SUM_SENDS,)),
    ]


def hidden_scores(scores, key_block, query_block, rows, begin):
    key_place = lax.broadcasted_iota(jnp.int32, scores.shape, 0) + key_block * rows
    query_place = lax.broadcasted_iota(jnp.int32, scores.shape, 1) + query_block * rows
    return jnp.where((key_place <= query_place) & (key_place >= begin), scores, NEG)


def attend_far_kernel(
    heads, n, q_ref, own_ref, begin_ref, cot_ref,
    raw_ref, mixed_ref, lse_ref, pair_ref, full_ref,
    high_ref, total_ref, acc_ref, s_ref, send, recv, zsend, zrecv,
):
    rows = q_ref.shape[0]
    span = heads * HD
    shard = cot_ref.shape[1]
    at = lax.axis_index("tp")
    cube = Cube(pair_ref, send, recv)
    me = cube.me
    barrier = pltpu.get_barrier_semaphore()
    cube.signal(barrier)

    @pl.when(at > 0)
    def _():
        pl.semaphore_signal(barrier, inc=1, device_id={"tp": at - 1}, device_id_type=MESH)

    @pl.when(at < n - 1)
    def _():
        pl.semaphore_signal(barrier, inc=1, device_id={"tp": at + 1}, device_id_type=MESH)

    pair_ref[pl.ds(pl.multiple_of(me * rows, 16), rows), :] = own_ref[...]
    full_ref[:, pl.ds(pl.multiple_of(at * shard, 128), shard)] = cot_ref[...]
    high_ref[...] = jnp.full_like(high_ref, NEG)
    total_ref[...] = jnp.zeros_like(total_ref)
    acc_ref[...] = jnp.zeros_like(acc_ref)
    pl.semaphore_wait(barrier, jnp.where((at > 0) & (at < n - 1), 5, 4))

    def pass_on(right, s, k):
        place = full_ref.at[:, pl.ds(pl.multiple_of(s * shard, 128), shard)]
        which = (1 if right else 0, k)
        return pltpu.make_async_remote_copy(
            src_ref=place, dst_ref=place, send_sem=zsend.at[which], recv_sem=zrecv.at[which],
            device_id={"tp": at + 1 if right else at - 1}, device_id_type=MESH,
        )

    def line_step(k):
        @pl.when(at >= k)
        def _():
            if k > 0:
                pass_on(True, at - k, k - 1).wait_recv()

            @pl.when(at < n - 1)
            def _():
                pass_on(True, at - k, k).start()

        @pl.when(at + k < n)
        def _():
            if k > 0:
                pass_on(False, at + k, k - 1).wait_recv()

            @pl.when(at > 0)
            def _():
                pass_on(False, at + k, k).start()

    def turn(step, carry):
        cube.advance(step)
        for k in range(n):
            @pl.when(step == min(k * 2, CUBE - 1 - (n - 1 - k)) if n <= CUBE else k)
            def _():
                line_step(k)
        block = cube.block(step)

        @pl.when(block <= me)
        def _():
            place = pl.ds(pl.multiple_of(block * rows, 16), rows)

            def score(h):
                hs = slice(h * HD, (h + 1) * HD)
                s = lax.dot_general(
                    pair_ref[place, hs], q_ref[:, hs], NT, preferred_element_type=F32
                )
                s_ref[h % 2] = hidden_scores(s, block, me, rows, begin_ref[...])

            def spread(h):
                s = s_ref[h % 2]
                old = high_ref[h : h + 1, :]
                new = jnp.maximum(old, jnp.max(s, axis=0, keepdims=True))
                high_ref[h : h + 1, :] = new
                p = jnp.exp2(s * C2 - new * C2)
                decay = jnp.exp2((old - new) * C2)
                total_ref[h : h + 1, :] = total_ref[h : h + 1, :] * decay + jnp.sum(
                    p, axis=0, keepdims=True
                )
                acc_ref[h] = acc_ref[h] * decay + lax.dot_general(
                    pair_ref[place, span + h * HD : span + (h + 1) * HD], p.astype(BF16), TN,
                    preferred_element_type=F32,
                )

            score(0)
            for h in range(heads):
                if h + 1 < heads:
                    score(h + 1)
                spread(h)

        return carry

    lax.fori_loop(0, CUBE, turn, 0)
    for h in range(heads):
        hs = slice(h * HD, (h + 1) * HD)
        out = (acc_ref[h] / total_ref[h : h + 1, :]).T
        raw_ref[:, hs] = out
        mixed_ref[:, hs] = out.astype(BF16)
    lse_ref[...] = high_ref[...] * C2 + jnp.log2(total_ref[...])
    cube.finish()
    for k in range(n):
        @pl.when((at >= k) & (at < n - 1))
        def _():
            pass_on(True, at - k, k).wait_send()

        @pl.when((at + k < n) & (at > 0))
        def _():
            pass_on(False, at + k, k).wait_send()


def attend_far(query, pairs, begin, cot, heads, n):
    rows = query.shape[0]
    span = heads * HD
    vmem = pl.BlockSpec(memory_space=pltpu.VMEM)
    return pl.pallas_call(
        functools.partial(attend_far_kernel, heads, n),
        in_specs=[vmem] * 4,
        out_specs=[vmem] * 5,
        out_shape=[
            jax.ShapeDtypeStruct((rows, span), F32),
            jax.ShapeDtypeStruct((rows, span), BF16),
            jax.ShapeDtypeStruct((heads, rows), F32),
            jax.ShapeDtypeStruct((CUBE * rows, 2 * span), BF16),
            jax.ShapeDtypeStruct((rows, n * cot.shape[1]), BF16),
        ],
        scratch_shapes=[
            pltpu.VMEM((heads, rows), F32),
            pltpu.VMEM((heads, rows), F32),
            pltpu.VMEM((heads, HD, rows), F32),
            pltpu.VMEM((2, rows, rows), F32),
            pltpu.SemaphoreType.DMA((CUBE_SENDS,)),
            pltpu.SemaphoreType.DMA((CUBE_SENDS,)),
            pltpu.SemaphoreType.DMA((2, n)),
            pltpu.SemaphoreType.DMA((2, n)),
        ],
        compiler_params=params(58, collective_id=2, has_side_effects=True),
        cost_estimate=cost(1e6, 1e6),
        name="attend_far",
    )(query, pairs, begin, cot)


def attend_back_far_kernel(
    heads, n, g_ref, q_ref, pair_ref, begin_ref, part_ref,
    dq_ref, dk_ref, dv_ref, layer_ref,
    all_ref, acc_ref, rows_ref, s_ref, p_ref, land_ref, send, recv, zsend, zrecv,
):
    rows = g_ref.shape[0]
    span = heads * HD
    shard = layer_ref.shape[1]
    at = lax.axis_index("tp")
    cube = Cube(all_ref, send, recv)
    me = cube.me
    barrier = pltpu.get_barrier_semaphore()
    cube.signal(barrier)
    for o in range(1, n):
        pl.semaphore_signal(
            barrier, inc=1, device_id={"tp": lax.rem(at + o, n)}, device_id_type=MESH
        )
    all_ref[pl.ds(pl.multiple_of(me * rows, 16), rows), :] = g_ref[...]
    acc_ref[...] = jnp.zeros_like(acc_ref)
    dk_ref[...] = jnp.zeros_like(dk_ref)
    dv_ref[...] = jnp.zeros_like(dv_ref)
    pl.semaphore_wait(barrier, 3 + n - 1)

    def term(o):
        target = lax.rem(at + o, n)
        return pltpu.make_async_remote_copy(
            src_ref=part_ref.at[:, pl.ds(pl.multiple_of(target * shard, 128), shard)],
            dst_ref=land_ref.at[o - 1],
            send_sem=zsend.at[o - 1], recv_sem=zrecv.at[o - 1],
            device_id={"tp": target}, device_id_type=MESH,
        )

    own = pl.ds(pl.multiple_of(me * rows, 16), rows)

    def turn(step, carry):
        cube.advance(step)

        @pl.when(step == 0)
        def _():
            for o in range(1, n):
                term(o).start()

        block = cube.block(step)
        place = pl.ds(pl.multiple_of(block * rows, 16), rows)

        def scores(h, key_block, key_place, query_block, query_place):
            hs = slice(h * HD, (h + 1) * HD)
            vs = slice(span + h * HD, span + (h + 1) * HD)
            s = lax.dot_general(
                pair_ref[key_place, hs], q_ref[query_place, hs], NT, preferred_element_type=F32
            )
            begin = begin_ref[pl.ds(query_block, 1), :]
            s_ref[h % 2] = hidden_scores(s, key_block, query_block, rows, begin)
            p_ref[h % 2] = lax.dot_general(
                pair_ref[key_place, vs], all_ref[query_place, hs], NT, preferred_element_type=F32
            )

        def read_rows(query_place):
            coded = all_ref[query_place, span:].astype(F32).T
            for k in range(2 * heads):
                rows_ref[k : k + 1, :] = (
                    coded[3 * k : 3 * k + 1]
                    + coded[3 * k + 1 : 3 * k + 2]
                    + coded[3 * k + 2 : 3 * k + 3]
                )

        def weights(h):
            p = jnp.exp2(s_ref[h % 2] * C2 - rows_ref[h : h + 1, :])
            ds = p * (p_ref[h % 2] - rows_ref[heads + h : heads + h + 1, :])
            return p.astype(BF16), ds.astype(BF16)

        @pl.when(block <= me)
        def _():
            read_rows(own)
            scores(0, block, place, me, own)
            for h in range(heads):
                if h + 1 < heads:
                    scores(h + 1, block, place, me, own)
                _, ds = weights(h)
                acc_ref[h] = acc_ref[h] + lax.dot_general(
                    pair_ref[place, h * HD : (h + 1) * HD], ds, TN, preferred_element_type=F32
                )

        @pl.when(block >= me)
        def _():
            read_rows(place)
            scores(0, me, own, block, place)
            for h in range(heads):
                hs = slice(h * HD, (h + 1) * HD)
                if h + 1 < heads:
                    scores(h + 1, me, own, block, place)
                p, ds = weights(h)
                dv_ref[:, hs] += jnp.dot(p, all_ref[place, hs], preferred_element_type=F32)
                dk_ref[:, hs] += jnp.dot(ds, q_ref[place, hs], preferred_element_type=F32)

        return carry

    lax.fori_loop(0, CUBE, turn, 0)
    for h in range(heads):
        dq_ref[:, h * HD : (h + 1) * HD] = (acc_ref[h] * SCALE).T
    dk_ref[...] = dk_ref[...] * SCALE
    total = part_ref[:, pl.ds(pl.multiple_of(at * shard, 128), shard)].astype(F32)
    for o in range(1, n):
        term(o).wait_recv()
        total = total + land_ref[o - 1].astype(F32)
    layer_ref[...] = total.astype(BF16)
    cube.finish()
    for o in range(1, n):
        term(o).wait_send()


def attend_back_far(grad, all_query, all_pairs, all_begin, part, heads, n):
    rows = grad.shape[0]
    span = heads * HD
    shard = part.shape[1] // n
    vmem = pl.BlockSpec(memory_space=pltpu.VMEM)
    wide = jax.ShapeDtypeStruct((rows, span), F32)
    return pl.pallas_call(
        functools.partial(attend_back_far_kernel, heads, n),
        in_specs=[vmem] * 5,
        out_specs=[vmem] * 4,
        out_shape=[wide, wide, wide, jax.ShapeDtypeStruct((rows, shard), BF16)],
        scratch_shapes=[
            pltpu.VMEM((CUBE * rows, span + HD), BF16),
            pltpu.VMEM((heads, HD, rows), F32),
            pltpu.VMEM((2 * heads, rows), F32),
            pltpu.VMEM((2, rows, rows), F32),
            pltpu.VMEM((2, rows, rows), F32),
            pltpu.VMEM((n - 1, rows, shard), BF16),
            pltpu.SemaphoreType.DMA((CUBE_SENDS,)),
            pltpu.SemaphoreType.DMA((CUBE_SENDS,)),
            pltpu.SemaphoreType.DMA((n - 1,)),
            pltpu.SemaphoreType.DMA((n - 1,)),
        ],
        compiler_params=params(60, collective_id=3, has_side_effects=True),
        cost_estimate=cost(1e6, 1e6),
        name="attend_back_far",
    )(grad, all_query, all_pairs, all_begin, part)


def query_grad_kernel(
    heads, info, q_ref, do_ref, lse_ref, delta_ref, k_ref, v_ref, begin_ref,
    dq_ref, acc_ref, s_ref, g_ref,
):
    me, first, clear = info[0], info[1], info[2]
    j = pl.program_id(0)
    rows = q_ref.shape[0]

    @pl.when(j == 0)
    def _():
        acc_ref[...] = jnp.zeros_like(acc_ref)

    def block(hide):
        def score(h):
            hs = slice(h * HD, (h + 1) * HD)
            s = lax.dot_general(k_ref[:, hs], q_ref[:, hs], NT, preferred_element_type=F32)
            if hide:
                s = masked(s, j, me, rows, begin_ref[...])
            s_ref[h % 2] = s
            g_ref[h % 2] = lax.dot_general(
                v_ref[:, hs], do_ref[:, hs], NT, preferred_element_type=F32
            )

        def spread(h):
            hs = slice(h * HD, (h + 1) * HD)
            p = jnp.exp2(s_ref[h % 2] * C2 - lse_ref[h : h + 1, :])
            ds = (p * (g_ref[h % 2] - delta_ref[h : h + 1, :])).astype(BF16)
            acc_ref[h] = acc_ref[h] + lax.dot_general(
                k_ref[:, hs], ds, TN, preferred_element_type=F32
            )

        score(0)
        for h in range(heads):
            if h + 1 < heads:
                score(h + 1)
            spread(h)

    @pl.when((j >= clear) & (j < me))
    def _():
        block(False)

    @pl.when(((j >= first) & (j < clear) & (j < me)) | (j == me))
    def _():
        block(True)

    @pl.when(j == me)
    def _():
        for h in range(heads):
            dq_ref[:, h * HD : (h + 1) * HD] = (acc_ref[h] * SCALE).T


def query_grad(info, query, grad_mixed, lse, delta, pairs, begin, heads):
    rows = query.shape[0]
    total = pairs.shape[0]
    span = heads * HD
    full = lambda shape: pl.BlockSpec(shape, lambda j, s: (0, 0))
    key = pl.BlockSpec((rows, span), lambda j, s: (jnp.clip(j, s[1], s[0]), 0))
    value = pl.BlockSpec((rows, span), lambda j, s: (jnp.clip(j, s[1], s[0]), 1))
    wide = full((rows, span))
    thin = full((heads, rows))
    return pl.pallas_call(
        functools.partial(query_grad_kernel, heads),
        grid_spec=pltpu.PrefetchScalarGridSpec(
            num_scalar_prefetch=1,
            grid=(total // rows,),
            in_specs=[wide, wide, thin, thin, key, value, full((1, rows))],
            out_specs=wide,
            scratch_shapes=[
                pltpu.VMEM((heads, HD, rows), F32),
                pltpu.VMEM((2, rows, rows), F32),
                pltpu.VMEM((2, rows, rows), F32),
            ],
        ),
        out_shape=jax.ShapeDtypeStruct((rows, span), F32),
        compiler_params=params(58),
        cost_estimate=cost(6 * rows * total * span, 4 * total * span, rows * total * heads),
        name="query_grad",
    )(info, query, grad_mixed, lse, delta, pairs, pairs, begin)


def key_grad_kernel(
    heads, info, k_ref, v_ref, q_ref, g_ref, begin_ref, dk_ref, dv_ref,
    rows_ref, s_ref, p_ref,
):
    me, last, clear = info[0], info[1], info[2]
    j = pl.program_id(0)
    rows = k_ref.shape[0]
    span = heads * HD

    @pl.when(j == me)
    def _():
        dk_ref[...] = jnp.zeros_like(dk_ref)
        dv_ref[...] = jnp.zeros_like(dv_ref)

    def block(hide):
        coded = g_ref[:, span:].astype(F32).T
        for n in range(2 * heads):
            rows_ref[n : n + 1, :] = (
                coded[3 * n : 3 * n + 1] + coded[3 * n + 1 : 3 * n + 2] + coded[3 * n + 2 : 3 * n + 3]
            )

        def score(h):
            hs = slice(h * HD, (h + 1) * HD)
            s = lax.dot_general(k_ref[:, hs], q_ref[:, hs], NT, preferred_element_type=F32)
            if hide:
                key_place = lax.broadcasted_iota(jnp.int32, s.shape, 0) + me * rows
                query_place = lax.broadcasted_iota(jnp.int32, s.shape, 1) + j * rows
                s = jnp.where(
                    (key_place <= query_place) & (key_place >= begin_ref[...]), s, NEG
                )
            s_ref[h % 2] = s
            p_ref[h % 2] = lax.dot_general(
                v_ref[:, hs], g_ref[:, hs], NT, preferred_element_type=F32
            )

        def spread(h):
            hs = slice(h * HD, (h + 1) * HD)
            p = jnp.exp2(s_ref[h % 2] * C2 - rows_ref[h : h + 1, :])
            ds = (p * (p_ref[h % 2] - rows_ref[heads + h : heads + h + 1, :])).astype(BF16)
            dv_ref[:, hs] += jnp.dot(p.astype(BF16), g_ref[:, hs], preferred_element_type=F32)
            dk_ref[:, hs] += jnp.dot(ds, q_ref[:, hs], preferred_element_type=F32)

        score(0)
        for h in range(heads):
            if h + 1 < heads:
                score(h + 1)
            spread(h)

    @pl.when((j > me) & (j <= clear))
    def _():
        block(False)

    @pl.when((j == me) | ((j > me) & (j > clear) & (j <= last)))
    def _():
        block(True)

    @pl.when(j == pl.num_programs(0) - 1)
    def _():
        dk_ref[...] = dk_ref[...] * SCALE


def key_grad(info, pairs, all_query, all_grad, all_begin, heads):
    rows = pairs.shape[0]
    total = all_query.shape[0]
    span = heads * HD
    full = lambda shape, at=0: pl.BlockSpec(shape, lambda j, s: (0, at))
    near = lambda j, s: (jnp.clip(j, s[0], s[1]), 0)
    wide = full((rows, span))
    return pl.pallas_call(
        functools.partial(key_grad_kernel, heads),
        grid_spec=pltpu.PrefetchScalarGridSpec(
            num_scalar_prefetch=1,
            grid=(total // rows,),
            in_specs=[
                wide, full((rows, span), 1),
                pl.BlockSpec((rows, span), near),
                pl.BlockSpec((rows, span + HD), near),
                pl.BlockSpec((1, rows), lambda j, s: (0, jnp.clip(j, s[0], s[1]))),
            ],
            out_specs=[wide, wide],
            scratch_shapes=[
                pltpu.VMEM((2 * heads, rows), F32),
                pltpu.VMEM((2, rows, rows), F32),
                pltpu.VMEM((2, rows, rows), F32),
            ],
        ),
        out_shape=[jax.ShapeDtypeStruct((rows, span), F32)] * 2,
        compiler_params=params(58),
        cost_estimate=cost(8 * rows * total * span, 4 * total * span, rows * total * heads),
        name="key_grad",
    )(info, pairs, pairs, all_query, all_grad, all_begin)


def mixed_grad_kernel(heads, branch_ref, w_ref, raw_ref, lse_ref, out_ref, delta_ref):
    span = heads * HD
    low = lax.dot_general(
        branch_ref[...], w_ref[...], NT, preferred_element_type=F32
    ).astype(BF16)
    out_ref[:, :span] = low
    count = low.shape[0]
    both = low.astype(F32) * raw_ref[...]
    for h in range(heads):
        delta_ref[h : h + 1, :] = jnp.sum(both[:, h * HD : (h + 1) * HD].T, axis=0, keepdims=True)
    lines = []
    for n in range(2 * heads):
        value = lse_ref[n : n + 1, :] if n < heads else delta_ref[n - heads : n - heads + 1, :]
        for _ in range(3):
            piece = value.astype(BF16).astype(F32)
            lines.append(piece)
            value = value - piece
    lines.append(jnp.zeros((HD - len(lines), count), F32))
    out_ref[:, span:] = jnp.concatenate(lines, axis=0).T.astype(BF16)


def mixed_grad(branch, weight, raw, lse, heads):
    rows, width = branch.shape
    span = heads * HD
    block = 256
    row = lambda n: pl.BlockSpec((block, n), lambda i: (i, 0))
    line = pl.BlockSpec((heads, block), lambda i: (0, i))
    return pl.pallas_call(
        functools.partial(mixed_grad_kernel, heads),
        grid=(rows // block,),
        in_specs=[row(width), pl.BlockSpec((span, width), lambda i: (0, 0)), row(span), line],
        out_specs=[row(span + HD), line],
        out_shape=[
            jax.ShapeDtypeStruct((rows, span + HD), BF16),
            jax.ShapeDtypeStruct((heads, rows), F32),
        ],
        compiler_params=params(56),
        cost_estimate=cost(2 * rows * width * span, 2 * width * span + 4 * rows * width),
        name="mixed_grad",
    )(branch, weight, raw, lse)


def feed_kernel(inner_ref, cot_ref, w_ref, down_ref, hidden_ref, dgu_ref):
    block = down_ref.shape[0]
    both = jnp.dot(inner_ref[...], w_ref[...], preferred_element_type=F32)
    grad = lax.dot_general(cot_ref[...], down_ref[...], NT, preferred_element_type=F32)
    gate, up = both[:, :block], both[:, block:]
    sigma = 1.0 / (1.0 + jnp.exp(-gate))
    active = gate * sigma
    hidden_ref[...] = (active * up).astype(BF16)
    dgu_ref[:, :block] = (grad * up * sigma * (1.0 + gate * (1.0 - sigma))).astype(BF16)
    dgu_ref[:, block:] = (grad * active).astype(BF16)


def feed(inner, cot, weight, down, block):
    rows, width = inner.shape
    units = down.shape[0]
    whole = pl.BlockSpec((rows, width), lambda j: (0, 0))
    return pl.pallas_call(
        feed_kernel,
        grid=(units // block,),
        in_specs=[
            whole, whole,
            pl.BlockSpec((width, 2 * block), lambda j: (0, j)),
            pl.BlockSpec((block, width), lambda j: (j, 0)),
        ],
        out_specs=[
            pl.BlockSpec((rows, block), lambda j: (0, j)),
            pl.BlockSpec((rows, 2 * block), lambda j: (0, j)),
        ],
        out_shape=[
            jax.ShapeDtypeStruct((rows, units), BF16),
            jax.ShapeDtypeStruct((rows, 2 * units), BF16),
        ],
        compiler_params=params(56),
        cost_estimate=cost(
            6 * rows * width * units, 6 * width * units + 4 * rows * width, rows * units
        ),
        name="feed",
    )(inner, cot, weight, down)


def weave_kernel(block, sum_ref, out_ref):
    for j in range(sum_ref.shape[1] // (2 * block)):
        for k in range(2):
            at = (2 * j + k) * block
            out_ref[:, k, j * block : (j + 1) * block] = sum_ref[:, at : at + block].astype(F32)


def weave(summed, block):
    width, both = summed.shape
    rows = 256
    return pl.pallas_call(
        functools.partial(weave_kernel, block),
        grid=(width // rows,),
        in_specs=[pl.BlockSpec((rows, both), lambda i: (i, 0))],
        out_specs=pl.BlockSpec((rows, 2, both // 2), lambda i: (i, 0, 0)),
        out_shape=jax.ShapeDtypeStruct((width, 2, both // 2), F32),
        compiler_params=params(56),
        cost_estimate=cost(width * both, 6 * width * both),
        name="weave",
    )(summed)


def line_barrier(at, n):
    barrier = pltpu.get_barrier_semaphore()

    @pl.when(at > 0)
    def _():
        pl.semaphore_signal(barrier, inc=1, device_id={"tp": at - 1}, device_id_type=MESH)

    @pl.when(at < n - 1)
    def _():
        pl.semaphore_signal(barrier, inc=1, device_id={"tp": at + 1}, device_id_type=MESH)

    pl.semaphore_wait(barrier, jnp.where((at > 0) & (at < n - 1), 2, 1))


def sum_rows(n, sub, part_ref, out_ref, row_fn, from_left, from_right, send, recv):
    at = lax.axis_index("tp")
    chunks = part_ref.shape[0] // sub
    middle = (n // 2 - 1, n // 2)

    def link(kind, right, src, dst, c):
        which = (kind * 2 + (1 if right else 0), c)
        return pltpu.make_async_remote_copy(
            src_ref=src.at[pl.ds(c * sub, sub)],
            dst_ref=dst.at[pl.ds(c * sub, sub)],
            send_sem=send.at[which],
            recv_sem=recv.at[which],
            device_id={"tp": at + 1 if right else at - 1},
            device_id_type=MESH,
        )

    def came(right):
        return from_left if right else from_right

    def first(right, c):
        return link(0, right, part_ref, came(right), c)

    def onward(right, c):
        return link(0, right, came(right), came(right), c)

    def hand(right, c):
        return link(1, right, out_ref, out_ref, c)

    def reduce_step(c):
        owner = middle[c % 2]
        rows = slice(c * sub, (c + 1) * sub)
        for right in (True, False):
            edge = 0 if right else n - 1
            held = came(right)

            @pl.when(((at < owner) if right else (at > owner)) & (at != edge))
            def _():
                copy = onward(right, c)
                copy.wait_recv()
                held[rows, :] = (
                    held[rows, :].astype(F32) + part_ref[rows, :].astype(F32)
                ).astype(BF16)
                copy.start()

    def final_step(c):
        owner = middle[c % 2]
        rows = slice(c * sub, (c + 1) * sub)

        @pl.when(at == owner)
        def _():
            total = part_ref[rows, :].astype(F32)
            onward(True, c).wait_recv()
            total = total + from_left[rows, :].astype(F32)
            onward(False, c).wait_recv()
            total = total + from_right[rows, :].astype(F32)
            row_fn(total, rows)
            hand(True, c).start()
            hand(False, c).start()

    def hand_step(c):
        owner = middle[c % 2]
        for right in (True, False):
            edge = n - 1 if right else 0

            @pl.when((at > owner) if right else (at < owner))
            def _():
                copy = hand(right, c)
                copy.wait_recv()

                @pl.when(at != edge)
                def _():
                    copy.start()

    for c in range(chunks):
        @pl.when(at == 0)
        def _():
            first(True, c).start()

        @pl.when(at == n - 1)
        def _():
            first(False, c).start()

    for c in range(chunks + 4):
        if c < chunks:
            reduce_step(c)
        if 2 <= c < chunks + 2:
            final_step(c - 2)
        if c >= 4:
            hand_step(c - 4)
    for c in range(chunks):
        owner = middle[c % 2]

        @pl.when(at < owner)
        def _():
            first(True, c).wait_send()

        @pl.when(at > owner)
        def _():
            first(False, c).wait_send()

        @pl.when((at >= owner) & (at < n - 1))
        def _():
            hand(True, c).wait_send()

        @pl.when((at <= owner) & (at > 0))
        def _():
            hand(False, c).wait_send()


def merge_kernel(
    n, sub, part_ref, tok_ref, inner_ref, resid_ref, stat_ref, from_left, from_right, send, recv
):
    line_barrier(lax.axis_index("tp"), n)
    resid_ref[...] = jnp.zeros_like(resid_ref)
    stat_ref[...] = jnp.zeros_like(stat_ref)

    def row_fn(total, rows):
        x = tok_ref[rows, :].astype(F32) + total
        mean = jnp.mean(x, axis=1, keepdims=True)
        center = x - mean
        inverse = lax.rsqrt(jnp.mean(center * center, axis=1, keepdims=True) + EPS)
        resid_ref[rows, :] = x
        stat_ref[rows, :] = jnp.concatenate([mean, inverse], axis=1)
        inner_ref[rows, :] = (center * inverse).astype(BF16)

    sum_rows(n, sub, part_ref, inner_ref, row_fn, from_left, from_right, send, recv)


def merge(part, tok_full, n):
    rows, width = part.shape
    sub = 32
    vmem = pl.BlockSpec(memory_space=pltpu.VMEM)
    return pl.pallas_call(
        functools.partial(merge_kernel, n, sub),
        in_specs=[vmem] * 2,
        out_specs=[vmem] * 3,
        out_shape=[
            jax.ShapeDtypeStruct((rows, width), BF16),
            jax.ShapeDtypeStruct((rows, width), F32),
            jax.ShapeDtypeStruct((rows, 2), F32),
        ],
        scratch_shapes=[pltpu.VMEM((rows, width), BF16)] * 2
        + [pltpu.SemaphoreType.DMA((4, rows // sub))] * 2,
        compiler_params=params(56, collective_id=5, has_side_effects=True),
        cost_estimate=cost(1e6, 1e6),
        name="merge",
    )(part, tok_full)


def norm_back_kernel(
    n, sub, part_ref, cot_ref, resid_ref, stat_ref, out_ref, from_left, from_right, send, recv
):
    line_barrier(lax.axis_index("tp"), n)

    def row_fn(total, rows):
        inverse = stat_ref[rows, 1:2]
        normed = (resid_ref[rows, :] - stat_ref[rows, 0:1]) * inverse
        mean = jnp.mean(total, axis=1, keepdims=True)
        inner = jnp.mean(total * normed, axis=1, keepdims=True)
        out = cot_ref[rows, :].astype(F32) + inverse * (total - mean - normed * inner)
        out_ref[rows, :] = out.astype(BF16)

    sum_rows(n, sub, part_ref, out_ref, row_fn, from_left, from_right, send, recv)


def norm_back(part, cot, resid, stat, n):
    rows, width = part.shape
    sub = 32
    vmem = pl.BlockSpec(memory_space=pltpu.VMEM)
    return pl.pallas_call(
        functools.partial(norm_back_kernel, n, sub),
        in_specs=[vmem] * 4,
        out_specs=vmem,
        out_shape=jax.ShapeDtypeStruct((rows, width), BF16),
        scratch_shapes=[pltpu.VMEM((rows, width), BF16)] * 2
        + [pltpu.SemaphoreType.DMA((4, rows // sub))] * 2,
        compiler_params=params(56, collective_id=1, has_side_effects=True),
        cost_estimate=cost(1e6, 1e6),
        name="norm_back",
    )(part, cot, resid, stat)


def unrotate_kernel(heads, dq_ref, dk_ref, dv_ref, cos_ref, sin_ref, dproj_ref):
    cosine, sine = cos_ref[...], sin_ref[...]
    span = heads * HD

    def back(piece):
        return (piece * cosine - pltpu.roll(piece, HD // 2, 1) * sine).astype(BF16)

    for h in range(heads):
        hs = slice(h * HD, (h + 1) * HD)
        dproj_ref[:, hs] = back(dq_ref[:, hs])
        dproj_ref[:, span + h * HD : span + (h + 1) * HD] = back(dk_ref[:, hs])
    dproj_ref[:, 2 * span :] = dv_ref[...].astype(BF16)


def unrotate(dq, dk, dv, cosine, sine, heads):
    rows, span = dq.shape
    block = 256
    row = lambda n: pl.BlockSpec((block, n), lambda i: (i, 0))
    return pl.pallas_call(
        functools.partial(unrotate_kernel, heads),
        grid=(rows // block,),
        in_specs=[row(span), row(span), row(span), row(HD), row(HD)],
        out_specs=row(3 * span),
        out_shape=jax.ShapeDtypeStruct((rows, 3 * span), BF16),
        compiler_params=params(56),
        cost_estimate=cost(1e6, 18 * rows * span),
        name="unrotate",
    )(dq, dk, dv, cosine, sine)


def unproject_kernel(heads, n, cube, dproj_ref, tok_ref, stat_ref, w_ref, branch_ref, *refs):
    sums = []
    if cube:
        in_ref, og_ref, out_ref, in_out, og_out = refs[:5]
        part_ref, mine_ref, land_ref, sums_ref, far_ref, send, recv, ssend, srecv = refs[5:14]
        sums = [CubeSum(in_ref, in_out, *refs[14:17]), CubeSum(og_ref, og_out, *refs[17:20])]
    else:
        out_ref, part_ref, mine_ref, land_ref, sums_ref, far_ref, send, recv, ssend, srecv = refs

    def advance(k):
        for item in sums:
            item.step(k)

    rows, width = tok_ref.shape
    shard = width // n
    span = heads * HD
    at = lax.axis_index("tp")
    barrier = pltpu.get_barrier_semaphore()
    for o in range(1, n):
        pl.semaphore_signal(
            barrier, inc=1, device_id={"tp": lax.rem(at + o, n)}, device_id_type=MESH
        )
    if cube:
        sums[0].signal(barrier)
    pl.semaphore_wait(barrier, n - 1 + (3 if cube else 0))
    advance(0)
    block = 256
    count = rows // block

    def term(o, i):
        target = lax.rem(at + o, n)
        place = pl.ds(i * block, block)
        return pltpu.make_async_remote_copy(
            src_ref=part_ref.at[place, pl.ds(pl.multiple_of(target * shard, 128), shard)],
            dst_ref=land_ref.at[o - 1, place],
            send_sem=send.at[o - 1, i], recv_sem=recv.at[o - 1, i],
            device_id={"tp": target}, device_id_type=MESH,
        )

    def totals(o):
        return pltpu.make_async_remote_copy(
            src_ref=sums_ref, dst_ref=far_ref.at[o - 1],
            send_sem=ssend.at[o - 1], recv_sem=srecv.at[o - 1],
            device_id={"tp": lax.rem(at + o, n)}, device_id_type=MESH,
        )

    own = pl.ds(pl.multiple_of(at * shard, 128), shard)
    for i in range(count):
        place = pl.ds(i * block, block)
        total = None
        for part in range(3):
            piece = lax.dot_general(
                dproj_ref[place, part * span : (part + 1) * span], w_ref[part], NT,
                preferred_element_type=F32,
            )
            total = piece if total is None else total + piece
        part_ref[place, :] = total.astype(BF16)
        for o in range(1, n):
            term(o, i).start()
        normed = (tok_ref[place, :].astype(F32) - stat_ref[place, 0:1]) * stat_ref[place, 1:2]
        first = jnp.sum(total, axis=1, keepdims=True)
        second = jnp.sum(total * normed, axis=1, keepdims=True)
        lane = lax.broadcasted_iota(jnp.int32, (block, HD), 1)
        both = jnp.where(lane == 0, first, jnp.where(lane == 1, second, 0.0))
        sums_ref[:, i * block : (i + 1) * block] = both.T[:8]
    for o in range(1, n):
        totals(o).start()
    for k in range(1, 5):
        advance(k)
    total = sums_ref[...]
    for o in range(1, n):
        totals(o).wait_recv()
        total = total + far_ref[o - 1]
    mine_ref[...] = total
    advance(5)
    for i in range(count):
        place = pl.ds(i * block, block)
        spread = jnp.concatenate(
            [mine_ref[:, i * block : (i + 1) * block], jnp.zeros((HD - 8, block), F32)], axis=0
        ).T / width
        total = part_ref[place, own].astype(F32)
        for o in range(1, n):
            term(o, i).wait_recv()
            total = total + land_ref[o - 1, place].astype(F32)
        inverse = stat_ref[place, 1:2]
        normed = (tok_ref[place, own].astype(F32) - stat_ref[place, 0:1]) * inverse
        out_ref[place, :] = branch_ref[place, own].astype(F32) + inverse * (
            total - spread[:, 0:1] - normed * spread[:, 1:2]
        )
    advance(6)
    for o in range(1, n):
        totals(o).wait_send()
        for i in range(count):
            term(o, i).wait_send()


def unproject(dproj, tok_full, stat, weight, branch, heads, n, grads):
    rows, width = tok_full.shape
    shard = width // n
    vmem = pl.BlockSpec(memory_space=pltpu.VMEM)
    extra = []
    for grad in grads:
        extra += sum_scratch(grad.shape)
    result = pl.pallas_call(
        functools.partial(unproject_kernel, heads, n, len(grads) > 0),
        in_specs=[vmem] * (5 + len(grads)),
        out_specs=[vmem] * (1 + len(grads)),
        out_shape=[jax.ShapeDtypeStruct((rows, shard), F32)]
        + [jax.ShapeDtypeStruct(grad.shape, BF16) for grad in grads],
        scratch_shapes=[
            pltpu.VMEM((rows, width), BF16),
            pltpu.VMEM((8, rows), F32),
            pltpu.VMEM((n - 1, rows, shard), BF16),
            pltpu.VMEM((8, rows), F32),
            pltpu.VMEM((n - 1, 8, rows), F32),
            pltpu.SemaphoreType.DMA((n - 1, rows // 256)),
            pltpu.SemaphoreType.DMA((n - 1, rows // 256)),
            pltpu.SemaphoreType.DMA((n - 1,)),
            pltpu.SemaphoreType.DMA((n - 1,)),
        ]
        + extra,
        compiler_params=params(60, collective_id=4, has_side_effects=True),
        cost_estimate=cost(1e6, 1e6),
        name="unproject",
    )(dproj, tok_full, stat, weight, branch, *grads)
    return result


def per_device(tokens, segment_ids, in_weight, out_weight, gate_up_weight, down_weight, cotangent):
    rows = tokens.shape[0]
    width = in_weight.shape[0]
    span = in_weight.shape[2]
    heads = span // HD
    hidden_local = down_weight.shape[0]
    me = lax.axis_index("ctx")
    tp_size = lax.axis_size("tp")
    cube = lax.axis_size("ctx") == CUBE

    def gather(local, axis=1):
        return lax.all_gather(local, "tp", axis=axis, tiled=True)

    places = me * rows + jnp.arange(rows, dtype=jnp.int32)
    cosine, sine = rope_tables(places)
    in_w = jnp.transpose(in_weight, (1, 0, 2))
    gu_w = jnp.transpose(
        gate_up_weight.reshape(width, 2, hidden_local // BLOCK, BLOCK), (0, 2, 1, 3)
    )
    gu_w = gu_w.reshape(width, 2 * hidden_local)

    all_seg = lax.all_gather(segment_ids, "ctx", axis=0, tiled=True)
    count = all_seg.shape[0]
    every = jnp.arange(count, dtype=jnp.int32)
    opens = jnp.concatenate([jnp.ones((1,), jnp.bool_), all_seg[1:] != all_seg[:-1]])
    all_begin = lax.cummax(jnp.where(opens, every, 0))
    blocks = all_begin.reshape(count // rows, rows)

    tok_full, gu_w, blocks, all_begin = lax.optimization_barrier(
        (gather(tokens), gu_w, blocks, all_begin)
    )
    key_info = jnp.stack(
        [me, blocks[me, 0] // rows, (blocks[me, rows - 1] + rows - 1) // rows]
    ).astype(jnp.int32)
    query_info = jnp.stack(
        [
            me,
            jnp.sum((blocks[:, 0] < (me + 1) * rows).astype(jnp.int32)) - 1,
            jnp.sum((blocks[:, rows - 1] <= me * rows).astype(jnp.int32)) - 1,
        ]
    ).astype(jnp.int32)
    begin = lax.dynamic_slice_in_dim(blocks, me, 1, 0)
    all_begin = all_begin[None, :]
    inner1, stat1, query, pairs = project(tok_full, in_w, cosine, sine, heads)
    if cube:
        raw, mixed, lse, all_pairs, cot_full = attend_far(
            query, pairs, begin, cotangent, heads, tp_size
        )
    else:
        all_pairs = lax.all_gather(pairs, "ctx", axis=0, tiled=True)
        cot_full = gather(cotangent)
        raw, mixed, lse = attend(key_info, query, all_pairs, begin, heads)
    late_query, mixed = lax.optimization_barrier((query, mixed))
    all_query = lax.all_gather(late_query, "ctx", axis=0, tiled=True)
    out_part = jnp.dot(mixed, out_weight, preferred_element_type=F32).astype(BF16)
    inner2, resid1, stat2 = merge(out_part, tok_full, tp_size)

    hidden, grad_gu = feed(inner2, cot_full, gu_w, down_weight, BLOCK)
    down_grad = lax.dot_general(hidden, cot_full, TN, preferred_element_type=F32).astype(BF16)
    gu_grad = lax.dot_general(inner2, grad_gu, TN, preferred_element_type=F32).astype(BF16)
    down_grad, gu_grad, all_query, grad_gu, hidden = lax.optimization_barrier(
        (down_grad, gu_grad, all_query, grad_gu, hidden)
    )
    down_grad, gu_grad = lax.optimization_barrier(lax.psum((down_grad, gu_grad), "ctx"))

    grad_part = lax.dot_general(grad_gu, gu_w, NT, preferred_element_type=F32).astype(BF16)
    branch_grad = norm_back(grad_part, cot_full, resid1, stat2, tp_size)
    out_grad = lax.dot_general(mixed, branch_grad, TN, preferred_element_type=F32).astype(BF16)
    grad_mixed, delta = mixed_grad(branch_grad, out_weight, raw, lse, heads)
    branch = (resid1 + jnp.dot(hidden, down_weight, preferred_element_type=F32)).astype(BF16)
    if cube:
        dq, dk, dv, layer_out = attend_back_far(
            grad_mixed, all_query, all_pairs, blocks, branch, heads, tp_size
        )
    else:
        branch = lax.psum_scatter(branch, "tp", scatter_dimension=1, tiled=True)
        layer_out = branch
        all_grad = lax.all_gather(grad_mixed, "ctx", axis=0, tiled=True)
        dq = query_grad(key_info, query, grad_mixed, lse, delta, all_pairs, begin, heads)
        dk, dv = key_grad(query_info, pairs, all_query, all_grad, all_begin, heads)

    dproj = unrotate(dq, dk, dv, cosine, sine, heads)
    in_grad = jnp.stack(
        [
            lax.dot_general(
                inner1, dproj[:, i * span : (i + 1) * span], TN, preferred_element_type=F32
            ).astype(BF16)
            for i in range(3)
        ]
    )
    if cube:
        tokens_grad, in_grad, out_grad = unproject(
            dproj, tok_full, stat1, in_w, branch_grad, heads, tp_size,
            [in_grad.reshape(3 * width, span), out_grad],
        )
        in_grad = in_grad.reshape(3, width, span)
    else:
        in_grad, out_grad, down_grad, gu_grad = lax.optimization_barrier(
            (in_grad, out_grad, down_grad, gu_grad)
        )
        in_grad, out_grad = lax.psum((in_grad, out_grad), "ctx")
        (tokens_grad,) = unproject(
            dproj, tok_full, stat1, in_w, branch_grad, heads, tp_size, []
        )
    return (
        layer_out,
        tokens_grad,
        jnp.transpose(in_grad, (1, 0, 2)).astype(F32),
        out_grad.astype(F32),
        weave(gu_grad, BLOCK),
        down_grad.astype(F32),
    )


def solution(mesh):
    placed = (
        P("ctx", "tp"),
        P("ctx"),
        P(None, None, "tp"),
        P("tp", None),
        P(None, None, "tp"),
        P("tp", None),
        P("ctx", "tp"),
    )
    return jax.shard_map(
        per_device,
        mesh=mesh,
        in_specs=placed,
        out_specs=(
            P("ctx", "tp"),
            P("ctx", "tp"),
            P(None, None, "tp"),
            P("tp", None),
            P(None, None, "tp"),
            P("tp", None),
        ),
        check_vma=False,
    )
```

```python
import functools

import jax
import jax.numpy as jnp
from jax import lax
from jax.experimental import pallas as pl
from jax.experimental.pallas import tpu as pltpu
from jax.sharding import PartitionSpec as P

HD = 128
EPS = 1e-05
NEG = -1e30
SCALE = HD ** (-0.5)
LOG2E = 1.4426950408889634
C2 = SCALE * LOG2E
F32 = jnp.float32
BF16 = jnp.bfloat16
NT = (((1,), (1,)), ((), ()))
TN = (((0,), (0,)), ((), ()))
MESH = pl.DeviceIdType.MESH
BLOCK = 256


def params(mib, **more):
    return pltpu.CompilerParams(vmem_limit_bytes=mib << 20, **more)


def cost(flops, nbytes, trans=0):
    return pl.CostEstimate(flops=int(flops), bytes_accessed=int(nbytes), transcendentals=int(trans))


def rope_tables(places):
    half = HD // 2
    freq = 10000.0 ** (-jnp.arange(half, dtype=F32) * 2.0 / HD)
    angle = places.astype(F32)[:, None] * freq[None, :]
    cosine, sine = jnp.cos(angle), jnp.sin(angle)
    return jnp.concatenate([cosine, cosine], axis=1), jnp.concatenate([-sine, sine], axis=1)


def project_kernel(heads, tok_ref, w_ref, cos_ref, sin_ref, inner_ref, stat_ref, q_ref, kv_ref):
    x = tok_ref[...].astype(F32)
    center = x - jnp.mean(x, axis=1, keepdims=True)
    inverse = lax.rsqrt(jnp.mean(center * center, axis=1, keepdims=True) + EPS)
    inner = (center * inverse).astype(BF16)
    inner_ref[...] = inner
    stat_ref[...] = jnp.concatenate(
        [jnp.mean(x, axis=1, keepdims=True), inverse], axis=1
    )
    cosine, sine = cos_ref[...], sin_ref[...]
    span = heads * HD
    for part in range(3):
        out = jnp.dot(inner, w_ref[part], preferred_element_type=F32)
        if part == 2:
            kv_ref[:, span:] = out.astype(BF16)
            continue
        for h in range(heads):
            piece = out[:, h * HD : (h + 1) * HD]
            turned = (piece * cosine + pltpu.roll(piece, HD // 2, 1) * sine).astype(BF16)
            if part == 0:
                q_ref[:, h * HD : (h + 1) * HD] = turned
            else:
                kv_ref[:, h * HD : (h + 1) * HD] = turned


def project(tok_full, weight, cosine, sine, heads):
    rows, width = tok_full.shape
    span = heads * HD
    block = 256
    row = lambda n: pl.BlockSpec((block, n), lambda i: (i, 0))
    return pl.pallas_call(
        functools.partial(project_kernel, heads),
        grid=(rows // block,),
        in_specs=[
            row(width),
            pl.BlockSpec((3, width, span), lambda i: (0, 0, 0)),
            row(HD),
            row(HD),
        ],
        out_specs=[row(width), row(2), row(span), row(2 * span)],
        out_shape=[
            jax.ShapeDtypeStruct((rows, width), BF16),
            jax.ShapeDtypeStruct((rows, 2), F32),
            jax.ShapeDtypeStruct((rows, span), BF16),
            jax.ShapeDtypeStruct((rows, 2 * span), BF16),
        ],
        compiler_params=params(56),
        cost_estimate=cost(6 * rows * width * span, 6 * width * span + 6 * rows * width),
        name="project",
    )(tok_full, weight, cosine, sine)


def masked(scores, j, me, rows, begin):
    key_place = lax.broadcasted_iota(jnp.int32, scores.shape, 0) + j * rows
    query_place = lax.broadcasted_iota(jnp.int32, scores.shape, 1) + me * rows
    return jnp.where((key_place <= query_place) & (key_place >= begin), scores, NEG)


def attend_kernel(
    heads, info, q_ref, k_ref, v_ref, begin_ref, raw_ref, mixed_ref, lse_ref,
    high_ref, total_ref, acc_ref, s_ref,
):
    me, first, clear = info[0], info[1], info[2]
    j = pl.program_id(0)
    rows = q_ref.shape[0]

    @pl.when(j == 0)
    def _():
        high_ref[...] = jnp.full_like(high_ref, NEG)
        total_ref[...] = jnp.zeros_like(total_ref)
        acc_ref[...] = jnp.zeros_like(acc_ref)

    def block(hide):
        def score(h):
            hs = slice(h * HD, (h + 1) * HD)
            s = lax.dot_general(k_ref[:, hs], q_ref[:, hs], NT, preferred_element_type=F32)
            if hide:
                s = masked(s, j, me, rows, begin_ref[...])
            s_ref[h % 2] = s

        def spread(h):
            hs = slice(h * HD, (h + 1) * HD)
            s = s_ref[h % 2]
            old = high_ref[h : h + 1, :]
            new = jnp.maximum(old, jnp.max(s, axis=0, keepdims=True))
            high_ref[h : h + 1, :] = new
            p = jnp.exp2(s * C2 - new * C2)
            decay = jnp.exp2((old - new) * C2)
            total_ref[h : h + 1, :] = total_ref[h : h + 1, :] * decay + jnp.sum(
                p, axis=0, keepdims=True
            )
            acc_ref[h] = acc_ref[h] * decay + lax.dot_general(
                v_ref[:, hs], p.astype(BF16), TN, preferred_element_type=F32
            )

        score(0)
        for h in range(heads):
            if h + 1 < heads:
                score(h + 1)
            spread(h)

    @pl.when((j >= clear) & (j < me))
    def _():
        block(False)

    @pl.when(((j >= first) & (j < clear) & (j < me)) | (j == me))
    def _():
        block(True)

    @pl.when(j == me)
    def _():
        for h in range(heads):
            hs = slice(h * HD, (h + 1) * HD)
            out = (acc_ref[h] / total_ref[h : h + 1, :]).T
            raw_ref[:, hs] = out
            mixed_ref[:, hs] = out.astype(BF16)
        lse_ref[...] = high_ref[...] * C2 + jnp.log2(total_ref[...])


def attend(info, query, pairs, begin, heads):
    rows = query.shape[0]
    total = pairs.shape[0]
    span = heads * HD
    full = lambda shape: pl.BlockSpec(shape, lambda j, s: (0, 0))
    key = pl.BlockSpec((rows, span), lambda j, s: (jnp.clip(j, s[1], s[0]), 0))
    value = pl.BlockSpec((rows, span), lambda j, s: (jnp.clip(j, s[1], s[0]), 1))
    return pl.pallas_call(
        functools.partial(attend_kernel, heads),
        grid_spec=pltpu.PrefetchScalarGridSpec(
            num_scalar_prefetch=1,
            grid=(total // rows,),
            in_specs=[full((rows, span)), key, value, full((1, rows))],
            out_specs=[full((rows, span)), full((rows, span)), full((heads, rows))],
            scratch_shapes=[
                pltpu.VMEM((heads, rows), F32),
                pltpu.VMEM((heads, rows), F32),
                pltpu.VMEM((heads, HD, rows), F32),
                pltpu.VMEM((2, rows, rows), F32),
            ],
        ),
        out_shape=[
            jax.ShapeDtypeStruct((rows, span), F32),
            jax.ShapeDtypeStruct((rows, span), BF16),
            jax.ShapeDtypeStruct((heads, rows), F32),
        ],
        compiler_params=params(56),
        cost_estimate=cost(4 * rows * total * span, 4 * total * span, rows * total * heads),
        name="attend",
    )(info, query, pairs, pairs, begin)


CUBE = 8
CUBE_SENDS = 10


class Cube:
    def __init__(self, buf, send, recv):
        me = lax.axis_index("ctx")
        flip = (1 - 2 * (me % 2), 2 - 4 * ((me // 2) % 2), 4 - 8 * (me // 4))
        self.me, self.flip, self.buf, self.send, self.recv = me, flip, buf, send, recv
        self.rows = buf.shape[0] // CUBE

    def copy(self, n):
        core, x, y = self.flip
        half = self.rows // 2
        block, part, target = (
            (0, None, core),
            (0, 0, x), (0, 1, x), (0, 1, y), (0, 0, y),
            (x, 0, y), (y, 1, x),
            (x, None, core), (y, None, core), (x + y, None, core),
        )[n]
        start = (self.me + block) * self.rows
        size = self.rows
        if part is not None:
            start, size = start + part * half, half
        place = self.buf.at[pl.ds(pl.multiple_of(start, 16), size)]
        return pltpu.make_async_remote_copy(
            src_ref=place, dst_ref=place, send_sem=self.send.at[n], recv_sem=self.recv.at[n],
            device_id={"ctx": self.me + target}, device_id_type=MESH,
        )

    def arrived(self, n):
        self.copy(n).wait_recv()

    def start(self, *which):
        for n in which:
            self.copy(n).start()

    def signal(self, barrier):
        for target in self.flip:
            pl.semaphore_signal(
                barrier, inc=1, device_id={"ctx": self.me + target}, device_id_type=MESH
            )

    def block(self, step):
        core, x, y = self.flip
        on = lambda *steps: sum((step == n).astype(jnp.int32) for n in steps)
        return self.me + on(1, 4, 5, 7) * core + on(2, 4, 6, 7) * x + on(3, 5, 6, 7) * y

    def advance(self, step):
        @pl.when(step == 0)
        def _():
            self.start(0, 1, 3, 2, 4)

        @pl.when(step == 1)
        def _():
            self.arrived(0)

        @pl.when(step == 2)
        def _():
            self.arrived(1)
            self.start(5)
            self.arrived(3)
            self.start(6)
            self.arrived(2)
            self.start(7)

        @pl.when(step == 3)
        def _():
            self.arrived(4)
            self.start(8)

        @pl.when(step == 4)
        def _():
            self.arrived(7)

        @pl.when(step == 5)
        def _():
            self.arrived(8)

        @pl.when(step == 6)
        def _():
            self.arrived(5)
            self.arrived(6)
            self.start(9)

        @pl.when(step == 7)
        def _():
            self.arrived(9)

    def finish(self):
        for n in range(CUBE_SENDS):
            self.copy(n).wait_send()


SUM_SENDS = 11


class CubeSum:
    def __init__(self, own, out, land, send, recv):
        me = lax.axis_index("ctx")
        core, x, y = me % 2, (me // 2) % 2, me // 4
        self.me, self.own, self.out, self.land = me, own, out, land
        self.send, self.recv = send, recv
        rows = own.shape[0]
        self.half, self.quarter = rows // 2, rows // 4
        self.eighth, self.last = rows // 8, rows // 16
        mine = core * self.half
        first, second = mine, mine + self.quarter
        self.to = (1 - 2 * core, 2 - 4 * x, 4 - 8 * y)
        self.mine, self.other = mine, (1 - core) * self.half
        self.keep1 = (first + x * self.eighth, second + y * self.eighth)
        self.give1 = (first + (1 - x) * self.eighth, second + (1 - y) * self.eighth)
        self.keep2 = (self.keep1[0] + y * self.last, self.keep1[1] + x * self.last)
        self.give2 = (self.keep1[0] + (1 - y) * self.last, self.keep1[1] + (1 - x) * self.last)

    def place(self, ref, start, size):
        return ref.at[pl.ds(pl.multiple_of(start, 16), size)]

    def copy(self, n):
        core, x, y = self.to
        half, eighth, last, out, land = self.half, self.eighth, self.last, self.out, self.land
        landing = (0, half, half + eighth, half + 2 * eighth, half + 2 * eighth + last)
        mine = self.mine
        source, start, size, target = (
            (self.own, self.other, half, core),
            (land, self.give1[0] - mine, eighth, x), (land, self.give1[1] - mine, eighth, y),
            (land, self.give2[0] - mine, last, y), (land, self.give2[1] - mine, last, x),
            (out, self.keep2[0], last, y), (out, self.keep2[1], last, x),
            (out, self.keep1[0], eighth, x), (out, self.keep1[1], eighth, y),
            (out, mine, self.quarter, core),
            (out, mine + self.quarter, self.quarter, core),
        )[n]
        src = self.place(source, start, size)
        dst = land.at[pl.ds(landing[n], size)] if n < 5 else src
        return pltpu.make_async_remote_copy(
            src_ref=src, dst_ref=dst, send_sem=self.send.at[n], recv_sem=self.recv.at[n],
            device_id={"ctx": self.me + target}, device_id_type=MESH,
        )

    def add(self, target, to, source, at, landed, size):
        step = size
        while step * self.own.shape[1] > 256 * 1024 and step % 32 == 0:
            step = step // 2

        def part(i, carry):
            rows = lambda begin: pl.ds(pl.multiple_of(begin + i * step, 16), step)
            total = source[rows(at), :].astype(F32) + self.land[rows(landed), :].astype(F32)
            target[rows(to), :] = total.astype(BF16)
            return carry

        lax.fori_loop(0, size // step, part, 0)

    def step(self, k):
        half, eighth, last, land, mine = self.half, self.eighth, self.last, self.land, self.mine
        if k == 0:
            self.copy(0).start()
        if k == 1:
            self.copy(0).wait_recv()
            for i in range(2):
                at = self.give1[i]
                self.add(land, at - mine, self.own, at, at - mine, eighth)
                self.copy(1 + i).start()
            for i in range(2):
                at = self.keep1[i]
                self.add(land, at - mine, self.own, at, at - mine, eighth)
        if k == 2:
            for i in range(2):
                self.copy(1 + i).wait_recv()
                landed = half + i * eighth - self.keep1[i]
                at = self.give2[i]
                self.add(land, at - mine, land, at - mine, landed + at, last)
                self.copy(3 + i).start()
                at = self.keep2[i]
                self.add(land, at - mine, land, at - mine, landed + at, last)
        if k == 3:
            for i in range(2):
                self.copy(3 + i).wait_recv()
                at = self.keep2[i]
                self.add(self.out, at, land, at - mine, half + 2 * eighth + i * last, last)
                self.copy(5 + i).start()
        if k == 4:
            for i in range(2):
                self.copy(5 + i).wait_recv()
                self.copy(7 + i).start()
        if k == 5:
            for i in range(2):
                self.copy(7 + i).wait_recv()
                self.copy(9 + i).start()
        if k == 6:
            for i in range(2):
                self.copy(9 + i).wait_recv()
            for n in range(SUM_SENDS):
                self.copy(n).wait_send()

    def signal(self, barrier):
        for target in self.to:
            pl.semaphore_signal(
                barrier, inc=1, device_id={"ctx": self.me + target}, device_id_type=MESH
            )


def sum_scratch(shape):
    return [
        pltpu.VMEM((shape[0] // 2 + 3 * (shape[0] // 8), shape[1]), BF16),
        pltpu.SemaphoreType.DMA((SUM_SENDS,)),
        pltpu.SemaphoreType.DMA((SUM_SENDS,)),
    ]


def hidden_scores(scores, key_block, query_block, rows, begin):
    key_place = lax.broadcasted_iota(jnp.int32, scores.shape, 0) + key_block * rows
    query_place = lax.broadcasted_iota(jnp.int32, scores.shape, 1) + query_block * rows
    return jnp.where((key_place <= query_place) & (key_place >= begin), scores, NEG)


def attend_far_kernel(
    heads, n, q_ref, own_ref, begin_ref, cot_ref, w_ref,
    raw_ref, mixed_ref, lse_ref, keep_ref, full_ref, part_ref,
    pair_ref, high_ref, total_ref, acc_ref, s_ref, send, recv, zsend, zrecv, keep_sem,
):
    rows = q_ref.shape[0]
    span = heads * HD
    shard = cot_ref.shape[1]
    at = lax.axis_index("tp")
    cube = Cube(pair_ref, send, recv)
    me = cube.me
    barrier = pltpu.get_barrier_semaphore()
    cube.signal(barrier)

    @pl.when(at > 0)
    def _():
        pl.semaphore_signal(barrier, inc=1, device_id={"tp": at - 1}, device_id_type=MESH)

    @pl.when(at < n - 1)
    def _():
        pl.semaphore_signal(barrier, inc=1, device_id={"tp": at + 1}, device_id_type=MESH)

    pair_ref[pl.ds(pl.multiple_of(me * rows, 16), rows), :] = own_ref[...]
    full_ref[:, pl.ds(pl.multiple_of(at * shard, 128), shard)] = cot_ref[...]
    high_ref[...] = jnp.full_like(high_ref, NEG)
    total_ref[...] = jnp.zeros_like(total_ref)
    acc_ref[...] = jnp.zeros_like(acc_ref)
    pl.semaphore_wait(barrier, jnp.where((at > 0) & (at < n - 1), 5, 4))

    def pass_on(right, s, k):
        place = full_ref.at[:, pl.ds(pl.multiple_of(s * shard, 128), shard)]
        which = (1 if right else 0, k)
        return pltpu.make_async_remote_copy(
            src_ref=place, dst_ref=place, send_sem=zsend.at[which], recv_sem=zrecv.at[which],
            device_id={"tp": at + 1 if right else at - 1}, device_id_type=MESH,
        )

    def line_step(k):
        @pl.when(at >= k)
        def _():
            if k > 0:
                pass_on(True, at - k, k - 1).wait_recv()

            @pl.when(at < n - 1)
            def _():
                pass_on(True, at - k, k).start()

        @pl.when(at + k < n)
        def _():
            if k > 0:
                pass_on(False, at + k, k - 1).wait_recv()

            @pl.when(at > 0)
            def _():
                pass_on(False, at + k, k).start()

    def keep(step):
        place = pl.ds(pl.multiple_of(cube.block(step) * rows, 16), rows)
        return pltpu.make_async_copy(pair_ref.at[place], keep_ref.at[place], keep_sem.at[step])

    def turn(step, carry):
        cube.advance(step)
        keep(step).start()
        for k in range(n):
            @pl.when(step == min(k * 2, CUBE - 1 - (n - 1 - k)) if n <= CUBE else k)
            def _():
                line_step(k)
        block = cube.block(step)

        @pl.when(block <= me)
        def _():
            place = pl.ds(pl.multiple_of(block * rows, 16), rows)

            def score(h):
                hs = slice(h * HD, (h + 1) * HD)
                s = lax.dot_general(
                    pair_ref[place, hs], q_ref[:, hs], NT, preferred_element_type=F32
                )
                s_ref[h % 2] = hidden_scores(s, block, me, rows, begin_ref[...])

            def spread(h):
                s = s_ref[h % 2]
                old = high_ref[h : h + 1, :]
                new = jnp.maximum(old, jnp.max(s, axis=0, keepdims=True))
                high_ref[h : h + 1, :] = new
                p = jnp.exp2(s * C2 - new * C2)
                decay = jnp.exp2((old - new) * C2)
                total_ref[h : h + 1, :] = total_ref[h : h + 1, :] * decay + jnp.sum(
                    p, axis=0, keepdims=True
                )
                acc_ref[h] = acc_ref[h] * decay + lax.dot_general(
                    pair_ref[place, span + h * HD : span + (h + 1) * HD], p.astype(BF16), TN,
                    preferred_element_type=F32,
                )

            score(0)
            for h in range(heads):
                if h + 1 < heads:
                    score(h + 1)
                spread(h)

        return carry

    lax.fori_loop(0, CUBE, turn, 0)
    for h in range(heads):
        hs = slice(h * HD, (h + 1) * HD)
        out = (acc_ref[h] / total_ref[h : h + 1, :]).T
        raw_ref[:, hs] = out
        mixed_ref[:, hs] = out.astype(BF16)
    part_ref[...] = jnp.dot(
        mixed_ref[...], w_ref[...], preferred_element_type=F32
    ).astype(BF16)
    lse_ref[...] = high_ref[...] * C2 + jnp.log2(total_ref[...])

    def kept(step, carry):
        keep(step).wait()
        return carry

    lax.fori_loop(0, CUBE, kept, 0)
    cube.finish()
    for k in range(n):
        @pl.when((at >= k) & (at < n - 1))
        def _():
            pass_on(True, at - k, k).wait_send()

        @pl.when((at + k < n) & (at > 0))
        def _():
            pass_on(False, at + k, k).wait_send()


def attend_far(query, pairs, begin, cot, weight, heads, n):
    rows = query.shape[0]
    width = weight.shape[1]
    span = heads * HD
    vmem = pl.BlockSpec(memory_space=pltpu.VMEM)
    return pl.pallas_call(
        functools.partial(attend_far_kernel, heads, n),
        in_specs=[vmem] * 5,
        out_specs=[vmem] * 3 + [pl.BlockSpec(memory_space=pl.ANY)] + [vmem] * 2,
        out_shape=[
            jax.ShapeDtypeStruct((rows, span), F32),
            jax.ShapeDtypeStruct((rows, span), BF16),
            jax.ShapeDtypeStruct((heads, rows), F32),
            jax.ShapeDtypeStruct((CUBE * rows, 2 * span), BF16),
            jax.ShapeDtypeStruct((rows, n * cot.shape[1]), BF16),
            jax.ShapeDtypeStruct((rows, width), BF16),
        ],
        scratch_shapes=[
            pltpu.VMEM((CUBE * rows, 2 * span), BF16),
            pltpu.VMEM((heads, rows), F32),
            pltpu.VMEM((heads, rows), F32),
            pltpu.VMEM((heads, HD, rows), F32),
            pltpu.VMEM((2, rows, rows), F32),
            pltpu.SemaphoreType.DMA((CUBE_SENDS,)),
            pltpu.SemaphoreType.DMA((CUBE_SENDS,)),
            pltpu.SemaphoreType.DMA((2, n)),
            pltpu.SemaphoreType.DMA((2, n)),
            pltpu.SemaphoreType.DMA((CUBE,)),
        ],
        compiler_params=params(58, collective_id=2, has_side_effects=True),
        cost_estimate=cost(1e6, 1e6),
        name="attend_far",
    )(query, pairs, begin, cot, weight)


def attend_back_far_kernel(
    heads, n, g_ref, far_q_ref, far_pair_ref, begin_ref, part_ref,
    dq_ref, dk_ref, dv_ref, layer_ref,
    all_ref, acc_ref, rows_ref, s_ref, p_ref, land_ref, pair_ref, q_ref,
    send, recv, zsend, zrecv, read_sem,
):
    rows = g_ref.shape[0]
    span = heads * HD
    shard = layer_ref.shape[1]
    at = lax.axis_index("tp")
    cube = Cube(all_ref, send, recv)
    me = cube.me
    barrier = pltpu.get_barrier_semaphore()
    cube.signal(barrier)
    for o in range(1, n):
        pl.semaphore_signal(
            barrier, inc=1, device_id={"tp": lax.rem(at + o, n)}, device_id_type=MESH
        )

    def read(step, keys):
        place = pl.ds(pl.multiple_of(cube.block(step) * rows, 16), rows)
        far, near = (far_pair_ref, pair_ref) if keys else (far_q_ref, q_ref)
        return pltpu.make_async_copy(
            far.at[place], near.at[place], read_sem.at[0 if keys else 1, step]
        )

    def read_all(step, carry):
        block = cube.block(step)

        @pl.when(block <= me)
        def _():
            read(step, True).start()

        @pl.when(block >= me)
        def _():
            read(step, False).start()

        return carry

    lax.fori_loop(0, CUBE, read_all, 0)
    all_ref[pl.ds(pl.multiple_of(me * rows, 16), rows), :] = g_ref[...]
    acc_ref[...] = jnp.zeros_like(acc_ref)
    dk_ref[...] = jnp.zeros_like(dk_ref)
    dv_ref[...] = jnp.zeros_like(dv_ref)
    pl.semaphore_wait(barrier, 3 + n - 1)

    def term(o):
        target = lax.rem(at + o, n)
        return pltpu.make_async_remote_copy(
            src_ref=part_ref.at[:, pl.ds(pl.multiple_of(target * shard, 128), shard)],
            dst_ref=land_ref.at[o - 1],
            send_sem=zsend.at[o - 1], recv_sem=zrecv.at[o - 1],
            device_id={"tp": target}, device_id_type=MESH,
        )

    own = pl.ds(pl.multiple_of(me * rows, 16), rows)

    def turn(step, carry):
        cube.advance(step)

        @pl.when(step == 0)
        def _():
            for o in range(1, n):
                term(o).start()

        block = cube.block(step)
        place = pl.ds(pl.multiple_of(block * rows, 16), rows)

        @pl.when(block <= me)
        def _():
            read(step, True).wait()

        @pl.when(block >= me)
        def _():
            read(step, False).wait()

        def scores(h, key_block, key_place, query_block, query_place):
            hs = slice(h * HD, (h + 1) * HD)
            vs = slice(span + h * HD, span + (h + 1) * HD)
            s = lax.dot_general(
                pair_ref[key_place, hs], q_ref[query_place, hs], NT, preferred_element_type=F32
            )
            begin = begin_ref[pl.ds(query_block, 1), :]
            s_ref[h % 2] = hidden_scores(s, key_block, query_block, rows, begin)
            p_ref[h % 2] = lax.dot_general(
                pair_ref[key_place, vs], all_ref[query_place, hs], NT, preferred_element_type=F32
            )

        def read_rows(query_place):
            coded = all_ref[query_place, span:].astype(F32).T
            for k in range(2 * heads):
                rows_ref[k : k + 1, :] = (
                    coded[3 * k : 3 * k + 1]
                    + coded[3 * k + 1 : 3 * k + 2]
                    + coded[3 * k + 2 : 3 * k + 3]
                )

        def weights(h):
            p = jnp.exp2(s_ref[h % 2] * C2 - rows_ref[h : h + 1, :])
            ds = p * (p_ref[h % 2] - rows_ref[heads + h : heads + h + 1, :])
            return p.astype(BF16), ds.astype(BF16)

        @pl.when(block <= me)
        def _():
            read_rows(own)
            scores(0, block, place, me, own)
            for h in range(heads):
                if h + 1 < heads:
                    scores(h + 1, block, place, me, own)
                _, ds = weights(h)
                acc_ref[h] = acc_ref[h] + lax.dot_general(
                    pair_ref[place, h * HD : (h + 1) * HD], ds, TN, preferred_element_type=F32
                )

        @pl.when(block >= me)
        def _():
            read_rows(place)
            scores(0, me, own, block, place)
            for h in range(heads):
                hs = slice(h * HD, (h + 1) * HD)
                if h + 1 < heads:
                    scores(h + 1, me, own, block, place)
                p, ds = weights(h)
                dv_ref[:, hs] += jnp.dot(p, all_ref[place, hs], preferred_element_type=F32)
                dk_ref[:, hs] += jnp.dot(ds, q_ref[place, hs], preferred_element_type=F32)

        return carry

    lax.fori_loop(0, CUBE, turn, 0)
    for h in range(heads):
        dq_ref[:, h * HD : (h + 1) * HD] = (acc_ref[h] * SCALE).T
    dk_ref[...] = dk_ref[...] * SCALE
    total = part_ref[:, pl.ds(pl.multiple_of(at * shard, 128), shard)].astype(F32)
    for o in range(1, n):
        term(o).wait_recv()
        total = total + land_ref[o - 1].astype(F32)
    layer_ref[...] = total.astype(BF16)
    cube.finish()
    for o in range(1, n):
        term(o).wait_send()


def attend_back_far(grad, all_query, all_pairs, all_begin, part, heads, n):
    rows = grad.shape[0]
    span = heads * HD
    shard = part.shape[1] // n
    vmem = pl.BlockSpec(memory_space=pltpu.VMEM)
    wide = jax.ShapeDtypeStruct((rows, span), F32)
    return pl.pallas_call(
        functools.partial(attend_back_far_kernel, heads, n),
        in_specs=[vmem] + [pl.BlockSpec(memory_space=pl.ANY)] * 2 + [vmem] * 2,
        out_specs=[vmem] * 4,
        out_shape=[wide, wide, wide, jax.ShapeDtypeStruct((rows, shard), BF16)],
        scratch_shapes=[
            pltpu.VMEM((CUBE * rows, span + HD), BF16),
            pltpu.VMEM((heads, HD, rows), F32),
            pltpu.VMEM((2 * heads, rows), F32),
            pltpu.VMEM((2, rows, rows), F32),
            pltpu.VMEM((2, rows, rows), F32),
            pltpu.VMEM((n - 1, rows, shard), BF16),
            pltpu.VMEM((CUBE * rows, 2 * span), BF16),
            pltpu.VMEM((CUBE * rows, span), BF16),
            pltpu.SemaphoreType.DMA((CUBE_SENDS,)),
            pltpu.SemaphoreType.DMA((CUBE_SENDS,)),
            pltpu.SemaphoreType.DMA((n - 1,)),
            pltpu.SemaphoreType.DMA((n - 1,)),
            pltpu.SemaphoreType.DMA((2, CUBE)),
        ],
        compiler_params=params(60, collective_id=3, has_side_effects=True),
        cost_estimate=cost(1e6, 1e6),
        name="attend_back_far",
    )(grad, all_query, all_pairs, all_begin, part)


def query_grad_kernel(
    heads, info, q_ref, do_ref, lse_ref, delta_ref, k_ref, v_ref, begin_ref,
    dq_ref, acc_ref, s_ref, g_ref,
):
    me, first, clear = info[0], info[1], info[2]
    j = pl.program_id(0)
    rows = q_ref.shape[0]

    @pl.when(j == 0)
    def _():
        acc_ref[...] = jnp.zeros_like(acc_ref)

    def block(hide):
        def score(h):
            hs = slice(h * HD, (h + 1) * HD)
            s = lax.dot_general(k_ref[:, hs], q_ref[:, hs], NT, preferred_element_type=F32)
            if hide:
                s = masked(s, j, me, rows, begin_ref[...])
            s_ref[h % 2] = s
            g_ref[h % 2] = lax.dot_general(
                v_ref[:, hs], do_ref[:, hs], NT, preferred_element_type=F32
            )

        def spread(h):
            hs = slice(h * HD, (h + 1) * HD)
            p = jnp.exp2(s_ref[h % 2] * C2 - lse_ref[h : h + 1, :])
            ds = (p * (g_ref[h % 2] - delta_ref[h : h + 1, :])).astype(BF16)
            acc_ref[h] = acc_ref[h] + lax.dot_general(
                k_ref[:, hs], ds, TN, preferred_element_type=F32
            )

        score(0)
        for h in range(heads):
            if h + 1 < heads:
                score(h + 1)
            spread(h)

    @pl.when((j >= clear) & (j < me))
    def _():
        block(False)

    @pl.when(((j >= first) & (j < clear) & (j < me)) | (j == me))
    def _():
        block(True)

    @pl.when(j == me)
    def _():
        for h in range(heads):
            dq_ref[:, h * HD : (h + 1) * HD] = (acc_ref[h] * SCALE).T


def query_grad(info, query, grad_mixed, lse, delta, pairs, begin, heads):
    rows = query.shape[0]
    total = pairs.shape[0]
    span = heads * HD
    full = lambda shape: pl.BlockSpec(shape, lambda j, s: (0, 0))
    key = pl.BlockSpec((rows, span), lambda j, s: (jnp.clip(j, s[1], s[0]), 0))
    value = pl.BlockSpec((rows, span), lambda j, s: (jnp.clip(j, s[1], s[0]), 1))
    wide = full((rows, span))
    thin = full((heads, rows))
    return pl.pallas_call(
        functools.partial(query_grad_kernel, heads),
        grid_spec=pltpu.PrefetchScalarGridSpec(
            num_scalar_prefetch=1,
            grid=(total // rows,),
            in_specs=[wide, wide, thin, thin, key, value, full((1, rows))],
            out_specs=wide,
            scratch_shapes=[
                pltpu.VMEM((heads, HD, rows), F32),
                pltpu.VMEM((2, rows, rows), F32),
                pltpu.VMEM((2, rows, rows), F32),
            ],
        ),
        out_shape=jax.ShapeDtypeStruct((rows, span), F32),
        compiler_params=params(58),
        cost_estimate=cost(6 * rows * total * span, 4 * total * span, rows * total * heads),
        name="query_grad",
    )(info, query, grad_mixed, lse, delta, pairs, pairs, begin)


def key_grad_kernel(
    heads, info, k_ref, v_ref, q_ref, g_ref, begin_ref, dk_ref, dv_ref,
    rows_ref, s_ref, p_ref,
):
    me, last, clear = info[0], info[1], info[2]
    j = pl.program_id(0)
    rows = k_ref.shape[0]
    span = heads * HD

    @pl.when(j == me)
    def _():
        dk_ref[...] = jnp.zeros_like(dk_ref)
        dv_ref[...] = jnp.zeros_like(dv_ref)

    def block(hide):
        coded = g_ref[:, span:].astype(F32).T
        for n in range(2 * heads):
            rows_ref[n : n + 1, :] = (
                coded[3 * n : 3 * n + 1] + coded[3 * n + 1 : 3 * n + 2] + coded[3 * n + 2 : 3 * n + 3]
            )

        def score(h):
            hs = slice(h * HD, (h + 1) * HD)
            s = lax.dot_general(k_ref[:, hs], q_ref[:, hs], NT, preferred_element_type=F32)
            if hide:
                key_place = lax.broadcasted_iota(jnp.int32, s.shape, 0) + me * rows
                query_place = lax.broadcasted_iota(jnp.int32, s.shape, 1) + j * rows
                s = jnp.where(
                    (key_place <= query_place) & (key_place >= begin_ref[...]), s, NEG
                )
            s_ref[h % 2] = s
            p_ref[h % 2] = lax.dot_general(
                v_ref[:, hs], g_ref[:, hs], NT, preferred_element_type=F32
            )

        def spread(h):
            hs = slice(h * HD, (h + 1) * HD)
            p = jnp.exp2(s_ref[h % 2] * C2 - rows_ref[h : h + 1, :])
            ds = (p * (p_ref[h % 2] - rows_ref[heads + h : heads + h + 1, :])).astype(BF16)
            dv_ref[:, hs] += jnp.dot(p.astype(BF16), g_ref[:, hs], preferred_element_type=F32)
            dk_ref[:, hs] += jnp.dot(ds, q_ref[:, hs], preferred_element_type=F32)

        score(0)
        for h in range(heads):
            if h + 1 < heads:
                score(h + 1)
            spread(h)

    @pl.when((j > me) & (j <= clear))
    def _():
        block(False)

    @pl.when((j == me) | ((j > me) & (j > clear) & (j <= last)))
    def _():
        block(True)

    @pl.when(j == pl.num_programs(0) - 1)
    def _():
        dk_ref[...] = dk_ref[...] * SCALE


def key_grad(info, pairs, all_query, all_grad, all_begin, heads):
    rows = pairs.shape[0]
    total = all_query.shape[0]
    span = heads * HD
    full = lambda shape, at=0: pl.BlockSpec(shape, lambda j, s: (0, at))
    near = lambda j, s: (jnp.clip(j, s[0], s[1]), 0)
    wide = full((rows, span))
    return pl.pallas_call(
        functools.partial(key_grad_kernel, heads),
        grid_spec=pltpu.PrefetchScalarGridSpec(
            num_scalar_prefetch=1,
            grid=(total // rows,),
            in_specs=[
                wide, full((rows, span), 1),
                pl.BlockSpec((rows, span), near),
                pl.BlockSpec((rows, span + HD), near),
                pl.BlockSpec((1, rows), lambda j, s: (0, jnp.clip(j, s[0], s[1]))),
            ],
            out_specs=[wide, wide],
            scratch_shapes=[
                pltpu.VMEM((2 * heads, rows), F32),
                pltpu.VMEM((2, rows, rows), F32),
                pltpu.VMEM((2, rows, rows), F32),
            ],
        ),
        out_shape=[jax.ShapeDtypeStruct((rows, span), F32)] * 2,
        compiler_params=params(58),
        cost_estimate=cost(8 * rows * total * span, 4 * total * span, rows * total * heads),
        name="key_grad",
    )(info, pairs, pairs, all_query, all_grad, all_begin)


def mixed_grad_kernel(heads, branch_ref, w_ref, raw_ref, lse_ref, out_ref, delta_ref):
    span = heads * HD
    low = lax.dot_general(
        branch_ref[...], w_ref[...], NT, preferred_element_type=F32
    ).astype(BF16)
    out_ref[:, :span] = low
    count = low.shape[0]
    both = low.astype(F32) * raw_ref[...]
    for h in range(heads):
        delta_ref[h : h + 1, :] = jnp.sum(both[:, h * HD : (h + 1) * HD].T, axis=0, keepdims=True)
    lines = []
    for n in range(2 * heads):
        value = lse_ref[n : n + 1, :] if n < heads else delta_ref[n - heads : n - heads + 1, :]
        for _ in range(3):
            piece = value.astype(BF16).astype(F32)
            lines.append(piece)
            value = value - piece
    lines.append(jnp.zeros((HD - len(lines), count), F32))
    out_ref[:, span:] = jnp.concatenate(lines, axis=0).T.astype(BF16)


def mixed_grad(branch, weight, raw, lse, heads):
    rows, width = branch.shape
    span = heads * HD
    block = 256
    row = lambda n: pl.BlockSpec((block, n), lambda i: (i, 0))
    line = pl.BlockSpec((heads, block), lambda i: (0, i))
    return pl.pallas_call(
        functools.partial(mixed_grad_kernel, heads),
        grid=(rows // block,),
        in_specs=[row(width), pl.BlockSpec((span, width), lambda i: (0, 0)), row(span), line],
        out_specs=[row(span + HD), line],
        out_shape=[
            jax.ShapeDtypeStruct((rows, span + HD), BF16),
            jax.ShapeDtypeStruct((heads, rows), F32),
        ],
        compiler_params=params(56),
        cost_estimate=cost(2 * rows * width * span, 2 * width * span + 4 * rows * width),
        name="mixed_grad",
    )(branch, weight, raw, lse)


def feed_kernel(
    inner_ref, cot_ref, w_ref, down_ref, hidden_ref, dgu_ref, down_grad_ref, gu_grad_ref
):
    block = down_ref.shape[0]
    both = jnp.dot(inner_ref[...], w_ref[...], preferred_element_type=F32)
    grad = lax.dot_general(cot_ref[...], down_ref[...], NT, preferred_element_type=F32)
    gate, up = both[:, :block], both[:, block:]
    sigma = 1.0 / (1.0 + jnp.exp(-gate))
    active = gate * sigma
    hidden_ref[...] = (active * up).astype(BF16)
    dgu_ref[:, :block] = (grad * up * sigma * (1.0 + gate * (1.0 - sigma))).astype(BF16)
    dgu_ref[:, block:] = (grad * active).astype(BF16)
    down_grad_ref[...] = lax.dot_general(
        hidden_ref[...], cot_ref[...], TN, preferred_element_type=F32
    ).astype(BF16)
    gu_grad_ref[...] = lax.dot_general(
        inner_ref[...], dgu_ref[...], TN, preferred_element_type=F32
    ).astype(BF16)


def feed(inner, cot, weight, down, block):
    rows, width = inner.shape
    units = down.shape[0]
    whole = pl.BlockSpec((rows, width), lambda j: (0, 0))
    column = lambda high, wide: pl.BlockSpec((high, wide), lambda j: (0, j))
    line = pl.BlockSpec((block, width), lambda j: (j, 0))
    return pl.pallas_call(
        feed_kernel,
        grid=(units // block,),
        in_specs=[whole, whole, column(width, 2 * block), line],
        out_specs=[column(rows, block), column(rows, 2 * block), line, column(width, 2 * block)],
        out_shape=[
            jax.ShapeDtypeStruct((rows, units), BF16),
            jax.ShapeDtypeStruct((rows, 2 * units), BF16),
            jax.ShapeDtypeStruct((units, width), BF16),
            jax.ShapeDtypeStruct((width, 2 * units), BF16),
        ],
        compiler_params=params(60),
        cost_estimate=cost(
            12 * rows * width * units, 12 * width * units + 4 * rows * width, rows * units
        ),
        name="feed",
    )(inner, cot, weight, down)


def weave_kernel(block, sum_ref, out_ref):
    for j in range(sum_ref.shape[1] // (2 * block)):
        for k in range(2):
            at = (2 * j + k) * block
            out_ref[:, k, j * block : (j + 1) * block] = sum_ref[:, at : at + block].astype(F32)


def weave(summed, block):
    width, both = summed.shape
    rows = 512
    return pl.pallas_call(
        functools.partial(weave_kernel, block),
        grid=(width // rows,),
        in_specs=[pl.BlockSpec((rows, both), lambda i: (i, 0))],
        out_specs=pl.BlockSpec((rows, 2, both // 2), lambda i: (i, 0, 0)),
        out_shape=jax.ShapeDtypeStruct((width, 2, both // 2), F32),
        compiler_params=params(56),
        cost_estimate=cost(width * both, 6 * width * both),
        name="weave",
    )(summed)


def widen_kernel(in_ref, out_ref):
    out_ref[...] = in_ref[...].astype(F32)


def widen(summed):
    high, wide = summed.shape
    block = pl.BlockSpec((512, wide), lambda i: (i, 0))
    return pl.pallas_call(
        widen_kernel,
        grid=(high // 512,),
        in_specs=[block],
        out_specs=block,
        out_shape=jax.ShapeDtypeStruct((high, wide), F32),
        compiler_params=params(56),
        cost_estimate=cost(high * wide, 6 * high * wide),
        name="widen",
    )(summed)


def line_barrier(at, n):
    barrier = pltpu.get_barrier_semaphore()

    @pl.when(at > 0)
    def _():
        pl.semaphore_signal(barrier, inc=1, device_id={"tp": at - 1}, device_id_type=MESH)

    @pl.when(at < n - 1)
    def _():
        pl.semaphore_signal(barrier, inc=1, device_id={"tp": at + 1}, device_id_type=MESH)

    pl.semaphore_wait(barrier, jnp.where((at > 0) & (at < n - 1), 2, 1))


def sum_rows(n, sub, part_ref, out_ref, row_fn, from_left, from_right, send, recv):
    at = lax.axis_index("tp")
    chunks = part_ref.shape[0] // sub
    middle = (n // 2 - 1, n // 2)

    def link(kind, right, src, dst, c):
        which = (kind * 2 + (1 if right else 0), c)
        return pltpu.make_async_remote_copy(
            src_ref=src.at[pl.ds(c * sub, sub)],
            dst_ref=dst.at[pl.ds(c * sub, sub)],
            send_sem=send.at[which],
            recv_sem=recv.at[which],
            device_id={"tp": at + 1 if right else at - 1},
            device_id_type=MESH,
        )

    def came(right):
        return from_left if right else from_right

    def first(right, c):
        return link(0, right, part_ref, came(right), c)

    def onward(right, c):
        return link(0, right, came(right), came(right), c)

    def hand(right, c):
        return link(1, right, out_ref, out_ref, c)

    def reduce_step(c):
        owner = middle[c % 2]
        rows = slice(c * sub, (c + 1) * sub)
        for right in (True, False):
            edge = 0 if right else n - 1
            held = came(right)

            @pl.when(((at < owner) if right else (at > owner)) & (at != edge))
            def _():
                copy = onward(right, c)
                copy.wait_recv()
                held[rows, :] = (
                    held[rows, :].astype(F32) + part_ref[rows, :].astype(F32)
                ).astype(BF16)
                copy.start()

    def final_step(c):
        owner = middle[c % 2]
        rows = slice(c * sub, (c + 1) * sub)

        @pl.when(at == owner)
        def _():
            total = part_ref[rows, :].astype(F32)
            onward(True, c).wait_recv()
            total = total + from_left[rows, :].astype(F32)
            onward(False, c).wait_recv()
            total = total + from_right[rows, :].astype(F32)
            row_fn(total, rows)
            hand(True, c).start()
            hand(False, c).start()

    def hand_step(c):
        owner = middle[c % 2]
        for right in (True, False):
            edge = n - 1 if right else 0

            @pl.when((at > owner) if right else (at < owner))
            def _():
                copy = hand(right, c)
                copy.wait_recv()

                @pl.when(at != edge)
                def _():
                    copy.start()

    for c in range(chunks):
        @pl.when(at == 0)
        def _():
            first(True, c).start()

        @pl.when(at == n - 1)
        def _():
            first(False, c).start()

    for c in range(chunks + 4):
        if c < chunks:
            reduce_step(c)
        if 2 <= c < chunks + 2:
            final_step(c - 2)
        if c >= 4:
            hand_step(c - 4)
    for c in range(chunks):
        owner = middle[c % 2]

        @pl.when(at < owner)
        def _():
            first(True, c).wait_send()

        @pl.when(at > owner)
        def _():
            first(False, c).wait_send()

        @pl.when((at >= owner) & (at < n - 1))
        def _():
            hand(True, c).wait_send()

        @pl.when((at <= owner) & (at > 0))
        def _():
            hand(False, c).wait_send()


def merge_kernel(
    n, sub, part_ref, tok_ref, inner_ref, resid_ref, stat_ref, from_left, from_right, send, recv
):
    line_barrier(lax.axis_index("tp"), n)
    resid_ref[...] = jnp.zeros_like(resid_ref)
    stat_ref[...] = jnp.zeros_like(stat_ref)

    def row_fn(total, rows):
        x = tok_ref[rows, :].astype(F32) + total
        mean = jnp.mean(x, axis=1, keepdims=True)
        center = x - mean
        inverse = lax.rsqrt(jnp.mean(center * center, axis=1, keepdims=True) + EPS)
        resid_ref[rows, :] = x
        stat_ref[rows, :] = jnp.concatenate([mean, inverse], axis=1)
        inner_ref[rows, :] = (center * inverse).astype(BF16)

    sum_rows(n, sub, part_ref, inner_ref, row_fn, from_left, from_right, send, recv)


def merge(part, tok_full, n):
    rows, width = part.shape
    sub = 32
    vmem = pl.BlockSpec(memory_space=pltpu.VMEM)
    return pl.pallas_call(
        functools.partial(merge_kernel, n, sub),
        in_specs=[vmem] * 2,
        out_specs=[vmem] * 3,
        out_shape=[
            jax.ShapeDtypeStruct((rows, width), BF16),
            jax.ShapeDtypeStruct((rows, width), F32),
            jax.ShapeDtypeStruct((rows, 2), F32),
        ],
        scratch_shapes=[pltpu.VMEM((rows, width), BF16)] * 2
        + [pltpu.SemaphoreType.DMA((4, rows // sub))] * 2,
        compiler_params=params(56, collective_id=5, has_side_effects=True),
        cost_estimate=cost(1e6, 1e6),
        name="merge",
    )(part, tok_full)


def norm_back_kernel(
    n, sub, part_ref, cot_ref, resid_ref, stat_ref, out_ref, from_left, from_right, send, recv
):
    line_barrier(lax.axis_index("tp"), n)

    def row_fn(total, rows):
        inverse = stat_ref[rows, 1:2]
        normed = (resid_ref[rows, :] - stat_ref[rows, 0:1]) * inverse
        mean = jnp.mean(total, axis=1, keepdims=True)
        inner = jnp.mean(total * normed, axis=1, keepdims=True)
        out = cot_ref[rows, :].astype(F32) + inverse * (total - mean - normed * inner)
        out_ref[rows, :] = out.astype(BF16)

    sum_rows(n, sub, part_ref, out_ref, row_fn, from_left, from_right, send, recv)


def norm_back(part, cot, resid, stat, n):
    rows, width = part.shape
    sub = 32
    vmem = pl.BlockSpec(memory_space=pltpu.VMEM)
    return pl.pallas_call(
        functools.partial(norm_back_kernel, n, sub),
        in_specs=[vmem] * 4,
        out_specs=vmem,
        out_shape=jax.ShapeDtypeStruct((rows, width), BF16),
        scratch_shapes=[pltpu.VMEM((rows, width), BF16)] * 2
        + [pltpu.SemaphoreType.DMA((4, rows // sub))] * 2,
        compiler_params=params(56, collective_id=1, has_side_effects=True),
        cost_estimate=cost(1e6, 1e6),
        name="norm_back",
    )(part, cot, resid, stat)


def unrotate_kernel(
    heads, dq_ref, dk_ref, dv_ref, cos_ref, sin_ref, inner_ref, dproj_ref, grad_ref
):
    def back(ref):
        for h in range(heads):
            hs = slice(h * HD, (h + 1) * HD)
            piece = ref[:, hs]
            dproj_ref[:, hs] = (
                piece * cos_ref[...] - pltpu.roll(piece, HD // 2, 1) * sin_ref[...]
            ).astype(BF16)

    part = pl.program_id(0)

    @pl.when(part == 0)
    def _():
        back(dq_ref)

    @pl.when(part == 1)
    def _():
        back(dk_ref)

    @pl.when(part == 2)
    def _():
        dproj_ref[...] = dv_ref[...].astype(BF16)

    grad_ref[...] = lax.dot_general(
        inner_ref[...], dproj_ref[...], TN, preferred_element_type=F32
    ).astype(BF16)


def unrotate(dq, dk, dv, cosine, sine, inner, heads):
    rows, span = dq.shape
    width = inner.shape[1]
    whole = lambda n: pl.BlockSpec((rows, n), lambda i: (0, 0))
    return pl.pallas_call(
        functools.partial(unrotate_kernel, heads),
        grid=(3,),
        in_specs=[whole(span)] * 3 + [whole(HD)] * 2 + [whole(width)],
        out_specs=[
            pl.BlockSpec((rows, span), lambda i: (0, i)),
            pl.BlockSpec((width, span), lambda i: (i, 0)),
        ],
        out_shape=[
            jax.ShapeDtypeStruct((rows, 3 * span), BF16),
            jax.ShapeDtypeStruct((3 * width, span), BF16),
        ],
        compiler_params=params(56),
        cost_estimate=cost(6 * rows * span * width, 12 * rows * span + 6 * width * span),
        name="unrotate",
    )(dq, dk, dv, cosine, sine, inner)


def unproject_kernel(heads, n, cube, dproj_ref, tok_ref, stat_ref, w_ref, branch_ref, *refs):
    sums = []
    if cube:
        in_ref, og_ref, out_ref, in_out, og_out = refs[:5]
        part_ref, mine_ref, land_ref, sums_ref, far_ref, send, recv, ssend, srecv = refs[5:14]
        sums = [CubeSum(in_ref, in_out, *refs[14:17]), CubeSum(og_ref, og_out, *refs[17:20])]
    else:
        out_ref, part_ref, mine_ref, land_ref, sums_ref, far_ref, send, recv, ssend, srecv = refs

    def advance(k):
        for item in sums:
            item.step(k)

    rows, width = tok_ref.shape
    shard = width // n
    span = heads * HD
    at = lax.axis_index("tp")
    barrier = pltpu.get_barrier_semaphore()
    for o in range(1, n):
        pl.semaphore_signal(
            barrier, inc=1, device_id={"tp": lax.rem(at + o, n)}, device_id_type=MESH
        )
    if cube:
        sums[0].signal(barrier)
    pl.semaphore_wait(barrier, n - 1 + (3 if cube else 0))
    advance(0)
    block = 256
    count = rows // block

    def term(o, i):
        target = lax.rem(at + o, n)
        place = pl.ds(i * block, block)
        return pltpu.make_async_remote_copy(
            src_ref=part_ref.at[place, pl.ds(pl.multiple_of(target * shard, 128), shard)],
            dst_ref=land_ref.at[o - 1, place],
            send_sem=send.at[o - 1, i], recv_sem=recv.at[o - 1, i],
            device_id={"tp": target}, device_id_type=MESH,
        )

    def totals(o):
        return pltpu.make_async_remote_copy(
            src_ref=sums_ref, dst_ref=far_ref.at[o - 1],
            send_sem=ssend.at[o - 1], recv_sem=srecv.at[o - 1],
            device_id={"tp": lax.rem(at + o, n)}, device_id_type=MESH,
        )

    own = pl.ds(pl.multiple_of(at * shard, 128), shard)
    for i in range(count):
        place = pl.ds(i * block, block)
        total = None
        for part in range(3):
            piece = lax.dot_general(
                dproj_ref[place, part * span : (part + 1) * span], w_ref[part], NT,
                preferred_element_type=F32,
            )
            total = piece if total is None else total + piece
        part_ref[place, :] = total.astype(BF16)
        for o in range(1, n):
            term(o, i).start()
        normed = (tok_ref[place, :].astype(F32) - stat_ref[place, 0:1]) * stat_ref[place, 1:2]
        first = jnp.sum(total, axis=1, keepdims=True)
        second = jnp.sum(total * normed, axis=1, keepdims=True)
        lane = lax.broadcasted_iota(jnp.int32, (block, HD), 1)
        both = jnp.where(lane == 0, first, jnp.where(lane == 1, second, 0.0))
        sums_ref[:, i * block : (i + 1) * block] = both.T[:8]
    for o in range(1, n):
        totals(o).start()
    for k in range(1, 5):
        advance(k)
    total = sums_ref[...]
    for o in range(1, n):
        totals(o).wait_recv()
        total = total + far_ref[o - 1]
    mine_ref[...] = total
    advance(5)
    for i in range(count):
        place = pl.ds(i * block, block)
        spread = jnp.concatenate(
            [mine_ref[:, i * block : (i + 1) * block], jnp.zeros((HD - 8, block), F32)], axis=0
        ).T / width
        total = part_ref[place, own].astype(F32)
        for o in range(1, n):
            term(o, i).wait_recv()
            total = total + land_ref[o - 1, place].astype(F32)
        inverse = stat_ref[place, 1:2]
        normed = (tok_ref[place, own].astype(F32) - stat_ref[place, 0:1]) * inverse
        out_ref[place, :] = branch_ref[place, own].astype(F32) + inverse * (
            total - spread[:, 0:1] - normed * spread[:, 1:2]
        )
    advance(6)
    for o in range(1, n):
        totals(o).wait_send()
        for i in range(count):
            term(o, i).wait_send()


def unproject(dproj, tok_full, stat, weight, branch, heads, n, grads):
    rows, width = tok_full.shape
    shard = width // n
    vmem = pl.BlockSpec(memory_space=pltpu.VMEM)
    extra = []
    for grad in grads:
        extra += sum_scratch(grad.shape)
    result = pl.pallas_call(
        functools.partial(unproject_kernel, heads, n, len(grads) > 0),
        in_specs=[vmem] * (5 + len(grads)),
        out_specs=[vmem] * (1 + len(grads)),
        out_shape=[jax.ShapeDtypeStruct((rows, shard), F32)]
        + [jax.ShapeDtypeStruct(grad.shape, BF16) for grad in grads],
        scratch_shapes=[
            pltpu.VMEM((rows, width), BF16),
            pltpu.VMEM((8, rows), F32),
            pltpu.VMEM((n - 1, rows, shard), BF16),
            pltpu.VMEM((8, rows), F32),
            pltpu.VMEM((n - 1, 8, rows), F32),
            pltpu.SemaphoreType.DMA((n - 1, rows // 256)),
            pltpu.SemaphoreType.DMA((n - 1, rows // 256)),
            pltpu.SemaphoreType.DMA((n - 1,)),
            pltpu.SemaphoreType.DMA((n - 1,)),
        ]
        + extra,
        compiler_params=params(60, collective_id=4, has_side_effects=True),
        cost_estimate=cost(1e6, 1e6),
        name="unproject",
    )(dproj, tok_full, stat, weight, branch, *grads)
    return result


def per_device(tokens, segment_ids, in_weight, out_weight, gate_up_weight, down_weight, cotangent):
    rows = tokens.shape[0]
    width = in_weight.shape[0]
    span = in_weight.shape[2]
    heads = span // HD
    hidden_local = down_weight.shape[0]
    me = lax.axis_index("ctx")
    tp_size = lax.axis_size("tp")
    cube = lax.axis_size("ctx") == CUBE

    def gather(local, axis=1):
        return lax.all_gather(local, "tp", axis=axis, tiled=True)

    places = me * rows + jnp.arange(rows, dtype=jnp.int32)
    cosine, sine = rope_tables(places)
    in_w = jnp.transpose(in_weight, (1, 0, 2))
    gu_w = jnp.transpose(
        gate_up_weight.reshape(width, 2, hidden_local // BLOCK, BLOCK), (0, 2, 1, 3)
    )
    gu_w = gu_w.reshape(width, 2 * hidden_local)

    all_seg = lax.all_gather(segment_ids, "ctx", axis=0, tiled=True)
    count = all_seg.shape[0]
    every = jnp.arange(count, dtype=jnp.int32)
    opens = jnp.concatenate([jnp.ones((1,), jnp.bool_), all_seg[1:] != all_seg[:-1]])
    all_begin = lax.cummax(jnp.where(opens, every, 0))
    blocks = all_begin.reshape(count // rows, rows)

    tok_full, gu_w, blocks, all_begin = lax.optimization_barrier(
        (gather(tokens), gu_w, blocks, all_begin)
    )
    key_info = jnp.stack(
        [me, blocks[me, 0] // rows, (blocks[me, rows - 1] + rows - 1) // rows]
    ).astype(jnp.int32)
    query_info = jnp.stack(
        [
            me,
            jnp.sum((blocks[:, 0] < (me + 1) * rows).astype(jnp.int32)) - 1,
            jnp.sum((blocks[:, rows - 1] <= me * rows).astype(jnp.int32)) - 1,
        ]
    ).astype(jnp.int32)
    begin = lax.dynamic_slice_in_dim(blocks, me, 1, 0)
    all_begin = all_begin[None, :]
    inner1, stat1, query, pairs = project(tok_full, in_w, cosine, sine, heads)
    if cube:
        raw, mixed, lse, all_pairs, cot_full, out_part = attend_far(
            query, pairs, begin, cotangent, out_weight, heads, tp_size
        )
    else:
        all_pairs = lax.all_gather(pairs, "ctx", axis=0, tiled=True)
        cot_full = gather(cotangent)
        raw, mixed, lse = attend(key_info, query, all_pairs, begin, heads)
        out_part = jnp.dot(mixed, out_weight, preferred_element_type=F32).astype(BF16)
    late_query, mixed = lax.optimization_barrier((query, mixed))
    all_query = lax.all_gather(late_query, "ctx", axis=0, tiled=True)
    inner2, resid1, stat2 = merge(out_part, tok_full, tp_size)

    hidden, grad_gu, down_grad, gu_grad = feed(inner2, cot_full, gu_w, down_weight, BLOCK)
    down_grad, gu_grad, all_query, grad_gu, hidden = lax.optimization_barrier(
        (down_grad, gu_grad, all_query, grad_gu, hidden)
    )
    down_grad, gu_grad = lax.optimization_barrier(lax.psum((down_grad, gu_grad), "ctx"))

    grad_part = lax.dot_general(grad_gu, gu_w, NT, preferred_element_type=F32).astype(BF16)
    branch_grad = norm_back(grad_part, cot_full, resid1, stat2, tp_size)
    out_grad = lax.dot_general(mixed, branch_grad, TN, preferred_element_type=F32).astype(BF16)
    grad_mixed, delta = mixed_grad(branch_grad, out_weight, raw, lse, heads)
    branch = (resid1 + jnp.dot(hidden, down_weight, preferred_element_type=F32)).astype(BF16)
    if cube:
        dq, dk, dv, layer_out = attend_back_far(
            grad_mixed, all_query, all_pairs, blocks, branch, heads, tp_size
        )
    else:
        branch = lax.psum_scatter(branch, "tp", scatter_dimension=1, tiled=True)
        layer_out = branch
        all_grad = lax.all_gather(grad_mixed, "ctx", axis=0, tiled=True)
        dq = query_grad(key_info, query, grad_mixed, lse, delta, all_pairs, begin, heads)
        dk, dv = key_grad(query_info, pairs, all_query, all_grad, all_begin, heads)

    dproj, in_grad = unrotate(dq, dk, dv, cosine, sine, inner1, heads)
    if cube:
        tokens_grad, in_grad, out_grad = unproject(
            dproj, tok_full, stat1, in_w, branch_grad, heads, tp_size,
            [in_grad, out_grad],
        )
    else:
        in_grad, out_grad, down_grad, gu_grad = lax.optimization_barrier(
            (in_grad, out_grad, down_grad, gu_grad)
        )
        in_grad, out_grad = lax.psum((in_grad, out_grad), "ctx")
        (tokens_grad,) = unproject(
            dproj, tok_full, stat1, in_w, branch_grad, heads, tp_size, []
        )
    return (
        layer_out,
        tokens_grad,
        jnp.transpose(widen(in_grad).reshape(3, width, span), (1, 0, 2)),
        out_grad.astype(F32),
        weave(gu_grad, BLOCK),
        widen(down_grad),
    )


def solution(mesh):
    placed = (
        P("ctx", "tp"),
        P("ctx"),
        P(None, None, "tp"),
        P("tp", None),
        P(None, None, "tp"),
        P("tp", None),
        P("ctx", "tp"),
    )
    return jax.shard_map(
        per_device,
        mesh=mesh,
        in_specs=placed,
        out_specs=(
            P("ctx", "tp"),
            P("ctx", "tp"),
            P(None, None, "tp"),
            P("tp", None),
            P(None, None, "tp"),
            P("tp", None),
        ),
        check_vma=False,
    )
```

```python
import functools

import jax
import jax.numpy as jnp
from jax import lax
from jax.experimental import pallas as pl
from jax.experimental.pallas import tpu as pltpu
from jax.sharding import PartitionSpec as P

HD = 128
EPS = 1e-05
NEG = -1e30
SCALE = HD ** (-0.5)
LOG2E = 1.4426950408889634
C2 = SCALE * LOG2E
F32 = jnp.float32
BF16 = jnp.bfloat16
NT = (((1,), (1,)), ((), ()))
TN = (((0,), (0,)), ((), ()))
MESH = pl.DeviceIdType.MESH
BLOCK = 256


def params(mib, **more):
    return pltpu.CompilerParams(vmem_limit_bytes=mib << 20, **more)


def cost(flops, nbytes, trans=0):
    return pl.CostEstimate(flops=int(flops), bytes_accessed=int(nbytes), transcendentals=int(trans))


def rope_tables(places):
    half = HD // 2
    freq = 10000.0 ** (-jnp.arange(half, dtype=F32) * 2.0 / HD)
    angle = places.astype(F32)[:, None] * freq[None, :]
    cosine, sine = jnp.cos(angle), jnp.sin(angle)
    return jnp.concatenate([cosine, cosine], axis=1), jnp.concatenate([-sine, sine], axis=1)


def project_kernel(heads, tok_ref, w_ref, cos_ref, sin_ref, inner_ref, stat_ref, q_ref, kv_ref):
    x = tok_ref[...].astype(F32)
    center = x - jnp.mean(x, axis=1, keepdims=True)
    inverse = lax.rsqrt(jnp.mean(center * center, axis=1, keepdims=True) + EPS)
    inner = (center * inverse).astype(BF16)
    inner_ref[...] = inner
    stat_ref[...] = jnp.concatenate(
        [jnp.mean(x, axis=1, keepdims=True), inverse], axis=1
    )
    cosine, sine = cos_ref[...], sin_ref[...]
    span = heads * HD
    for part in range(3):
        out = jnp.dot(inner, w_ref[part], preferred_element_type=F32)
        if part == 2:
            kv_ref[:, span:] = out.astype(BF16)
            continue
        for h in range(heads):
            piece = out[:, h * HD : (h + 1) * HD]
            turned = (piece * cosine + pltpu.roll(piece, HD // 2, 1) * sine).astype(BF16)
            if part == 0:
                q_ref[:, h * HD : (h + 1) * HD] = turned
            else:
                kv_ref[:, h * HD : (h + 1) * HD] = turned


def project(tok_full, weight, cosine, sine, heads):
    rows, width = tok_full.shape
    span = heads * HD
    block = 256
    row = lambda n: pl.BlockSpec((block, n), lambda i: (i, 0))
    return pl.pallas_call(
        functools.partial(project_kernel, heads),
        grid=(rows // block,),
        in_specs=[
            row(width),
            pl.BlockSpec((3, width, span), lambda i: (0, 0, 0)),
            row(HD),
            row(HD),
        ],
        out_specs=[row(width), row(2), row(span), row(2 * span)],
        out_shape=[
            jax.ShapeDtypeStruct((rows, width), BF16),
            jax.ShapeDtypeStruct((rows, 2), F32),
            jax.ShapeDtypeStruct((rows, span), BF16),
            jax.ShapeDtypeStruct((rows, 2 * span), BF16),
        ],
        compiler_params=params(56),
        cost_estimate=cost(6 * rows * width * span, 6 * width * span + 6 * rows * width),
        name="project",
    )(tok_full, weight, cosine, sine)


def masked(scores, j, me, rows, begin):
    key_place = lax.broadcasted_iota(jnp.int32, scores.shape, 0) + j * rows
    query_place = lax.broadcasted_iota(jnp.int32, scores.shape, 1) + me * rows
    return jnp.where((key_place <= query_place) & (key_place >= begin), scores, NEG)


def attend_kernel(
    heads, info, q_ref, k_ref, v_ref, begin_ref, raw_ref, mixed_ref, lse_ref,
    high_ref, total_ref, acc_ref, s_ref,
):
    me, first, clear = info[0], info[1], info[2]
    j = pl.program_id(0)
    rows = q_ref.shape[0]

    @pl.when(j == 0)
    def _():
        high_ref[...] = jnp.full_like(high_ref, NEG)
        total_ref[...] = jnp.zeros_like(total_ref)
        acc_ref[...] = jnp.zeros_like(acc_ref)

    def block(hide):
        def score(h):
            hs = slice(h * HD, (h + 1) * HD)
            s = lax.dot_general(k_ref[:, hs], q_ref[:, hs], NT, preferred_element_type=F32)
            if hide:
                s = masked(s, j, me, rows, begin_ref[...])
            s_ref[h % 2] = s

        def spread(h):
            hs = slice(h * HD, (h + 1) * HD)
            s = s_ref[h % 2]
            old = high_ref[h : h + 1, :]
            new = jnp.maximum(old, jnp.max(s, axis=0, keepdims=True))
            high_ref[h : h + 1, :] = new
            p = jnp.exp2(s * C2 - new * C2)
            decay = jnp.exp2((old - new) * C2)
            total_ref[h : h + 1, :] = total_ref[h : h + 1, :] * decay + jnp.sum(
                p, axis=0, keepdims=True
            )
            acc_ref[h] = acc_ref[h] * decay + lax.dot_general(
                v_ref[:, hs], p.astype(BF16), TN, preferred_element_type=F32
            )

        score(0)
        for h in range(heads):
            if h + 1 < heads:
                score(h + 1)
            spread(h)

    @pl.when((j >= clear) & (j < me))
    def _():
        block(False)

    @pl.when(((j >= first) & (j < clear) & (j < me)) | (j == me))
    def _():
        block(True)

    @pl.when(j == me)
    def _():
        for h in range(heads):
            hs = slice(h * HD, (h + 1) * HD)
            out = (acc_ref[h] / total_ref[h : h + 1, :]).T
            raw_ref[:, hs] = out
            mixed_ref[:, hs] = out.astype(BF16)
        lse_ref[...] = high_ref[...] * C2 + jnp.log2(total_ref[...])


def attend(info, query, pairs, begin, heads):
    rows = query.shape[0]
    total = pairs.shape[0]
    span = heads * HD
    full = lambda shape: pl.BlockSpec(shape, lambda j, s: (0, 0))
    key = pl.BlockSpec((rows, span), lambda j, s: (jnp.clip(j, s[1], s[0]), 0))
    value = pl.BlockSpec((rows, span), lambda j, s: (jnp.clip(j, s[1], s[0]), 1))
    return pl.pallas_call(
        functools.partial(attend_kernel, heads),
        grid_spec=pltpu.PrefetchScalarGridSpec(
            num_scalar_prefetch=1,
            grid=(total // rows,),
            in_specs=[full((rows, span)), key, value, full((1, rows))],
            out_specs=[full((rows, span)), full((rows, span)), full((heads, rows))],
            scratch_shapes=[
                pltpu.VMEM((heads, rows), F32),
                pltpu.VMEM((heads, rows), F32),
                pltpu.VMEM((heads, HD, rows), F32),
                pltpu.VMEM((2, rows, rows), F32),
            ],
        ),
        out_shape=[
            jax.ShapeDtypeStruct((rows, span), F32),
            jax.ShapeDtypeStruct((rows, span), BF16),
            jax.ShapeDtypeStruct((heads, rows), F32),
        ],
        compiler_params=params(56),
        cost_estimate=cost(4 * rows * total * span, 4 * total * span, rows * total * heads),
        name="attend",
    )(info, query, pairs, pairs, begin)


CUBE = 8
CUBE_SENDS = 10


class Cube:
    def __init__(self, buf, send, recv):
        me = lax.axis_index("ctx")
        flip = (1 - 2 * (me % 2), 2 - 4 * ((me // 2) % 2), 4 - 8 * (me // 4))
        self.me, self.flip, self.buf, self.send, self.recv = me, flip, buf, send, recv
        self.rows = buf.shape[0] // CUBE

    def copy(self, n):
        core, x, y = self.flip
        half = self.rows // 2
        block, part, target = (
            (0, None, core),
            (0, 0, x), (0, 1, x), (0, 1, y), (0, 0, y),
            (x, 0, y), (y, 1, x),
            (x, None, core), (y, None, core), (x + y, None, core),
        )[n]
        start = (self.me + block) * self.rows
        size = self.rows
        if part is not None:
            start, size = start + part * half, half
        place = self.buf.at[pl.ds(pl.multiple_of(start, 16), size)]
        return pltpu.make_async_remote_copy(
            src_ref=place, dst_ref=place, send_sem=self.send.at[n], recv_sem=self.recv.at[n],
            device_id={"ctx": self.me + target}, device_id_type=MESH,
        )

    def arrived(self, n):
        self.copy(n).wait_recv()

    def start(self, *which):
        for n in which:
            self.copy(n).start()

    def signal(self, barrier):
        for target in self.flip:
            pl.semaphore_signal(
                barrier, inc=1, device_id={"ctx": self.me + target}, device_id_type=MESH
            )

    def block(self, step):
        core, x, y = self.flip
        on = lambda *steps: sum((step == n).astype(jnp.int32) for n in steps)
        return self.me + on(1, 4, 5, 7) * core + on(2, 4, 6, 7) * x + on(3, 5, 6, 7) * y

    def advance(self, step):
        @pl.when(step == 0)
        def _():
            self.start(0, 1, 3, 2, 4)

        @pl.when(step == 1)
        def _():
            self.arrived(0)

        @pl.when(step == 2)
        def _():
            self.arrived(1)
            self.start(5)
            self.arrived(3)
            self.start(6)
            self.arrived(2)
            self.start(7)

        @pl.when(step == 3)
        def _():
            self.arrived(4)
            self.start(8)

        @pl.when(step == 4)
        def _():
            self.arrived(7)

        @pl.when(step == 5)
        def _():
            self.arrived(8)

        @pl.when(step == 6)
        def _():
            self.arrived(5)
            self.arrived(6)
            self.start(9)

        @pl.when(step == 7)
        def _():
            self.arrived(9)

    def finish(self):
        for n in range(CUBE_SENDS):
            self.copy(n).wait_send()


SUM_SENDS = 11


class CubeSum:
    def __init__(self, rows, send, recv, own=None, land=None, out=None, shard=None, local=None):
        me = lax.axis_index("ctx")
        core, x, y = me % 2, (me // 2) % 2, me // 4
        self.me, self.own, self.out, self.land = me, own, out, land
        self.send, self.recv, self.shard, self.local = send, recv, shard, local
        self.half, self.quarter = rows // 2, rows // 4
        self.eighth, self.last = rows // 8, rows // 16
        mine = core * self.half
        first, second = mine, mine + self.quarter
        self.to = (1 - 2 * core, 2 - 4 * x, 4 - 8 * y)
        self.mine, self.other = mine, (1 - core) * self.half
        self.keep1 = (first + x * self.eighth, second + y * self.eighth)
        self.give1 = (first + (1 - x) * self.eighth, second + (1 - y) * self.eighth)
        self.keep2 = (self.keep1[0] + y * self.last, self.keep1[1] + x * self.last)
        self.give2 = (self.keep1[0] + (1 - y) * self.last, self.keep1[1] + (1 - x) * self.last)

    def place(self, ref, start, size):
        return ref.at[pl.ds(start if isinstance(start, int) else pl.multiple_of(start, 16), size)]

    def final(self, i):
        if self.shard is not None:
            return self.shard, i * self.last
        return self.out, self.keep2[i]

    def copy(self, n):
        core, x, y = self.to
        half, eighth, last, out, land = self.half, self.eighth, self.last, self.out, self.land
        mine = self.mine
        if n < 5:
            source, start, size, target = (
                (self.own, self.other, half, core),
                (land, self.give1[0] - mine, eighth, x), (land, self.give1[1] - mine, eighth, y),
                (land, self.give2[0] - mine, last, y), (land, self.give2[1] - mine, last, x),
            )[n]
            landing = (0, half, half + eighth, half + 2 * eighth, half + 2 * eighth + last)[n]
            src, dst = self.place(source, start, size), self.place(land, landing, size)
        else:
            start, size, target = (
                (self.keep2[0], last, y), (self.keep2[1], last, x),
                (self.keep1[0], eighth, x), (self.keep1[1], eighth, y),
                (mine, self.quarter, core), (mine + self.quarter, self.quarter, core),
            )[n - 5]
            dst = self.place(out, start, size)
            src = self.place(*self.final(n - 5), size) if n < 7 else dst
        return pltpu.make_async_remote_copy(
            src_ref=src, dst_ref=dst, send_sem=self.send.at[n], recv_sem=self.recv.at[n],
            device_id={"ctx": self.me + target}, device_id_type=MESH,
        )

    def add(self, target, to, source, at, landed, size):
        step = size
        while step * self.own.shape[1] > 256 * 1024 and step % 32 == 0:
            step = step // 2

        def part(i, carry):
            def rows(begin):
                return pl.ds(pl.multiple_of(begin + i * step, 16), step)

            total = source[rows(at), :].astype(F32) + self.land[rows(landed), :].astype(F32)
            target[rows(to), :] = total.astype(BF16)
            return carry

        lax.fori_loop(0, size // step, part, 0)

    def begin(self):
        self.copy(0).start()

    def reduce(self, k):
        half, eighth, last, land, mine = self.half, self.eighth, self.last, self.land, self.mine
        i = k % 2
        if k == 0:
            self.copy(0).wait_recv()
        if k < 2:
            at = self.give1[i]
            self.add(land, at - mine, self.own, at, at - mine, eighth)
            self.copy(1 + i).start()
        elif k < 4:
            at = self.keep1[i]
            self.add(land, at - mine, self.own, at, at - mine, eighth)
        elif k < 6:
            self.copy(1 + i).wait_recv()
            landed = half + i * eighth - self.keep1[i]
            at = self.give2[i]
            self.add(land, at - mine, land, at - mine, landed + at, last)
            self.copy(3 + i).start()
            at = self.keep2[i]
            self.add(land, at - mine, land, at - mine, landed + at, last)
        else:
            self.copy(3 + i).wait_recv()
            target, to = self.final(i)
            at = self.keep2[i]
            self.add(target, to, land, at - mine, half + 2 * eighth + i * last, last)

    def keep(self, i):
        return pltpu.make_async_copy(
            self.place(self.shard, i * self.last, self.last),
            self.place(self.out, self.keep2[i], self.last),
            self.local.at[i],
        )

    def gather(self, k):
        for i in range(2):
            if k == 0:
                self.copy(5 + i).start()
                if self.shard is not None:
                    self.keep(i).start()
            if k == 1:
                self.copy(5 + i).wait_recv()
                if self.shard is not None:
                    self.keep(i).wait()
                self.copy(7 + i).start()
            if k == 2:
                self.copy(7 + i).wait_recv()
                self.copy(9 + i).start()
            if k == 3:
                self.copy(9 + i).wait_recv()

    def finish(self):
        for n in range(0 if self.own is not None else 5, SUM_SENDS if self.out is not None else 5):
            self.copy(n).wait_send()

    def signal(self, barrier):
        for target in self.to:
            pl.semaphore_signal(
                barrier, inc=1, device_id={"ctx": self.me + target}, device_id_type=MESH
            )


def sum_scratch(shape):
    return [
        pltpu.VMEM((shape[0] // 2 + 3 * (shape[0] // 8), shape[1]), BF16),
        pltpu.SemaphoreType.DMA((SUM_SENDS,)),
        pltpu.SemaphoreType.DMA((SUM_SENDS,)),
    ]


def hidden_scores(scores, key_block, query_block, rows, begin):
    key_place = lax.broadcasted_iota(jnp.int32, scores.shape, 0) + key_block * rows
    query_place = lax.broadcasted_iota(jnp.int32, scores.shape, 1) + query_block * rows
    return jnp.where((key_place <= query_place) & (key_place >= begin), scores, NEG)


def attend_far_kernel(
    heads, n, q_ref, own_ref, begin_ref, cot_ref, w_ref,
    raw_ref, mixed_ref, lse_ref, keep_ref, full_ref, part_ref,
    pair_ref, high_ref, total_ref, acc_ref, s_ref, send, recv, zsend, zrecv, keep_sem,
):
    rows = q_ref.shape[0]
    span = heads * HD
    shard = cot_ref.shape[1]
    at = lax.axis_index("tp")
    cube = Cube(pair_ref, send, recv)
    me = cube.me
    barrier = pltpu.get_barrier_semaphore()
    cube.signal(barrier)

    @pl.when(at > 0)
    def _():
        pl.semaphore_signal(barrier, inc=1, device_id={"tp": at - 1}, device_id_type=MESH)

    @pl.when(at < n - 1)
    def _():
        pl.semaphore_signal(barrier, inc=1, device_id={"tp": at + 1}, device_id_type=MESH)

    pair_ref[pl.ds(pl.multiple_of(me * rows, 16), rows), :] = own_ref[...]
    full_ref[:, pl.ds(pl.multiple_of(at * shard, 128), shard)] = cot_ref[...]
    high_ref[...] = jnp.full_like(high_ref, NEG)
    total_ref[...] = jnp.zeros_like(total_ref)
    acc_ref[...] = jnp.zeros_like(acc_ref)
    pl.semaphore_wait(barrier, jnp.where((at > 0) & (at < n - 1), 5, 4))

    def pass_on(right, s, k):
        place = full_ref.at[:, pl.ds(pl.multiple_of(s * shard, 128), shard)]
        which = (1 if right else 0, k)
        return pltpu.make_async_remote_copy(
            src_ref=place, dst_ref=place, send_sem=zsend.at[which], recv_sem=zrecv.at[which],
            device_id={"tp": at + 1 if right else at - 1}, device_id_type=MESH,
        )

    def line_step(k):
        @pl.when(at >= k)
        def _():
            if k > 0:
                pass_on(True, at - k, k - 1).wait_recv()

            @pl.when(at < n - 1)
            def _():
                pass_on(True, at - k, k).start()

        @pl.when(at + k < n)
        def _():
            if k > 0:
                pass_on(False, at + k, k - 1).wait_recv()

            @pl.when(at > 0)
            def _():
                pass_on(False, at + k, k).start()

    def keep(step):
        place = pl.ds(pl.multiple_of(cube.block(step) * rows, 16), rows)
        return pltpu.make_async_copy(pair_ref.at[place], keep_ref.at[place], keep_sem.at[step])

    def turn(step, carry):
        cube.advance(step)
        keep(step).start()
        for k in range(n):
            @pl.when(step == min(k * 2, CUBE - 1 - (n - 1 - k)) if n <= CUBE else k)
            def _():
                line_step(k)
        block = cube.block(step)

        @pl.when(block <= me)
        def _():
            place = pl.ds(pl.multiple_of(block * rows, 16), rows)

            def score(h):
                hs = slice(h * HD, (h + 1) * HD)
                s = lax.dot_general(
                    pair_ref[place, hs], q_ref[:, hs], NT, preferred_element_type=F32
                )
                s_ref[h % 2] = hidden_scores(s, block, me, rows, begin_ref[...])

            def spread(h):
                s = s_ref[h % 2]
                old = high_ref[h : h + 1, :]
                new = jnp.maximum(old, jnp.max(s, axis=0, keepdims=True))
                high_ref[h : h + 1, :] = new
                p = jnp.exp2(s * C2 - new * C2)
                decay = jnp.exp2((old - new) * C2)
                total_ref[h : h + 1, :] = total_ref[h : h + 1, :] * decay + jnp.sum(
                    p, axis=0, keepdims=True
                )
                acc_ref[h] = acc_ref[h] * decay + lax.dot_general(
                    pair_ref[place, span + h * HD : span + (h + 1) * HD], p.astype(BF16), TN,
                    preferred_element_type=F32,
                )

            score(0)
            for h in range(heads):
                if h + 1 < heads:
                    score(h + 1)
                spread(h)

        return carry

    lax.fori_loop(0, CUBE, turn, 0)
    for h in range(heads):
        hs = slice(h * HD, (h + 1) * HD)
        out = (acc_ref[h] / total_ref[h : h + 1, :]).T
        raw_ref[:, hs] = out
        mixed_ref[:, hs] = out.astype(BF16)
    part_ref[...] = jnp.dot(
        mixed_ref[...], w_ref[...], preferred_element_type=F32
    ).astype(BF16)
    lse_ref[...] = high_ref[...] * C2 + jnp.log2(total_ref[...])

    def kept(step, carry):
        keep(step).wait()
        return carry

    lax.fori_loop(0, CUBE, kept, 0)
    cube.finish()
    for k in range(n):
        @pl.when((at >= k) & (at < n - 1))
        def _():
            pass_on(True, at - k, k).wait_send()

        @pl.when((at + k < n) & (at > 0))
        def _():
            pass_on(False, at + k, k).wait_send()


def attend_far(query, pairs, begin, cot, weight, heads, n):
    rows = query.shape[0]
    width = weight.shape[1]
    span = heads * HD
    vmem = pl.BlockSpec(memory_space=pltpu.VMEM)
    return pl.pallas_call(
        functools.partial(attend_far_kernel, heads, n),
        in_specs=[vmem] * 5,
        out_specs=[vmem] * 3 + [pl.BlockSpec(memory_space=pl.ANY)] + [vmem] * 2,
        out_shape=[
            jax.ShapeDtypeStruct((rows, span), F32),
            jax.ShapeDtypeStruct((rows, span), BF16),
            jax.ShapeDtypeStruct((heads, rows), F32),
            jax.ShapeDtypeStruct((CUBE * rows, 2 * span), BF16),
            jax.ShapeDtypeStruct((rows, n * cot.shape[1]), BF16),
            jax.ShapeDtypeStruct((rows, width), BF16),
        ],
        scratch_shapes=[
            pltpu.VMEM((CUBE * rows, 2 * span), BF16),
            pltpu.VMEM((heads, rows), F32),
            pltpu.VMEM((heads, rows), F32),
            pltpu.VMEM((heads, HD, rows), F32),
            pltpu.VMEM((2, rows, rows), F32),
            pltpu.SemaphoreType.DMA((CUBE_SENDS,)),
            pltpu.SemaphoreType.DMA((CUBE_SENDS,)),
            pltpu.SemaphoreType.DMA((2, n)),
            pltpu.SemaphoreType.DMA((2, n)),
            pltpu.SemaphoreType.DMA((CUBE,)),
        ],
        compiler_params=params(58, collective_id=2, has_side_effects=True),
        cost_estimate=cost(1e6, 1e6),
        name="attend_far",
    )(query, pairs, begin, cot, weight)


def attend_back_far_kernel(
    heads, n, g_ref, far_q_ref, far_pair_ref, begin_ref, part_ref,
    dq_ref, dk_ref, dv_ref, layer_ref,
    all_ref, acc_ref, rows_ref, s_ref, p_ref, land_ref, pair_ref, q_ref,
    send, recv, zsend, zrecv, read_sem,
):
    rows = g_ref.shape[0]
    span = heads * HD
    shard = layer_ref.shape[1]
    at = lax.axis_index("tp")
    cube = Cube(all_ref, send, recv)
    me = cube.me
    barrier = pltpu.get_barrier_semaphore()
    cube.signal(barrier)
    for o in range(1, n):
        pl.semaphore_signal(
            barrier, inc=1, device_id={"tp": lax.rem(at + o, n)}, device_id_type=MESH
        )

    def read(step, keys):
        place = pl.ds(pl.multiple_of(cube.block(step) * rows, 16), rows)
        far, near = (far_pair_ref, pair_ref) if keys else (far_q_ref, q_ref)
        return pltpu.make_async_copy(
            far.at[place], near.at[place], read_sem.at[0 if keys else 1, step]
        )

    def read_all(step, carry):
        block = cube.block(step)

        @pl.when(block <= me)
        def _():
            read(step, True).start()

        @pl.when(block >= me)
        def _():
            read(step, False).start()

        return carry

    lax.fori_loop(0, CUBE, read_all, 0)
    all_ref[pl.ds(pl.multiple_of(me * rows, 16), rows), :] = g_ref[...]
    acc_ref[...] = jnp.zeros_like(acc_ref)
    dk_ref[...] = jnp.zeros_like(dk_ref)
    dv_ref[...] = jnp.zeros_like(dv_ref)
    pl.semaphore_wait(barrier, 3 + n - 1)

    def term(o):
        target = lax.rem(at + o, n)
        return pltpu.make_async_remote_copy(
            src_ref=part_ref.at[:, pl.ds(pl.multiple_of(target * shard, 128), shard)],
            dst_ref=land_ref.at[o - 1],
            send_sem=zsend.at[o - 1], recv_sem=zrecv.at[o - 1],
            device_id={"tp": target}, device_id_type=MESH,
        )

    own = pl.ds(pl.multiple_of(me * rows, 16), rows)

    def turn(step, carry):
        cube.advance(step)

        @pl.when(step == 0)
        def _():
            for o in range(1, n):
                term(o).start()

        block = cube.block(step)
        place = pl.ds(pl.multiple_of(block * rows, 16), rows)

        @pl.when(block <= me)
        def _():
            read(step, True).wait()

        @pl.when(block >= me)
        def _():
            read(step, False).wait()

        def scores(h, key_block, key_place, query_block, query_place):
            hs = slice(h * HD, (h + 1) * HD)
            vs = slice(span + h * HD, span + (h + 1) * HD)
            s = lax.dot_general(
                pair_ref[key_place, hs], q_ref[query_place, hs], NT, preferred_element_type=F32
            )
            begin = begin_ref[pl.ds(query_block, 1), :]
            s_ref[h % 2] = hidden_scores(s, key_block, query_block, rows, begin)
            p_ref[h % 2] = lax.dot_general(
                pair_ref[key_place, vs], all_ref[query_place, hs], NT, preferred_element_type=F32
            )

        def read_rows(query_place):
            coded = all_ref[query_place, span:].astype(F32).T
            for k in range(2 * heads):
                rows_ref[k : k + 1, :] = (
                    coded[3 * k : 3 * k + 1]
                    + coded[3 * k + 1 : 3 * k + 2]
                    + coded[3 * k + 2 : 3 * k + 3]
                )

        def weights(h):
            p = jnp.exp2(s_ref[h % 2] * C2 - rows_ref[h : h + 1, :])
            ds = p * (p_ref[h % 2] - rows_ref[heads + h : heads + h + 1, :])
            return p.astype(BF16), ds.astype(BF16)

        @pl.when(block <= me)
        def _():
            read_rows(own)
            scores(0, block, place, me, own)
            for h in range(heads):
                if h + 1 < heads:
                    scores(h + 1, block, place, me, own)
                _, ds = weights(h)
                acc_ref[h] = acc_ref[h] + lax.dot_general(
                    pair_ref[place, h * HD : (h + 1) * HD], ds, TN, preferred_element_type=F32
                )

        @pl.when(block >= me)
        def _():
            read_rows(place)
            scores(0, me, own, block, place)
            for h in range(heads):
                hs = slice(h * HD, (h + 1) * HD)
                if h + 1 < heads:
                    scores(h + 1, me, own, block, place)
                p, ds = weights(h)
                dv_ref[:, hs] += jnp.dot(p, all_ref[place, hs], preferred_element_type=F32)
                dk_ref[:, hs] += jnp.dot(ds, q_ref[place, hs], preferred_element_type=F32)

        return carry

    lax.fori_loop(0, CUBE, turn, 0)
    for h in range(heads):
        dq_ref[:, h * HD : (h + 1) * HD] = (acc_ref[h] * SCALE).T
    dk_ref[...] = dk_ref[...] * SCALE
    total = part_ref[:, pl.ds(pl.multiple_of(at * shard, 128), shard)].astype(F32)
    for o in range(1, n):
        term(o).wait_recv()
        total = total + land_ref[o - 1].astype(F32)
    layer_ref[...] = total.astype(BF16)
    cube.finish()
    for o in range(1, n):
        term(o).wait_send()


def attend_back_far(grad, all_query, all_pairs, all_begin, part, heads, n):
    rows = grad.shape[0]
    span = heads * HD
    shard = part.shape[1] // n
    vmem = pl.BlockSpec(memory_space=pltpu.VMEM)
    wide = jax.ShapeDtypeStruct((rows, span), F32)
    return pl.pallas_call(
        functools.partial(attend_back_far_kernel, heads, n),
        in_specs=[vmem] + [pl.BlockSpec(memory_space=pl.ANY)] * 2 + [vmem] * 2,
        out_specs=[vmem] * 4,
        out_shape=[wide, wide, wide, jax.ShapeDtypeStruct((rows, shard), BF16)],
        scratch_shapes=[
            pltpu.VMEM((CUBE * rows, span + HD), BF16),
            pltpu.VMEM((heads, HD, rows), F32),
            pltpu.VMEM((2 * heads, rows), F32),
            pltpu.VMEM((2, rows, rows), F32),
            pltpu.VMEM((2, rows, rows), F32),
            pltpu.VMEM((n - 1, rows, shard), BF16),
            pltpu.VMEM((CUBE * rows, 2 * span), BF16),
            pltpu.VMEM((CUBE * rows, span), BF16),
            pltpu.SemaphoreType.DMA((CUBE_SENDS,)),
            pltpu.SemaphoreType.DMA((CUBE_SENDS,)),
            pltpu.SemaphoreType.DMA((n - 1,)),
            pltpu.SemaphoreType.DMA((n - 1,)),
            pltpu.SemaphoreType.DMA((2, CUBE)),
        ],
        compiler_params=params(60, collective_id=3, has_side_effects=True),
        cost_estimate=cost(1e6, 1e6),
        name="attend_back_far",
    )(grad, all_query, all_pairs, all_begin, part)


def query_grad_kernel(
    heads, info, q_ref, do_ref, lse_ref, delta_ref, k_ref, v_ref, begin_ref,
    dq_ref, acc_ref, s_ref, g_ref,
):
    me, first, clear = info[0], info[1], info[2]
    j = pl.program_id(0)
    rows = q_ref.shape[0]

    @pl.when(j == 0)
    def _():
        acc_ref[...] = jnp.zeros_like(acc_ref)

    def block(hide):
        def score(h):
            hs = slice(h * HD, (h + 1) * HD)
            s = lax.dot_general(k_ref[:, hs], q_ref[:, hs], NT, preferred_element_type=F32)
            if hide:
                s = masked(s, j, me, rows, begin_ref[...])
            s_ref[h % 2] = s
            g_ref[h % 2] = lax.dot_general(
                v_ref[:, hs], do_ref[:, hs], NT, preferred_element_type=F32
            )

        def spread(h):
            hs = slice(h * HD, (h + 1) * HD)
            p = jnp.exp2(s_ref[h % 2] * C2 - lse_ref[h : h + 1, :])
            ds = (p * (g_ref[h % 2] - delta_ref[h : h + 1, :])).astype(BF16)
            acc_ref[h] = acc_ref[h] + lax.dot_general(
                k_ref[:, hs], ds, TN, preferred_element_type=F32
            )

        score(0)
        for h in range(heads):
            if h + 1 < heads:
                score(h + 1)
            spread(h)

    @pl.when((j >= clear) & (j < me))
    def _():
        block(False)

    @pl.when(((j >= first) & (j < clear) & (j < me)) | (j == me))
    def _():
        block(True)

    @pl.when(j == me)
    def _():
        for h in range(heads):
            dq_ref[:, h * HD : (h + 1) * HD] = (acc_ref[h] * SCALE).T


def query_grad(info, query, grad_mixed, lse, delta, pairs, begin, heads):
    rows = query.shape[0]
    total = pairs.shape[0]
    span = heads * HD
    full = lambda shape: pl.BlockSpec(shape, lambda j, s: (0, 0))
    key = pl.BlockSpec((rows, span), lambda j, s: (jnp.clip(j, s[1], s[0]), 0))
    value = pl.BlockSpec((rows, span), lambda j, s: (jnp.clip(j, s[1], s[0]), 1))
    wide = full((rows, span))
    thin = full((heads, rows))
    return pl.pallas_call(
        functools.partial(query_grad_kernel, heads),
        grid_spec=pltpu.PrefetchScalarGridSpec(
            num_scalar_prefetch=1,
            grid=(total // rows,),
            in_specs=[wide, wide, thin, thin, key, value, full((1, rows))],
            out_specs=wide,
            scratch_shapes=[
                pltpu.VMEM((heads, HD, rows), F32),
                pltpu.VMEM((2, rows, rows), F32),
                pltpu.VMEM((2, rows, rows), F32),
            ],
        ),
        out_shape=jax.ShapeDtypeStruct((rows, span), F32),
        compiler_params=params(58),
        cost_estimate=cost(6 * rows * total * span, 4 * total * span, rows * total * heads),
        name="query_grad",
    )(info, query, grad_mixed, lse, delta, pairs, pairs, begin)


def key_grad_kernel(
    heads, info, k_ref, v_ref, q_ref, g_ref, begin_ref, dk_ref, dv_ref,
    rows_ref, s_ref, p_ref,
):
    me, last, clear = info[0], info[1], info[2]
    j = pl.program_id(0)
    rows = k_ref.shape[0]
    span = heads * HD

    @pl.when(j == me)
    def _():
        dk_ref[...] = jnp.zeros_like(dk_ref)
        dv_ref[...] = jnp.zeros_like(dv_ref)

    def block(hide):
        coded = g_ref[:, span:].astype(F32).T
        for n in range(2 * heads):
            rows_ref[n : n + 1, :] = (
                coded[3 * n : 3 * n + 1] + coded[3 * n + 1 : 3 * n + 2] + coded[3 * n + 2 : 3 * n + 3]
            )

        def score(h):
            hs = slice(h * HD, (h + 1) * HD)
            s = lax.dot_general(k_ref[:, hs], q_ref[:, hs], NT, preferred_element_type=F32)
            if hide:
                key_place = lax.broadcasted_iota(jnp.int32, s.shape, 0) + me * rows
                query_place = lax.broadcasted_iota(jnp.int32, s.shape, 1) + j * rows
                s = jnp.where(
                    (key_place <= query_place) & (key_place >= begin_ref[...]), s, NEG
                )
            s_ref[h % 2] = s
            p_ref[h % 2] = lax.dot_general(
                v_ref[:, hs], g_ref[:, hs], NT, preferred_element_type=F32
            )

        def spread(h):
            hs = slice(h * HD, (h + 1) * HD)
            p = jnp.exp2(s_ref[h % 2] * C2 - rows_ref[h : h + 1, :])
            ds = (p * (p_ref[h % 2] - rows_ref[heads + h : heads + h + 1, :])).astype(BF16)
            dv_ref[:, hs] += jnp.dot(p.astype(BF16), g_ref[:, hs], preferred_element_type=F32)
            dk_ref[:, hs] += jnp.dot(ds, q_ref[:, hs], preferred_element_type=F32)

        score(0)
        for h in range(heads):
            if h + 1 < heads:
                score(h + 1)
            spread(h)

    @pl.when((j > me) & (j <= clear))
    def _():
        block(False)

    @pl.when((j == me) | ((j > me) & (j > clear) & (j <= last)))
    def _():
        block(True)

    @pl.when(j == pl.num_programs(0) - 1)
    def _():
        dk_ref[...] = dk_ref[...] * SCALE


def key_grad(info, pairs, all_query, all_grad, all_begin, heads):
    rows = pairs.shape[0]
    total = all_query.shape[0]
    span = heads * HD
    full = lambda shape, at=0: pl.BlockSpec(shape, lambda j, s: (0, at))
    near = lambda j, s: (jnp.clip(j, s[0], s[1]), 0)
    wide = full((rows, span))
    return pl.pallas_call(
        functools.partial(key_grad_kernel, heads),
        grid_spec=pltpu.PrefetchScalarGridSpec(
            num_scalar_prefetch=1,
            grid=(total // rows,),
            in_specs=[
                wide, full((rows, span), 1),
                pl.BlockSpec((rows, span), near),
                pl.BlockSpec((rows, span + HD), near),
                pl.BlockSpec((1, rows), lambda j, s: (0, jnp.clip(j, s[0], s[1]))),
            ],
            out_specs=[wide, wide],
            scratch_shapes=[
                pltpu.VMEM((2 * heads, rows), F32),
                pltpu.VMEM((2, rows, rows), F32),
                pltpu.VMEM((2, rows, rows), F32),
            ],
        ),
        out_shape=[jax.ShapeDtypeStruct((rows, span), F32)] * 2,
        compiler_params=params(58),
        cost_estimate=cost(8 * rows * total * span, 4 * total * span, rows * total * heads),
        name="key_grad",
    )(info, pairs, pairs, all_query, all_grad, all_begin)


def mixed_grad_kernel(heads, branch_ref, w_ref, raw_ref, lse_ref, out_ref, delta_ref):
    span = heads * HD
    low = lax.dot_general(
        branch_ref[...], w_ref[...], NT, preferred_element_type=F32
    ).astype(BF16)
    out_ref[:, :span] = low
    count = low.shape[0]
    both = low.astype(F32) * raw_ref[...]
    for h in range(heads):
        delta_ref[h : h + 1, :] = jnp.sum(both[:, h * HD : (h + 1) * HD].T, axis=0, keepdims=True)
    lines = []
    for n in range(2 * heads):
        value = lse_ref[n : n + 1, :] if n < heads else delta_ref[n - heads : n - heads + 1, :]
        for _ in range(3):
            piece = value.astype(BF16).astype(F32)
            lines.append(piece)
            value = value - piece
    lines.append(jnp.zeros((HD - len(lines), count), F32))
    out_ref[:, span:] = jnp.concatenate(lines, axis=0).T.astype(BF16)


def mixed_grad(branch, weight, raw, lse, heads):
    rows, width = branch.shape
    span = heads * HD
    block = 256
    row = lambda n: pl.BlockSpec((block, n), lambda i: (i, 0))
    line = pl.BlockSpec((heads, block), lambda i: (0, i))
    return pl.pallas_call(
        functools.partial(mixed_grad_kernel, heads),
        grid=(rows // block,),
        in_specs=[row(width), pl.BlockSpec((span, width), lambda i: (0, 0)), row(span), line],
        out_specs=[row(span + HD), line],
        out_shape=[
            jax.ShapeDtypeStruct((rows, span + HD), BF16),
            jax.ShapeDtypeStruct((heads, rows), F32),
        ],
        compiler_params=params(56),
        cost_estimate=cost(2 * rows * width * span, 2 * width * span + 4 * rows * width),
        name="mixed_grad",
    )(branch, weight, raw, lse)


def feed_kernel(
    inner_ref, cot_ref, w_ref, down_ref, hidden_ref, dgu_ref, down_grad_ref, gu_grad_ref
):
    block = down_ref.shape[0]
    both = jnp.dot(inner_ref[...], w_ref[...], preferred_element_type=F32)
    grad = lax.dot_general(cot_ref[...], down_ref[...], NT, preferred_element_type=F32)
    gate, up = both[:, :block], both[:, block:]
    sigma = 1.0 / (1.0 + jnp.exp(-gate))
    active = gate * sigma
    hidden_ref[...] = (active * up).astype(BF16)
    dgu_ref[:, :block] = (grad * up * sigma * (1.0 + gate * (1.0 - sigma))).astype(BF16)
    dgu_ref[:, block:] = (grad * active).astype(BF16)
    down_grad_ref[...] = lax.dot_general(
        hidden_ref[...], cot_ref[...], TN, preferred_element_type=F32
    ).astype(BF16)
    gu_grad_ref[...] = lax.dot_general(
        inner_ref[...], dgu_ref[...], TN, preferred_element_type=F32
    ).astype(BF16)


def feed(inner, cot, weight, down, block):
    rows, width = inner.shape
    units = down.shape[0]
    whole = pl.BlockSpec((rows, width), lambda j: (0, 0))
    column = lambda high, wide: pl.BlockSpec((high, wide), lambda j: (0, j))
    line = pl.BlockSpec((block, width), lambda j: (j, 0))
    return pl.pallas_call(
        feed_kernel,
        grid=(units // block,),
        in_specs=[whole, whole, column(width, 2 * block), line],
        out_specs=[column(rows, block), column(rows, 2 * block), line, column(width, 2 * block)],
        out_shape=[
            jax.ShapeDtypeStruct((rows, units), BF16),
            jax.ShapeDtypeStruct((rows, 2 * units), BF16),
            jax.ShapeDtypeStruct((units, width), BF16),
            jax.ShapeDtypeStruct((width, 2 * units), BF16),
        ],
        compiler_params=params(60),
        cost_estimate=cost(
            12 * rows * width * units, 12 * width * units + 4 * rows * width, rows * units
        ),
        name="feed",
    )(inner, cot, weight, down)


def weave_kernel(block, sum_ref, out_ref):
    for j in range(sum_ref.shape[1] // (2 * block)):
        for k in range(2):
            at = (2 * j + k) * block
            out_ref[:, k, j * block : (j + 1) * block] = sum_ref[:, at : at + block].astype(F32)


def weave(summed, block):
    width, both = summed.shape
    rows = 256
    return pl.pallas_call(
        functools.partial(weave_kernel, block),
        grid=(width // rows,),
        in_specs=[pl.BlockSpec((rows, both), lambda i: (i, 0))],
        out_specs=pl.BlockSpec((rows, 2, both // 2), lambda i: (i, 0, 0)),
        out_shape=jax.ShapeDtypeStruct((width, 2, both // 2), F32),
        compiler_params=params(56),
        cost_estimate=cost(width * both, 6 * width * both),
        name="weave",
    )(summed)


def widen_kernel(in_ref, out_ref):
    out_ref[...] = in_ref[...].astype(F32)


def widen(summed):
    high, wide = summed.shape
    block = pl.BlockSpec((512, wide), lambda i: (i, 0))
    return pl.pallas_call(
        widen_kernel,
        grid=(high // 512,),
        in_specs=[block],
        out_specs=block,
        out_shape=jax.ShapeDtypeStruct((high, wide), F32),
        compiler_params=params(56),
        cost_estimate=cost(high * wide, 6 * high * wide),
        name="widen",
    )(summed)


def line_barrier(at, n, cube=None):
    barrier = pltpu.get_barrier_semaphore()
    if cube is not None:
        cube.signal(barrier)

    @pl.when(at > 0)
    def _():
        pl.semaphore_signal(barrier, inc=1, device_id={"tp": at - 1}, device_id_type=MESH)

    @pl.when(at < n - 1)
    def _():
        pl.semaphore_signal(barrier, inc=1, device_id={"tp": at + 1}, device_id_type=MESH)

    near = jnp.where((at > 0) & (at < n - 1), 2, 1)
    pl.semaphore_wait(barrier, near + (0 if cube is None else 3))


def sum_rows(n, sub, part_ref, out_ref, row_fn, from_left, from_right, send, recv, aside={}):
    at = lax.axis_index("tp")
    chunks = part_ref.shape[0] // sub
    middle = (n // 2 - 1, n // 2)

    def link(kind, right, src, dst, c):
        which = (kind * 2 + (1 if right else 0), c)
        return pltpu.make_async_remote_copy(
            src_ref=src.at[pl.ds(c * sub, sub)],
            dst_ref=dst.at[pl.ds(c * sub, sub)],
            send_sem=send.at[which],
            recv_sem=recv.at[which],
            device_id={"tp": at + 1 if right else at - 1},
            device_id_type=MESH,
        )

    def came(right):
        return from_left if right else from_right

    def first(right, c):
        return link(0, right, part_ref, came(right), c)

    def onward(right, c):
        return link(0, right, came(right), came(right), c)

    def hand(right, c):
        return link(1, right, out_ref, out_ref, c)

    def reduce_step(c):
        owner = middle[c % 2]
        rows = slice(c * sub, (c + 1) * sub)
        for right in (True, False):
            edge = 0 if right else n - 1
            held = came(right)

            @pl.when(((at < owner) if right else (at > owner)) & (at != edge))
            def _():
                copy = onward(right, c)
                copy.wait_recv()
                held[rows, :] = (
                    held[rows, :].astype(F32) + part_ref[rows, :].astype(F32)
                ).astype(BF16)
                copy.start()

    def final_step(c):
        owner = middle[c % 2]
        rows = slice(c * sub, (c + 1) * sub)

        @pl.when(at == owner)
        def _():
            total = part_ref[rows, :].astype(F32)
            onward(True, c).wait_recv()
            total = total + from_left[rows, :].astype(F32)
            onward(False, c).wait_recv()
            total = total + from_right[rows, :].astype(F32)
            row_fn(total, rows)
            hand(True, c).start()
            hand(False, c).start()

    def hand_step(c):
        owner = middle[c % 2]
        for right in (True, False):
            edge = n - 1 if right else 0

            @pl.when((at > owner) if right else (at < owner))
            def _():
                copy = hand(right, c)
                copy.wait_recv()

                @pl.when(at != edge)
                def _():
                    copy.start()

    for c in range(chunks):
        @pl.when(at == 0)
        def _():
            first(True, c).start()

        @pl.when(at == n - 1)
        def _():
            first(False, c).start()

    for c in range(chunks + 4):
        for piece in aside.get(c, ()):
            piece()
        if c < chunks:
            reduce_step(c)
        if 2 <= c < chunks + 2:
            final_step(c - 2)
        if c >= 4:
            hand_step(c - 4)
    for c in range(chunks):
        owner = middle[c % 2]

        @pl.when(at < owner)
        def _():
            first(True, c).wait_send()

        @pl.when(at > owner)
        def _():
            first(False, c).wait_send()

        @pl.when((at >= owner) & (at < n - 1))
        def _():
            hand(True, c).wait_send()

        @pl.when((at <= owner) & (at > 0))
        def _():
            hand(False, c).wait_send()


def merge_kernel(
    n, sub, part_ref, tok_ref, inner_ref, resid_ref, stat_ref, from_left, from_right, send, recv
):
    line_barrier(lax.axis_index("tp"), n)
    resid_ref[...] = jnp.zeros_like(resid_ref)
    stat_ref[...] = jnp.zeros_like(stat_ref)

    def row_fn(total, rows):
        x = tok_ref[rows, :].astype(F32) + total
        mean = jnp.mean(x, axis=1, keepdims=True)
        center = x - mean
        inverse = lax.rsqrt(jnp.mean(center * center, axis=1, keepdims=True) + EPS)
        resid_ref[rows, :] = x
        stat_ref[rows, :] = jnp.concatenate([mean, inverse], axis=1)
        inner_ref[rows, :] = (center * inverse).astype(BF16)

    sum_rows(n, sub, part_ref, inner_ref, row_fn, from_left, from_right, send, recv)


def merge(part, tok_full, n):
    rows, width = part.shape
    sub = 32
    vmem = pl.BlockSpec(memory_space=pltpu.VMEM)
    return pl.pallas_call(
        functools.partial(merge_kernel, n, sub),
        in_specs=[vmem] * 2,
        out_specs=[vmem] * 3,
        out_shape=[
            jax.ShapeDtypeStruct((rows, width), BF16),
            jax.ShapeDtypeStruct((rows, width), F32),
            jax.ShapeDtypeStruct((rows, 2), F32),
        ],
        scratch_shapes=[pltpu.VMEM((rows, width), BF16)] * 2
        + [pltpu.SemaphoreType.DMA((4, rows // sub))] * 2,
        compiler_params=params(56, collective_id=5, has_side_effects=True),
        cost_estimate=cost(1e6, 1e6),
        name="merge",
    )(part, tok_full)


def norm_back_kernel(n, sub, cube, part_ref, cot_ref, resid_ref, stat_ref, *refs):
    total = None
    if cube:
        own_ref, out_ref, shard_ref, from_left, from_right, send, recv, land, csend, crecv = refs
        total = CubeSum(own_ref.shape[0], csend, crecv, own=own_ref, land=land, shard=shard_ref)
    else:
        out_ref, from_left, from_right, send, recv = refs
    line_barrier(lax.axis_index("tp"), n, total)
    aside = {}
    if cube:
        total.begin()
        for k, c in enumerate((7, 8, 9, 10, 19, 20)):
            aside[c] = (functools.partial(total.reduce, k),)

    def row_fn(summed, rows):
        inverse = stat_ref[rows, 1:2]
        normed = (resid_ref[rows, :] - stat_ref[rows, 0:1]) * inverse
        mean = jnp.mean(summed, axis=1, keepdims=True)
        inner = jnp.mean(summed * normed, axis=1, keepdims=True)
        out = cot_ref[rows, :].astype(F32) + inverse * (summed - mean - normed * inner)
        out_ref[rows, :] = out.astype(BF16)

    sum_rows(n, sub, part_ref, out_ref, row_fn, from_left, from_right, send, recv, aside)
    if cube:
        total.reduce(6)
        total.reduce(7)
        total.finish()


def norm_back(part, cot, resid, stat, n, grads):
    rows, width = part.shape
    sub = 32
    vmem = pl.BlockSpec(memory_space=pltpu.VMEM)
    extra = []
    for grad in grads:
        extra += sum_scratch(grad.shape)
    return pl.pallas_call(
        functools.partial(norm_back_kernel, n, sub, len(grads) > 0),
        in_specs=[vmem] * (4 + len(grads)),
        out_specs=[vmem] * (1 + len(grads)),
        out_shape=[jax.ShapeDtypeStruct((rows, width), BF16)]
        + [jax.ShapeDtypeStruct((grad.shape[0] // 8, grad.shape[1]), BF16) for grad in grads],
        scratch_shapes=[pltpu.VMEM((rows, width), BF16)] * 2
        + [pltpu.SemaphoreType.DMA((4, rows // sub))] * 2
        + extra,
        compiler_params=params(56, collective_id=1, has_side_effects=True),
        cost_estimate=cost(1e6, 1e6),
        name="norm_back",
    )(part, cot, resid, stat, *grads)


def unrotate_kernel(
    heads, dq_ref, dk_ref, dv_ref, cos_ref, sin_ref, inner_ref, dproj_ref, grad_ref
):
    def back(ref):
        for h in range(heads):
            hs = slice(h * HD, (h + 1) * HD)
            piece = ref[:, hs]
            dproj_ref[:, hs] = (
                piece * cos_ref[...] - pltpu.roll(piece, HD // 2, 1) * sin_ref[...]
            ).astype(BF16)

    part = pl.program_id(0)

    @pl.when(part == 0)
    def _():
        back(dq_ref)

    @pl.when(part == 1)
    def _():
        back(dk_ref)

    @pl.when(part == 2)
    def _():
        dproj_ref[...] = dv_ref[...].astype(BF16)

    grad_ref[...] = lax.dot_general(
        inner_ref[...], dproj_ref[...], TN, preferred_element_type=F32
    ).astype(BF16)


def unrotate(dq, dk, dv, cosine, sine, inner, heads):
    rows, span = dq.shape
    width = inner.shape[1]
    whole = lambda n: pl.BlockSpec((rows, n), lambda i: (0, 0))
    return pl.pallas_call(
        functools.partial(unrotate_kernel, heads),
        grid=(3,),
        in_specs=[whole(span)] * 3 + [whole(HD)] * 2 + [whole(width)],
        out_specs=[
            pl.BlockSpec((rows, span), lambda i: (0, i)),
            pl.BlockSpec((width, span), lambda i: (i, 0)),
        ],
        out_shape=[
            jax.ShapeDtypeStruct((rows, 3 * span), BF16),
            jax.ShapeDtypeStruct((3 * width, span), BF16),
        ],
        compiler_params=params(56),
        cost_estimate=cost(6 * rows * span * width, 12 * rows * span + 6 * width * span),
        name="unrotate",
    )(dq, dk, dv, cosine, sine, inner)


def unproject_kernel(heads, n, cube, dproj_ref, tok_ref, stat_ref, w_ref, branch_ref, *refs):
    sums, rest = [], None
    if cube:
        in_ref, og_ref, shard_ref, out_ref, in_out, og_out, down_out = refs[:7]
        part_ref, mine_ref, land_ref, sums_ref, far_ref, send, recv, ssend, srecv = refs[7:16]
        for own, out, at in ((in_ref, in_out, 16), (og_ref, og_out, 19)):
            land, csend, crecv = refs[at : at + 3]
            sums.append(CubeSum(own.shape[0], csend, crecv, own=own, land=land, out=out))
        rest = CubeSum(
            down_out.shape[0], refs[22], refs[23], out=down_out, shard=shard_ref, local=refs[24]
        )
    else:
        out_ref, part_ref, mine_ref, land_ref, sums_ref, far_ref, send, recv, ssend, srecv = refs

    def reduce(*pieces):
        for k in pieces:
            for item in sums:
                item.reduce(k)

    def gather(k):
        for item in sums:
            item.gather(k)

    def rest_gather(k):
        if rest is not None:
            rest.gather(k)

    rows, width = tok_ref.shape
    shard = width // n
    span = heads * HD
    at = lax.axis_index("tp")
    barrier = pltpu.get_barrier_semaphore()
    for o in range(1, n):
        pl.semaphore_signal(
            barrier, inc=1, device_id={"tp": lax.rem(at + o, n)}, device_id_type=MESH
        )
    if cube:
        sums[0].signal(barrier)
    pl.semaphore_wait(barrier, n - 1 + (3 if cube else 0))
    for item in sums:
        item.begin()
    rest_gather(0)
    block = 256
    count = rows // block

    def term(o, i):
        target = lax.rem(at + o, n)
        place = pl.ds(i * block, block)
        return pltpu.make_async_remote_copy(
            src_ref=part_ref.at[place, pl.ds(pl.multiple_of(target * shard, 128), shard)],
            dst_ref=land_ref.at[o - 1, place],
            send_sem=send.at[o - 1, i], recv_sem=recv.at[o - 1, i],
            device_id={"tp": target}, device_id_type=MESH,
        )

    def totals(o):
        return pltpu.make_async_remote_copy(
            src_ref=sums_ref, dst_ref=far_ref.at[o - 1],
            send_sem=ssend.at[o - 1], recv_sem=srecv.at[o - 1],
            device_id={"tp": lax.rem(at + o, n)}, device_id_type=MESH,
        )

    own = pl.ds(pl.multiple_of(at * shard, 128), shard)
    for i in range(count):
        place = pl.ds(i * block, block)
        total = None
        for part in range(3):
            piece = lax.dot_general(
                dproj_ref[place, part * span : (part + 1) * span], w_ref[part], NT,
                preferred_element_type=F32,
            )
            total = piece if total is None else total + piece
        part_ref[place, :] = total.astype(BF16)
        for o in range(1, n):
            term(o, i).start()
        normed = (tok_ref[place, :].astype(F32) - stat_ref[place, 0:1]) * stat_ref[place, 1:2]
        first = jnp.sum(total, axis=1, keepdims=True)
        second = jnp.sum(total * normed, axis=1, keepdims=True)
        lane = lax.broadcasted_iota(jnp.int32, (block, HD), 1)
        both = jnp.where(lane == 0, first, jnp.where(lane == 1, second, 0.0))
        sums_ref[:, i * block : (i + 1) * block] = both.T[:8]
    for o in range(1, n):
        totals(o).start()
    reduce(0, 1, 2, 3)
    rest_gather(1)
    reduce(4, 5)
    rest_gather(2)
    reduce(6, 7)
    gather(0)
    gather(1)
    total = sums_ref[...]
    for o in range(1, n):
        totals(o).wait_recv()
        total = total + far_ref[o - 1]
    mine_ref[...] = total
    gather(2)
    for i in range(count):
        place = pl.ds(i * block, block)
        spread = jnp.concatenate(
            [mine_ref[:, i * block : (i + 1) * block], jnp.zeros((HD - 8, block), F32)], axis=0
        ).T / width
        total = part_ref[place, own].astype(F32)
        for o in range(1, n):
            term(o, i).wait_recv()
            total = total + land_ref[o - 1, place].astype(F32)
        inverse = stat_ref[place, 1:2]
        normed = (tok_ref[place, own].astype(F32) - stat_ref[place, 0:1]) * inverse
        out_ref[place, :] = branch_ref[place, own].astype(F32) + inverse * (
            total - spread[:, 0:1] - normed * spread[:, 1:2]
        )
    rest_gather(3)
    gather(3)
    for item in sums + ([rest] if cube else []):
        item.finish()
    for o in range(1, n):
        totals(o).wait_send()
        for i in range(count):
            term(o, i).wait_send()


def unproject(dproj, tok_full, stat, weight, branch, heads, n, grads, shards):
    rows, width = tok_full.shape
    shard = width // n
    vmem = pl.BlockSpec(memory_space=pltpu.VMEM)
    extra = []
    for grad in grads:
        extra += sum_scratch(grad.shape)
    for _ in shards:
        extra += [pltpu.SemaphoreType.DMA((SUM_SENDS,))] * 2 + [pltpu.SemaphoreType.DMA((2,))]
    return pl.pallas_call(
        functools.partial(unproject_kernel, heads, n, len(grads) > 0),
        in_specs=[vmem] * (5 + len(grads) + len(shards)),
        out_specs=[vmem] * (1 + len(grads)) + [pl.BlockSpec(memory_space=pl.ANY)] * len(shards),
        out_shape=[jax.ShapeDtypeStruct((rows, shard), F32)]
        + [jax.ShapeDtypeStruct(grad.shape, BF16) for grad in grads]
        + [jax.ShapeDtypeStruct((8 * piece.shape[0], piece.shape[1]), BF16) for piece in shards],
        scratch_shapes=[
            pltpu.VMEM((rows, width), BF16),
            pltpu.VMEM((8, rows), F32),
            pltpu.VMEM((n - 1, rows, shard), BF16),
            pltpu.VMEM((8, rows), F32),
            pltpu.VMEM((n - 1, 8, rows), F32),
            pltpu.SemaphoreType.DMA((n - 1, rows // 256)),
            pltpu.SemaphoreType.DMA((n - 1, rows // 256)),
            pltpu.SemaphoreType.DMA((n - 1,)),
            pltpu.SemaphoreType.DMA((n - 1,)),
        ]
        + extra,
        compiler_params=params(60, collective_id=4, has_side_effects=True),
        cost_estimate=cost(1e6, 1e6),
        name="unproject",
    )(dproj, tok_full, stat, weight, branch, *grads, *shards)


def per_device(tokens, segment_ids, in_weight, out_weight, gate_up_weight, down_weight, cotangent):
    rows = tokens.shape[0]
    width = in_weight.shape[0]
    span = in_weight.shape[2]
    heads = span // HD
    hidden_local = down_weight.shape[0]
    me = lax.axis_index("ctx")
    tp_size = lax.axis_size("tp")
    cube = lax.axis_size("ctx") == CUBE

    def gather(local, axis=1):
        return lax.all_gather(local, "tp", axis=axis, tiled=True)

    places = me * rows + jnp.arange(rows, dtype=jnp.int32)
    cosine, sine = rope_tables(places)
    in_w = jnp.transpose(in_weight, (1, 0, 2))
    gu_w = jnp.transpose(
        gate_up_weight.reshape(width, 2, hidden_local // BLOCK, BLOCK), (0, 2, 1, 3)
    )
    gu_w = gu_w.reshape(width, 2 * hidden_local)

    all_seg = lax.all_gather(segment_ids, "ctx", axis=0, tiled=True)
    count = all_seg.shape[0]
    every = jnp.arange(count, dtype=jnp.int32)
    opens = jnp.concatenate([jnp.ones((1,), jnp.bool_), all_seg[1:] != all_seg[:-1]])
    all_begin = lax.cummax(jnp.where(opens, every, 0))
    blocks = all_begin.reshape(count // rows, rows)

    tok_full, gu_w, blocks, all_begin = lax.optimization_barrier(
        (gather(tokens), gu_w, blocks, all_begin)
    )
    key_info = jnp.stack(
        [me, blocks[me, 0] // rows, (blocks[me, rows - 1] + rows - 1) // rows]
    ).astype(jnp.int32)
    query_info = jnp.stack(
        [
            me,
            jnp.sum((blocks[:, 0] < (me + 1) * rows).astype(jnp.int32)) - 1,
            jnp.sum((blocks[:, rows - 1] <= me * rows).astype(jnp.int32)) - 1,
        ]
    ).astype(jnp.int32)
    begin = lax.dynamic_slice_in_dim(blocks, me, 1, 0)
    all_begin = all_begin[None, :]
    inner1, stat1, query, pairs = project(tok_full, in_w, cosine, sine, heads)
    if cube:
        raw, mixed, lse, all_pairs, cot_full, out_part = attend_far(
            query, pairs, begin, cotangent, out_weight, heads, tp_size
        )
    else:
        all_pairs = lax.all_gather(pairs, "ctx", axis=0, tiled=True)
        cot_full = gather(cotangent)
        raw, mixed, lse = attend(key_info, query, all_pairs, begin, heads)
        out_part = jnp.dot(mixed, out_weight, preferred_element_type=F32).astype(BF16)
    late_query, mixed = lax.optimization_barrier((query, mixed))
    all_query = lax.all_gather(late_query, "ctx", axis=0, tiled=True)
    inner2, resid1, stat2 = merge(out_part, tok_full, tp_size)

    hidden, grad_gu, down_grad, gu_grad = feed(inner2, cot_full, gu_w, down_weight, BLOCK)
    down_grad, gu_grad, all_query, grad_gu, hidden = lax.optimization_barrier(
        (down_grad, gu_grad, all_query, grad_gu, hidden)
    )
    if not cube:
        down_grad = lax.psum(down_grad, "ctx")
    gu_grad = lax.optimization_barrier(lax.psum(gu_grad, "ctx"))

    grad_part = lax.dot_general(grad_gu, gu_w, NT, preferred_element_type=F32).astype(BF16)
    branch_grad, *shards = norm_back(
        grad_part, cot_full, resid1, stat2, tp_size, [down_grad] if cube else []
    )
    out_grad = lax.dot_general(mixed, branch_grad, TN, preferred_element_type=F32).astype(BF16)
    grad_mixed, delta = mixed_grad(branch_grad, out_weight, raw, lse, heads)
    branch = (resid1 + jnp.dot(hidden, down_weight, preferred_element_type=F32)).astype(BF16)
    if cube:
        dq, dk, dv, layer_out = attend_back_far(
            grad_mixed, all_query, all_pairs, blocks, branch, heads, tp_size
        )
    else:
        branch = lax.psum_scatter(branch, "tp", scatter_dimension=1, tiled=True)
        layer_out = branch
        all_grad = lax.all_gather(grad_mixed, "ctx", axis=0, tiled=True)
        dq = query_grad(key_info, query, grad_mixed, lse, delta, all_pairs, begin, heads)
        dk, dv = key_grad(query_info, pairs, all_query, all_grad, all_begin, heads)

    dproj, in_grad = unrotate(dq, dk, dv, cosine, sine, inner1, heads)
    if cube:
        tokens_grad, in_grad, out_grad, down_grad = unproject(
            dproj, tok_full, stat1, in_w, branch_grad, heads, tp_size,
            [in_grad, out_grad], shards,
        )
    else:
        in_grad, out_grad, down_grad, gu_grad = lax.optimization_barrier(
            (in_grad, out_grad, down_grad, gu_grad)
        )
        in_grad, out_grad = lax.psum((in_grad, out_grad), "ctx")
        (tokens_grad,) = unproject(
            dproj, tok_full, stat1, in_w, branch_grad, heads, tp_size, [], []
        )
    return (
        layer_out,
        tokens_grad,
        jnp.transpose(widen(in_grad).reshape(3, width, span), (1, 0, 2)),
        out_grad.astype(F32),
        weave(gu_grad, BLOCK),
        widen(down_grad),
    )


def solution(mesh):
    placed = (
        P("ctx", "tp"),
        P("ctx"),
        P(None, None, "tp"),
        P("tp", None),
        P(None, None, "tp"),
        P("tp", None),
        P("ctx", "tp"),
    )
    return jax.shard_map(
        per_device,
        mesh=mesh,
        in_specs=placed,
        out_specs=(
            P("ctx", "tp"),
            P("ctx", "tp"),
            P(None, None, "tp"),
            P("tp", None),
            P(None, None, "tp"),
            P("tp", None),
        ),
        check_vma=False,
    )
```

```python
import functools

import jax
import jax.numpy as jnp
from jax import lax
from jax.experimental import pallas as pl
from jax.experimental.pallas import tpu as pltpu
from jax.sharding import PartitionSpec as P

HD = 128
EPS = 1e-05
NEG = -1e30
SCALE = HD ** (-0.5)
LOG2E = 1.4426950408889634
C2 = SCALE * LOG2E
F32 = jnp.float32
BF16 = jnp.bfloat16
NT = (((1,), (1,)), ((), ()))
TN = (((0,), (0,)), ((), ()))
MESH = pl.DeviceIdType.MESH
BLOCK = 512


def params(mib, **more):
    return pltpu.CompilerParams(vmem_limit_bytes=mib << 20, **more)


def cost(flops, nbytes, trans=0):
    return pl.CostEstimate(flops=int(flops), bytes_accessed=int(nbytes), transcendentals=int(trans))


def rope_tables(places):
    half = HD // 2
    freq = 10000.0 ** (-jnp.arange(half, dtype=F32) * 2.0 / HD)
    angle = places.astype(F32)[:, None] * freq[None, :]
    cosine, sine = jnp.cos(angle), jnp.sin(angle)
    return jnp.concatenate([cosine, cosine], axis=1), jnp.concatenate([-sine, sine], axis=1)


def project_kernel(heads, tok_ref, w_ref, cos_ref, sin_ref, inner_ref, stat_ref, q_ref, kv_ref):
    x = tok_ref[...].astype(F32)
    center = x - jnp.mean(x, axis=1, keepdims=True)
    inverse = lax.rsqrt(jnp.mean(center * center, axis=1, keepdims=True) + EPS)
    inner = (center * inverse).astype(BF16)
    inner_ref[...] = inner
    stat_ref[...] = jnp.concatenate(
        [jnp.mean(x, axis=1, keepdims=True), inverse], axis=1
    )
    cosine, sine = cos_ref[...], sin_ref[...]
    span = heads * HD
    for part in range(3):
        out = jnp.dot(inner, w_ref[part], preferred_element_type=F32)
        if part == 2:
            kv_ref[:, span:] = out.astype(BF16)
            continue
        for h in range(heads):
            piece = out[:, h * HD : (h + 1) * HD]
            turned = (piece * cosine + pltpu.roll(piece, HD // 2, 1) * sine).astype(BF16)
            if part == 0:
                q_ref[:, h * HD : (h + 1) * HD] = turned
            else:
                kv_ref[:, h * HD : (h + 1) * HD] = turned


def project(tok_full, weight, cosine, sine, heads):
    rows, width = tok_full.shape
    span = heads * HD
    block = 256
    row = lambda n: pl.BlockSpec((block, n), lambda i: (i, 0))
    return pl.pallas_call(
        functools.partial(project_kernel, heads),
        grid=(rows // block,),
        in_specs=[
            row(width),
            pl.BlockSpec((3, width, span), lambda i: (0, 0, 0)),
            row(HD),
            row(HD),
        ],
        out_specs=[row(width), row(2), row(span), row(2 * span)],
        out_shape=[
            jax.ShapeDtypeStruct((rows, width), BF16),
            jax.ShapeDtypeStruct((rows, 2), F32),
            jax.ShapeDtypeStruct((rows, span), BF16),
            jax.ShapeDtypeStruct((rows, 2 * span), BF16),
        ],
        compiler_params=params(56),
        cost_estimate=cost(6 * rows * width * span, 6 * width * span + 6 * rows * width),
        name="project",
    )(tok_full, weight, cosine, sine)


def masked(scores, j, me, rows, begin):
    key_place = lax.broadcasted_iota(jnp.int32, scores.shape, 0) + j * rows
    query_place = lax.broadcasted_iota(jnp.int32, scores.shape, 1) + me * rows
    return jnp.where((key_place <= query_place) & (key_place >= begin), scores, NEG)


def attend_kernel(
    heads, info, q_ref, k_ref, v_ref, begin_ref, raw_ref, mixed_ref, lse_ref,
    high_ref, total_ref, acc_ref, s_ref,
):
    me, first, clear = info[0], info[1], info[2]
    j = pl.program_id(0)
    rows = q_ref.shape[0]

    @pl.when(j == 0)
    def _():
        high_ref[...] = jnp.full_like(high_ref, NEG)
        total_ref[...] = jnp.zeros_like(total_ref)
        acc_ref[...] = jnp.zeros_like(acc_ref)

    def block(hide):
        def score(h):
            hs = slice(h * HD, (h + 1) * HD)
            s = lax.dot_general(k_ref[:, hs], q_ref[:, hs], NT, preferred_element_type=F32)
            if hide:
                s = masked(s, j, me, rows, begin_ref[...])
            s_ref[h % 2] = s

        def spread(h):
            hs = slice(h * HD, (h + 1) * HD)
            s = s_ref[h % 2]
            old = high_ref[h : h + 1, :]
            new = jnp.maximum(old, jnp.max(s, axis=0, keepdims=True))
            high_ref[h : h + 1, :] = new
            p = jnp.exp2(s * C2 - new * C2)
            decay = jnp.exp2((old - new) * C2)
            total_ref[h : h + 1, :] = total_ref[h : h + 1, :] * decay + jnp.sum(
                p, axis=0, keepdims=True
            )
            acc_ref[h] = acc_ref[h] * decay + lax.dot_general(
                v_ref[:, hs], p.astype(BF16), TN, preferred_element_type=F32
            )

        score(0)
        for h in range(heads):
            if h + 1 < heads:
                score(h + 1)
            spread(h)

    @pl.when((j >= clear) & (j < me))
    def _():
        block(False)

    @pl.when(((j >= first) & (j < clear) & (j < me)) | (j == me))
    def _():
        block(True)

    @pl.when(j == me)
    def _():
        for h in range(heads):
            hs = slice(h * HD, (h + 1) * HD)
            out = (acc_ref[h] / total_ref[h : h + 1, :]).T
            raw_ref[:, hs] = out
            mixed_ref[:, hs] = out.astype(BF16)
        lse_ref[...] = high_ref[...] * C2 + jnp.log2(total_ref[...])


def attend(info, query, pairs, begin, heads):
    rows = query.shape[0]
    total = pairs.shape[0]
    span = heads * HD
    full = lambda shape: pl.BlockSpec(shape, lambda j, s: (0, 0))
    key = pl.BlockSpec((rows, span), lambda j, s: (jnp.clip(j, s[1], s[0]), 0))
    value = pl.BlockSpec((rows, span), lambda j, s: (jnp.clip(j, s[1], s[0]), 1))
    return pl.pallas_call(
        functools.partial(attend_kernel, heads),
        grid_spec=pltpu.PrefetchScalarGridSpec(
            num_scalar_prefetch=1,
            grid=(total // rows,),
            in_specs=[full((rows, span)), key, value, full((1, rows))],
            out_specs=[full((rows, span)), full((rows, span)), full((heads, rows))],
            scratch_shapes=[
                pltpu.VMEM((heads, rows), F32),
                pltpu.VMEM((heads, rows), F32),
                pltpu.VMEM((heads, HD, rows), F32),
                pltpu.VMEM((2, rows, rows), F32),
            ],
        ),
        out_shape=[
            jax.ShapeDtypeStruct((rows, span), F32),
            jax.ShapeDtypeStruct((rows, span), BF16),
            jax.ShapeDtypeStruct((heads, rows), F32),
        ],
        compiler_params=params(56),
        cost_estimate=cost(4 * rows * total * span, 4 * total * span, rows * total * heads),
        name="attend",
    )(info, query, pairs, pairs, begin)


CUBE = 8
CUBE_SENDS = 10


class Cube:
    def __init__(self, buf, send, recv):
        me = lax.axis_index("ctx")
        flip = (1 - 2 * (me % 2), 2 - 4 * ((me // 2) % 2), 4 - 8 * (me // 4))
        self.me, self.flip, self.buf, self.send, self.recv = me, flip, buf, send, recv
        self.rows = buf.shape[0] // CUBE

    def copy(self, n):
        core, x, y = self.flip
        half = self.rows // 2
        block, part, target = (
            (0, None, core),
            (0, 0, x), (0, 1, x), (0, 1, y), (0, 0, y),
            (x, 0, y), (y, 1, x),
            (x, None, core), (y, None, core), (x + y, None, core),
        )[n]
        start = (self.me + block) * self.rows
        size = self.rows
        if part is not None:
            start, size = start + part * half, half
        place = self.buf.at[pl.ds(pl.multiple_of(start, 16), size)]
        return pltpu.make_async_remote_copy(
            src_ref=place, dst_ref=place, send_sem=self.send.at[n], recv_sem=self.recv.at[n],
            device_id={"ctx": self.me + target}, device_id_type=MESH,
        )

    def arrived(self, n):
        self.copy(n).wait_recv()

    def start(self, *which):
        for n in which:
            self.copy(n).start()

    def signal(self, barrier):
        for target in self.flip:
            pl.semaphore_signal(
                barrier, inc=1, device_id={"ctx": self.me + target}, device_id_type=MESH
            )

    def block(self, step):
        core, x, y = self.flip
        on = lambda *steps: sum((step == n).astype(jnp.int32) for n in steps)
        return self.me + on(1, 4, 5, 7) * core + on(2, 4, 6, 7) * x + on(3, 5, 6, 7) * y

    def advance(self, step):
        @pl.when(step == 0)
        def _():
            self.start(0, 1, 3, 2, 4)

        @pl.when(step == 1)
        def _():
            self.arrived(0)

        @pl.when(step == 2)
        def _():
            self.arrived(1)
            self.start(5)
            self.arrived(3)
            self.start(6)
            self.arrived(2)
            self.start(7)

        @pl.when(step == 3)
        def _():
            self.arrived(4)
            self.start(8)

        @pl.when(step == 4)
        def _():
            self.arrived(7)

        @pl.when(step == 5)
        def _():
            self.arrived(8)

        @pl.when(step == 6)
        def _():
            self.arrived(5)
            self.arrived(6)
            self.start(9)

        @pl.when(step == 7)
        def _():
            self.arrived(9)

    def finish(self):
        for n in range(CUBE_SENDS):
            self.copy(n).wait_send()


SUM_SENDS = 9


class CubeSum:
    def __init__(self, own, land, send, recv, out=None, mid=None):
        me = lax.axis_index("ctx")
        core, x, y = me % 2, (me // 2) % 2, me // 4
        self.me, self.own, self.out, self.land, self.mid = me, own, out, land, mid
        self.send, self.recv = send, recv
        rows = own.shape[0]
        self.half, self.eighth, self.last = rows // 2, rows // 8, rows // 16
        second = rows // 4
        self.to = (1 - 2 * core, 2 - 4 * x, 4 - 8 * y)
        self.mine, self.other = core * self.half, (1 - core) * self.half
        self.keep1 = (x * self.eighth, second + y * self.eighth)
        self.give1 = ((1 - x) * self.eighth, second + (1 - y) * self.eighth)
        self.keep2 = (self.keep1[0] + y * self.last, self.keep1[1] + x * self.last)
        self.give2 = (self.keep1[0] + (1 - y) * self.last, self.keep1[1] + (1 - x) * self.last)

    def copy(self, n):
        core, x, y = self.to
        half, eighth, last, out, land = self.half, self.eighth, self.last, self.out, self.land
        source, start, size, target = (
            (self.own, self.other, half, core),
            (land, self.give1[0], eighth, x), (land, self.give1[1], eighth, y),
            (land, self.give2[0], last, y), (land, self.give2[1], last, x),
            (out, self.keep2[0], last, y), (out, self.keep2[1], last, x),
            (out, self.keep1[0], eighth, x), (out, self.keep1[1], eighth, y),
        )[n]
        src = source.at[pl.ds(pl.multiple_of(start, 16), size)]
        if n < 5:
            landing = (0, half, half + eighth, half + 2 * eighth, half + 2 * eighth + last)[n]
            dst = land.at[pl.ds(landing, size)]
        else:
            dst = src
        return pltpu.make_async_remote_copy(
            src_ref=src, dst_ref=dst, send_sem=self.send.at[n], recv_sem=self.recv.at[n],
            device_id={"ctx": self.me + target}, device_id_type=MESH,
        )

    def add(self, target, to, source, at, landed, size):
        step = size
        while step * self.own.shape[1] > 256 * 1024 and step % 32 == 0:
            step = step // 2

        def part(i, carry):
            def rows(begin):
                return pl.ds(pl.multiple_of(begin + i * step, 16), step)

            total = source[rows(at), :].astype(F32) + self.land[rows(landed), :].astype(F32)
            target[rows(to), :] = total.astype(BF16)
            return carry

        lax.fori_loop(0, size // step, part, 0)

    def begin(self):
        self.copy(0).start()

    def reduce(self, k):
        half, eighth, last, land = self.half, self.eighth, self.last, self.land
        i = k % 2
        if k == 0:
            self.copy(0).wait_recv()
        if k < 2:
            at = self.give1[i]
            self.add(land, at, self.own, self.mine + at, at, eighth)
            self.copy(1 + i).start()
        elif k < 4:
            at = self.keep1[i]
            self.add(land, at, self.own, self.mine + at, at, eighth)
        elif k < 6:
            self.copy(1 + i).wait_recv()
            landed = half + i * eighth - self.keep1[i]
            if self.out is None:
                at = self.keep1[i]
                self.add(self.mid, i * eighth, land, at, landed + at, eighth)
                return
            at = self.give2[i]
            self.add(land, at, land, at, landed + at, last)
            self.copy(3 + i).start()
            at = self.keep2[i]
            self.add(land, at, land, at, landed + at, last)
        else:
            self.copy(3 + i).wait_recv()
            at = self.keep2[i]
            self.add(self.out, at, land, at, half + 2 * eighth + i * last, last)

    def gather(self, k):
        for i in range(2):
            if k == 0:
                self.copy(5 + i).start()
            if k == 1:
                self.copy(5 + i).wait_recv()
                self.copy(7 + i).start()
            if k == 2:
                self.copy(7 + i).wait_recv()

    def finish(self):
        for n in range(3 if self.out is None else SUM_SENDS):
            self.copy(n).wait_send()

    def signal(self, barrier):
        for target in self.to:
            pl.semaphore_signal(
                barrier, inc=1, device_id={"ctx": self.me + target}, device_id_type=MESH
            )


class MidSum:
    def __init__(self, mid, land, out, send, recv):
        me = lax.axis_index("ctx")
        x, y = (me // 2) % 2, me // 4
        self.me, self.mid, self.land, self.out, self.send, self.recv = me, mid, land, out, send, recv
        self.eighth, self.last = mid.shape[0] // 2, mid.shape[0] // 4
        self.bit = (y, x)
        self.to = (4 - 8 * y, 2 - 4 * x)

    def copy(self, n):
        i = n % 2
        keep = i * self.eighth + self.bit[i] * self.last
        give = i * self.eighth + (1 - self.bit[i]) * self.last
        if n < 2:
            src = self.mid.at[pl.ds(pl.multiple_of(give, 16), self.last)]
            dst = self.land.at[pl.ds(i * self.last, self.last)]
        else:
            src = dst = self.out.at[pl.ds(pl.multiple_of(keep, 16), self.last)]
        return pltpu.make_async_remote_copy(
            src_ref=src, dst_ref=dst, send_sem=self.send.at[n], recv_sem=self.recv.at[n],
            device_id={"ctx": self.me + self.to[i]}, device_id_type=MESH,
        )

    def begin(self):
        for i in range(2):
            self.copy(i).start()

    def turn(self):
        for i in range(2):
            self.copy(i).wait_recv()
            keep = i * self.eighth + self.bit[i] * self.last
            rows = pl.ds(pl.multiple_of(keep, 16), self.last)
            landed = self.land[i * self.last : (i + 1) * self.last, :]
            self.out[rows, :] = (
                self.mid[rows, :].astype(F32) + landed.astype(F32)
            ).astype(BF16)
            self.copy(2 + i).start()

    def finish(self):
        for i in range(2):
            self.copy(2 + i).wait_recv()
        for n in range(4):
            self.copy(n).wait_send()


class LastGather:
    def __init__(self, mid, out, send, recv, local):
        me = lax.axis_index("ctx")
        x, y = (me // 2) % 2, me // 4
        self.me, self.mid, self.out = me, mid, out
        self.send, self.recv, self.local = send, recv, local
        self.eighth = mid.shape[0] // 2
        self.start_at = (x * self.eighth, (2 + y) * self.eighth)
        self.to = (2 - 4 * x, 4 - 8 * y)

    def ends(self, i):
        src = self.mid.at[pl.ds(i * self.eighth, self.eighth)]
        return src, self.out.at[pl.ds(pl.multiple_of(self.start_at[i], 16), self.eighth)]

    def copy(self, i):
        src, dst = self.ends(i)
        return pltpu.make_async_remote_copy(
            src_ref=src, dst_ref=dst, send_sem=self.send.at[i], recv_sem=self.recv.at[i],
            device_id={"ctx": self.me + self.to[i]}, device_id_type=MESH,
        )

    def keep(self, i):
        src, dst = self.ends(i)
        return pltpu.make_async_copy(src, dst, self.local.at[i])

    def begin(self):
        for i in range(2):
            self.copy(i).start()
            self.keep(i).start()

    def finish(self):
        for i in range(2):
            self.copy(i).wait()
            self.keep(i).wait()


def sum_scratch(shape):
    return [
        pltpu.VMEM((shape[0] // 2 + 3 * (shape[0] // 8), shape[1]), BF16),
        pltpu.SemaphoreType.DMA((SUM_SENDS,)),
        pltpu.SemaphoreType.DMA((SUM_SENDS,)),
    ]


def join_kernel(core_ref, own_ref, far_ref, out_ref):
    @pl.when(pl.program_id(0) == 0)
    def _():
        out_ref[...] = own_ref[...].astype(F32)

    @pl.when(pl.program_id(0) == 1)
    def _():
        out_ref[...] = far_ref[...].astype(F32)


def join(core, own, far):
    high, wide = own.shape
    rows = high
    while rows * wide > 1024 * 1024:
        rows = rows // 2
    count = high // rows
    return pl.pallas_call(
        join_kernel,
        grid_spec=pltpu.PrefetchScalarGridSpec(
            num_scalar_prefetch=1,
            grid=(2, count),
            in_specs=[
                pl.BlockSpec((rows, wide), lambda h, b, s: (jnp.where(h == 0, b, count - 1), 0)),
                pl.BlockSpec((rows, wide), lambda h, b, s: (jnp.where(h == 0, 0, b), 0)),
            ],
            out_specs=pl.BlockSpec(
                (rows, wide), lambda h, b, s: (jnp.where(h == 0, s[0], 1 - s[0]) * count + b, 0)
            ),
        ),
        out_shape=jax.ShapeDtypeStruct((2 * high, wide), F32),
        compiler_params=params(56),
        cost_estimate=cost(2 * high * wide, 12 * high * wide),
        name="join",
    )(core, own, far)


def hidden_scores(scores, key_block, query_block, rows, begin):
    key_place = lax.broadcasted_iota(jnp.int32, scores.shape, 0) + key_block * rows
    query_place = lax.broadcasted_iota(jnp.int32, scores.shape, 1) + query_block * rows
    return jnp.where((key_place <= query_place) & (key_place >= begin), scores, NEG)


def attend_far_kernel(
    heads, n, q_ref, own_ref, begin_ref, cot_ref, w_ref,
    raw_ref, mixed_ref, lse_ref, keep_ref, full_ref, part_ref,
    pair_ref, high_ref, total_ref, acc_ref, s_ref, send, recv, zsend, zrecv, keep_sem,
):
    rows = q_ref.shape[0]
    span = heads * HD
    shard = cot_ref.shape[1]
    at = lax.axis_index("tp")
    cube = Cube(pair_ref, send, recv)
    me = cube.me
    barrier = pltpu.get_barrier_semaphore()
    cube.signal(barrier)

    @pl.when(at > 0)
    def _():
        pl.semaphore_signal(barrier, inc=1, device_id={"tp": at - 1}, device_id_type=MESH)

    @pl.when(at < n - 1)
    def _():
        pl.semaphore_signal(barrier, inc=1, device_id={"tp": at + 1}, device_id_type=MESH)

    pair_ref[pl.ds(pl.multiple_of(me * rows, 16), rows), :] = own_ref[...]
    full_ref[:, pl.ds(pl.multiple_of(at * shard, 128), shard)] = cot_ref[...]
    high_ref[...] = jnp.full_like(high_ref, NEG)
    total_ref[...] = jnp.zeros_like(total_ref)
    acc_ref[...] = jnp.zeros_like(acc_ref)
    pl.semaphore_wait(barrier, jnp.where((at > 0) & (at < n - 1), 5, 4))

    def pass_on(right, s, k):
        place = full_ref.at[:, pl.ds(pl.multiple_of(s * shard, 128), shard)]
        which = (1 if right else 0, k)
        return pltpu.make_async_remote_copy(
            src_ref=place, dst_ref=place, send_sem=zsend.at[which], recv_sem=zrecv.at[which],
            device_id={"tp": at + 1 if right else at - 1}, device_id_type=MESH,
        )

    def line_step(k):
        @pl.when(at >= k)
        def _():
            if k > 0:
                pass_on(True, at - k, k - 1).wait_recv()

            @pl.when(at < n - 1)
            def _():
                pass_on(True, at - k, k).start()

        @pl.when(at + k < n)
        def _():
            if k > 0:
                pass_on(False, at + k, k - 1).wait_recv()

            @pl.when(at > 0)
            def _():
                pass_on(False, at + k, k).start()

    def keep(step):
        place = pl.ds(pl.multiple_of(cube.block(step) * rows, 16), rows)
        return pltpu.make_async_copy(pair_ref.at[place], keep_ref.at[place], keep_sem.at[step])

    def turn(step, carry):
        cube.advance(step)
        keep(step).start()
        for k in range(n):
            @pl.when(step == min(k * 2, CUBE - 1 - (n - 1 - k)) if n <= CUBE else k)
            def _():
                line_step(k)
        block = cube.block(step)

        @pl.when(block <= me)
        def _():
            place = pl.ds(pl.multiple_of(block * rows, 16), rows)

            def score(h):
                hs = slice(h * HD, (h + 1) * HD)
                s = lax.dot_general(
                    pair_ref[place, hs], q_ref[:, hs], NT, preferred_element_type=F32
                )
                s_ref[h % 2] = hidden_scores(s, block, me, rows, begin_ref[...])

            def spread(h):
                s = s_ref[h % 2]
                old = high_ref[h : h + 1, :]
                new = jnp.maximum(old, jnp.max(s, axis=0, keepdims=True))
                high_ref[h : h + 1, :] = new
                p = jnp.exp2(s * C2 - new * C2)
                decay = jnp.exp2((old - new) * C2)
                total_ref[h : h + 1, :] = total_ref[h : h + 1, :] * decay + jnp.sum(
                    p, axis=0, keepdims=True
                )
                acc_ref[h] = acc_ref[h] * decay + lax.dot_general(
                    pair_ref[place, span + h * HD : span + (h + 1) * HD], p.astype(BF16), TN,
                    preferred_element_type=F32,
                )

            score(0)
            for h in range(heads):
                if h + 1 < heads:
                    score(h + 1)
                spread(h)

        return carry

    lax.fori_loop(0, CUBE, turn, 0)
    for h in range(heads):
        hs = slice(h * HD, (h + 1) * HD)
        out = (acc_ref[h] / total_ref[h : h + 1, :]).T
        raw_ref[:, hs] = out
        mixed_ref[:, hs] = out.astype(BF16)
    part_ref[...] = jnp.dot(
        mixed_ref[...], w_ref[...], preferred_element_type=F32
    ).astype(BF16)
    lse_ref[...] = high_ref[...] * C2 + jnp.log2(total_ref[...])

    def kept(step, carry):
        keep(step).wait()
        return carry

    lax.fori_loop(0, CUBE, kept, 0)
    cube.finish()
    for k in range(n):
        @pl.when((at >= k) & (at < n - 1))
        def _():
            pass_on(True, at - k, k).wait_send()

        @pl.when((at + k < n) & (at > 0))
        def _():
            pass_on(False, at + k, k).wait_send()


def attend_far(query, pairs, begin, cot, weight, heads, n):
    rows = query.shape[0]
    width = weight.shape[1]
    span = heads * HD
    vmem = pl.BlockSpec(memory_space=pltpu.VMEM)
    return pl.pallas_call(
        functools.partial(attend_far_kernel, heads, n),
        in_specs=[vmem] * 5,
        out_specs=[vmem] * 3 + [pl.BlockSpec(memory_space=pl.ANY)] + [vmem] * 2,
        out_shape=[
            jax.ShapeDtypeStruct((rows, span), F32),
            jax.ShapeDtypeStruct((rows, span), BF16),
            jax.ShapeDtypeStruct((heads, rows), F32),
            jax.ShapeDtypeStruct((CUBE * rows, 2 * span), BF16),
            jax.ShapeDtypeStruct((rows, n * cot.shape[1]), BF16),
            jax.ShapeDtypeStruct((rows, width), BF16),
        ],
        scratch_shapes=[
            pltpu.VMEM((CUBE * rows, 2 * span), BF16),
            pltpu.VMEM((heads, rows), F32),
            pltpu.VMEM((heads, rows), F32),
            pltpu.VMEM((heads, HD, rows), F32),
            pltpu.VMEM((2, rows, rows), F32),
            pltpu.SemaphoreType.DMA((CUBE_SENDS,)),
            pltpu.SemaphoreType.DMA((CUBE_SENDS,)),
            pltpu.SemaphoreType.DMA((2, n)),
            pltpu.SemaphoreType.DMA((2, n)),
            pltpu.SemaphoreType.DMA((CUBE,)),
        ],
        compiler_params=params(58, collective_id=2, has_side_effects=True),
        cost_estimate=cost(1e6, 1e6),
        name="attend_far",
    )(query, pairs, begin, cot, weight)


def attend_back_far_kernel(
    heads, n, g_ref, far_q_ref, far_pair_ref, begin_ref, part_ref, mid_ref,
    dq_ref, dk_ref, dv_ref, layer_ref, next_ref,
    all_ref, acc_ref, rows_ref, s_ref, p_ref, land_ref, pair_ref, q_ref,
    send, recv, zsend, zrecv, read_sem, mid_land, msend, mrecv,
):
    rows = g_ref.shape[0]
    span = heads * HD
    shard = layer_ref.shape[1]
    at = lax.axis_index("tp")
    cube = Cube(all_ref, send, recv)
    middle = MidSum(mid_ref, mid_land, next_ref, msend, mrecv)
    me = cube.me
    barrier = pltpu.get_barrier_semaphore()
    cube.signal(barrier)
    for o in range(1, n):
        pl.semaphore_signal(
            barrier, inc=1, device_id={"tp": lax.rem(at + o, n)}, device_id_type=MESH
        )

    def read(step, keys):
        place = pl.ds(pl.multiple_of(cube.block(step) * rows, 16), rows)
        far, near = (far_pair_ref, pair_ref) if keys else (far_q_ref, q_ref)
        return pltpu.make_async_copy(
            far.at[place], near.at[place], read_sem.at[0 if keys else 1, step]
        )

    def read_all(step, carry):
        block = cube.block(step)

        @pl.when(block <= me)
        def _():
            read(step, True).start()

        @pl.when(block >= me)
        def _():
            read(step, False).start()

        return carry

    lax.fori_loop(0, CUBE, read_all, 0)
    all_ref[pl.ds(pl.multiple_of(me * rows, 16), rows), :] = g_ref[...]
    acc_ref[...] = jnp.zeros_like(acc_ref)
    dk_ref[...] = jnp.zeros_like(dk_ref)
    dv_ref[...] = jnp.zeros_like(dv_ref)
    pl.semaphore_wait(barrier, 3 + n - 1)

    def term(o):
        target = lax.rem(at + o, n)
        return pltpu.make_async_remote_copy(
            src_ref=part_ref.at[:, pl.ds(pl.multiple_of(target * shard, 128), shard)],
            dst_ref=land_ref.at[o - 1],
            send_sem=zsend.at[o - 1], recv_sem=zrecv.at[o - 1],
            device_id={"tp": target}, device_id_type=MESH,
        )

    own = pl.ds(pl.multiple_of(me * rows, 16), rows)

    def turn(step, carry):
        cube.advance(step)

        @pl.when(step == 0)
        def _():
            for o in range(1, n):
                term(o).start()
            middle.begin()

        @pl.when(step == 3)
        def _():
            middle.turn()

        block = cube.block(step)
        place = pl.ds(pl.multiple_of(block * rows, 16), rows)

        @pl.when(block <= me)
        def _():
            read(step, True).wait()

        @pl.when(block >= me)
        def _():
            read(step, False).wait()

        def scores(h, key_block, key_place, query_block, query_place):
            hs = slice(h * HD, (h + 1) * HD)
            vs = slice(span + h * HD, span + (h + 1) * HD)
            s = lax.dot_general(
                pair_ref[key_place, hs], q_ref[query_place, hs], NT, preferred_element_type=F32
            )
            begin = begin_ref[pl.ds(query_block, 1), :]
            s_ref[h % 2] = hidden_scores(s, key_block, query_block, rows, begin)
            p_ref[h % 2] = lax.dot_general(
                pair_ref[key_place, vs], all_ref[query_place, hs], NT, preferred_element_type=F32
            )

        def read_rows(query_place):
            coded = all_ref[query_place, span:].astype(F32).T
            for k in range(2 * heads):
                rows_ref[k : k + 1, :] = (
                    coded[3 * k : 3 * k + 1]
                    + coded[3 * k + 1 : 3 * k + 2]
                    + coded[3 * k + 2 : 3 * k + 3]
                )

        def weights(h):
            p = jnp.exp2(s_ref[h % 2] * C2 - rows_ref[h : h + 1, :])
            ds = p * (p_ref[h % 2] - rows_ref[heads + h : heads + h + 1, :])
            return p.astype(BF16), ds.astype(BF16)

        @pl.when(block <= me)
        def _():
            read_rows(own)
            scores(0, block, place, me, own)
            for h in range(heads):
                if h + 1 < heads:
                    scores(h + 1, block, place, me, own)
                _, ds = weights(h)
                acc_ref[h] = acc_ref[h] + lax.dot_general(
                    pair_ref[place, h * HD : (h + 1) * HD], ds, TN, preferred_element_type=F32
                )

        @pl.when(block >= me)
        def _():
            read_rows(place)
            scores(0, me, own, block, place)
            for h in range(heads):
                hs = slice(h * HD, (h + 1) * HD)
                if h + 1 < heads:
                    scores(h + 1, me, own, block, place)
                p, ds = weights(h)
                dv_ref[:, hs] += jnp.dot(p, all_ref[place, hs], preferred_element_type=F32)
                dk_ref[:, hs] += jnp.dot(ds, q_ref[place, hs], preferred_element_type=F32)

        return carry

    lax.fori_loop(0, CUBE, turn, 0)
    for h in range(heads):
        dq_ref[:, h * HD : (h + 1) * HD] = (acc_ref[h] * SCALE).T
    dk_ref[...] = dk_ref[...] * SCALE
    total = part_ref[:, pl.ds(pl.multiple_of(at * shard, 128), shard)].astype(F32)
    for o in range(1, n):
        term(o).wait_recv()
        total = total + land_ref[o - 1].astype(F32)
    layer_ref[...] = total.astype(BF16)
    middle.finish()
    cube.finish()
    for o in range(1, n):
        term(o).wait_send()


def attend_back_far(grad, all_query, all_pairs, all_begin, part, mid, heads, n):
    rows = grad.shape[0]
    span = heads * HD
    shard = part.shape[1] // n
    vmem = pl.BlockSpec(memory_space=pltpu.VMEM)
    wide = jax.ShapeDtypeStruct((rows, span), F32)
    return pl.pallas_call(
        functools.partial(attend_back_far_kernel, heads, n),
        in_specs=[vmem] + [pl.BlockSpec(memory_space=pl.ANY)] * 2 + [vmem] * 3,
        out_specs=[vmem] * 5,
        out_shape=[wide, wide, wide, jax.ShapeDtypeStruct((rows, shard), BF16)]
        + [jax.ShapeDtypeStruct(mid.shape, BF16)],
        scratch_shapes=[
            pltpu.VMEM((CUBE * rows, span + HD), BF16),
            pltpu.VMEM((heads, HD, rows), F32),
            pltpu.VMEM((2 * heads, rows), F32),
            pltpu.VMEM((2, rows, rows), F32),
            pltpu.VMEM((2, rows, rows), F32),
            pltpu.VMEM((n - 1, rows, shard), BF16),
            pltpu.VMEM((CUBE * rows, 2 * span), BF16),
            pltpu.VMEM((CUBE * rows, span), BF16),
            pltpu.SemaphoreType.DMA((CUBE_SENDS,)),
            pltpu.SemaphoreType.DMA((CUBE_SENDS,)),
            pltpu.SemaphoreType.DMA((n - 1,)),
            pltpu.SemaphoreType.DMA((n - 1,)),
            pltpu.SemaphoreType.DMA((2, CUBE)),
            pltpu.VMEM((mid.shape[0] // 2, mid.shape[1]), BF16),
            pltpu.SemaphoreType.DMA((4,)),
            pltpu.SemaphoreType.DMA((4,)),
        ],
        compiler_params=params(62, collective_id=3, has_side_effects=True),
        cost_estimate=cost(1e6, 1e6),
        name="attend_back_far",
    )(grad, all_query, all_pairs, all_begin, part, mid)


def query_grad_kernel(
    heads, info, q_ref, do_ref, lse_ref, delta_ref, k_ref, v_ref, begin_ref,
    dq_ref, acc_ref, s_ref, g_ref,
):
    me, first, clear = info[0], info[1], info[2]
    j = pl.program_id(0)
    rows = q_ref.shape[0]

    @pl.when(j == 0)
    def _():
        acc_ref[...] = jnp.zeros_like(acc_ref)

    def block(hide):
        def score(h):
            hs = slice(h * HD, (h + 1) * HD)
            s = lax.dot_general(k_ref[:, hs], q_ref[:, hs], NT, preferred_element_type=F32)
            if hide:
                s = masked(s, j, me, rows, begin_ref[...])
            s_ref[h % 2] = s
            g_ref[h % 2] = lax.dot_general(
                v_ref[:, hs], do_ref[:, hs], NT, preferred_element_type=F32
            )

        def spread(h):
            hs = slice(h * HD, (h + 1) * HD)
            p = jnp.exp2(s_ref[h % 2] * C2 - lse_ref[h : h + 1, :])
            ds = (p * (g_ref[h % 2] - delta_ref[h : h + 1, :])).astype(BF16)
            acc_ref[h] = acc_ref[h] + lax.dot_general(
                k_ref[:, hs], ds, TN, preferred_element_type=F32
            )

        score(0)
        for h in range(heads):
            if h + 1 < heads:
                score(h + 1)
            spread(h)

    @pl.when((j >= clear) & (j < me))
    def _():
        block(False)

    @pl.when(((j >= first) & (j < clear) & (j < me)) | (j == me))
    def _():
        block(True)

    @pl.when(j == me)
    def _():
        for h in range(heads):
            dq_ref[:, h * HD : (h + 1) * HD] = (acc_ref[h] * SCALE).T


def query_grad(info, query, grad_mixed, lse, delta, pairs, begin, heads):
    rows = query.shape[0]
    total = pairs.shape[0]
    span = heads * HD
    full = lambda shape: pl.BlockSpec(shape, lambda j, s: (0, 0))
    key = pl.BlockSpec((rows, span), lambda j, s: (jnp.clip(j, s[1], s[0]), 0))
    value = pl.BlockSpec((rows, span), lambda j, s: (jnp.clip(j, s[1], s[0]), 1))
    wide = full((rows, span))
    thin = full((heads, rows))
    return pl.pallas_call(
        functools.partial(query_grad_kernel, heads),
        grid_spec=pltpu.PrefetchScalarGridSpec(
            num_scalar_prefetch=1,
            grid=(total // rows,),
            in_specs=[wide, wide, thin, thin, key, value, full((1, rows))],
            out_specs=wide,
            scratch_shapes=[
                pltpu.VMEM((heads, HD, rows), F32),
                pltpu.VMEM((2, rows, rows), F32),
                pltpu.VMEM((2, rows, rows), F32),
            ],
        ),
        out_shape=jax.ShapeDtypeStruct((rows, span), F32),
        compiler_params=params(58),
        cost_estimate=cost(6 * rows * total * span, 4 * total * span, rows * total * heads),
        name="query_grad",
    )(info, query, grad_mixed, lse, delta, pairs, pairs, begin)


def key_grad_kernel(
    heads, info, k_ref, v_ref, q_ref, g_ref, begin_ref, dk_ref, dv_ref,
    rows_ref, s_ref, p_ref,
):
    me, last, clear = info[0], info[1], info[2]
    j = pl.program_id(0)
    rows = k_ref.shape[0]
    span = heads * HD

    @pl.when(j == me)
    def _():
        dk_ref[...] = jnp.zeros_like(dk_ref)
        dv_ref[...] = jnp.zeros_like(dv_ref)

    def block(hide):
        coded = g_ref[:, span:].astype(F32).T
        for n in range(2 * heads):
            rows_ref[n : n + 1, :] = (
                coded[3 * n : 3 * n + 1] + coded[3 * n + 1 : 3 * n + 2] + coded[3 * n + 2 : 3 * n + 3]
            )

        def score(h):
            hs = slice(h * HD, (h + 1) * HD)
            s = lax.dot_general(k_ref[:, hs], q_ref[:, hs], NT, preferred_element_type=F32)
            if hide:
                key_place = lax.broadcasted_iota(jnp.int32, s.shape, 0) + me * rows
                query_place = lax.broadcasted_iota(jnp.int32, s.shape, 1) + j * rows
                s = jnp.where(
                    (key_place <= query_place) & (key_place >= begin_ref[...]), s, NEG
                )
            s_ref[h % 2] = s
            p_ref[h % 2] = lax.dot_general(
                v_ref[:, hs], g_ref[:, hs], NT, preferred_element_type=F32
            )

        def spread(h):
            hs = slice(h * HD, (h + 1) * HD)
            p = jnp.exp2(s_ref[h % 2] * C2 - rows_ref[h : h + 1, :])
            ds = (p * (p_ref[h % 2] - rows_ref[heads + h : heads + h + 1, :])).astype(BF16)
            dv_ref[:, hs] += jnp.dot(p.astype(BF16), g_ref[:, hs], preferred_element_type=F32)
            dk_ref[:, hs] += jnp.dot(ds, q_ref[:, hs], preferred_element_type=F32)

        score(0)
        for h in range(heads):
            if h + 1 < heads:
                score(h + 1)
            spread(h)

    @pl.when((j > me) & (j <= clear))
    def _():
        block(False)

    @pl.when((j == me) | ((j > me) & (j > clear) & (j <= last)))
    def _():
        block(True)

    @pl.when(j == pl.num_programs(0) - 1)
    def _():
        dk_ref[...] = dk_ref[...] * SCALE


def key_grad(info, pairs, all_query, all_grad, all_begin, heads):
    rows = pairs.shape[0]
    total = all_query.shape[0]
    span = heads * HD
    full = lambda shape, at=0: pl.BlockSpec(shape, lambda j, s: (0, at))
    near = lambda j, s: (jnp.clip(j, s[0], s[1]), 0)
    wide = full((rows, span))
    return pl.pallas_call(
        functools.partial(key_grad_kernel, heads),
        grid_spec=pltpu.PrefetchScalarGridSpec(
            num_scalar_prefetch=1,
            grid=(total // rows,),
            in_specs=[
                wide, full((rows, span), 1),
                pl.BlockSpec((rows, span), near),
                pl.BlockSpec((rows, span + HD), near),
                pl.BlockSpec((1, rows), lambda j, s: (0, jnp.clip(j, s[0], s[1]))),
            ],
            out_specs=[wide, wide],
            scratch_shapes=[
                pltpu.VMEM((2 * heads, rows), F32),
                pltpu.VMEM((2, rows, rows), F32),
                pltpu.VMEM((2, rows, rows), F32),
            ],
        ),
        out_shape=[jax.ShapeDtypeStruct((rows, span), F32)] * 2,
        compiler_params=params(58),
        cost_estimate=cost(8 * rows * total * span, 4 * total * span, rows * total * heads),
        name="key_grad",
    )(info, pairs, pairs, all_query, all_grad, all_begin)


def mixed_grad_kernel(heads, branch_ref, w_ref, raw_ref, lse_ref, out_ref, delta_ref):
    span = heads * HD
    low = lax.dot_general(
        branch_ref[...], w_ref[...], NT, preferred_element_type=F32
    ).astype(BF16)
    out_ref[:, :span] = low
    count = low.shape[0]
    both = low.astype(F32) * raw_ref[...]
    for h in range(heads):
        delta_ref[h : h + 1, :] = jnp.sum(both[:, h * HD : (h + 1) * HD].T, axis=0, keepdims=True)
    lines = []
    for n in range(2 * heads):
        value = lse_ref[n : n + 1, :] if n < heads else delta_ref[n - heads : n - heads + 1, :]
        for _ in range(3):
            piece = value.astype(BF16).astype(F32)
            lines.append(piece)
            value = value - piece
    lines.append(jnp.zeros((HD - len(lines), count), F32))
    out_ref[:, span:] = jnp.concatenate(lines, axis=0).T.astype(BF16)


def mixed_grad(branch, weight, raw, lse, heads):
    rows, width = branch.shape
    span = heads * HD
    block = 256
    row = lambda n: pl.BlockSpec((block, n), lambda i: (i, 0))
    line = pl.BlockSpec((heads, block), lambda i: (0, i))
    return pl.pallas_call(
        functools.partial(mixed_grad_kernel, heads),
        grid=(rows // block,),
        in_specs=[row(width), pl.BlockSpec((span, width), lambda i: (0, 0)), row(span), line],
        out_specs=[row(span + HD), line],
        out_shape=[
            jax.ShapeDtypeStruct((rows, span + HD), BF16),
            jax.ShapeDtypeStruct((heads, rows), F32),
        ],
        compiler_params=params(56),
        cost_estimate=cost(2 * rows * width * span, 2 * width * span + 4 * rows * width),
        name="mixed_grad",
    )(branch, weight, raw, lse)


def feed_kernel(
    inner_ref, cot_ref, w_ref, grad_ref, hidden_ref, dgu_ref, down_grad_ref, gu_grad_ref
):
    block = grad_ref.shape[1]
    both = jnp.dot(inner_ref[...], w_ref[...], preferred_element_type=F32)
    grad = grad_ref[...].astype(F32)
    gate, up = both[:, :block], both[:, block:]
    sigma = 1.0 / (1.0 + jnp.exp(-gate))
    active = gate * sigma
    hidden_ref[...] = (active * up).astype(BF16)
    dgu_ref[:, :block] = (grad * up * sigma * (1.0 + gate * (1.0 - sigma))).astype(BF16)
    dgu_ref[:, block:] = (grad * active).astype(BF16)
    down_grad_ref[...] = lax.dot_general(
        hidden_ref[...], cot_ref[...], TN, preferred_element_type=F32
    ).astype(BF16)
    gu_grad_ref[...] = lax.dot_general(
        inner_ref[...], dgu_ref[...], TN, preferred_element_type=F32
    ).astype(BF16)


def feed(inner, cot, weight, grad, block):
    rows, width = inner.shape
    units = grad.shape[1]
    whole = pl.BlockSpec((rows, width), lambda j: (0, 0))
    column = lambda high, wide: pl.BlockSpec((high, wide), lambda j: (0, j))
    line = pl.BlockSpec((block, width), lambda j: (j, 0))
    return pl.pallas_call(
        feed_kernel,
        grid=(units // block,),
        in_specs=[whole, whole, column(width, 2 * block), column(rows, block)],
        out_specs=[column(rows, block), column(rows, 2 * block), line, column(width, 2 * block)],
        out_shape=[
            jax.ShapeDtypeStruct((rows, units), BF16),
            jax.ShapeDtypeStruct((rows, 2 * units), BF16),
            jax.ShapeDtypeStruct((units, width), BF16),
            jax.ShapeDtypeStruct((width, 2 * units), BF16),
        ],
        compiler_params=params(60),
        cost_estimate=cost(
            12 * rows * width * units, 12 * width * units + 4 * rows * width, rows * units
        ),
        name="feed",
    )(inner, cot, weight, grad)


def weave_kernel(block, sum_ref, out_ref):
    for j in range(sum_ref.shape[1] // (2 * block)):
        for k in range(2):
            at = (2 * j + k) * block
            out_ref[:, k, j * block : (j + 1) * block] = sum_ref[:, at : at + block].astype(F32)


def weave(summed, block):
    width, both = summed.shape
    rows = 256
    return pl.pallas_call(
        functools.partial(weave_kernel, block),
        grid=(width // rows,),
        in_specs=[pl.BlockSpec((rows, both), lambda i: (i, 0))],
        out_specs=pl.BlockSpec((rows, 2, both // 2), lambda i: (i, 0, 0)),
        out_shape=jax.ShapeDtypeStruct((width, 2, both // 2), F32),
        compiler_params=params(56),
        cost_estimate=cost(width * both, 6 * width * both),
        name="weave",
    )(summed)


def widen_kernel(in_ref, out_ref):
    out_ref[...] = in_ref[...].astype(F32)


def widen(summed):
    high, wide = summed.shape
    block = pl.BlockSpec((512, wide), lambda i: (i, 0))
    return pl.pallas_call(
        widen_kernel,
        grid=(high // 512,),
        in_specs=[block],
        out_specs=block,
        out_shape=jax.ShapeDtypeStruct((high, wide), F32),
        compiler_params=params(56),
        cost_estimate=cost(high * wide, 6 * high * wide),
        name="widen",
    )(summed)


def line_barrier(at, n, cube=None):
    barrier = pltpu.get_barrier_semaphore()
    if cube is not None:
        cube.signal(barrier)

    @pl.when(at > 0)
    def _():
        pl.semaphore_signal(barrier, inc=1, device_id={"tp": at - 1}, device_id_type=MESH)

    @pl.when(at < n - 1)
    def _():
        pl.semaphore_signal(barrier, inc=1, device_id={"tp": at + 1}, device_id_type=MESH)

    near = jnp.where((at > 0) & (at < n - 1), 2, 1)
    pl.semaphore_wait(barrier, near + (0 if cube is None else 3))


def sum_rows(n, sub, part_ref, out_ref, row_fn, from_left, from_right, send, recv, aside={}):
    at = lax.axis_index("tp")
    chunks = part_ref.shape[0] // sub
    middle = (n // 2 - 1, n // 2)

    def link(kind, right, src, dst, c):
        which = (kind * 2 + (1 if right else 0), c)
        return pltpu.make_async_remote_copy(
            src_ref=src.at[pl.ds(c * sub, sub)],
            dst_ref=dst.at[pl.ds(c * sub, sub)],
            send_sem=send.at[which],
            recv_sem=recv.at[which],
            device_id={"tp": at + 1 if right else at - 1},
            device_id_type=MESH,
        )

    def came(right):
        return from_left if right else from_right

    def first(right, c):
        return link(0, right, part_ref, came(right), c)

    def onward(right, c):
        return link(0, right, came(right), came(right), c)

    def hand(right, c):
        return link(1, right, out_ref, out_ref, c)

    def reduce_step(c):
        owner = middle[c % 2]
        rows = slice(c * sub, (c + 1) * sub)
        for right in (True, False):
            edge = 0 if right else n - 1
            held = came(right)

            @pl.when(((at < owner) if right else (at > owner)) & (at != edge))
            def _():
                copy = onward(right, c)
                copy.wait_recv()
                held[rows, :] = (
                    held[rows, :].astype(F32) + part_ref[rows, :].astype(F32)
                ).astype(BF16)
                copy.start()

    def final_step(c):
        owner = middle[c % 2]
        rows = slice(c * sub, (c + 1) * sub)

        @pl.when(at == owner)
        def _():
            total = part_ref[rows, :].astype(F32)
            onward(True, c).wait_recv()
            total = total + from_left[rows, :].astype(F32)
            onward(False, c).wait_recv()
            total = total + from_right[rows, :].astype(F32)
            row_fn(total, rows)
            hand(True, c).start()
            hand(False, c).start()

    def hand_step(c):
        owner = middle[c % 2]
        for right in (True, False):
            edge = n - 1 if right else 0

            @pl.when((at > owner) if right else (at < owner))
            def _():
                copy = hand(right, c)
                copy.wait_recv()

                @pl.when(at != edge)
                def _():
                    copy.start()

    for c in range(chunks):
        @pl.when(at == 0)
        def _():
            first(True, c).start()

        @pl.when(at == n - 1)
        def _():
            first(False, c).start()

    for c in range(chunks + 4):
        for piece in aside.get(c, ()):
            piece()
        if c < chunks:
            reduce_step(c)
        if 2 <= c < chunks + 2:
            final_step(c - 2)
        if c >= 4:
            hand_step(c - 4)
    for c in range(chunks):
        owner = middle[c % 2]

        @pl.when(at < owner)
        def _():
            first(True, c).wait_send()

        @pl.when(at > owner)
        def _():
            first(False, c).wait_send()

        @pl.when((at >= owner) & (at < n - 1))
        def _():
            hand(True, c).wait_send()

        @pl.when((at <= owner) & (at > 0))
        def _():
            hand(False, c).wait_send()


def merge_kernel(
    n, sub, part_ref, tok_ref, cot_ref, down_ref, inner_ref, resid_ref, stat_ref, hidden_ref,
    from_left, from_right, send, recv,
):
    line_barrier(lax.axis_index("tp"), n)
    resid_ref[...] = jnp.zeros_like(resid_ref)
    stat_ref[...] = jnp.zeros_like(stat_ref)

    def row_fn(total, rows):
        x = tok_ref[rows, :].astype(F32) + total
        mean = jnp.mean(x, axis=1, keepdims=True)
        center = x - mean
        inverse = lax.rsqrt(jnp.mean(center * center, axis=1, keepdims=True) + EPS)
        resid_ref[rows, :] = x
        stat_ref[rows, :] = jnp.concatenate([mean, inverse], axis=1)
        inner_ref[rows, :] = (center * inverse).astype(BF16)

    def piece(at):
        hidden_ref[:, at : at + 256] = lax.dot_general(
            cot_ref[...], down_ref[at : at + 256, :], NT, preferred_element_type=F32
        ).astype(BF16)

    aside = {}
    for k in range(down_ref.shape[0] // 256):
        aside[1 + 2 * k] = (functools.partial(piece, k * 256),)
    sum_rows(n, sub, part_ref, inner_ref, row_fn, from_left, from_right, send, recv, aside)


def merge(part, tok_full, cot_full, down, n):
    rows, width = part.shape
    sub = 32
    vmem = pl.BlockSpec(memory_space=pltpu.VMEM)
    return pl.pallas_call(
        functools.partial(merge_kernel, n, sub),
        in_specs=[vmem] * 4,
        out_specs=[vmem] * 4,
        out_shape=[
            jax.ShapeDtypeStruct((rows, width), BF16),
            jax.ShapeDtypeStruct((rows, width), F32),
            jax.ShapeDtypeStruct((rows, 2), F32),
            jax.ShapeDtypeStruct((rows, down.shape[0]), BF16),
        ],
        scratch_shapes=[pltpu.VMEM((rows, width), BF16)] * 2
        + [pltpu.SemaphoreType.DMA((4, rows // sub))] * 2,
        compiler_params=params(56, collective_id=5, has_side_effects=True),
        cost_estimate=cost(1e6, 1e6),
        name="merge",
    )(part, tok_full, cot_full, down)


def norm_back_kernel(
    n, sub, cube, part_ref, cot_ref, resid_ref, stat_ref, hidden_ref, down_ref, *refs
):
    total = None
    if cube:
        own, out_ref, layer_ref, mid, from_left, from_right, send, recv, land, csend, crecv = refs
        total = CubeSum(own, land, csend, crecv, mid=mid)
    else:
        out_ref, layer_ref, from_left, from_right, send, recv = refs
    line_barrier(lax.axis_index("tp"), n, total)
    aside = {}

    def piece(at):
        cols = slice(at, at + 256)
        layer_ref[:, cols] = (
            resid_ref[:, cols]
            + jnp.dot(hidden_ref[...], down_ref[:, cols], preferred_element_type=F32)
        ).astype(BF16)

    for k in range(down_ref.shape[1] // 256):
        aside[1 + 2 * k] = (functools.partial(piece, k * 256),)
    if cube:
        total.begin()
        for k, c in enumerate((6, 8, 10, 12)):
            aside[c] = (functools.partial(total.reduce, k),)

    def row_fn(summed, rows):
        inverse = stat_ref[rows, 1:2]
        normed = (resid_ref[rows, :] - stat_ref[rows, 0:1]) * inverse
        mean = jnp.mean(summed, axis=1, keepdims=True)
        inner = jnp.mean(summed * normed, axis=1, keepdims=True)
        out = cot_ref[rows, :].astype(F32) + inverse * (summed - mean - normed * inner)
        out_ref[rows, :] = out.astype(BF16)

    sum_rows(n, sub, part_ref, out_ref, row_fn, from_left, from_right, send, recv, aside)
    if cube:
        total.reduce(4)
        total.reduce(5)
        total.finish()


def norm_back(part, cot, resid, stat, hidden, down, n, grads):
    rows, width = part.shape
    sub = 32
    vmem = pl.BlockSpec(memory_space=pltpu.VMEM)
    extra = []
    for grad in grads:
        extra += sum_scratch(grad.shape)
    return pl.pallas_call(
        functools.partial(norm_back_kernel, n, sub, len(grads) > 0),
        in_specs=[vmem] * (6 + len(grads)),
        out_specs=[vmem] * (2 + len(grads)),
        out_shape=[jax.ShapeDtypeStruct((rows, width), BF16)] * 2
        + [jax.ShapeDtypeStruct((grad.shape[0] // 4, grad.shape[1]), BF16) for grad in grads],
        scratch_shapes=[pltpu.VMEM((rows, width), BF16)] * 2
        + [pltpu.SemaphoreType.DMA((4, rows // sub))] * 2
        + extra,
        compiler_params=params(60, collective_id=1, has_side_effects=True),
        cost_estimate=cost(1e6, 1e6),
        name="norm_back",
    )(part, cot, resid, stat, hidden, down, *grads)


def unrotate_kernel(
    heads, dq_ref, dk_ref, dv_ref, cos_ref, sin_ref, inner_ref, dproj_ref, grad_ref
):
    def back(ref):
        for h in range(heads):
            hs = slice(h * HD, (h + 1) * HD)
            piece = ref[:, hs]
            dproj_ref[:, hs] = (
                piece * cos_ref[...] - pltpu.roll(piece, HD // 2, 1) * sin_ref[...]
            ).astype(BF16)

    part = pl.program_id(0)

    @pl.when(part == 0)
    def _():
        back(dq_ref)

    @pl.when(part == 1)
    def _():
        back(dk_ref)

    @pl.when(part == 2)
    def _():
        dproj_ref[...] = dv_ref[...].astype(BF16)

    grad_ref[...] = lax.dot_general(
        inner_ref[...], dproj_ref[...], TN, preferred_element_type=F32
    ).astype(BF16)


def unrotate(dq, dk, dv, cosine, sine, inner, heads):
    rows, span = dq.shape
    width = inner.shape[1]
    whole = lambda n: pl.BlockSpec((rows, n), lambda i: (0, 0))
    return pl.pallas_call(
        functools.partial(unrotate_kernel, heads),
        grid=(3,),
        in_specs=[whole(span)] * 3 + [whole(HD)] * 2 + [whole(width)],
        out_specs=[
            pl.BlockSpec((rows, span), lambda i: (0, i)),
            pl.BlockSpec((width, span), lambda i: (i, 0)),
        ],
        out_shape=[
            jax.ShapeDtypeStruct((rows, 3 * span), BF16),
            jax.ShapeDtypeStruct((3 * width, span), BF16),
        ],
        compiler_params=params(56),
        cost_estimate=cost(6 * rows * span * width, 12 * rows * span + 6 * width * span),
        name="unrotate",
    )(dq, dk, dv, cosine, sine, inner)


def unproject_kernel(heads, n, cube, dproj_ref, tok_ref, stat_ref, w_ref, branch_ref, *refs):
    sums, rest = [], None
    if cube:
        in_ref, og_ref, mid_ref, out_ref, in_out, og_out, down_out = refs[:7]
        part_ref, mine_ref, land_ref, sums_ref, far_ref, send, recv, ssend, srecv = refs[7:16]
        for own, out, at in ((in_ref, in_out, 16), (og_ref, og_out, 19)):
            land, csend, crecv = refs[at : at + 3]
            sums.append(CubeSum(own, land, csend, crecv, out=out))
        rest = LastGather(mid_ref, down_out, *refs[22:25])
    else:
        out_ref, part_ref, mine_ref, land_ref, sums_ref, far_ref, send, recv, ssend, srecv = refs

    def reduce(*pieces):
        for k in pieces:
            for item in sums:
                item.reduce(k)

    def gather(k):
        for item in sums:
            item.gather(k)

    rows, width = tok_ref.shape
    shard = width // n
    span = heads * HD
    at = lax.axis_index("tp")
    barrier = pltpu.get_barrier_semaphore()
    for o in range(1, n):
        pl.semaphore_signal(
            barrier, inc=1, device_id={"tp": lax.rem(at + o, n)}, device_id_type=MESH
        )
    if cube:
        sums[0].signal(barrier)
    pl.semaphore_wait(barrier, n - 1 + (3 if cube else 0))
    for item in sums:
        item.begin()
    if cube:
        rest.begin()
    block = 256
    count = rows // block

    def term(o, i):
        target = lax.rem(at + o, n)
        place = pl.ds(i * block, block)
        return pltpu.make_async_remote_copy(
            src_ref=part_ref.at[place, pl.ds(pl.multiple_of(target * shard, 128), shard)],
            dst_ref=land_ref.at[o - 1, place],
            send_sem=send.at[o - 1, i], recv_sem=recv.at[o - 1, i],
            device_id={"tp": target}, device_id_type=MESH,
        )

    def totals(o):
        return pltpu.make_async_remote_copy(
            src_ref=sums_ref, dst_ref=far_ref.at[o - 1],
            send_sem=ssend.at[o - 1], recv_sem=srecv.at[o - 1],
            device_id={"tp": lax.rem(at + o, n)}, device_id_type=MESH,
        )

    own = pl.ds(pl.multiple_of(at * shard, 128), shard)
    for i in range(count):
        place = pl.ds(i * block, block)
        total = None
        for part in range(3):
            piece = lax.dot_general(
                dproj_ref[place, part * span : (part + 1) * span], w_ref[part], NT,
                preferred_element_type=F32,
            )
            total = piece if total is None else total + piece
        part_ref[place, :] = total.astype(BF16)
        for o in range(1, n):
            term(o, i).start()
        normed = (tok_ref[place, :].astype(F32) - stat_ref[place, 0:1]) * stat_ref[place, 1:2]
        first = jnp.sum(total, axis=1, keepdims=True)
        second = jnp.sum(total * normed, axis=1, keepdims=True)
        lane = lax.broadcasted_iota(jnp.int32, (block, HD), 1)
        both = jnp.where(lane == 0, first, jnp.where(lane == 1, second, 0.0))
        sums_ref[:, i * block : (i + 1) * block] = both.T[:8]
    for o in range(1, n):
        totals(o).start()
    reduce(0, 1, 2, 3, 4, 5, 6, 7)
    gather(0)
    gather(1)
    total = sums_ref[...]
    for o in range(1, n):
        totals(o).wait_recv()
        total = total + far_ref[o - 1]
    mine_ref[...] = total
    for i in range(count):
        place = pl.ds(i * block, block)
        spread = jnp.concatenate(
            [mine_ref[:, i * block : (i + 1) * block], jnp.zeros((HD - 8, block), F32)], axis=0
        ).T / width
        total = part_ref[place, own].astype(F32)
        for o in range(1, n):
            term(o, i).wait_recv()
            total = total + land_ref[o - 1, place].astype(F32)
        inverse = stat_ref[place, 1:2]
        normed = (tok_ref[place, own].astype(F32) - stat_ref[place, 0:1]) * inverse
        out_ref[place, :] = branch_ref[place, own].astype(F32) + inverse * (
            total - spread[:, 0:1] - normed * spread[:, 1:2]
        )
    gather(2)
    for item in sums + ([rest] if cube else []):
        item.finish()
    for o in range(1, n):
        totals(o).wait_send()
        for i in range(count):
            term(o, i).wait_send()


def unproject(dproj, tok_full, stat, weight, branch, heads, n, grads, mids):
    rows, width = tok_full.shape
    shard = width // n
    vmem = pl.BlockSpec(memory_space=pltpu.VMEM)
    extra = []
    for grad in grads:
        extra += sum_scratch(grad.shape)
    for _ in mids:
        extra += [pltpu.SemaphoreType.DMA((2,))] * 3
    return pl.pallas_call(
        functools.partial(unproject_kernel, heads, n, len(grads) > 0),
        in_specs=[vmem] * (5 + len(grads) + len(mids)),
        out_specs=[vmem] * (1 + len(grads)) + [pl.BlockSpec(memory_space=pl.ANY)] * len(mids),
        out_shape=[jax.ShapeDtypeStruct((rows, shard), F32)]
        + [jax.ShapeDtypeStruct((grad.shape[0] // 2, grad.shape[1]), BF16) for grad in grads]
        + [jax.ShapeDtypeStruct((2 * mid.shape[0], mid.shape[1]), BF16) for mid in mids],
        scratch_shapes=[
            pltpu.VMEM((rows, width), BF16),
            pltpu.VMEM((8, rows), F32),
            pltpu.VMEM((n - 1, rows, shard), BF16),
            pltpu.VMEM((8, rows), F32),
            pltpu.VMEM((n - 1, 8, rows), F32),
            pltpu.SemaphoreType.DMA((n - 1, rows // 256)),
            pltpu.SemaphoreType.DMA((n - 1, rows // 256)),
            pltpu.SemaphoreType.DMA((n - 1,)),
            pltpu.SemaphoreType.DMA((n - 1,)),
        ]
        + extra,
        compiler_params=params(60, collective_id=4, has_side_effects=True),
        cost_estimate=cost(1e6, 1e6),
        name="unproject",
    )(dproj, tok_full, stat, weight, branch, *grads, *mids)


def per_device(tokens, segment_ids, in_weight, out_weight, gate_up_weight, down_weight, cotangent):
    rows = tokens.shape[0]
    width = in_weight.shape[0]
    span = in_weight.shape[2]
    heads = span // HD
    hidden_local = down_weight.shape[0]
    me = lax.axis_index("ctx")
    tp_size = lax.axis_size("tp")
    cube = lax.axis_size("ctx") == CUBE

    def gather(local, axis=1):
        return lax.all_gather(local, "tp", axis=axis, tiled=True)

    places = me * rows + jnp.arange(rows, dtype=jnp.int32)
    cosine, sine = rope_tables(places)
    in_w = jnp.transpose(in_weight, (1, 0, 2))
    gu_w = jnp.transpose(
        gate_up_weight.reshape(width, 2, hidden_local // BLOCK, BLOCK), (0, 2, 1, 3)
    )
    gu_w = gu_w.reshape(width, 2 * hidden_local)

    all_seg = lax.all_gather(segment_ids, "ctx", axis=0, tiled=True)
    count = all_seg.shape[0]
    every = jnp.arange(count, dtype=jnp.int32)
    opens = jnp.concatenate([jnp.ones((1,), jnp.bool_), all_seg[1:] != all_seg[:-1]])
    all_begin = lax.cummax(jnp.where(opens, every, 0))
    blocks = all_begin.reshape(count // rows, rows)

    tok_full, gu_w, blocks, all_begin = lax.optimization_barrier(
        (gather(tokens), gu_w, blocks, all_begin)
    )
    key_info = jnp.stack(
        [me, blocks[me, 0] // rows, (blocks[me, rows - 1] + rows - 1) // rows]
    ).astype(jnp.int32)
    query_info = jnp.stack(
        [
            me,
            jnp.sum((blocks[:, 0] < (me + 1) * rows).astype(jnp.int32)) - 1,
            jnp.sum((blocks[:, rows - 1] <= me * rows).astype(jnp.int32)) - 1,
        ]
    ).astype(jnp.int32)
    begin = lax.dynamic_slice_in_dim(blocks, me, 1, 0)
    all_begin = all_begin[None, :]
    inner1, stat1, query, pairs = project(tok_full, in_w, cosine, sine, heads)
    if cube:
        raw, mixed, lse, all_pairs, cot_full, out_part = attend_far(
            query, pairs, begin, cotangent, out_weight, heads, tp_size
        )
    else:
        all_pairs = lax.all_gather(pairs, "ctx", axis=0, tiled=True)
        cot_full = gather(cotangent)
        raw, mixed, lse = attend(key_info, query, all_pairs, begin, heads)
        out_part = jnp.dot(mixed, out_weight, preferred_element_type=F32).astype(BF16)
    late_query, mixed = lax.optimization_barrier((query, mixed))
    all_query = lax.all_gather(late_query, "ctx", axis=0, tiled=True)
    inner2, resid1, stat2, grad_hidden = merge(
        out_part, tok_full, cot_full, down_weight, tp_size
    )

    hidden, grad_gu, down_grad, gu_grad = feed(inner2, cot_full, gu_w, grad_hidden, BLOCK)
    down_grad, gu_grad, all_query, grad_gu, hidden = lax.optimization_barrier(
        (down_grad, gu_grad, all_query, grad_gu, hidden)
    )
    if not cube:
        down_grad = lax.psum(down_grad, "ctx")
    gu_grad = lax.optimization_barrier(lax.psum(gu_grad, "ctx"))

    grad_part = lax.dot_general(grad_gu, gu_w, NT, preferred_element_type=F32).astype(BF16)
    branch_grad, branch, *mids = norm_back(
        grad_part, cot_full, resid1, stat2, hidden, down_weight, tp_size,
        [down_grad] if cube else [],
    )
    out_grad = lax.dot_general(mixed, branch_grad, TN, preferred_element_type=F32).astype(BF16)
    grad_mixed, delta = mixed_grad(branch_grad, out_weight, raw, lse, heads)
    if cube:
        dq, dk, dv, layer_out, mid = attend_back_far(
            grad_mixed, all_query, all_pairs, blocks, branch, mids[0], heads, tp_size
        )
    else:
        branch = lax.psum_scatter(branch, "tp", scatter_dimension=1, tiled=True)
        layer_out = branch
        all_grad = lax.all_gather(grad_mixed, "ctx", axis=0, tiled=True)
        dq = query_grad(key_info, query, grad_mixed, lse, delta, all_pairs, begin, heads)
        dk, dv = key_grad(query_info, pairs, all_query, all_grad, all_begin, heads)

    dproj, in_grad = unrotate(dq, dk, dv, cosine, sine, inner1, heads)
    if cube:
        tokens_grad, *halves = unproject(
            dproj, tok_full, stat1, in_w, branch_grad, heads, tp_size, [in_grad, out_grad], [mid]
        )
        swap = [(i, i + 1 - 2 * (i % 2)) for i in range(CUBE)]
        core = (me % 2)[None]
        far = [lax.ppermute(half, "ctx", swap) for half in halves]
        *far, gu_grad = lax.optimization_barrier((*far, weave(gu_grad, BLOCK)))
        in_grad, out_grad, down_grad = [join(core, *both) for both in zip(halves, far)]
    else:
        in_grad, out_grad, down_grad, gu_grad = lax.optimization_barrier(
            (in_grad, out_grad, down_grad, gu_grad)
        )
        in_grad, out_grad = lax.psum((in_grad, out_grad), "ctx")
        (tokens_grad,) = unproject(
            dproj, tok_full, stat1, in_w, branch_grad, heads, tp_size, [], []
        )
        in_grad, out_grad, down_grad = widen(in_grad), out_grad.astype(F32), widen(down_grad)
        gu_grad = weave(gu_grad, BLOCK)
    return (
        layer_out,
        tokens_grad,
        jnp.transpose(in_grad.reshape(3, width, span), (1, 0, 2)),
        out_grad,
        gu_grad,
        down_grad,
    )


def solution(mesh):
    placed = (
        P("ctx", "tp"),
        P("ctx"),
        P(None, None, "tp"),
        P("tp", None),
        P(None, None, "tp"),
        P("tp", None),
        P("ctx", "tp"),
    )
    return jax.shard_map(
        per_device,
        mesh=mesh,
        in_specs=placed,
        out_specs=(
            P("ctx", "tp"),
            P("ctx", "tp"),
            P(None, None, "tp"),
            P("tp", None),
            P(None, None, "tp"),
            P("tp", None),
        ),
        check_vma=False,
    )
```

```python
import functools

import jax
import jax.numpy as jnp
from jax import lax
from jax.experimental import pallas as pl
from jax.experimental.pallas import tpu as pltpu
from jax.sharding import PartitionSpec as P

HD = 128
EPS = 1e-05
NEG = -1e30
SCALE = HD ** (-0.5)
LOG2E = 1.4426950408889634
C2 = SCALE * LOG2E
F32 = jnp.float32
BF16 = jnp.bfloat16
NT = (((1,), (1,)), ((), ()))
TN = (((0,), (0,)), ((), ()))
MESH = pl.DeviceIdType.MESH
BLOCK = 512
SUB = 32


def params(mib, **more):
    return pltpu.CompilerParams(vmem_limit_bytes=mib << 20, **more)


def cost(flops, nbytes, trans=0):
    return pl.CostEstimate(flops=int(flops), bytes_accessed=int(nbytes), transcendentals=int(trans))


def rope_tables(places):
    half = HD // 2
    freq = 10000.0 ** (-jnp.arange(half, dtype=F32) * 2.0 / HD)
    angle = places.astype(F32)[:, None] * freq[None, :]
    cosine, sine = jnp.cos(angle), jnp.sin(angle)
    return jnp.concatenate([cosine, cosine], axis=1), jnp.concatenate([-sine, sine], axis=1)


def project_kernel(heads, tok_ref, w_ref, cos_ref, sin_ref, inner_ref, stat_ref, q_ref, kv_ref):
    x = tok_ref[...].astype(F32)
    center = x - jnp.mean(x, axis=1, keepdims=True)
    inverse = lax.rsqrt(jnp.mean(center * center, axis=1, keepdims=True) + EPS)
    inner = (center * inverse).astype(BF16)
    inner_ref[...] = inner
    stat_ref[...] = jnp.concatenate(
        [jnp.mean(x, axis=1, keepdims=True), inverse], axis=1
    )
    cosine, sine = cos_ref[...], sin_ref[...]
    span = heads * HD
    for part in range(3):
        out = jnp.dot(inner, w_ref[part], preferred_element_type=F32)
        if part == 2:
            kv_ref[:, span:] = out.astype(BF16)
            continue
        for h in range(heads):
            piece = out[:, h * HD : (h + 1) * HD]
            turned = (piece * cosine + pltpu.roll(piece, HD // 2, 1) * sine).astype(BF16)
            if part == 0:
                q_ref[:, h * HD : (h + 1) * HD] = turned
            else:
                kv_ref[:, h * HD : (h + 1) * HD] = turned


def project(tok_full, weight, cosine, sine, heads):
    rows, width = tok_full.shape
    span = heads * HD
    block = 256
    row = lambda n: pl.BlockSpec((block, n), lambda i: (i, 0))
    return pl.pallas_call(
        functools.partial(project_kernel, heads),
        grid=(rows // block,),
        in_specs=[
            row(width),
            pl.BlockSpec((3, width, span), lambda i: (0, 0, 0)),
            row(HD),
            row(HD),
        ],
        out_specs=[row(width), row(2), row(span), row(2 * span)],
        out_shape=[
            jax.ShapeDtypeStruct((rows, width), BF16),
            jax.ShapeDtypeStruct((rows, 2), F32),
            jax.ShapeDtypeStruct((rows, span), BF16),
            jax.ShapeDtypeStruct((rows, 2 * span), BF16),
        ],
        compiler_params=params(56),
        cost_estimate=cost(6 * rows * width * span, 6 * width * span + 6 * rows * width),
        name="project",
    )(tok_full, weight, cosine, sine)


def masked(scores, j, me, rows, begin):
    key_place = lax.broadcasted_iota(jnp.int32, scores.shape, 0) + j * rows
    query_place = lax.broadcasted_iota(jnp.int32, scores.shape, 1) + me * rows
    return jnp.where((key_place <= query_place) & (key_place >= begin), scores, NEG)


def attend_kernel(
    heads, info, q_ref, k_ref, v_ref, begin_ref, raw_ref, mixed_ref, lse_ref,
    high_ref, total_ref, acc_ref, s_ref,
):
    me, first, clear = info[0], info[1], info[2]
    j = pl.program_id(0)
    rows = q_ref.shape[0]

    @pl.when(j == 0)
    def _():
        high_ref[...] = jnp.full_like(high_ref, NEG)
        total_ref[...] = jnp.zeros_like(total_ref)
        acc_ref[...] = jnp.zeros_like(acc_ref)

    def block(hide):
        def score(h):
            hs = slice(h * HD, (h + 1) * HD)
            s = lax.dot_general(k_ref[:, hs], q_ref[:, hs], NT, preferred_element_type=F32)
            if hide:
                s = masked(s, j, me, rows, begin_ref[...])
            s_ref[h % 2] = s

        def spread(h):
            hs = slice(h * HD, (h + 1) * HD)
            s = s_ref[h % 2]
            old = high_ref[h : h + 1, :]
            new = jnp.maximum(old, jnp.max(s, axis=0, keepdims=True))
            high_ref[h : h + 1, :] = new
            p = jnp.exp2(s * C2 - new * C2)
            decay = jnp.exp2((old - new) * C2)
            total_ref[h : h + 1, :] = total_ref[h : h + 1, :] * decay + jnp.sum(
                p, axis=0, keepdims=True
            )
            acc_ref[h] = acc_ref[h] * decay + lax.dot_general(
                v_ref[:, hs], p.astype(BF16), TN, preferred_element_type=F32
            )

        score(0)
        for h in range(heads):
            if h + 1 < heads:
                score(h + 1)
            spread(h)

    @pl.when((j >= clear) & (j < me))
    def _():
        block(False)

    @pl.when(((j >= first) & (j < clear) & (j < me)) | (j == me))
    def _():
        block(True)

    @pl.when(j == me)
    def _():
        for h in range(heads):
            hs = slice(h * HD, (h + 1) * HD)
            out = (acc_ref[h] / total_ref[h : h + 1, :]).T
            raw_ref[:, hs] = out
            mixed_ref[:, hs] = out.astype(BF16)
        lse_ref[...] = high_ref[...] * C2 + jnp.log2(total_ref[...])


def attend(info, query, pairs, begin, heads):
    rows = query.shape[0]
    total = pairs.shape[0]
    span = heads * HD
    full = lambda shape: pl.BlockSpec(shape, lambda j, s: (0, 0))
    key = pl.BlockSpec((rows, span), lambda j, s: (jnp.clip(j, s[1], s[0]), 0))
    value = pl.BlockSpec((rows, span), lambda j, s: (jnp.clip(j, s[1], s[0]), 1))
    return pl.pallas_call(
        functools.partial(attend_kernel, heads),
        grid_spec=pltpu.PrefetchScalarGridSpec(
            num_scalar_prefetch=1,
            grid=(total // rows,),
            in_specs=[full((rows, span)), key, value, full((1, rows))],
            out_specs=[full((rows, span)), full((rows, span)), full((heads, rows))],
            scratch_shapes=[
                pltpu.VMEM((heads, rows), F32),
                pltpu.VMEM((heads, rows), F32),
                pltpu.VMEM((heads, HD, rows), F32),
                pltpu.VMEM((2, rows, rows), F32),
            ],
        ),
        out_shape=[
            jax.ShapeDtypeStruct((rows, span), F32),
            jax.ShapeDtypeStruct((rows, span), BF16),
            jax.ShapeDtypeStruct((heads, rows), F32),
        ],
        compiler_params=params(56),
        cost_estimate=cost(4 * rows * total * span, 4 * total * span, rows * total * heads),
        name="attend",
    )(info, query, pairs, pairs, begin)


CUBE = 8
CUBE_SENDS = 10


class Cube:
    def __init__(self, buf, send, recv):
        me = lax.axis_index("ctx")
        flip = (1 - 2 * (me % 2), 2 - 4 * ((me // 2) % 2), 4 - 8 * (me // 4))
        self.me, self.flip, self.buf, self.send, self.recv = me, flip, buf, send, recv
        self.rows = buf.shape[0] // CUBE

    def copy(self, n):
        core, x, y = self.flip
        half = self.rows // 2
        block, part, target = (
            (0, None, core),
            (0, 0, x), (0, 1, x), (0, 1, y), (0, 0, y),
            (x, 0, y), (y, 1, x),
            (x, None, core), (y, None, core), (x + y, None, core),
        )[n]
        start = (self.me + block) * self.rows
        size = self.rows
        if part is not None:
            start, size = start + part * half, half
        place = self.buf.at[pl.ds(pl.multiple_of(start, 16), size)]
        return pltpu.make_async_remote_copy(
            src_ref=place, dst_ref=place, send_sem=self.send.at[n], recv_sem=self.recv.at[n],
            device_id={"ctx": self.me + target}, device_id_type=MESH,
        )

    def arrived(self, n):
        self.copy(n).wait_recv()

    def start(self, *which):
        for n in which:
            self.copy(n).start()

    def signal(self, barrier):
        for target in self.flip:
            pl.semaphore_signal(
                barrier, inc=1, device_id={"ctx": self.me + target}, device_id_type=MESH
            )

    def block(self, step):
        core, x, y = self.flip
        on = lambda *steps: sum((step == n).astype(jnp.int32) for n in steps)
        return self.me + on(1, 4, 5, 7) * core + on(2, 4, 6, 7) * x + on(3, 5, 6, 7) * y

    def advance(self, step):
        @pl.when(step == 0)
        def _():
            self.start(0, 1, 3, 2, 4)

        @pl.when(step == 1)
        def _():
            self.arrived(0)

        @pl.when(step == 2)
        def _():
            self.arrived(1)
            self.start(5)
            self.arrived(3)
            self.start(6)
            self.arrived(2)
            self.start(7)

        @pl.when(step == 3)
        def _():
            self.arrived(4)
            self.start(8)

        @pl.when(step == 4)
        def _():
            self.arrived(7)

        @pl.when(step == 5)
        def _():
            self.arrived(8)

        @pl.when(step == 6)
        def _():
            self.arrived(5)
            self.arrived(6)
            self.start(9)

        @pl.when(step == 7)
        def _():
            self.arrived(9)

    def finish(self):
        for n in range(CUBE_SENDS):
            self.copy(n).wait_send()


SUM_SENDS = 9


class CubeSum:
    def __init__(self, own, near, land, send, recv, local, out=None, mid=None):
        me = lax.axis_index("ctx")
        core, x, y = me % 2, (me // 2) % 2, me // 4
        self.me, self.own, self.out, self.land, self.mid = me, own, out, land, mid
        self.near, self.send, self.recv, self.local = near, send, recv, local
        rows = own.shape[0]
        self.half, self.eighth, self.last = rows // 2, rows // 8, rows // 16
        second = rows // 4
        self.to = (1 - 2 * core, 2 - 4 * x, 4 - 8 * y)
        self.mine, self.other = core * self.half, (1 - core) * self.half
        self.keep1 = (x * self.eighth, second + y * self.eighth)
        self.give1 = ((1 - x) * self.eighth, second + (1 - y) * self.eighth)
        self.keep2 = (self.keep1[0] + y * self.last, self.keep1[1] + x * self.last)
        self.give2 = (self.keep1[0] + (1 - y) * self.last, self.keep1[1] + (1 - x) * self.last)

    def copy(self, n):
        core, x, y = self.to
        half, eighth, last, out, land = self.half, self.eighth, self.last, self.out, self.land
        source, start, size, target = (
            (self.own, self.other, half, core),
            (land, self.give1[0], eighth, x), (land, self.give1[1], eighth, y),
            (land, self.give2[0], last, y), (land, self.give2[1], last, x),
            (out, self.keep2[0], last, y), (out, self.keep2[1], last, x),
            (out, self.keep1[0], eighth, x), (out, self.keep1[1], eighth, y),
        )[n]
        src = source.at[pl.ds(pl.multiple_of(start, 16), size)]
        if n < 5:
            landing = (0, half, half + eighth, half + 2 * eighth, half + 2 * eighth + last)[n]
            dst = land.at[pl.ds(landing, size)]
        else:
            dst = src
        return pltpu.make_async_remote_copy(
            src_ref=src, dst_ref=dst, send_sem=self.send.at[n], recv_sem=self.recv.at[n],
            device_id={"ctx": self.me + target}, device_id_type=MESH,
        )

    def add(self, target, to, source, at, landed, size):
        step = size
        while step * self.own.shape[1] > 256 * 1024 and step % 32 == 0:
            step = step // 2

        def part(i, carry):
            def rows(begin):
                return pl.ds(pl.multiple_of(begin + i * step, 16), step)

            total = source[rows(at), :].astype(F32) + self.land[rows(landed), :].astype(F32)
            target[rows(to), :] = total.astype(BF16)
            return carry

        lax.fori_loop(0, size // step, part, 0)

    def read(self):
        rows = pl.ds(pl.multiple_of(self.mine, 16), self.half)
        return pltpu.make_async_copy(self.own.at[rows], self.near, self.local.at[0])

    def begin(self):
        self.copy(0).start()
        self.read().start()

    def reduce(self, k):
        half, eighth, last, land = self.half, self.eighth, self.last, self.land
        i = k % 2
        if k == 0:
            self.read().wait()
            self.copy(0).wait_recv()
        if k < 2:
            at = self.give1[i]
            self.add(land, at, self.near, at, at, eighth)
            self.copy(1 + i).start()
        elif k < 4:
            at = self.keep1[i]
            self.add(land, at, self.near, at, at, eighth)
        elif k < 6:
            self.copy(1 + i).wait_recv()
            landed = half + i * eighth - self.keep1[i]
            if self.out is None:
                at = self.keep1[i]
                self.add(self.mid, i * eighth, land, at, landed + at, eighth)
                return
            at = self.give2[i]
            self.add(land, at, land, at, landed + at, last)
            self.copy(3 + i).start()
            at = self.keep2[i]
            self.add(land, at, land, at, landed + at, last)
        else:
            self.copy(3 + i).wait_recv()
            at = self.keep2[i]
            self.add(self.out, at, land, at, half + 2 * eighth + i * last, last)

    def gather(self, k):
        for i in range(2):
            if k == 0:
                self.copy(5 + i).start()
            if k == 1:
                self.copy(5 + i).wait_recv()
                self.copy(7 + i).start()
            if k == 2:
                self.copy(7 + i).wait_recv()

    def finish(self):
        for n in range(3 if self.out is None else SUM_SENDS):
            self.copy(n).wait_send()

    def signal(self, barrier):
        for target in self.to:
            pl.semaphore_signal(
                barrier, inc=1, device_id={"ctx": self.me + target}, device_id_type=MESH
            )


class MidSum:
    def __init__(self, mid, land, out, send, recv):
        me = lax.axis_index("ctx")
        x, y = (me // 2) % 2, me // 4
        self.me, self.mid, self.land, self.out, self.send, self.recv = me, mid, land, out, send, recv
        self.eighth, self.last = mid.shape[0] // 2, mid.shape[0] // 4
        self.bit = (y, x)
        self.to = (4 - 8 * y, 2 - 4 * x)

    def copy(self, n):
        i = n % 2
        keep = i * self.eighth + self.bit[i] * self.last
        give = i * self.eighth + (1 - self.bit[i]) * self.last
        if n < 2:
            src = self.mid.at[pl.ds(pl.multiple_of(give, 16), self.last)]
            dst = self.land.at[pl.ds(i * self.last, self.last)]
        else:
            src = dst = self.out.at[pl.ds(pl.multiple_of(keep, 16), self.last)]
        return pltpu.make_async_remote_copy(
            src_ref=src, dst_ref=dst, send_sem=self.send.at[n], recv_sem=self.recv.at[n],
            device_id={"ctx": self.me + self.to[i]}, device_id_type=MESH,
        )

    def begin(self):
        for i in range(2):
            self.copy(i).start()

    def turn(self):
        for i in range(2):
            self.copy(i).wait_recv()
            keep = i * self.eighth + self.bit[i] * self.last
            rows = pl.ds(pl.multiple_of(keep, 16), self.last)
            landed = self.land[i * self.last : (i + 1) * self.last, :]
            self.out[rows, :] = (
                self.mid[rows, :].astype(F32) + landed.astype(F32)
            ).astype(BF16)
            self.copy(2 + i).start()

    def finish(self):
        for i in range(2):
            self.copy(2 + i).wait_recv()
        for n in range(4):
            self.copy(n).wait_send()


class LastGather:
    def __init__(self, mid, out, send, recv, local):
        me = lax.axis_index("ctx")
        x, y = (me // 2) % 2, me // 4
        self.me, self.mid, self.out = me, mid, out
        self.send, self.recv, self.local = send, recv, local
        self.eighth = mid.shape[0] // 2
        self.start_at = (x * self.eighth, (2 + y) * self.eighth)
        self.to = (2 - 4 * x, 4 - 8 * y)

    def ends(self, i):
        src = self.mid.at[pl.ds(i * self.eighth, self.eighth)]
        return src, self.out.at[pl.ds(pl.multiple_of(self.start_at[i], 16), self.eighth)]

    def copy(self, i):
        src, dst = self.ends(i)
        return pltpu.make_async_remote_copy(
            src_ref=src, dst_ref=dst, send_sem=self.send.at[i], recv_sem=self.recv.at[i],
            device_id={"ctx": self.me + self.to[i]}, device_id_type=MESH,
        )

    def keep(self, i):
        src, dst = self.ends(i)
        return pltpu.make_async_copy(src, dst, self.local.at[i])

    def begin(self):
        for i in range(2):
            self.copy(i).start()
            self.keep(i).start()

    def finish(self):
        for i in range(2):
            self.copy(i).wait()
            self.keep(i).wait()


def sum_scratch(shape):
    return [
        pltpu.VMEM((shape[0] // 2, shape[1]), BF16),
        pltpu.VMEM((shape[0] // 2 + 3 * (shape[0] // 8), shape[1]), BF16),
        pltpu.SemaphoreType.DMA((SUM_SENDS,)),
        pltpu.SemaphoreType.DMA((SUM_SENDS,)),
        pltpu.SemaphoreType.DMA((1,)),
    ]


def join_kernel(count, core_ref, *refs):
    for own_ref, far_ref, out_ref in zip(refs[:count], refs[count : 2 * count], refs[2 * count :]):
        @pl.when(pl.program_id(0) == 0)
        def _():
            out_ref[...] = own_ref[...].astype(F32)

        @pl.when(pl.program_id(0) == 1)
        def _():
            out_ref[...] = far_ref[...].astype(F32)


def join(core, own, far):
    steps = 4
    block = lambda half, at: pl.BlockSpec((half.shape[0] // steps, half.shape[1]), at)
    first = lambda h, b, s: (jnp.where(h == 0, b, steps - 1), 0)
    second = lambda h, b, s: (jnp.where(h == 0, 0, b), 0)
    target = lambda h, b, s: (jnp.where(h == 0, s[0], 1 - s[0]) * steps + b, 0)
    size = sum(half.shape[0] * half.shape[1] for half in own)
    return pl.pallas_call(
        functools.partial(join_kernel, len(own)),
        grid_spec=pltpu.PrefetchScalarGridSpec(
            num_scalar_prefetch=1,
            grid=(2, steps),
            in_specs=[block(half, first) for half in own] + [block(half, second) for half in own],
            out_specs=[block(half, target) for half in own],
        ),
        out_shape=[
            jax.ShapeDtypeStruct((2 * half.shape[0], half.shape[1]), F32) for half in own
        ],
        compiler_params=params(56),
        cost_estimate=cost(2 * size, 12 * size),
        name="join",
    )(core, *own, *far)


def hidden_scores(scores, key_block, query_block, rows, begin):
    key_place = lax.broadcasted_iota(jnp.int32, scores.shape, 0) + key_block * rows
    query_place = lax.broadcasted_iota(jnp.int32, scores.shape, 1) + query_block * rows
    return jnp.where((key_place <= query_place) & (key_place >= begin), scores, NEG)


def attend_far_kernel(
    heads, n, q_ref, own_ref, begin_ref, cot_ref, w_ref,
    raw_ref, mixed_ref, lse_ref, keep_ref, full_ref, part_ref,
    pair_ref, high_ref, total_ref, acc_ref, s_ref, send, recv, zsend, zrecv, keep_sem,
):
    rows = q_ref.shape[0]
    span = heads * HD
    shard = cot_ref.shape[1]
    at = lax.axis_index("tp")
    cube = Cube(pair_ref, send, recv)
    me = cube.me
    barrier = pltpu.get_barrier_semaphore()
    cube.signal(barrier)

    @pl.when(at > 0)
    def _():
        pl.semaphore_signal(barrier, inc=1, device_id={"tp": at - 1}, device_id_type=MESH)

    @pl.when(at < n - 1)
    def _():
        pl.semaphore_signal(barrier, inc=1, device_id={"tp": at + 1}, device_id_type=MESH)

    pair_ref[pl.ds(pl.multiple_of(me * rows, 16), rows), :] = own_ref[...]
    full_ref[:, pl.ds(pl.multiple_of(at * shard, 128), shard)] = cot_ref[...]
    high_ref[...] = jnp.full_like(high_ref, NEG)
    total_ref[...] = jnp.zeros_like(total_ref)
    acc_ref[...] = jnp.zeros_like(acc_ref)
    pl.semaphore_wait(barrier, jnp.where((at > 0) & (at < n - 1), 5, 4))

    def pass_on(right, s, k):
        place = full_ref.at[:, pl.ds(pl.multiple_of(s * shard, 128), shard)]
        which = (1 if right else 0, k)
        return pltpu.make_async_remote_copy(
            src_ref=place, dst_ref=place, send_sem=zsend.at[which], recv_sem=zrecv.at[which],
            device_id={"tp": at + 1 if right else at - 1}, device_id_type=MESH,
        )

    def line_step(k):
        @pl.when(at >= k)
        def _():
            if k > 0:
                pass_on(True, at - k, k - 1).wait_recv()

            @pl.when(at < n - 1)
            def _():
                pass_on(True, at - k, k).start()

        @pl.when(at + k < n)
        def _():
            if k > 0:
                pass_on(False, at + k, k - 1).wait_recv()

            @pl.when(at > 0)
            def _():
                pass_on(False, at + k, k).start()

    def keep(step):
        place = pl.ds(pl.multiple_of(cube.block(step) * rows, 16), rows)
        return pltpu.make_async_copy(pair_ref.at[place], keep_ref.at[place], keep_sem.at[step])

    def turn(step, carry):
        cube.advance(step)
        keep(step).start()
        for k in range(n):
            @pl.when(step == min(k * 2, CUBE - 1 - (n - 1 - k)) if n <= CUBE else k)
            def _():
                line_step(k)
        block = cube.block(step)

        @pl.when(block <= me)
        def _():
            place = pl.ds(pl.multiple_of(block * rows, 16), rows)

            def score(h):
                hs = slice(h * HD, (h + 1) * HD)
                s = lax.dot_general(
                    pair_ref[place, hs], q_ref[:, hs], NT, preferred_element_type=F32
                )
                s_ref[h % 2] = hidden_scores(s, block, me, rows, begin_ref[...])

            def spread(h):
                s = s_ref[h % 2]
                old = high_ref[h : h + 1, :]
                new = jnp.maximum(old, jnp.max(s, axis=0, keepdims=True))
                high_ref[h : h + 1, :] = new
                p = jnp.exp2(s * C2 - new * C2)
                decay = jnp.exp2((old - new) * C2)
                total_ref[h : h + 1, :] = total_ref[h : h + 1, :] * decay + jnp.sum(
                    p, axis=0, keepdims=True
                )
                acc_ref[h] = acc_ref[h] * decay + lax.dot_general(
                    pair_ref[place, span + h * HD : span + (h + 1) * HD], p.astype(BF16), TN,
                    preferred_element_type=F32,
                )

            score(0)
            for h in range(heads):
                if h + 1 < heads:
                    score(h + 1)
                spread(h)

        return carry

    lax.fori_loop(0, CUBE, turn, 0)
    for h in range(heads):
        hs = slice(h * HD, (h + 1) * HD)
        out = (acc_ref[h] / total_ref[h : h + 1, :]).T
        raw_ref[:, hs] = out
        mixed_ref[:, hs] = out.astype(BF16)
    part_ref[...] = jnp.dot(
        mixed_ref[...], w_ref[...], preferred_element_type=F32
    ).astype(BF16)
    lse_ref[...] = high_ref[...] * C2 + jnp.log2(total_ref[...])

    def kept(step, carry):
        keep(step).wait()
        return carry

    lax.fori_loop(0, CUBE, kept, 0)
    cube.finish()
    for k in range(n):
        @pl.when((at >= k) & (at < n - 1))
        def _():
            pass_on(True, at - k, k).wait_send()

        @pl.when((at + k < n) & (at > 0))
        def _():
            pass_on(False, at + k, k).wait_send()


def attend_far(query, pairs, begin, cot, weight, heads, n):
    rows = query.shape[0]
    width = weight.shape[1]
    span = heads * HD
    vmem = pl.BlockSpec(memory_space=pltpu.VMEM)
    return pl.pallas_call(
        functools.partial(attend_far_kernel, heads, n),
        in_specs=[vmem] * 5,
        out_specs=[vmem] * 3 + [pl.BlockSpec(memory_space=pl.ANY)] + [vmem] * 2,
        out_shape=[
            jax.ShapeDtypeStruct((rows, span), F32),
            jax.ShapeDtypeStruct((rows, span), BF16),
            jax.ShapeDtypeStruct((heads, rows), F32),
            jax.ShapeDtypeStruct((CUBE * rows, 2 * span), BF16),
            jax.ShapeDtypeStruct((rows, n * cot.shape[1]), BF16),
            jax.ShapeDtypeStruct((rows, width), BF16),
        ],
        scratch_shapes=[
            pltpu.VMEM((CUBE * rows, 2 * span), BF16),
            pltpu.VMEM((heads, rows), F32),
            pltpu.VMEM((heads, rows), F32),
            pltpu.VMEM((heads, HD, rows), F32),
            pltpu.VMEM((2, rows, rows), F32),
            pltpu.SemaphoreType.DMA((CUBE_SENDS,)),
            pltpu.SemaphoreType.DMA((CUBE_SENDS,)),
            pltpu.SemaphoreType.DMA((2, n)),
            pltpu.SemaphoreType.DMA((2, n)),
            pltpu.SemaphoreType.DMA((CUBE,)),
        ],
        compiler_params=params(58, collective_id=2, has_side_effects=True),
        cost_estimate=cost(1e6, 1e6),
        name="attend_far",
    )(query, pairs, begin, cot, weight)


def attend_back_far_kernel(
    heads, n, g_ref, far_q_ref, far_pair_ref, begin_ref, part_ref, mid_ref,
    dq_ref, dk_ref, dv_ref, layer_ref, next_ref,
    all_ref, acc_ref, rows_ref, s_ref, p_ref, land_ref, pair_ref, q_ref,
    send, recv, zsend, zrecv, read_sem, mid_land, msend, mrecv,
):
    rows = g_ref.shape[0]
    span = heads * HD
    shard = layer_ref.shape[1]
    at = lax.axis_index("tp")
    cube = Cube(all_ref, send, recv)
    middle = MidSum(mid_ref, mid_land, next_ref, msend, mrecv)
    me = cube.me
    barrier = pltpu.get_barrier_semaphore()
    cube.signal(barrier)
    for o in range(1, n):
        pl.semaphore_signal(
            barrier, inc=1, device_id={"tp": lax.rem(at + o, n)}, device_id_type=MESH
        )

    def read(step, keys):
        place = pl.ds(pl.multiple_of(cube.block(step) * rows, 16), rows)
        far, near = (far_pair_ref, pair_ref) if keys else (far_q_ref, q_ref)
        return pltpu.make_async_copy(
            far.at[place], near.at[place], read_sem.at[0 if keys else 1, step]
        )

    def read_all(step, carry):
        block = cube.block(step)

        @pl.when(block <= me)
        def _():
            read(step, True).start()

        @pl.when(block >= me)
        def _():
            read(step, False).start()

        return carry

    lax.fori_loop(0, CUBE, read_all, 0)
    all_ref[pl.ds(pl.multiple_of(me * rows, 16), rows), :] = g_ref[...]
    acc_ref[...] = jnp.zeros_like(acc_ref)
    dk_ref[...] = jnp.zeros_like(dk_ref)
    dv_ref[...] = jnp.zeros_like(dv_ref)
    pl.semaphore_wait(barrier, 3 + n - 1)

    def term(o):
        target = lax.rem(at + o, n)
        return pltpu.make_async_remote_copy(
            src_ref=part_ref.at[:, pl.ds(pl.multiple_of(target * shard, 128), shard)],
            dst_ref=land_ref.at[o - 1],
            send_sem=zsend.at[o - 1], recv_sem=zrecv.at[o - 1],
            device_id={"tp": target}, device_id_type=MESH,
        )

    own = pl.ds(pl.multiple_of(me * rows, 16), rows)

    def turn(step, carry):
        cube.advance(step)

        @pl.when(step == 0)
        def _():
            for o in range(1, n):
                term(o).start()
            middle.begin()

        @pl.when(step == 3)
        def _():
            middle.turn()

        block = cube.block(step)
        place = pl.ds(pl.multiple_of(block * rows, 16), rows)

        @pl.when(block <= me)
        def _():
            read(step, True).wait()

        @pl.when(block >= me)
        def _():
            read(step, False).wait()

        def scores(h, key_block, key_place, query_block, query_place):
            hs = slice(h * HD, (h + 1) * HD)
            vs = slice(span + h * HD, span + (h + 1) * HD)
            s = lax.dot_general(
                pair_ref[key_place, hs], q_ref[query_place, hs], NT, preferred_element_type=F32
            )
            begin = begin_ref[pl.ds(query_block, 1), :]
            s_ref[h % 2] = hidden_scores(s, key_block, query_block, rows, begin)
            p_ref[h % 2] = lax.dot_general(
                pair_ref[key_place, vs], all_ref[query_place, hs], NT, preferred_element_type=F32
            )

        def read_rows(query_place):
            coded = all_ref[query_place, span:].astype(F32).T
            for k in range(2 * heads):
                rows_ref[k : k + 1, :] = (
                    coded[3 * k : 3 * k + 1]
                    + coded[3 * k + 1 : 3 * k + 2]
                    + coded[3 * k + 2 : 3 * k + 3]
                )

        def weights(h):
            p = jnp.exp2(s_ref[h % 2] * C2 - rows_ref[h : h + 1, :])
            ds = p * (p_ref[h % 2] - rows_ref[heads + h : heads + h + 1, :])
            return p.astype(BF16), ds.astype(BF16)

        @pl.when(block <= me)
        def _():
            read_rows(own)
            scores(0, block, place, me, own)
            for h in range(heads):
                if h + 1 < heads:
                    scores(h + 1, block, place, me, own)
                _, ds = weights(h)
                acc_ref[h] = acc_ref[h] + lax.dot_general(
                    pair_ref[place, h * HD : (h + 1) * HD], ds, TN, preferred_element_type=F32
                )

        @pl.when(block >= me)
        def _():
            read_rows(place)
            scores(0, me, own, block, place)
            for h in range(heads):
                hs = slice(h * HD, (h + 1) * HD)
                if h + 1 < heads:
                    scores(h + 1, me, own, block, place)
                p, ds = weights(h)
                dv_ref[:, hs] += jnp.dot(p, all_ref[place, hs], preferred_element_type=F32)
                dk_ref[:, hs] += jnp.dot(ds, q_ref[place, hs], preferred_element_type=F32)

        return carry

    lax.fori_loop(0, CUBE, turn, 0)
    for h in range(heads):
        dq_ref[:, h * HD : (h + 1) * HD] = (acc_ref[h] * SCALE).T
    dk_ref[...] = dk_ref[...] * SCALE
    total = part_ref[:, pl.ds(pl.multiple_of(at * shard, 128), shard)].astype(F32)
    for o in range(1, n):
        term(o).wait_recv()
        total = total + land_ref[o - 1].astype(F32)
    layer_ref[...] = total.astype(BF16)
    middle.finish()
    cube.finish()
    for o in range(1, n):
        term(o).wait_send()


def attend_back_far(grad, all_query, all_pairs, all_begin, part, mid, heads, n):
    rows = grad.shape[0]
    span = heads * HD
    shard = part.shape[1] // n
    vmem = pl.BlockSpec(memory_space=pltpu.VMEM)
    wide = jax.ShapeDtypeStruct((rows, span), F32)
    return pl.pallas_call(
        functools.partial(attend_back_far_kernel, heads, n),
        in_specs=[vmem] + [pl.BlockSpec(memory_space=pl.ANY)] * 2 + [vmem] * 3,
        out_specs=[vmem] * 5,
        out_shape=[wide, wide, wide, jax.ShapeDtypeStruct((rows, shard), BF16)]
        + [jax.ShapeDtypeStruct(mid.shape, BF16)],
        scratch_shapes=[
            pltpu.VMEM((CUBE * rows, span + HD), BF16),
            pltpu.VMEM((heads, HD, rows), F32),
            pltpu.VMEM((2 * heads, rows), F32),
            pltpu.VMEM((2, rows, rows), F32),
            pltpu.VMEM((2, rows, rows), F32),
            pltpu.VMEM((n - 1, rows, shard), BF16),
            pltpu.VMEM((CUBE * rows, 2 * span), BF16),
            pltpu.VMEM((CUBE * rows, span), BF16),
            pltpu.SemaphoreType.DMA((CUBE_SENDS,)),
            pltpu.SemaphoreType.DMA((CUBE_SENDS,)),
            pltpu.SemaphoreType.DMA((n - 1,)),
            pltpu.SemaphoreType.DMA((n - 1,)),
            pltpu.SemaphoreType.DMA((2, CUBE)),
            pltpu.VMEM((mid.shape[0] // 2, mid.shape[1]), BF16),
            pltpu.SemaphoreType.DMA((4,)),
            pltpu.SemaphoreType.DMA((4,)),
        ],
        compiler_params=params(62, collective_id=3, has_side_effects=True),
        cost_estimate=cost(1e6, 1e6),
        name="attend_back_far",
    )(grad, all_query, all_pairs, all_begin, part, mid)


def query_grad_kernel(
    heads, info, q_ref, do_ref, lse_ref, delta_ref, k_ref, v_ref, begin_ref,
    dq_ref, acc_ref, s_ref, g_ref,
):
    me, first, clear = info[0], info[1], info[2]
    j = pl.program_id(0)
    rows = q_ref.shape[0]

    @pl.when(j == 0)
    def _():
        acc_ref[...] = jnp.zeros_like(acc_ref)

    def block(hide):
        def score(h):
            hs = slice(h * HD, (h + 1) * HD)
            s = lax.dot_general(k_ref[:, hs], q_ref[:, hs], NT, preferred_element_type=F32)
            if hide:
                s = masked(s, j, me, rows, begin_ref[...])
            s_ref[h % 2] = s
            g_ref[h % 2] = lax.dot_general(
                v_ref[:, hs], do_ref[:, hs], NT, preferred_element_type=F32
            )

        def spread(h):
            hs = slice(h * HD, (h + 1) * HD)
            p = jnp.exp2(s_ref[h % 2] * C2 - lse_ref[h : h + 1, :])
            ds = (p * (g_ref[h % 2] - delta_ref[h : h + 1, :])).astype(BF16)
            acc_ref[h] = acc_ref[h] + lax.dot_general(
                k_ref[:, hs], ds, TN, preferred_element_type=F32
            )

        score(0)
        for h in range(heads):
            if h + 1 < heads:
                score(h + 1)
            spread(h)

    @pl.when((j >= clear) & (j < me))
    def _():
        block(False)

    @pl.when(((j >= first) & (j < clear) & (j < me)) | (j == me))
    def _():
        block(True)

    @pl.when(j == me)
    def _():
        for h in range(heads):
            dq_ref[:, h * HD : (h + 1) * HD] = (acc_ref[h] * SCALE).T


def query_grad(info, query, grad_mixed, lse, delta, pairs, begin, heads):
    rows = query.shape[0]
    total = pairs.shape[0]
    span = heads * HD
    full = lambda shape: pl.BlockSpec(shape, lambda j, s: (0, 0))
    key = pl.BlockSpec((rows, span), lambda j, s: (jnp.clip(j, s[1], s[0]), 0))
    value = pl.BlockSpec((rows, span), lambda j, s: (jnp.clip(j, s[1], s[0]), 1))
    wide = full((rows, span))
    thin = full((heads, rows))
    return pl.pallas_call(
        functools.partial(query_grad_kernel, heads),
        grid_spec=pltpu.PrefetchScalarGridSpec(
            num_scalar_prefetch=1,
            grid=(total // rows,),
            in_specs=[wide, wide, thin, thin, key, value, full((1, rows))],
            out_specs=wide,
            scratch_shapes=[
                pltpu.VMEM((heads, HD, rows), F32),
                pltpu.VMEM((2, rows, rows), F32),
                pltpu.VMEM((2, rows, rows), F32),
            ],
        ),
        out_shape=jax.ShapeDtypeStruct((rows, span), F32),
        compiler_params=params(58),
        cost_estimate=cost(6 * rows * total * span, 4 * total * span, rows * total * heads),
        name="query_grad",
    )(info, query, grad_mixed, lse, delta, pairs, pairs, begin)


def key_grad_kernel(
    heads, info, k_ref, v_ref, q_ref, g_ref, begin_ref, dk_ref, dv_ref,
    rows_ref, s_ref, p_ref,
):
    me, last, clear = info[0], info[1], info[2]
    j = pl.program_id(0)
    rows = k_ref.shape[0]
    span = heads * HD

    @pl.when(j == me)
    def _():
        dk_ref[...] = jnp.zeros_like(dk_ref)
        dv_ref[...] = jnp.zeros_like(dv_ref)

    def block(hide):
        coded = g_ref[:, span:].astype(F32).T
        for n in range(2 * heads):
            rows_ref[n : n + 1, :] = (
                coded[3 * n : 3 * n + 1] + coded[3 * n + 1 : 3 * n + 2] + coded[3 * n + 2 : 3 * n + 3]
            )

        def score(h):
            hs = slice(h * HD, (h + 1) * HD)
            s = lax.dot_general(k_ref[:, hs], q_ref[:, hs], NT, preferred_element_type=F32)
            if hide:
                key_place = lax.broadcasted_iota(jnp.int32, s.shape, 0) + me * rows
                query_place = lax.broadcasted_iota(jnp.int32, s.shape, 1) + j * rows
                s = jnp.where(
                    (key_place <= query_place) & (key_place >= begin_ref[...]), s, NEG
                )
            s_ref[h % 2] = s
            p_ref[h % 2] = lax.dot_general(
                v_ref[:, hs], g_ref[:, hs], NT, preferred_element_type=F32
            )

        def spread(h):
            hs = slice(h * HD, (h + 1) * HD)
            p = jnp.exp2(s_ref[h % 2] * C2 - rows_ref[h : h + 1, :])
            ds = (p * (p_ref[h % 2] - rows_ref[heads + h : heads + h + 1, :])).astype(BF16)
            dv_ref[:, hs] += jnp.dot(p.astype(BF16), g_ref[:, hs], preferred_element_type=F32)
            dk_ref[:, hs] += jnp.dot(ds, q_ref[:, hs], preferred_element_type=F32)

        score(0)
        for h in range(heads):
            if h + 1 < heads:
                score(h + 1)
            spread(h)

    @pl.when((j > me) & (j <= clear))
    def _():
        block(False)

    @pl.when((j == me) | ((j > me) & (j > clear) & (j <= last)))
    def _():
        block(True)

    @pl.when(j == pl.num_programs(0) - 1)
    def _():
        dk_ref[...] = dk_ref[...] * SCALE


def key_grad(info, pairs, all_query, all_grad, all_begin, heads):
    rows = pairs.shape[0]
    total = all_query.shape[0]
    span = heads * HD
    full = lambda shape, at=0: pl.BlockSpec(shape, lambda j, s: (0, at))
    near = lambda j, s: (jnp.clip(j, s[0], s[1]), 0)
    wide = full((rows, span))
    return pl.pallas_call(
        functools.partial(key_grad_kernel, heads),
        grid_spec=pltpu.PrefetchScalarGridSpec(
            num_scalar_prefetch=1,
            grid=(total // rows,),
            in_specs=[
                wide, full((rows, span), 1),
                pl.BlockSpec((rows, span), near),
                pl.BlockSpec((rows, span + HD), near),
                pl.BlockSpec((1, rows), lambda j, s: (0, jnp.clip(j, s[0], s[1]))),
            ],
            out_specs=[wide, wide],
            scratch_shapes=[
                pltpu.VMEM((2 * heads, rows), F32),
                pltpu.VMEM((2, rows, rows), F32),
                pltpu.VMEM((2, rows, rows), F32),
            ],
        ),
        out_shape=[jax.ShapeDtypeStruct((rows, span), F32)] * 2,
        compiler_params=params(58),
        cost_estimate=cost(8 * rows * total * span, 4 * total * span, rows * total * heads),
        name="key_grad",
    )(info, pairs, pairs, all_query, all_grad, all_begin)


def mixed_grad_kernel(heads, branch_ref, w_ref, raw_ref, lse_ref, out_ref, delta_ref):
    span = heads * HD
    low = lax.dot_general(
        branch_ref[...], w_ref[...], NT, preferred_element_type=F32
    ).astype(BF16)
    out_ref[:, :span] = low
    count = low.shape[0]
    both = low.astype(F32) * raw_ref[...]
    for h in range(heads):
        delta_ref[h : h + 1, :] = jnp.sum(both[:, h * HD : (h + 1) * HD].T, axis=0, keepdims=True)
    lines = []
    for n in range(2 * heads):
        value = lse_ref[n : n + 1, :] if n < heads else delta_ref[n - heads : n - heads + 1, :]
        for _ in range(3):
            piece = value.astype(BF16).astype(F32)
            lines.append(piece)
            value = value - piece
    lines.append(jnp.zeros((HD - len(lines), count), F32))
    out_ref[:, span:] = jnp.concatenate(lines, axis=0).T.astype(BF16)


def mixed_grad(branch, weight, raw, lse, heads):
    rows, width = branch.shape
    span = heads * HD
    block = 256
    row = lambda n: pl.BlockSpec((block, n), lambda i: (i, 0))
    line = pl.BlockSpec((heads, block), lambda i: (0, i))
    return pl.pallas_call(
        functools.partial(mixed_grad_kernel, heads),
        grid=(rows // block,),
        in_specs=[row(width), pl.BlockSpec((span, width), lambda i: (0, 0)), row(span), line],
        out_specs=[row(span + HD), line],
        out_shape=[
            jax.ShapeDtypeStruct((rows, span + HD), BF16),
            jax.ShapeDtypeStruct((heads, rows), F32),
        ],
        compiler_params=params(56),
        cost_estimate=cost(2 * rows * width * span, 2 * width * span + 4 * rows * width),
        name="mixed_grad",
    )(branch, weight, raw, lse)


def feed_kernel(
    inner_ref, cot_ref, w_ref, grad_ref, hidden_ref, dgu_ref, down_grad_ref, gu_grad_ref
):
    block = grad_ref.shape[1]
    both = jnp.dot(inner_ref[...], w_ref[...], preferred_element_type=F32)
    grad = grad_ref[...].astype(F32)
    gate, up = both[:, :block], both[:, block:]
    sigma = 1.0 / (1.0 + jnp.exp(-gate))
    active = gate * sigma
    hidden_ref[...] = (active * up).astype(BF16)
    dgu_ref[:, :block] = (grad * up * sigma * (1.0 + gate * (1.0 - sigma))).astype(BF16)
    dgu_ref[:, block:] = (grad * active).astype(BF16)
    down_grad_ref[...] = lax.dot_general(
        hidden_ref[...], cot_ref[...], TN, preferred_element_type=F32
    ).astype(BF16)
    gu_grad_ref[...] = lax.dot_general(
        inner_ref[...], dgu_ref[...], TN, preferred_element_type=F32
    ).astype(BF16)


def feed(inner, cot, weight, grad, block):
    rows, width = inner.shape
    units = grad.shape[1]
    whole = pl.BlockSpec((rows, width), lambda j: (0, 0))
    column = lambda high, wide: pl.BlockSpec((high, wide), lambda j: (0, j))
    line = pl.BlockSpec((block, width), lambda j: (j, 0))
    return pl.pallas_call(
        feed_kernel,
        grid=(units // block,),
        in_specs=[whole, whole, column(width, 2 * block), column(rows, block)],
        out_specs=[column(rows, block), column(rows, 2 * block), line, column(width, 2 * block)],
        out_shape=[
            jax.ShapeDtypeStruct((rows, units), BF16),
            jax.ShapeDtypeStruct((rows, 2 * units), BF16),
            jax.ShapeDtypeStruct((units, width), BF16),
            jax.ShapeDtypeStruct((width, 2 * units), BF16),
        ],
        compiler_params=params(60),
        cost_estimate=cost(
            12 * rows * width * units, 12 * width * units + 4 * rows * width, rows * units
        ),
        name="feed",
    )(inner, cot, weight, grad)


def weave_kernel(block, sum_ref, out_ref):
    for j in range(sum_ref.shape[1] // (2 * block)):
        for k in range(2):
            at = (2 * j + k) * block
            out_ref[:, k, j * block : (j + 1) * block] = sum_ref[:, at : at + block].astype(F32)


def weave(summed, block):
    width, both = summed.shape
    rows = 256
    return pl.pallas_call(
        functools.partial(weave_kernel, block),
        grid=(width // rows,),
        in_specs=[pl.BlockSpec((rows, both), lambda i: (i, 0))],
        out_specs=pl.BlockSpec((rows, 2, both // 2), lambda i: (i, 0, 0)),
        out_shape=jax.ShapeDtypeStruct((width, 2, both // 2), F32),
        compiler_params=params(56),
        cost_estimate=cost(width * both, 6 * width * both),
        name="weave",
    )(summed)


def widen_kernel(in_ref, out_ref):
    out_ref[...] = in_ref[...].astype(F32)


def widen(summed):
    high, wide = summed.shape
    block = pl.BlockSpec((512, wide), lambda i: (i, 0))
    return pl.pallas_call(
        widen_kernel,
        grid=(high // 512,),
        in_specs=[block],
        out_specs=block,
        out_shape=jax.ShapeDtypeStruct((high, wide), F32),
        compiler_params=params(56),
        cost_estimate=cost(high * wide, 6 * high * wide),
        name="widen",
    )(summed)


def line_barrier(at, n, cube=None):
    barrier = pltpu.get_barrier_semaphore()
    if cube is not None:
        cube.signal(barrier)

    @pl.when(at > 0)
    def _():
        pl.semaphore_signal(barrier, inc=1, device_id={"tp": at - 1}, device_id_type=MESH)

    @pl.when(at < n - 1)
    def _():
        pl.semaphore_signal(barrier, inc=1, device_id={"tp": at + 1}, device_id_type=MESH)

    near = jnp.where((at > 0) & (at < n - 1), 2, 1)
    pl.semaphore_wait(barrier, near + (0 if cube is None else 3))


def sum_rows(n, sub, part_ref, out_ref, row_fn, from_left, from_right, send, recv, aside={}):
    at = lax.axis_index("tp")
    chunks = part_ref.shape[0] // sub
    middle = (n // 2 - 1, n // 2)

    def link(kind, right, src, dst, c):
        which = (kind * 2 + (1 if right else 0), c)
        return pltpu.make_async_remote_copy(
            src_ref=src.at[pl.ds(c * sub, sub)],
            dst_ref=dst.at[pl.ds(c * sub, sub)],
            send_sem=send.at[which],
            recv_sem=recv.at[which],
            device_id={"tp": at + 1 if right else at - 1},
            device_id_type=MESH,
        )

    def came(right):
        return from_left if right else from_right

    def first(right, c):
        return link(0, right, part_ref, came(right), c)

    def onward(right, c):
        return link(0, right, came(right), came(right), c)

    def hand(right, c):
        return link(1, right, out_ref, out_ref, c)

    def reduce_step(c):
        owner = middle[c % 2]
        rows = slice(c * sub, (c + 1) * sub)
        for right in (True, False):
            edge = 0 if right else n - 1
            held = came(right)

            @pl.when(((at < owner) if right else (at > owner)) & (at != edge))
            def _():
                copy = onward(right, c)
                copy.wait_recv()
                held[rows, :] = (
                    held[rows, :].astype(F32) + part_ref[rows, :].astype(F32)
                ).astype(BF16)
                copy.start()

    def final_step(c):
        owner = middle[c % 2]
        rows = slice(c * sub, (c + 1) * sub)

        @pl.when(at == owner)
        def _():
            total = part_ref[rows, :].astype(F32)
            onward(True, c).wait_recv()
            total = total + from_left[rows, :].astype(F32)
            onward(False, c).wait_recv()
            total = total + from_right[rows, :].astype(F32)
            row_fn(total, rows)
            hand(True, c).start()
            hand(False, c).start()

    def hand_step(c):
        owner = middle[c % 2]
        for right in (True, False):
            edge = n - 1 if right else 0

            @pl.when((at > owner) if right else (at < owner))
            def _():
                copy = hand(right, c)
                copy.wait_recv()

                @pl.when(at != edge)
                def _():
                    copy.start()

    for c in range(chunks):
        @pl.when(at == 0)
        def _():
            first(True, c).start()

        @pl.when(at == n - 1)
        def _():
            first(False, c).start()

    for c in range(chunks + 4):
        for piece in aside.get(c, ()):
            piece()
        if c < chunks:
            reduce_step(c)
        if 2 <= c < chunks + 2:
            final_step(c - 2)
        if c >= 4:
            hand_step(c - 4)
    for c in range(chunks):
        owner = middle[c % 2]

        @pl.when(at < owner)
        def _():
            first(True, c).wait_send()

        @pl.when(at > owner)
        def _():
            first(False, c).wait_send()

        @pl.when((at >= owner) & (at < n - 1))
        def _():
            hand(True, c).wait_send()

        @pl.when((at <= owner) & (at > 0))
        def _():
            hand(False, c).wait_send()


def merge_kernel(
    n, sub, part_ref, tok_ref, far_cot, far_down, inner_ref, resid_out, stat_ref, hidden_ref,
    from_left, from_right, send, recv, cot_ref, down_ref, resid_ref, read_sem, keep_sem,
):
    reads = (
        pltpu.make_async_copy(far_cot, cot_ref, read_sem.at[0]),
        pltpu.make_async_copy(far_down, down_ref, read_sem.at[1]),
    )
    for read in reads:
        read.start()
    line_barrier(lax.axis_index("tp"), n)
    stat_ref[...] = jnp.zeros_like(stat_ref)

    def keep(rows):
        slot = rows.start // (2 * sub)
        held = resid_ref.at[pl.ds(slot * sub, sub)]
        return pltpu.make_async_copy(
            held, resid_out.at[pl.ds(rows.start, sub)], keep_sem.at[slot]
        )

    def row_fn(total, rows):
        x = tok_ref[rows, :].astype(F32) + total
        mean = jnp.mean(x, axis=1, keepdims=True)
        center = x - mean
        inverse = lax.rsqrt(jnp.mean(center * center, axis=1, keepdims=True) + EPS)
        slot = rows.start // (2 * sub)
        resid_ref[slot * sub : (slot + 1) * sub, :] = x
        keep(rows).start()
        stat_ref[rows, :] = jnp.concatenate([mean, inverse], axis=1)
        inner_ref[rows, :] = (center * inverse).astype(BF16)

    def piece(at):
        if at == 0:
            for read in reads:
                read.wait()
        hidden_ref[:, at : at + 256] = lax.dot_general(
            cot_ref[...], down_ref[at : at + 256, :], NT, preferred_element_type=F32
        ).astype(BF16)

    aside = {}
    for k in range(down_ref.shape[0] // 256):
        aside[1 + 2 * k] = (functools.partial(piece, k * 256),)
    sum_rows(n, sub, part_ref, inner_ref, row_fn, from_left, from_right, send, recv, aside)
    for c in range(part_ref.shape[0] // sub):
        @pl.when(lax.axis_index("tp") == n // 2 - 1 + c % 2)
        def _():
            keep(slice(c * sub, (c + 1) * sub)).wait()


def merge(part, tok_full, cot_full, down, n):
    rows, width = part.shape
    sub = SUB
    vmem = pl.BlockSpec(memory_space=pltpu.VMEM)
    far = pl.BlockSpec(memory_space=pl.ANY)
    return pl.pallas_call(
        functools.partial(merge_kernel, n, sub),
        in_specs=[vmem, vmem, far, far],
        out_specs=[vmem, far, vmem, vmem],
        out_shape=[
            jax.ShapeDtypeStruct((rows, width), BF16),
            jax.ShapeDtypeStruct((rows, width), F32),
            jax.ShapeDtypeStruct((rows, 2), F32),
            jax.ShapeDtypeStruct((rows, down.shape[0]), BF16),
        ],
        scratch_shapes=[pltpu.VMEM((rows, width), BF16)] * 2
        + [pltpu.SemaphoreType.DMA((4, rows // sub))] * 2
        + [
            pltpu.VMEM((rows, width), BF16),
            pltpu.VMEM(down.shape, BF16),
            pltpu.VMEM((rows // 2, width), F32),
            pltpu.SemaphoreType.DMA((2,)),
            pltpu.SemaphoreType.DMA((rows // (2 * sub),)),
        ],
        compiler_params=params(56, collective_id=5, has_side_effects=True),
        cost_estimate=cost(1e6, 1e6),
        name="merge",
    )(part, tok_full, cot_full, down)


def norm_back_kernel(
    n, sub, cube, part_ref, cot_ref, stat_ref, *refs
):
    total = None
    far, refs = refs[:3], refs[3:]
    if cube:
        own, out_ref, layer_ref, mid, from_left, from_right, send, recv = refs[:8]
        resid_ref, hidden_ref, down_ref, read_sem = refs[8:12]
        total = CubeSum(own, *refs[12:17], mid=mid)
    else:
        out_ref, layer_ref, from_left, from_right, send, recv = refs[:6]
        resid_ref, hidden_ref, down_ref, read_sem = refs[6:10]
    reads = [
        pltpu.make_async_copy(source, held, read_sem.at[k])
        for k, (source, held) in enumerate(zip(far, (resid_ref, hidden_ref, down_ref)))
    ]
    for read in reads:
        read.start()
    at = lax.axis_index("tp")
    line_barrier(lax.axis_index("tp"), n, total)
    aside = {}

    def piece(start):
        if start == 0:
            for read in reads:
                read.wait()
        cols = slice(start, start + 256)
        row = lax.broadcasted_iota(jnp.int32, (part_ref.shape[0], 256), 0)
        owned = (row // sub) % 2 == at - (n // 2 - 1)
        layer_ref[:, cols] = (
            jnp.where(owned, resid_ref[:, cols], 0.0)
            + jnp.dot(hidden_ref[...], down_ref[:, cols], preferred_element_type=F32)
        ).astype(BF16)

    for k in range(down_ref.shape[1] // 256):
        aside[1 + 2 * k] = (functools.partial(piece, k * 256),)
    if cube:
        total.begin()
        for k, c in enumerate((6, 8, 10, 12)):
            aside[c] = (functools.partial(total.reduce, k),)

    def row_fn(summed, rows):
        inverse = stat_ref[rows, 1:2]
        normed = (resid_ref[rows, :] - stat_ref[rows, 0:1]) * inverse
        mean = jnp.mean(summed, axis=1, keepdims=True)
        inner = jnp.mean(summed * normed, axis=1, keepdims=True)
        out = cot_ref[rows, :].astype(F32) + inverse * (summed - mean - normed * inner)
        out_ref[rows, :] = out.astype(BF16)

    sum_rows(n, sub, part_ref, out_ref, row_fn, from_left, from_right, send, recv, aside)
    if cube:
        total.reduce(4)
        total.reduce(5)
        total.finish()


def norm_back(part, cot, resid, stat, hidden, down, n, grads):
    rows, width = part.shape
    sub = SUB
    vmem = pl.BlockSpec(memory_space=pltpu.VMEM)
    far = pl.BlockSpec(memory_space=pl.ANY)
    extra = []
    for grad in grads:
        extra += sum_scratch(grad.shape)
    return pl.pallas_call(
        functools.partial(norm_back_kernel, n, sub, len(grads) > 0),
        in_specs=[vmem] * 3 + [far] * (3 + len(grads)),
        out_specs=[vmem] * (2 + len(grads)),
        out_shape=[jax.ShapeDtypeStruct((rows, width), BF16)] * 2
        + [jax.ShapeDtypeStruct((grad.shape[0] // 4, grad.shape[1]), BF16) for grad in grads],
        scratch_shapes=[pltpu.VMEM((rows, width), BF16)] * 2
        + [pltpu.SemaphoreType.DMA((4, rows // sub))] * 2
        + [
            pltpu.VMEM(resid.shape, F32),
            pltpu.VMEM(hidden.shape, BF16),
            pltpu.VMEM(down.shape, BF16),
            pltpu.SemaphoreType.DMA((3,)),
        ]
        + extra,
        compiler_params=params(60, collective_id=1, has_side_effects=True),
        cost_estimate=cost(1e6, 1e6),
        name="norm_back",
    )(part, cot, stat, resid, hidden, down, *grads)


def unrotate_kernel(
    heads, dq_ref, dk_ref, dv_ref, cos_ref, sin_ref, inner_ref, dproj_ref, grad_ref
):
    def back(ref):
        for h in range(heads):
            hs = slice(h * HD, (h + 1) * HD)
            piece = ref[:, hs]
            dproj_ref[:, hs] = (
                piece * cos_ref[...] - pltpu.roll(piece, HD // 2, 1) * sin_ref[...]
            ).astype(BF16)

    part = pl.program_id(0)

    @pl.when(part == 0)
    def _():
        back(dq_ref)

    @pl.when(part == 1)
    def _():
        back(dk_ref)

    @pl.when(part == 2)
    def _():
        dproj_ref[...] = dv_ref[...].astype(BF16)

    grad_ref[...] = lax.dot_general(
        inner_ref[...], dproj_ref[...], TN, preferred_element_type=F32
    ).astype(BF16)


def unrotate(dq, dk, dv, cosine, sine, inner, heads):
    rows, span = dq.shape
    width = inner.shape[1]
    whole = lambda n: pl.BlockSpec((rows, n), lambda i: (0, 0))
    return pl.pallas_call(
        functools.partial(unrotate_kernel, heads),
        grid=(3,),
        in_specs=[whole(span)] * 3 + [whole(HD)] * 2 + [whole(width)],
        out_specs=[
            pl.BlockSpec((rows, span), lambda i: (0, i)),
            pl.BlockSpec((width, span), lambda i: (i, 0)),
        ],
        out_shape=[
            jax.ShapeDtypeStruct((rows, 3 * span), BF16),
            jax.ShapeDtypeStruct((3 * width, span), BF16),
        ],
        compiler_params=params(56),
        cost_estimate=cost(6 * rows * span * width, 12 * rows * span + 6 * width * span),
        name="unrotate",
    )(dq, dk, dv, cosine, sine, inner)


def unproject_kernel(heads, n, cube, dproj_ref, tok_ref, stat_ref, w_ref, branch_ref, *refs):
    sums, rest = [], None
    if cube:
        in_ref, og_ref, mid_ref, out_ref, in_out, og_out, down_out = refs[:7]
        part_ref, mine_ref, land_ref, sums_ref, far_ref, send, recv, ssend, srecv = refs[7:16]
        for own, out, at in ((in_ref, in_out, 18), (og_ref, og_out, 23)):
            sums.append(CubeSum(own, *refs[at : at + 5], out=out))
        rest = LastGather(mid_ref, down_out, *refs[28:31])
        mine_branch, branch_sem = refs[16:18]
    else:
        out_ref, part_ref, mine_ref, land_ref, sums_ref, far_ref = refs[:6]
        send, recv, ssend, srecv, mine_branch, branch_sem = refs[6:12]

    def reduce(*pieces):
        for k in pieces:
            for item in sums:
                item.reduce(k)

    def gather(k):
        for item in sums:
            item.gather(k)

    rows, width = tok_ref.shape
    shard = width // n
    span = heads * HD
    at = lax.axis_index("tp")
    barrier = pltpu.get_barrier_semaphore()
    for o in range(1, n):
        pl.semaphore_signal(
            barrier, inc=1, device_id={"tp": lax.rem(at + o, n)}, device_id_type=MESH
        )
    if cube:
        sums[0].signal(barrier)
    pl.semaphore_wait(barrier, n - 1 + (3 if cube else 0))
    for item in sums:
        item.begin()
    if cube:
        rest.begin()
    block = 256
    count = rows // block

    def term(o, i):
        target = lax.rem(at + o, n)
        place = pl.ds(i * block, block)
        return pltpu.make_async_remote_copy(
            src_ref=part_ref.at[place, pl.ds(pl.multiple_of(target * shard, 128), shard)],
            dst_ref=land_ref.at[o - 1, place],
            send_sem=send.at[o - 1, i], recv_sem=recv.at[o - 1, i],
            device_id={"tp": target}, device_id_type=MESH,
        )

    def totals(o):
        return pltpu.make_async_remote_copy(
            src_ref=sums_ref, dst_ref=far_ref.at[o - 1],
            send_sem=ssend.at[o - 1], recv_sem=srecv.at[o - 1],
            device_id={"tp": lax.rem(at + o, n)}, device_id_type=MESH,
        )

    own = pl.ds(pl.multiple_of(at * shard, 128), shard)
    branch_read = pltpu.make_async_copy(branch_ref.at[:, own], mine_branch, branch_sem.at[0])
    branch_read.start()
    for i in range(count):
        place = pl.ds(i * block, block)
        total = None
        for part in range(3):
            piece = lax.dot_general(
                dproj_ref[place, part * span : (part + 1) * span], w_ref[part], NT,
                preferred_element_type=F32,
            )
            total = piece if total is None else total + piece
        part_ref[place, :] = total.astype(BF16)
        for o in range(1, n):
            term(o, i).start()
        normed = (tok_ref[place, :].astype(F32) - stat_ref[place, 0:1]) * stat_ref[place, 1:2]
        first = jnp.sum(total, axis=1, keepdims=True)
        second = jnp.sum(total * normed, axis=1, keepdims=True)
        lane = lax.broadcasted_iota(jnp.int32, (block, HD), 1)
        both = jnp.where(lane == 0, first, jnp.where(lane == 1, second, 0.0))
        sums_ref[:, i * block : (i + 1) * block] = both.T[:8]
    for o in range(1, n):
        totals(o).start()
    reduce(0, 1, 2, 3, 4, 5, 6, 7)
    gather(0)
    gather(1)
    total = sums_ref[...]
    for o in range(1, n):
        totals(o).wait_recv()
        total = total + far_ref[o - 1]
    mine_ref[...] = total
    branch_read.wait()
    for i in range(count):
        place = pl.ds(i * block, block)
        spread = jnp.concatenate(
            [mine_ref[:, i * block : (i + 1) * block], jnp.zeros((HD - 8, block), F32)], axis=0
        ).T / width
        total = part_ref[place, own].astype(F32)
        for o in range(1, n):
            term(o, i).wait_recv()
            total = total + land_ref[o - 1, place].astype(F32)
        inverse = stat_ref[place, 1:2]
        normed = (tok_ref[place, own].astype(F32) - stat_ref[place, 0:1]) * inverse
        out_ref[place, :] = mine_branch[place, :].astype(F32) + inverse * (
            total - spread[:, 0:1] - normed * spread[:, 1:2]
        )
    gather(2)
    for item in sums + ([rest] if cube else []):
        item.finish()
    for o in range(1, n):
        totals(o).wait_send()
        for i in range(count):
            term(o, i).wait_send()


def unproject(dproj, tok_full, stat, weight, branch, heads, n, grads, mids):
    rows, width = tok_full.shape
    shard = width // n
    vmem = pl.BlockSpec(memory_space=pltpu.VMEM)
    extra = []
    for grad in grads:
        extra += sum_scratch(grad.shape)
    for _ in mids:
        extra += [pltpu.SemaphoreType.DMA((2,))] * 3
    return pl.pallas_call(
        functools.partial(unproject_kernel, heads, n, len(grads) > 0),
        in_specs=[vmem] * 4
        + [pl.BlockSpec(memory_space=pl.ANY)] * (1 + len(grads))
        + [vmem] * len(mids),
        out_specs=[vmem] * (1 + len(grads)) + [pl.BlockSpec(memory_space=pl.ANY)] * len(mids),
        out_shape=[jax.ShapeDtypeStruct((rows, shard), F32)]
        + [jax.ShapeDtypeStruct((grad.shape[0] // 2, grad.shape[1]), BF16) for grad in grads]
        + [jax.ShapeDtypeStruct((2 * mid.shape[0], mid.shape[1]), BF16) for mid in mids],
        scratch_shapes=[
            pltpu.VMEM((rows, width), BF16),
            pltpu.VMEM((8, rows), F32),
            pltpu.VMEM((n - 1, rows, shard), BF16),
            pltpu.VMEM((8, rows), F32),
            pltpu.VMEM((n - 1, 8, rows), F32),
            pltpu.SemaphoreType.DMA((n - 1, rows // 256)),
            pltpu.SemaphoreType.DMA((n - 1, rows // 256)),
            pltpu.SemaphoreType.DMA((n - 1,)),
            pltpu.SemaphoreType.DMA((n - 1,)),
            pltpu.VMEM((rows, shard), BF16),
            pltpu.SemaphoreType.DMA((1,)),
        ]
        + extra,
        compiler_params=params(60, collective_id=4, has_side_effects=True),
        cost_estimate=cost(1e6, 1e6),
        name="unproject",
    )(dproj, tok_full, stat, weight, branch, *grads, *mids)


def per_device(tokens, segment_ids, in_weight, out_weight, gate_up_weight, down_weight, cotangent):
    rows = tokens.shape[0]
    width = in_weight.shape[0]
    span = in_weight.shape[2]
    heads = span // HD
    hidden_local = down_weight.shape[0]
    me = lax.axis_index("ctx")
    tp_size = lax.axis_size("tp")
    cube = lax.axis_size("ctx") == CUBE

    def gather(local, axis=1):
        return lax.all_gather(local, "tp", axis=axis, tiled=True)

    places = me * rows + jnp.arange(rows, dtype=jnp.int32)
    cosine, sine = rope_tables(places)
    in_w = jnp.transpose(in_weight, (1, 0, 2))
    gu_w = jnp.transpose(
        gate_up_weight.reshape(width, 2, hidden_local // BLOCK, BLOCK), (0, 2, 1, 3)
    )
    gu_w = gu_w.reshape(width, 2 * hidden_local)

    all_seg = lax.all_gather(segment_ids, "ctx", axis=0, tiled=True)
    count = all_seg.shape[0]
    every = jnp.arange(count, dtype=jnp.int32)
    opens = jnp.concatenate([jnp.ones((1,), jnp.bool_), all_seg[1:] != all_seg[:-1]])
    all_begin = lax.cummax(jnp.where(opens, every, 0))
    blocks = all_begin.reshape(count // rows, rows)

    tok_full, gu_w, blocks, all_begin = lax.optimization_barrier(
        (gather(tokens), gu_w, blocks, all_begin)
    )
    key_info = jnp.stack(
        [me, blocks[me, 0] // rows, (blocks[me, rows - 1] + rows - 1) // rows]
    ).astype(jnp.int32)
    query_info = jnp.stack(
        [
            me,
            jnp.sum((blocks[:, 0] < (me + 1) * rows).astype(jnp.int32)) - 1,
            jnp.sum((blocks[:, rows - 1] <= me * rows).astype(jnp.int32)) - 1,
        ]
    ).astype(jnp.int32)
    begin = lax.dynamic_slice_in_dim(blocks, me, 1, 0)
    all_begin = all_begin[None, :]
    inner1, stat1, query, pairs = project(tok_full, in_w, cosine, sine, heads)
    if cube:
        raw, mixed, lse, all_pairs, cot_full, out_part = attend_far(
            query, pairs, begin, cotangent, out_weight, heads, tp_size
        )
    else:
        all_pairs = lax.all_gather(pairs, "ctx", axis=0, tiled=True)
        cot_full = gather(cotangent)
        raw, mixed, lse = attend(key_info, query, all_pairs, begin, heads)
        out_part = jnp.dot(mixed, out_weight, preferred_element_type=F32).astype(BF16)
    late_query, mixed = lax.optimization_barrier((query, mixed))
    all_query = lax.all_gather(late_query, "ctx", axis=0, tiled=True)
    inner2, resid1, stat2, grad_hidden = merge(
        out_part, tok_full, cot_full, down_weight, tp_size
    )

    hidden, grad_gu, down_grad, gu_grad = feed(inner2, cot_full, gu_w, grad_hidden, BLOCK)
    down_grad, gu_grad, all_query, grad_gu, hidden = lax.optimization_barrier(
        (down_grad, gu_grad, all_query, grad_gu, hidden)
    )
    if not cube:
        down_grad = lax.psum(down_grad, "ctx")
    gu_grad = lax.optimization_barrier(lax.psum(gu_grad, "ctx"))

    grad_part = lax.dot_general(grad_gu, gu_w, NT, preferred_element_type=F32).astype(BF16)
    branch_grad, branch, *mids = norm_back(
        grad_part, cot_full, resid1, stat2, hidden, down_weight, tp_size,
        [down_grad] if cube else [],
    )
    out_grad = lax.dot_general(mixed, branch_grad, TN, preferred_element_type=F32).astype(BF16)
    grad_mixed, delta = mixed_grad(branch_grad, out_weight, raw, lse, heads)
    if cube:
        dq, dk, dv, layer_out, mid = attend_back_far(
            grad_mixed, all_query, all_pairs, blocks, branch, mids[0], heads, tp_size
        )
    else:
        branch = lax.psum_scatter(branch, "tp", scatter_dimension=1, tiled=True)
        layer_out = branch
        all_grad = lax.all_gather(grad_mixed, "ctx", axis=0, tiled=True)
        dq = query_grad(key_info, query, grad_mixed, lse, delta, all_pairs, begin, heads)
        dk, dv = key_grad(query_info, pairs, all_query, all_grad, all_begin, heads)

    dproj, in_grad = unrotate(dq, dk, dv, cosine, sine, inner1, heads)
    if cube:
        tokens_grad, *halves = unproject(
            dproj, tok_full, stat1, in_w, branch_grad, heads, tp_size, [in_grad, out_grad], [mid]
        )
        swap = [(i, i + 1 - 2 * (i % 2)) for i in range(CUBE)]
        core = (me % 2)[None]
        far = [lax.ppermute(half, "ctx", swap) for half in halves]
        *far, gu_grad = lax.optimization_barrier((*far, weave(gu_grad, BLOCK)))
        in_grad, out_grad, down_grad = join(core, halves, far)
    else:
        in_grad, out_grad, down_grad, gu_grad = lax.optimization_barrier(
            (in_grad, out_grad, down_grad, gu_grad)
        )
        in_grad, out_grad = lax.psum((in_grad, out_grad), "ctx")
        (tokens_grad,) = unproject(
            dproj, tok_full, stat1, in_w, branch_grad, heads, tp_size, [], []
        )
        in_grad, out_grad, down_grad = widen(in_grad), out_grad.astype(F32), widen(down_grad)
        gu_grad = weave(gu_grad, BLOCK)
    return (
        layer_out,
        tokens_grad,
        jnp.transpose(in_grad.reshape(3, width, span), (1, 0, 2)),
        out_grad,
        gu_grad,
        down_grad,
    )


def solution(mesh):
    placed = (
        P("ctx", "tp"),
        P("ctx"),
        P(None, None, "tp"),
        P("tp", None),
        P(None, None, "tp"),
        P("tp", None),
        P("ctx", "tp"),
    )
    return jax.shard_map(
        per_device,
        mesh=mesh,
        in_specs=placed,
        out_specs=(
            P("ctx", "tp"),
            P("ctx", "tp"),
            P(None, None, "tp"),
            P("tp", None),
            P(None, None, "tp"),
            P("tp", None),
        ),
        check_vma=False,
    )
```

```python
import functools

import jax
import jax.numpy as jnp
from jax import lax
from jax.experimental import pallas as pl
from jax.experimental.pallas import tpu as pltpu
from jax.sharding import PartitionSpec as P

HD = 128
EPS = 1e-05
NEG = -1e30
SCALE = HD ** (-0.5)
LOG2E = 1.4426950408889634
C2 = SCALE * LOG2E
F32 = jnp.float32
BF16 = jnp.bfloat16
NT = (((1,), (1,)), ((), ()))
TN = (((0,), (0,)), ((), ()))
MESH = pl.DeviceIdType.MESH
BLOCK = 512
SUB = 32


def params(mib, **more):
    return pltpu.CompilerParams(vmem_limit_bytes=mib << 20, **more)


def cost(flops, nbytes, trans=0):
    return pl.CostEstimate(flops=int(flops), bytes_accessed=int(nbytes), transcendentals=int(trans))


def rope_tables(places):
    half = HD // 2
    freq = 10000.0 ** (-jnp.arange(half, dtype=F32) * 2.0 / HD)
    angle = places.astype(F32)[:, None] * freq[None, :]
    cosine, sine = jnp.cos(angle), jnp.sin(angle)
    return jnp.concatenate([cosine, cosine], axis=1), jnp.concatenate([-sine, sine], axis=1)


def project_kernel(heads, tok_ref, w_ref, cos_ref, sin_ref, inner_ref, stat_ref, q_ref, kv_ref):
    x = tok_ref[...].astype(F32)
    center = x - jnp.mean(x, axis=1, keepdims=True)
    inverse = lax.rsqrt(jnp.mean(center * center, axis=1, keepdims=True) + EPS)
    inner = (center * inverse).astype(BF16)
    inner_ref[...] = inner
    stat_ref[...] = jnp.concatenate(
        [jnp.mean(x, axis=1, keepdims=True), inverse], axis=1
    )
    cosine, sine = cos_ref[...], sin_ref[...]
    span = heads * HD
    for part in range(3):
        out = jnp.dot(inner, w_ref[part], preferred_element_type=F32)
        if part == 2:
            kv_ref[:, span:] = out.astype(BF16)
            continue
        for h in range(heads):
            piece = out[:, h * HD : (h + 1) * HD]
            turned = (piece * cosine + pltpu.roll(piece, HD // 2, 1) * sine).astype(BF16)
            if part == 0:
                q_ref[:, h * HD : (h + 1) * HD] = turned
            else:
                kv_ref[:, h * HD : (h + 1) * HD] = turned


def project(tok_full, weight, cosine, sine, heads):
    rows, width = tok_full.shape
    span = heads * HD
    block = 256
    row = lambda n: pl.BlockSpec((block, n), lambda i: (i, 0))
    return pl.pallas_call(
        functools.partial(project_kernel, heads),
        grid=(rows // block,),
        in_specs=[
            row(width),
            pl.BlockSpec((3, width, span), lambda i: (0, 0, 0)),
            row(HD),
            row(HD),
        ],
        out_specs=[row(width), row(2), row(span), row(2 * span)],
        out_shape=[
            jax.ShapeDtypeStruct((rows, width), BF16),
            jax.ShapeDtypeStruct((rows, 2), F32),
            jax.ShapeDtypeStruct((rows, span), BF16),
            jax.ShapeDtypeStruct((rows, 2 * span), BF16),
        ],
        compiler_params=params(56),
        cost_estimate=cost(6 * rows * width * span, 6 * width * span + 6 * rows * width),
        name="project",
    )(tok_full, weight, cosine, sine)


def masked(scores, j, me, rows, begin):
    key_place = lax.broadcasted_iota(jnp.int32, scores.shape, 0) + j * rows
    query_place = lax.broadcasted_iota(jnp.int32, scores.shape, 1) + me * rows
    return jnp.where((key_place <= query_place) & (key_place >= begin), scores, NEG)


def attend_kernel(
    heads, info, q_ref, k_ref, v_ref, begin_ref, raw_ref, mixed_ref, lse_ref,
    high_ref, total_ref, acc_ref, s_ref,
):
    me, first, clear = info[0], info[1], info[2]
    j = pl.program_id(0)
    rows = q_ref.shape[0]

    @pl.when(j == 0)
    def _():
        high_ref[...] = jnp.full_like(high_ref, NEG)
        total_ref[...] = jnp.zeros_like(total_ref)
        acc_ref[...] = jnp.zeros_like(acc_ref)

    def block(hide):
        def score(h):
            hs = slice(h * HD, (h + 1) * HD)
            s = lax.dot_general(k_ref[:, hs], q_ref[:, hs], NT, preferred_element_type=F32)
            if hide:
                s = masked(s, j, me, rows, begin_ref[...])
            s_ref[h % 2] = s

        def spread(h):
            hs = slice(h * HD, (h + 1) * HD)
            s = s_ref[h % 2]
            old = high_ref[h : h + 1, :]
            new = jnp.maximum(old, jnp.max(s, axis=0, keepdims=True))
            high_ref[h : h + 1, :] = new
            p = jnp.exp2(s * C2 - new * C2)
            decay = jnp.exp2((old - new) * C2)
            total_ref[h : h + 1, :] = total_ref[h : h + 1, :] * decay + jnp.sum(
                p, axis=0, keepdims=True
            )
            acc_ref[h] = acc_ref[h] * decay + lax.dot_general(
                v_ref[:, hs], p.astype(BF16), TN, preferred_element_type=F32
            )

        score(0)
        for h in range(heads):
            if h + 1 < heads:
                score(h + 1)
            spread(h)

    @pl.when((j >= clear) & (j < me))
    def _():
        block(False)

    @pl.when(((j >= first) & (j < clear) & (j < me)) | (j == me))
    def _():
        block(True)

    @pl.when(j == me)
    def _():
        for h in range(heads):
            hs = slice(h * HD, (h + 1) * HD)
            out = (acc_ref[h] / total_ref[h : h + 1, :]).T
            raw_ref[:, hs] = out
            mixed_ref[:, hs] = out.astype(BF16)
        lse_ref[...] = high_ref[...] * C2 + jnp.log2(total_ref[...])


def attend(info, query, pairs, begin, heads):
    rows = query.shape[0]
    total = pairs.shape[0]
    span = heads * HD
    full = lambda shape: pl.BlockSpec(shape, lambda j, s: (0, 0))
    key = pl.BlockSpec((rows, span), lambda j, s: (jnp.clip(j, s[1], s[0]), 0))
    value = pl.BlockSpec((rows, span), lambda j, s: (jnp.clip(j, s[1], s[0]), 1))
    return pl.pallas_call(
        functools.partial(attend_kernel, heads),
        grid_spec=pltpu.PrefetchScalarGridSpec(
            num_scalar_prefetch=1,
            grid=(total // rows,),
            in_specs=[full((rows, span)), key, value, full((1, rows))],
            out_specs=[full((rows, span)), full((rows, span)), full((heads, rows))],
            scratch_shapes=[
                pltpu.VMEM((heads, rows), F32),
                pltpu.VMEM((heads, rows), F32),
                pltpu.VMEM((heads, HD, rows), F32),
                pltpu.VMEM((2, rows, rows), F32),
            ],
        ),
        out_shape=[
            jax.ShapeDtypeStruct((rows, span), F32),
            jax.ShapeDtypeStruct((rows, span), BF16),
            jax.ShapeDtypeStruct((heads, rows), F32),
        ],
        compiler_params=params(56),
        cost_estimate=cost(4 * rows * total * span, 4 * total * span, rows * total * heads),
        name="attend",
    )(info, query, pairs, pairs, begin)


CUBE = 8
CUBE_SENDS = 10


class Cube:
    def __init__(self, buf, send, recv):
        me = lax.axis_index("ctx")
        flip = (1 - 2 * (me % 2), 2 - 4 * ((me // 2) % 2), 4 - 8 * (me // 4))
        self.me, self.flip, self.buf, self.send, self.recv = me, flip, buf, send, recv
        self.rows = buf.shape[0] // CUBE

    def copy(self, n):
        core, x, y = self.flip
        half = self.rows // 2
        block, part, target = (
            (0, None, core),
            (0, 0, x), (0, 1, x), (0, 1, y), (0, 0, y),
            (x, 0, y), (y, 1, x),
            (x, None, core), (y, None, core), (x + y, None, core),
        )[n]
        start = (self.me + block) * self.rows
        size = self.rows
        if part is not None:
            start, size = start + part * half, half
        place = self.buf.at[pl.ds(pl.multiple_of(start, 16), size)]
        return pltpu.make_async_remote_copy(
            src_ref=place, dst_ref=place, send_sem=self.send.at[n], recv_sem=self.recv.at[n],
            device_id={"ctx": self.me + target}, device_id_type=MESH,
        )

    def arrived(self, n):
        self.copy(n).wait_recv()

    def start(self, *which):
        for n in which:
            self.copy(n).start()

    def signal(self, barrier):
        for target in self.flip:
            pl.semaphore_signal(
                barrier, inc=1, device_id={"ctx": self.me + target}, device_id_type=MESH
            )

    def block(self, step):
        core, x, y = self.flip
        on = lambda *steps: sum((step == n).astype(jnp.int32) for n in steps)
        return self.me + on(1, 4, 5, 7) * core + on(2, 4, 6, 7) * x + on(3, 5, 6, 7) * y

    def advance(self, step):
        @pl.when(step == 1)
        def _():
            self.arrived(0)

        @pl.when(step == 2)
        def _():
            self.arrived(1)
            self.start(5)
            self.arrived(3)
            self.start(6)
            self.arrived(2)
            self.start(7)

        @pl.when(step == 3)
        def _():
            self.arrived(4)
            self.start(8)

        @pl.when(step == 4)
        def _():
            self.arrived(7)

        @pl.when(step == 5)
        def _():
            self.arrived(8)

        @pl.when(step == 6)
        def _():
            self.arrived(5)
            self.arrived(6)
            self.start(9)

        @pl.when(step == 7)
        def _():
            self.arrived(9)

    def finish(self):
        for n in range(CUBE_SENDS):
            self.copy(n).wait_send()


SUM_SENDS = 9


class CubeSum:
    def __init__(self, own, near, land, send, recv, local, out=None, mid=None):
        me = lax.axis_index("ctx")
        core, x, y = me % 2, (me // 2) % 2, me // 4
        self.me, self.own, self.out, self.land, self.mid = me, own, out, land, mid
        self.near, self.send, self.recv, self.local = near, send, recv, local
        rows = own.shape[0]
        self.half, self.eighth, self.last = rows // 2, rows // 8, rows // 16
        second = rows // 4
        self.to = (1 - 2 * core, 2 - 4 * x, 4 - 8 * y)
        self.mine, self.other = core * self.half, (1 - core) * self.half
        self.offset = 0 if local is not None else self.mine
        self.keep1 = (x * self.eighth, second + y * self.eighth)
        self.give1 = ((1 - x) * self.eighth, second + (1 - y) * self.eighth)
        self.keep2 = (self.keep1[0] + y * self.last, self.keep1[1] + x * self.last)
        self.give2 = (self.keep1[0] + (1 - y) * self.last, self.keep1[1] + (1 - x) * self.last)

    def copy(self, n):
        core, x, y = self.to
        half, eighth, last, out, land = self.half, self.eighth, self.last, self.out, self.land
        source, start, size, target = (
            (self.own, self.other, half, core),
            (land, self.give1[0], eighth, x), (land, self.give1[1], eighth, y),
            (land, self.give2[0], last, y), (land, self.give2[1], last, x),
            (out, self.keep2[0], last, y), (out, self.keep2[1], last, x),
            (out, self.keep1[0], eighth, x), (out, self.keep1[1], eighth, y),
        )[n]
        src = source.at[pl.ds(pl.multiple_of(start, 16), size)]
        if n < 5:
            landing = (0, half, half + eighth, half + 2 * eighth, half + 2 * eighth + last)[n]
            dst = land.at[pl.ds(landing, size)]
        else:
            dst = src
        return pltpu.make_async_remote_copy(
            src_ref=src, dst_ref=dst, send_sem=self.send.at[n], recv_sem=self.recv.at[n],
            device_id={"ctx": self.me + target}, device_id_type=MESH,
        )

    def add(self, target, to, source, at, landed, size):
        step = size
        while step * self.own.shape[1] > 256 * 1024 and step % 32 == 0:
            step = step // 2

        def part(i, carry):
            def rows(begin):
                return pl.ds(pl.multiple_of(begin + i * step, 16), step)

            total = source[rows(at), :].astype(F32) + self.land[rows(landed), :].astype(F32)
            target[rows(to), :] = total.astype(BF16)
            return carry

        lax.fori_loop(0, size // step, part, 0)

    def read(self):
        rows = pl.ds(pl.multiple_of(self.mine, 16), self.half)
        return pltpu.make_async_copy(self.own.at[rows], self.near, self.local.at[0])

    def begin(self):
        self.copy(0).start()
        if self.local is not None:
            self.read().start()

    def reduce(self, k):
        half, eighth, last, land = self.half, self.eighth, self.last, self.land
        i = k % 2
        if k == 0:
            if self.local is not None:
                self.read().wait()
            self.copy(0).wait_recv()
        if k < 2:
            at = self.give1[i]
            self.add(land, at, self.near, self.offset + at, at, eighth)
            self.copy(1 + i).start()
        elif k < 4:
            at = self.keep1[i]
            self.add(land, at, self.near, self.offset + at, at, eighth)
        elif k < 6:
            self.copy(1 + i).wait_recv()
            landed = half + i * eighth - self.keep1[i]
            if self.out is None:
                at = self.keep1[i]
                self.add(self.mid, i * eighth, land, at, landed + at, eighth)
                return
            at = self.give2[i]
            self.add(land, at, land, at, landed + at, last)
            self.copy(3 + i).start()
            at = self.keep2[i]
            self.add(land, at, land, at, landed + at, last)
        else:
            self.copy(3 + i).wait_recv()
            at = self.keep2[i]
            self.add(self.out, at, land, at, half + 2 * eighth + i * last, last)

    def gather(self, k):
        for i in range(2):
            if k == 0:
                self.copy(5 + i).start()
            if k == 1:
                self.copy(5 + i).wait_recv()
                self.copy(7 + i).start()
            if k == 2:
                self.copy(7 + i).wait_recv()

    def finish(self):
        for n in range(3 if self.out is None else SUM_SENDS):
            self.copy(n).wait_send()

    def signal(self, barrier):
        for target in self.to:
            pl.semaphore_signal(
                barrier, inc=1, device_id={"ctx": self.me + target}, device_id_type=MESH
            )


class MidSum:
    def __init__(self, mid, land, out, send, recv):
        me = lax.axis_index("ctx")
        x, y = (me // 2) % 2, me // 4
        self.me, self.mid, self.land, self.out, self.send, self.recv = me, mid, land, out, send, recv
        self.eighth, self.last = mid.shape[0] // 2, mid.shape[0] // 4
        self.bit = (y, x)
        self.to = (4 - 8 * y, 2 - 4 * x)

    def copy(self, n):
        i = n % 2
        keep = i * self.eighth + self.bit[i] * self.last
        give = i * self.eighth + (1 - self.bit[i]) * self.last
        if n < 2:
            src = self.mid.at[pl.ds(pl.multiple_of(give, 16), self.last)]
            dst = self.land.at[pl.ds(i * self.last, self.last)]
        else:
            src = dst = self.out.at[pl.ds(pl.multiple_of(keep, 16), self.last)]
        return pltpu.make_async_remote_copy(
            src_ref=src, dst_ref=dst, send_sem=self.send.at[n], recv_sem=self.recv.at[n],
            device_id={"ctx": self.me + self.to[i]}, device_id_type=MESH,
        )

    def begin(self):
        for i in range(2):
            self.copy(i).start()

    def turn(self):
        for i in range(2):
            self.copy(i).wait_recv()
            keep = i * self.eighth + self.bit[i] * self.last
            rows = pl.ds(pl.multiple_of(keep, 16), self.last)
            landed = self.land[i * self.last : (i + 1) * self.last, :]
            self.out[rows, :] = (
                self.mid[rows, :].astype(F32) + landed.astype(F32)
            ).astype(BF16)
            self.copy(2 + i).start()

    def finish(self):
        for i in range(2):
            self.copy(2 + i).wait_recv()
        for n in range(4):
            self.copy(n).wait_send()


class LastGather:
    def __init__(self, mid, out, send, recv, local):
        me = lax.axis_index("ctx")
        x, y = (me // 2) % 2, me // 4
        self.me, self.mid, self.out = me, mid, out
        self.send, self.recv, self.local = send, recv, local
        self.eighth = mid.shape[0] // 2
        self.start_at = (x * self.eighth, (2 + y) * self.eighth)
        self.to = (2 - 4 * x, 4 - 8 * y)

    def ends(self, i):
        src = self.mid.at[pl.ds(i * self.eighth, self.eighth)]
        return src, self.out.at[pl.ds(pl.multiple_of(self.start_at[i], 16), self.eighth)]

    def copy(self, i):
        src, dst = self.ends(i)
        return pltpu.make_async_remote_copy(
            src_ref=src, dst_ref=dst, send_sem=self.send.at[i], recv_sem=self.recv.at[i],
            device_id={"ctx": self.me + self.to[i]}, device_id_type=MESH,
        )

    def keep(self, i):
        src, dst = self.ends(i)
        return pltpu.make_async_copy(src, dst, self.local.at[i])

    def begin(self):
        for i in range(2):
            self.copy(i).start()
            self.keep(i).start()

    def finish(self):
        for i in range(2):
            self.copy(i).wait()
            self.keep(i).wait()


def sum_scratch(shape):
    return [
        pltpu.VMEM((shape[0] // 2, shape[1]), BF16),
        pltpu.VMEM((shape[0] // 2 + 3 * (shape[0] // 8), shape[1]), BF16),
        pltpu.SemaphoreType.DMA((SUM_SENDS,)),
        pltpu.SemaphoreType.DMA((SUM_SENDS,)),
        pltpu.SemaphoreType.DMA((1,)),
    ]


def join_kernel(count, core_ref, *refs):
    for own_ref, far_ref, out_ref in zip(refs[:count], refs[count : 2 * count], refs[2 * count :]):
        @pl.when(pl.program_id(0) == 0)
        def _():
            out_ref[...] = own_ref[...].astype(F32)

        @pl.when(pl.program_id(0) == 1)
        def _():
            out_ref[...] = far_ref[...].astype(F32)


def join(core, own, far):
    steps = 4
    block = lambda half, at: pl.BlockSpec((half.shape[0] // steps, half.shape[1]), at)
    first = lambda h, b, s: (jnp.where(h == 0, b, steps - 1), 0)
    second = lambda h, b, s: (jnp.where(h == 0, 0, b), 0)
    target = lambda h, b, s: (jnp.where(h == 0, s[0], 1 - s[0]) * steps + b, 0)
    size = sum(half.shape[0] * half.shape[1] for half in own)
    return pl.pallas_call(
        functools.partial(join_kernel, len(own)),
        grid_spec=pltpu.PrefetchScalarGridSpec(
            num_scalar_prefetch=1,
            grid=(2, steps),
            in_specs=[block(half, first) for half in own] + [block(half, second) for half in own],
            out_specs=[block(half, target) for half in own],
        ),
        out_shape=[
            jax.ShapeDtypeStruct((2 * half.shape[0], half.shape[1]), F32) for half in own
        ],
        compiler_params=params(56),
        cost_estimate=cost(2 * size, 12 * size),
        name="join",
    )(core, *own, *far)


def hidden_scores(scores, key_block, query_block, rows, begin):
    key_place = lax.broadcasted_iota(jnp.int32, scores.shape, 0) + key_block * rows
    query_place = lax.broadcasted_iota(jnp.int32, scores.shape, 1) + query_block * rows
    return jnp.where((key_place <= query_place) & (key_place >= begin), scores, NEG)


def attend_far_kernel(
    heads, n, tok_ref, in_ref, cos_ref, sin_ref, begin_ref, cot_ref, w_ref,
    inner_ref, stat_ref, q_ref, raw_ref, mixed_ref, lse_ref, keep_ref, full_ref, part_ref,
    pair_ref, high_ref, total_ref, acc_ref, s_ref, send, recv, zsend, zrecv, keep_sem,
):
    rows = q_ref.shape[0]
    span = heads * HD
    shard = cot_ref.shape[1]
    at = lax.axis_index("tp")
    cube = Cube(pair_ref, send, recv)
    me = cube.me
    barrier = pltpu.get_barrier_semaphore()
    cube.signal(barrier)

    @pl.when(at > 0)
    def _():
        pl.semaphore_signal(barrier, inc=1, device_id={"tp": at - 1}, device_id_type=MESH)

    @pl.when(at < n - 1)
    def _():
        pl.semaphore_signal(barrier, inc=1, device_id={"tp": at + 1}, device_id_type=MESH)

    def project(rows_at, part):
        out = jnp.dot(inner_ref[rows_at, :], in_ref[part], preferred_element_type=F32)
        if part == 2:
            return out.astype(BF16)
        cosine, sine = cos_ref[rows_at, :], sin_ref[rows_at, :]
        pieces = []
        for h in range(heads):
            piece = out[:, h * HD : (h + 1) * HD]
            pieces.append((piece * cosine + pltpu.roll(piece, HD // 2, 1) * sine).astype(BF16))
        return jnp.concatenate(pieces, axis=1)

    def own_pairs(part):
        half = rows // 2
        here = slice(part * half, (part + 1) * half)
        x = tok_ref[here, :].astype(F32)
        mean = jnp.mean(x, axis=1, keepdims=True)
        center = x - mean
        inverse = lax.rsqrt(jnp.mean(center * center, axis=1, keepdims=True) + EPS)
        stat_ref[here, :] = jnp.concatenate([mean, inverse], axis=1)
        inner_ref[here, :] = (center * inverse).astype(BF16)
        place = pl.ds(pl.multiple_of(me * rows + part * half, 16), half)
        pair_ref[place, :span] = project(here, 1)
        pair_ref[place, span:] = project(here, 2)

    own_pairs(0)
    full_ref[:, pl.ds(pl.multiple_of(at * shard, 128), shard)] = cot_ref[...]
    high_ref[...] = jnp.full_like(high_ref, NEG)
    total_ref[...] = jnp.zeros_like(total_ref)
    acc_ref[...] = jnp.zeros_like(acc_ref)
    pl.semaphore_wait(barrier, jnp.where((at > 0) & (at < n - 1), 5, 4))
    cube.start(1, 4)
    own_pairs(1)
    cube.start(3, 2, 0)
    q_ref[...] = project(slice(0, rows), 0)

    def pass_on(right, s, k):
        place = full_ref.at[:, pl.ds(pl.multiple_of(s * shard, 128), shard)]
        which = (1 if right else 0, k)
        return pltpu.make_async_remote_copy(
            src_ref=place, dst_ref=place, send_sem=zsend.at[which], recv_sem=zrecv.at[which],
            device_id={"tp": at + 1 if right else at - 1}, device_id_type=MESH,
        )

    def line_step(k):
        @pl.when(at >= k)
        def _():
            if k > 0:
                pass_on(True, at - k, k - 1).wait_recv()

            @pl.when(at < n - 1)
            def _():
                pass_on(True, at - k, k).start()

        @pl.when(at + k < n)
        def _():
            if k > 0:
                pass_on(False, at + k, k - 1).wait_recv()

            @pl.when(at > 0)
            def _():
                pass_on(False, at + k, k).start()

    def keep(step):
        place = pl.ds(pl.multiple_of(cube.block(step) * rows, 16), rows)
        return pltpu.make_async_copy(pair_ref.at[place], keep_ref.at[place], keep_sem.at[step])

    def turn(step, carry):
        cube.advance(step)
        keep(step).start()
        for k in range(n):
            @pl.when(step == min(k * 2, CUBE - 1 - (n - 1 - k)) if n <= CUBE else k)
            def _():
                line_step(k)
        block = cube.block(step)

        @pl.when(block <= me)
        def _():
            place = pl.ds(pl.multiple_of(block * rows, 16), rows)

            def score(h):
                hs = slice(h * HD, (h + 1) * HD)
                s = lax.dot_general(
                    pair_ref[place, hs], q_ref[:, hs], NT, preferred_element_type=F32
                )
                s_ref[h % 2] = hidden_scores(s, block, me, rows, begin_ref[...])

            def spread(h):
                s = s_ref[h % 2]
                old = high_ref[h : h + 1, :]
                new = jnp.maximum(old, jnp.max(s, axis=0, keepdims=True))
                high_ref[h : h + 1, :] = new
                p = jnp.exp2(s * C2 - new * C2)
                decay = jnp.exp2((old - new) * C2)
                total_ref[h : h + 1, :] = total_ref[h : h + 1, :] * decay + jnp.sum(
                    p, axis=0, keepdims=True
                )
                acc_ref[h] = acc_ref[h] * decay + lax.dot_general(
                    pair_ref[place, span + h * HD : span + (h + 1) * HD], p.astype(BF16), TN,
                    preferred_element_type=F32,
                )

            score(0)
            for h in range(heads):
                if h + 1 < heads:
                    score(h + 1)
                spread(h)

        return carry

    lax.fori_loop(0, CUBE, turn, 0)
    for h in range(heads):
        hs = slice(h * HD, (h + 1) * HD)
        out = (acc_ref[h] / total_ref[h : h + 1, :]).T
        raw_ref[:, hs] = out
        mixed_ref[:, hs] = out.astype(BF16)
    part_ref[...] = jnp.dot(
        mixed_ref[...], w_ref[...], preferred_element_type=F32
    ).astype(BF16)
    lse_ref[...] = high_ref[...] * C2 + jnp.log2(total_ref[...])

    def kept(step, carry):
        keep(step).wait()
        return carry

    lax.fori_loop(0, CUBE, kept, 0)
    cube.finish()
    for k in range(n):
        @pl.when((at >= k) & (at < n - 1))
        def _():
            pass_on(True, at - k, k).wait_send()

        @pl.when((at + k < n) & (at > 0))
        def _():
            pass_on(False, at + k, k).wait_send()


def attend_far(tok_full, in_weight, cosine, sine, begin, cot, weight, heads, n):
    rows, width = tok_full.shape
    span = heads * HD
    vmem = pl.BlockSpec(memory_space=pltpu.VMEM)
    return pl.pallas_call(
        functools.partial(attend_far_kernel, heads, n),
        in_specs=[vmem] * 7,
        out_specs=[vmem] * 6 + [pl.BlockSpec(memory_space=pl.ANY)] + [vmem] * 2,
        out_shape=[
            jax.ShapeDtypeStruct((rows, width), BF16),
            jax.ShapeDtypeStruct((rows, 2), F32),
            jax.ShapeDtypeStruct((rows, span), BF16),
            jax.ShapeDtypeStruct((rows, span), F32),
            jax.ShapeDtypeStruct((rows, span), BF16),
            jax.ShapeDtypeStruct((heads, rows), F32),
            jax.ShapeDtypeStruct((CUBE * rows, 2 * span), BF16),
            jax.ShapeDtypeStruct((rows, n * cot.shape[1]), BF16),
            jax.ShapeDtypeStruct((rows, width), BF16),
        ],
        scratch_shapes=[
            pltpu.VMEM((CUBE * rows, 2 * span), BF16),
            pltpu.VMEM((heads, rows), F32),
            pltpu.VMEM((heads, rows), F32),
            pltpu.VMEM((heads, HD, rows), F32),
            pltpu.VMEM((2, rows, rows), F32),
            pltpu.SemaphoreType.DMA((CUBE_SENDS,)),
            pltpu.SemaphoreType.DMA((CUBE_SENDS,)),
            pltpu.SemaphoreType.DMA((2, n)),
            pltpu.SemaphoreType.DMA((2, n)),
            pltpu.SemaphoreType.DMA((CUBE,)),
        ],
        compiler_params=params(58, collective_id=2, has_side_effects=True),
        cost_estimate=cost(1e6, 1e6),
        name="attend_far",
    )(tok_full, in_weight, cosine, sine, begin, cot, weight)


def attend_back_far_kernel(
    heads, n, g_ref, far_q_ref, far_pair_ref, begin_ref, part_ref, mid_ref,
    dq_ref, dk_ref, dv_ref, layer_ref, next_ref,
    all_ref, acc_ref, rows_ref, s_ref, p_ref, land_ref, pair_ref, q_ref,
    send, recv, zsend, zrecv, read_sem, mid_land, msend, mrecv,
):
    rows = g_ref.shape[0]
    span = heads * HD
    shard = layer_ref.shape[1]
    at = lax.axis_index("tp")
    cube = Cube(all_ref, send, recv)
    middle = MidSum(mid_ref, mid_land, next_ref, msend, mrecv)
    me = cube.me
    barrier = pltpu.get_barrier_semaphore()
    cube.signal(barrier)
    for o in range(1, n):
        pl.semaphore_signal(
            barrier, inc=1, device_id={"tp": lax.rem(at + o, n)}, device_id_type=MESH
        )

    def read(step, keys):
        place = pl.ds(pl.multiple_of(cube.block(step) * rows, 16), rows)
        far, near = (far_pair_ref, pair_ref) if keys else (far_q_ref, q_ref)
        return pltpu.make_async_copy(
            far.at[place], near.at[place], read_sem.at[0 if keys else 1, step]
        )

    def read_all(step, carry):
        block = cube.block(step)

        @pl.when(block <= me)
        def _():
            read(step, True).start()

        @pl.when(block >= me)
        def _():
            read(step, False).start()

        return carry

    lax.fori_loop(0, CUBE, read_all, 0)
    all_ref[pl.ds(pl.multiple_of(me * rows, 16), rows), :] = g_ref[...]
    acc_ref[...] = jnp.zeros_like(acc_ref)
    dk_ref[...] = jnp.zeros_like(dk_ref)
    dv_ref[...] = jnp.zeros_like(dv_ref)
    pl.semaphore_wait(barrier, 3 + n - 1)

    def term(o):
        target = lax.rem(at + o, n)
        return pltpu.make_async_remote_copy(
            src_ref=part_ref.at[:, pl.ds(pl.multiple_of(target * shard, 128), shard)],
            dst_ref=land_ref.at[o - 1],
            send_sem=zsend.at[o - 1], recv_sem=zrecv.at[o - 1],
            device_id={"tp": target}, device_id_type=MESH,
        )

    own = pl.ds(pl.multiple_of(me * rows, 16), rows)

    cube.start(0, 1, 3, 2, 4)

    def turn(step, carry):
        cube.advance(step)

        @pl.when(step == 0)
        def _():
            for o in range(1, n):
                term(o).start()
            middle.begin()

        @pl.when(step == 3)
        def _():
            middle.turn()

        block = cube.block(step)
        place = pl.ds(pl.multiple_of(block * rows, 16), rows)

        @pl.when(block <= me)
        def _():
            read(step, True).wait()

        @pl.when(block >= me)
        def _():
            read(step, False).wait()

        def scores(h, key_block, key_place, query_block, query_place):
            hs = slice(h * HD, (h + 1) * HD)
            vs = slice(span + h * HD, span + (h + 1) * HD)
            s = lax.dot_general(
                pair_ref[key_place, hs], q_ref[query_place, hs], NT, preferred_element_type=F32
            )
            begin = begin_ref[pl.ds(query_block, 1), :]
            s_ref[h % 2] = hidden_scores(s, key_block, query_block, rows, begin)
            p_ref[h % 2] = lax.dot_general(
                pair_ref[key_place, vs], all_ref[query_place, hs], NT, preferred_element_type=F32
            )

        def read_rows(query_place):
            coded = all_ref[query_place, span:].astype(F32).T
            for k in range(2 * heads):
                rows_ref[k : k + 1, :] = (
                    coded[3 * k : 3 * k + 1]
                    + coded[3 * k + 1 : 3 * k + 2]
                    + coded[3 * k + 2 : 3 * k + 3]
                )

        def weights(h):
            p = jnp.exp2(s_ref[h % 2] * C2 - rows_ref[h : h + 1, :])
            ds = p * (p_ref[h % 2] - rows_ref[heads + h : heads + h + 1, :])
            return p.astype(BF16), ds.astype(BF16)

        @pl.when(block <= me)
        def _():
            read_rows(own)
            scores(0, block, place, me, own)
            for h in range(heads):
                if h + 1 < heads:
                    scores(h + 1, block, place, me, own)
                _, ds = weights(h)
                acc_ref[h] = acc_ref[h] + lax.dot_general(
                    pair_ref[place, h * HD : (h + 1) * HD], ds, TN, preferred_element_type=F32
                )

        @pl.when(block >= me)
        def _():
            read_rows(place)
            scores(0, me, own, block, place)
            for h in range(heads):
                hs = slice(h * HD, (h + 1) * HD)
                if h + 1 < heads:
                    scores(h + 1, me, own, block, place)
                p, ds = weights(h)
                dv_ref[:, hs] += jnp.dot(p, all_ref[place, hs], preferred_element_type=F32)
                dk_ref[:, hs] += jnp.dot(ds, q_ref[place, hs], preferred_element_type=F32)

        return carry

    lax.fori_loop(0, CUBE, turn, 0)
    for h in range(heads):
        dq_ref[:, h * HD : (h + 1) * HD] = (acc_ref[h] * SCALE).T
    dk_ref[...] = dk_ref[...] * SCALE
    total = part_ref[:, pl.ds(pl.multiple_of(at * shard, 128), shard)].astype(F32)
    for o in range(1, n):
        term(o).wait_recv()
        total = total + land_ref[o - 1].astype(F32)
    layer_ref[...] = total.astype(BF16)
    middle.finish()
    cube.finish()
    for o in range(1, n):
        term(o).wait_send()


def attend_back_far(grad, all_query, all_pairs, all_begin, part, mid, heads, n):
    rows = grad.shape[0]
    span = heads * HD
    shard = part.shape[1] // n
    vmem = pl.BlockSpec(memory_space=pltpu.VMEM)
    wide = jax.ShapeDtypeStruct((rows, span), F32)
    return pl.pallas_call(
        functools.partial(attend_back_far_kernel, heads, n),
        in_specs=[vmem] + [pl.BlockSpec(memory_space=pl.ANY)] * 2 + [vmem] * 3,
        out_specs=[vmem] * 5,
        out_shape=[wide, wide, wide, jax.ShapeDtypeStruct((rows, shard), BF16)]
        + [jax.ShapeDtypeStruct(mid.shape, BF16)],
        scratch_shapes=[
            pltpu.VMEM((CUBE * rows, span + HD), BF16),
            pltpu.VMEM((heads, HD, rows), F32),
            pltpu.VMEM((2 * heads, rows), F32),
            pltpu.VMEM((2, rows, rows), F32),
            pltpu.VMEM((2, rows, rows), F32),
            pltpu.VMEM((n - 1, rows, shard), BF16),
            pltpu.VMEM((CUBE * rows, 2 * span), BF16),
            pltpu.VMEM((CUBE * rows, span), BF16),
            pltpu.SemaphoreType.DMA((CUBE_SENDS,)),
            pltpu.SemaphoreType.DMA((CUBE_SENDS,)),
            pltpu.SemaphoreType.DMA((n - 1,)),
            pltpu.SemaphoreType.DMA((n - 1,)),
            pltpu.SemaphoreType.DMA((2, CUBE)),
            pltpu.VMEM((mid.shape[0] // 2, mid.shape[1]), BF16),
            pltpu.SemaphoreType.DMA((4,)),
            pltpu.SemaphoreType.DMA((4,)),
        ],
        compiler_params=params(62, collective_id=3, has_side_effects=True),
        cost_estimate=cost(1e6, 1e6),
        name="attend_back_far",
    )(grad, all_query, all_pairs, all_begin, part, mid)


def query_grad_kernel(
    heads, info, q_ref, do_ref, lse_ref, delta_ref, k_ref, v_ref, begin_ref,
    dq_ref, acc_ref, s_ref, g_ref,
):
    me, first, clear = info[0], info[1], info[2]
    j = pl.program_id(0)
    rows = q_ref.shape[0]

    @pl.when(j == 0)
    def _():
        acc_ref[...] = jnp.zeros_like(acc_ref)

    def block(hide):
        def score(h):
            hs = slice(h * HD, (h + 1) * HD)
            s = lax.dot_general(k_ref[:, hs], q_ref[:, hs], NT, preferred_element_type=F32)
            if hide:
                s = masked(s, j, me, rows, begin_ref[...])
            s_ref[h % 2] = s
            g_ref[h % 2] = lax.dot_general(
                v_ref[:, hs], do_ref[:, hs], NT, preferred_element_type=F32
            )

        def spread(h):
            hs = slice(h * HD, (h + 1) * HD)
            p = jnp.exp2(s_ref[h % 2] * C2 - lse_ref[h : h + 1, :])
            ds = (p * (g_ref[h % 2] - delta_ref[h : h + 1, :])).astype(BF16)
            acc_ref[h] = acc_ref[h] + lax.dot_general(
                k_ref[:, hs], ds, TN, preferred_element_type=F32
            )

        score(0)
        for h in range(heads):
            if h + 1 < heads:
                score(h + 1)
            spread(h)

    @pl.when((j >= clear) & (j < me))
    def _():
        block(False)

    @pl.when(((j >= first) & (j < clear) & (j < me)) | (j == me))
    def _():
        block(True)

    @pl.when(j == me)
    def _():
        for h in range(heads):
            dq_ref[:, h * HD : (h + 1) * HD] = (acc_ref[h] * SCALE).T


def query_grad(info, query, grad_mixed, lse, delta, pairs, begin, heads):
    rows = query.shape[0]
    total = pairs.shape[0]
    span = heads * HD
    full = lambda shape: pl.BlockSpec(shape, lambda j, s: (0, 0))
    key = pl.BlockSpec((rows, span), lambda j, s: (jnp.clip(j, s[1], s[0]), 0))
    value = pl.BlockSpec((rows, span), lambda j, s: (jnp.clip(j, s[1], s[0]), 1))
    wide = full((rows, span))
    thin = full((heads, rows))
    return pl.pallas_call(
        functools.partial(query_grad_kernel, heads),
        grid_spec=pltpu.PrefetchScalarGridSpec(
            num_scalar_prefetch=1,
            grid=(total // rows,),
            in_specs=[wide, wide, thin, thin, key, value, full((1, rows))],
            out_specs=wide,
            scratch_shapes=[
                pltpu.VMEM((heads, HD, rows), F32),
                pltpu.VMEM((2, rows, rows), F32),
                pltpu.VMEM((2, rows, rows), F32),
            ],
        ),
        out_shape=jax.ShapeDtypeStruct((rows, span), F32),
        compiler_params=params(58),
        cost_estimate=cost(6 * rows * total * span, 4 * total * span, rows * total * heads),
        name="query_grad",
    )(info, query, grad_mixed, lse, delta, pairs, pairs, begin)


def key_grad_kernel(
    heads, info, k_ref, v_ref, q_ref, g_ref, begin_ref, dk_ref, dv_ref,
    rows_ref, s_ref, p_ref,
):
    me, last, clear = info[0], info[1], info[2]
    j = pl.program_id(0)
    rows = k_ref.shape[0]
    span = heads * HD

    @pl.when(j == me)
    def _():
        dk_ref[...] = jnp.zeros_like(dk_ref)
        dv_ref[...] = jnp.zeros_like(dv_ref)

    def block(hide):
        coded = g_ref[:, span:].astype(F32).T
        for n in range(2 * heads):
            rows_ref[n : n + 1, :] = (
                coded[3 * n : 3 * n + 1] + coded[3 * n + 1 : 3 * n + 2] + coded[3 * n + 2 : 3 * n + 3]
            )

        def score(h):
            hs = slice(h * HD, (h + 1) * HD)
            s = lax.dot_general(k_ref[:, hs], q_ref[:, hs], NT, preferred_element_type=F32)
            if hide:
                key_place = lax.broadcasted_iota(jnp.int32, s.shape, 0) + me * rows
                query_place = lax.broadcasted_iota(jnp.int32, s.shape, 1) + j * rows
                s = jnp.where(
                    (key_place <= query_place) & (key_place >= begin_ref[...]), s, NEG
                )
            s_ref[h % 2] = s
            p_ref[h % 2] = lax.dot_general(
                v_ref[:, hs], g_ref[:, hs], NT, preferred_element_type=F32
            )

        def spread(h):
            hs = slice(h * HD, (h + 1) * HD)
            p = jnp.exp2(s_ref[h % 2] * C2 - rows_ref[h : h + 1, :])
            ds = (p * (p_ref[h % 2] - rows_ref[heads + h : heads + h + 1, :])).astype(BF16)
            dv_ref[:, hs] += jnp.dot(p.astype(BF16), g_ref[:, hs], preferred_element_type=F32)
            dk_ref[:, hs] += jnp.dot(ds, q_ref[:, hs], preferred_element_type=F32)

        score(0)
        for h in range(heads):
            if h + 1 < heads:
                score(h + 1)
            spread(h)

    @pl.when((j > me) & (j <= clear))
    def _():
        block(False)

    @pl.when((j == me) | ((j > me) & (j > clear) & (j <= last)))
    def _():
        block(True)

    @pl.when(j == pl.num_programs(0) - 1)
    def _():
        dk_ref[...] = dk_ref[...] * SCALE


def key_grad(info, pairs, all_query, all_grad, all_begin, heads):
    rows = pairs.shape[0]
    total = all_query.shape[0]
    span = heads * HD
    full = lambda shape, at=0: pl.BlockSpec(shape, lambda j, s: (0, at))
    near = lambda j, s: (jnp.clip(j, s[0], s[1]), 0)
    wide = full((rows, span))
    return pl.pallas_call(
        functools.partial(key_grad_kernel, heads),
        grid_spec=pltpu.PrefetchScalarGridSpec(
            num_scalar_prefetch=1,
            grid=(total // rows,),
            in_specs=[
                wide, full((rows, span), 1),
                pl.BlockSpec((rows, span), near),
                pl.BlockSpec((rows, span + HD), near),
                pl.BlockSpec((1, rows), lambda j, s: (0, jnp.clip(j, s[0], s[1]))),
            ],
            out_specs=[wide, wide],
            scratch_shapes=[
                pltpu.VMEM((2 * heads, rows), F32),
                pltpu.VMEM((2, rows, rows), F32),
                pltpu.VMEM((2, rows, rows), F32),
            ],
        ),
        out_shape=[jax.ShapeDtypeStruct((rows, span), F32)] * 2,
        compiler_params=params(58),
        cost_estimate=cost(8 * rows * total * span, 4 * total * span, rows * total * heads),
        name="key_grad",
    )(info, pairs, pairs, all_query, all_grad, all_begin)


def mixed_grad_kernel(heads, branch_ref, w_ref, raw_ref, lse_ref, out_ref, delta_ref):
    span = heads * HD
    low = lax.dot_general(
        branch_ref[...], w_ref[...], NT, preferred_element_type=F32
    ).astype(BF16)
    out_ref[:, :span] = low
    count = low.shape[0]
    both = low.astype(F32) * raw_ref[...]
    for h in range(heads):
        delta_ref[h : h + 1, :] = jnp.sum(both[:, h * HD : (h + 1) * HD].T, axis=0, keepdims=True)
    lines = []
    for n in range(2 * heads):
        value = lse_ref[n : n + 1, :] if n < heads else delta_ref[n - heads : n - heads + 1, :]
        for _ in range(3):
            piece = value.astype(BF16).astype(F32)
            lines.append(piece)
            value = value - piece
    lines.append(jnp.zeros((HD - len(lines), count), F32))
    out_ref[:, span:] = jnp.concatenate(lines, axis=0).T.astype(BF16)


def mixed_grad(branch, weight, raw, lse, heads):
    rows, width = branch.shape
    span = heads * HD
    block = 256
    row = lambda n: pl.BlockSpec((block, n), lambda i: (i, 0))
    line = pl.BlockSpec((heads, block), lambda i: (0, i))
    return pl.pallas_call(
        functools.partial(mixed_grad_kernel, heads),
        grid=(rows // block,),
        in_specs=[row(width), pl.BlockSpec((span, width), lambda i: (0, 0)), row(span), line],
        out_specs=[row(span + HD), line],
        out_shape=[
            jax.ShapeDtypeStruct((rows, span + HD), BF16),
            jax.ShapeDtypeStruct((heads, rows), F32),
        ],
        compiler_params=params(56),
        cost_estimate=cost(2 * rows * width * span, 2 * width * span + 4 * rows * width),
        name="mixed_grad",
    )(branch, weight, raw, lse)


def feed_kernel(
    inner_ref, cot_ref, w_ref, grad_ref, hidden_ref, dgu_ref, down_grad_ref, gu_grad_ref
):
    block = grad_ref.shape[1]
    both = jnp.dot(inner_ref[...], w_ref[...], preferred_element_type=F32)
    grad = grad_ref[...].astype(F32)
    gate, up = both[:, :block], both[:, block:]
    sigma = 1.0 / (1.0 + jnp.exp(-gate))
    active = gate * sigma
    hidden_ref[...] = (active * up).astype(BF16)
    dgu_ref[:, :block] = (grad * up * sigma * (1.0 + gate * (1.0 - sigma))).astype(BF16)
    dgu_ref[:, block:] = (grad * active).astype(BF16)
    down_grad_ref[...] = lax.dot_general(
        hidden_ref[...], cot_ref[...], TN, preferred_element_type=F32
    ).astype(BF16)
    gu_grad_ref[...] = lax.dot_general(
        inner_ref[...], dgu_ref[...], TN, preferred_element_type=F32
    ).astype(BF16)


def feed(inner, cot, weight, grad, block):
    rows, width = inner.shape
    units = grad.shape[1]
    whole = pl.BlockSpec((rows, width), lambda j: (0, 0))
    column = lambda high, wide: pl.BlockSpec((high, wide), lambda j: (0, j))
    line = pl.BlockSpec((block, width), lambda j: (j, 0))
    return pl.pallas_call(
        feed_kernel,
        grid=(units // block,),
        in_specs=[whole, whole, column(width, 2 * block), column(rows, block)],
        out_specs=[column(rows, block), column(rows, 2 * block), line, column(width, 2 * block)],
        out_shape=[
            jax.ShapeDtypeStruct((rows, units), BF16),
            jax.ShapeDtypeStruct((rows, 2 * units), BF16),
            jax.ShapeDtypeStruct((units, width), BF16),
            jax.ShapeDtypeStruct((width, 2 * units), BF16),
        ],
        compiler_params=params(60),
        cost_estimate=cost(
            12 * rows * width * units, 12 * width * units + 4 * rows * width, rows * units
        ),
        name="feed",
    )(inner, cot, weight, grad)


def weave_kernel(block, sum_ref, out_ref):
    for j in range(sum_ref.shape[1] // (2 * block)):
        for k in range(2):
            at = (2 * j + k) * block
            out_ref[:, k, j * block : (j + 1) * block] = sum_ref[:, at : at + block].astype(F32)


def weave(summed, block):
    width, both = summed.shape
    rows = 256
    return pl.pallas_call(
        functools.partial(weave_kernel, block),
        grid=(width // rows,),
        in_specs=[pl.BlockSpec((rows, both), lambda i: (i, 0))],
        out_specs=pl.BlockSpec((rows, 2, both // 2), lambda i: (i, 0, 0)),
        out_shape=jax.ShapeDtypeStruct((width, 2, both // 2), F32),
        compiler_params=params(56),
        cost_estimate=cost(width * both, 6 * width * both),
        name="weave",
    )(summed)


def widen_kernel(in_ref, out_ref):
    out_ref[...] = in_ref[...].astype(F32)


def widen(summed):
    high, wide = summed.shape
    block = pl.BlockSpec((512, wide), lambda i: (i, 0))
    return pl.pallas_call(
        widen_kernel,
        grid=(high // 512,),
        in_specs=[block],
        out_specs=block,
        out_shape=jax.ShapeDtypeStruct((high, wide), F32),
        compiler_params=params(56),
        cost_estimate=cost(high * wide, 6 * high * wide),
        name="widen",
    )(summed)


def line_barrier(at, n, cube=None):
    barrier = pltpu.get_barrier_semaphore()
    if cube is not None:
        cube.signal(barrier)

    @pl.when(at > 0)
    def _():
        pl.semaphore_signal(barrier, inc=1, device_id={"tp": at - 1}, device_id_type=MESH)

    @pl.when(at < n - 1)
    def _():
        pl.semaphore_signal(barrier, inc=1, device_id={"tp": at + 1}, device_id_type=MESH)

    near = jnp.where((at > 0) & (at < n - 1), 2, 1)
    pl.semaphore_wait(barrier, near + (0 if cube is None else 3))


def sum_rows(n, sub, part_ref, out_ref, row_fn, from_left, from_right, send, recv, aside={}):
    at = lax.axis_index("tp")
    chunks = part_ref.shape[0] // sub
    middle = (n // 2 - 1, n // 2)

    def link(kind, right, src, dst, c):
        which = (kind * 2 + (1 if right else 0), c)
        return pltpu.make_async_remote_copy(
            src_ref=src.at[pl.ds(c * sub, sub)],
            dst_ref=dst.at[pl.ds(c * sub, sub)],
            send_sem=send.at[which],
            recv_sem=recv.at[which],
            device_id={"tp": at + 1 if right else at - 1},
            device_id_type=MESH,
        )

    def came(right):
        return from_left if right else from_right

    def first(right, c):
        return link(0, right, part_ref, came(right), c)

    def onward(right, c):
        return link(0, right, came(right), came(right), c)

    def hand(right, c):
        return link(1, right, out_ref, out_ref, c)

    def reduce_step(c):
        owner = middle[c % 2]
        rows = slice(c * sub, (c + 1) * sub)
        for right in (True, False):
            edge = 0 if right else n - 1
            held = came(right)

            @pl.when(((at < owner) if right else (at > owner)) & (at != edge))
            def _():
                copy = onward(right, c)
                copy.wait_recv()
                held[rows, :] = (
                    held[rows, :].astype(F32) + part_ref[rows, :].astype(F32)
                ).astype(BF16)
                copy.start()

    def final_step(c):
        owner = middle[c % 2]
        rows = slice(c * sub, (c + 1) * sub)

        @pl.when(at == owner)
        def _():
            total = part_ref[rows, :].astype(F32)
            onward(True, c).wait_recv()
            total = total + from_left[rows, :].astype(F32)
            onward(False, c).wait_recv()
            total = total + from_right[rows, :].astype(F32)
            row_fn(total, rows)
            hand(True, c).start()
            hand(False, c).start()

    def hand_step(c):
        owner = middle[c % 2]
        for right in (True, False):
            edge = n - 1 if right else 0

            @pl.when((at > owner) if right else (at < owner))
            def _():
                copy = hand(right, c)
                copy.wait_recv()

                @pl.when(at != edge)
                def _():
                    copy.start()

    for c in range(chunks):
        @pl.when(at == 0)
        def _():
            first(True, c).start()

        @pl.when(at == n - 1)
        def _():
            first(False, c).start()

    for c in range(chunks + 4):
        for piece in aside.get(c, ()):
            piece()
        if c < chunks:
            reduce_step(c)
        if 2 <= c < chunks + 2:
            final_step(c - 2)
        if c >= 4:
            hand_step(c - 4)
    for c in range(chunks):
        owner = middle[c % 2]

        @pl.when(at < owner)
        def _():
            first(True, c).wait_send()

        @pl.when(at > owner)
        def _():
            first(False, c).wait_send()

        @pl.when((at >= owner) & (at < n - 1))
        def _():
            hand(True, c).wait_send()

        @pl.when((at <= owner) & (at > 0))
        def _():
            hand(False, c).wait_send()


def merge_kernel(
    n, sub, part_ref, tok_ref, far_cot, far_down, inner_ref, resid_out, stat_ref, hidden_ref,
    from_left, from_right, send, recv, cot_ref, down_ref, resid_ref, read_sem, keep_sem,
):
    reads = (
        pltpu.make_async_copy(far_cot, cot_ref, read_sem.at[0]),
        pltpu.make_async_copy(far_down, down_ref, read_sem.at[1]),
    )
    for read in reads:
        read.start()
    line_barrier(lax.axis_index("tp"), n)
    stat_ref[...] = jnp.zeros_like(stat_ref)

    def keep(rows):
        slot = rows.start // (2 * sub)
        held = resid_ref.at[pl.ds(slot * sub, sub)]
        return pltpu.make_async_copy(
            held, resid_out.at[pl.ds(rows.start, sub)], keep_sem.at[slot]
        )

    def row_fn(total, rows):
        x = tok_ref[rows, :].astype(F32) + total
        mean = jnp.mean(x, axis=1, keepdims=True)
        center = x - mean
        inverse = lax.rsqrt(jnp.mean(center * center, axis=1, keepdims=True) + EPS)
        slot = rows.start // (2 * sub)
        resid_ref[slot * sub : (slot + 1) * sub, :] = x
        keep(rows).start()
        stat_ref[rows, :] = jnp.concatenate([mean, inverse], axis=1)
        inner_ref[rows, :] = (center * inverse).astype(BF16)

    def piece(at):
        if at == 0:
            for read in reads:
                read.wait()
        hidden_ref[:, at : at + 256] = lax.dot_general(
            cot_ref[...], down_ref[at : at + 256, :], NT, preferred_element_type=F32
        ).astype(BF16)

    aside = {}
    for k in range(down_ref.shape[0] // 256):
        aside[1 + 2 * k] = (functools.partial(piece, k * 256),)
    sum_rows(n, sub, part_ref, inner_ref, row_fn, from_left, from_right, send, recv, aside)
    for c in range(part_ref.shape[0] // sub):
        @pl.when(lax.axis_index("tp") == n // 2 - 1 + c % 2)
        def _():
            keep(slice(c * sub, (c + 1) * sub)).wait()


def merge(part, tok_full, cot_full, down, n):
    rows, width = part.shape
    sub = SUB
    vmem = pl.BlockSpec(memory_space=pltpu.VMEM)
    far = pl.BlockSpec(memory_space=pl.ANY)
    return pl.pallas_call(
        functools.partial(merge_kernel, n, sub),
        in_specs=[vmem, vmem, far, far],
        out_specs=[vmem, far, vmem, vmem],
        out_shape=[
            jax.ShapeDtypeStruct((rows, width), BF16),
            jax.ShapeDtypeStruct((rows, width), F32),
            jax.ShapeDtypeStruct((rows, 2), F32),
            jax.ShapeDtypeStruct((rows, down.shape[0]), BF16),
        ],
        scratch_shapes=[pltpu.VMEM((rows, width), BF16)] * 2
        + [pltpu.SemaphoreType.DMA((4, rows // sub))] * 2
        + [
            pltpu.VMEM((rows, width), BF16),
            pltpu.VMEM(down.shape, BF16),
            pltpu.VMEM((rows // 2, width), F32),
            pltpu.SemaphoreType.DMA((2,)),
            pltpu.SemaphoreType.DMA((rows // (2 * sub),)),
        ],
        compiler_params=params(56, collective_id=5, has_side_effects=True),
        cost_estimate=cost(1e6, 1e6),
        name="merge",
    )(part, tok_full, cot_full, down)


def norm_back_kernel(
    n, sub, cube, part_ref, cot_ref, stat_ref, *refs
):
    total = None
    far, refs = refs[:3], refs[3:]
    if cube:
        own, out_ref, layer_ref, mid, from_left, from_right, send, recv = refs[:8]
        resid_ref, hidden_ref, down_ref, read_sem = refs[8:12]
        total = CubeSum(own, *refs[12:17], mid=mid)
    else:
        out_ref, layer_ref, from_left, from_right, send, recv = refs[:6]
        resid_ref, hidden_ref, down_ref, read_sem = refs[6:10]
    reads = [
        pltpu.make_async_copy(source, held, read_sem.at[k])
        for k, (source, held) in enumerate(zip(far, (resid_ref, hidden_ref, down_ref)))
    ]
    for read in reads:
        read.start()
    at = lax.axis_index("tp")
    line_barrier(lax.axis_index("tp"), n, total)
    aside = {}

    def piece(start):
        if start == 0:
            for read in reads:
                read.wait()
        cols = slice(start, start + 256)
        row = lax.broadcasted_iota(jnp.int32, (part_ref.shape[0], 256), 0)
        owned = (row // sub) % 2 == at - (n // 2 - 1)
        layer_ref[:, cols] = (
            jnp.where(owned, resid_ref[:, cols], 0.0)
            + jnp.dot(hidden_ref[...], down_ref[:, cols], preferred_element_type=F32)
        ).astype(BF16)

    for k in range(down_ref.shape[1] // 256):
        aside[1 + 2 * k] = (functools.partial(piece, k * 256),)
    if cube:
        total.begin()
        for k, c in enumerate((6, 8, 10, 12)):
            aside[c] = (functools.partial(total.reduce, k),)

    def row_fn(summed, rows):
        inverse = stat_ref[rows, 1:2]
        normed = (resid_ref[rows, :] - stat_ref[rows, 0:1]) * inverse
        mean = jnp.mean(summed, axis=1, keepdims=True)
        inner = jnp.mean(summed * normed, axis=1, keepdims=True)
        out = cot_ref[rows, :].astype(F32) + inverse * (summed - mean - normed * inner)
        out_ref[rows, :] = out.astype(BF16)

    sum_rows(n, sub, part_ref, out_ref, row_fn, from_left, from_right, send, recv, aside)
    if cube:
        total.reduce(4)
        total.reduce(5)
        total.finish()


def norm_back(part, cot, resid, stat, hidden, down, n, grads):
    rows, width = part.shape
    sub = SUB
    vmem = pl.BlockSpec(memory_space=pltpu.VMEM)
    far = pl.BlockSpec(memory_space=pl.ANY)
    extra = []
    for grad in grads:
        extra += sum_scratch(grad.shape)
    return pl.pallas_call(
        functools.partial(norm_back_kernel, n, sub, len(grads) > 0),
        in_specs=[vmem] * 3 + [far] * (3 + len(grads)),
        out_specs=[vmem] * (2 + len(grads)),
        out_shape=[jax.ShapeDtypeStruct((rows, width), BF16)] * 2
        + [jax.ShapeDtypeStruct((grad.shape[0] // 4, grad.shape[1]), BF16) for grad in grads],
        scratch_shapes=[pltpu.VMEM((rows, width), BF16)] * 2
        + [pltpu.SemaphoreType.DMA((4, rows // sub))] * 2
        + [
            pltpu.VMEM(resid.shape, F32),
            pltpu.VMEM(hidden.shape, BF16),
            pltpu.VMEM(down.shape, BF16),
            pltpu.SemaphoreType.DMA((3,)),
        ]
        + extra,
        compiler_params=params(60, collective_id=1, has_side_effects=True),
        cost_estimate=cost(1e6, 1e6),
        name="norm_back",
    )(part, cot, stat, resid, hidden, down, *grads)


def unrotate_kernel(
    heads, dq_ref, dk_ref, dv_ref, cos_ref, sin_ref, inner_ref, dproj_ref, grad_ref
):
    def back(ref):
        for h in range(heads):
            hs = slice(h * HD, (h + 1) * HD)
            piece = ref[:, hs]
            dproj_ref[:, hs] = (
                piece * cos_ref[...] - pltpu.roll(piece, HD // 2, 1) * sin_ref[...]
            ).astype(BF16)

    part = pl.program_id(0)

    @pl.when(part == 0)
    def _():
        back(dq_ref)

    @pl.when(part == 1)
    def _():
        back(dk_ref)

    @pl.when(part == 2)
    def _():
        dproj_ref[...] = dv_ref[...].astype(BF16)

    grad_ref[...] = lax.dot_general(
        inner_ref[...], dproj_ref[...], TN, preferred_element_type=F32
    ).astype(BF16)


def unrotate(dq, dk, dv, cosine, sine, inner, heads):
    rows, span = dq.shape
    width = inner.shape[1]
    whole = lambda n: pl.BlockSpec((rows, n), lambda i: (0, 0))
    return pl.pallas_call(
        functools.partial(unrotate_kernel, heads),
        grid=(3,),
        in_specs=[whole(span)] * 3 + [whole(HD)] * 2 + [whole(width)],
        out_specs=[
            pl.BlockSpec((rows, span), lambda i: (0, i)),
            pl.BlockSpec((width, span), lambda i: (i, 0)),
        ],
        out_shape=[
            jax.ShapeDtypeStruct((rows, 3 * span), BF16),
            jax.ShapeDtypeStruct((3 * width, span), BF16),
        ],
        compiler_params=params(56),
        cost_estimate=cost(6 * rows * span * width, 12 * rows * span + 6 * width * span),
        name="unrotate",
    )(dq, dk, dv, cosine, sine, inner)


def unproject_kernel(heads, n, cube, *refs):
    sums, rest = [], None
    if cube:
        dq_ref, dk_ref, dv_ref, cos_ref, sin_ref, inner_ref, mixed_ref = refs[:7]
        branch_ref, mid_ref, tok_ref, stat_ref, w_ref = refs[7:12]
        out_ref, in_out, og_out, down_out, dproj_ref, in_ref, og_ref = refs[12:19]
        part_ref, mine_ref, land_ref, sums_ref, far_ref, send, recv, ssend, srecv = refs[19:28]
        for own, out, at in ((in_ref, in_out, 28), (og_ref, og_out, 31)):
            sums.append(CubeSum(own, own, *refs[at : at + 3], None, out=out))
        rest = LastGather(mid_ref, down_out, *refs[34:37])
    else:
        dproj_ref, branch_ref, tok_ref, stat_ref, w_ref, out_ref = refs[:6]
        part_ref, mine_ref, land_ref, sums_ref, far_ref, send, recv, ssend, srecv = refs[6:15]

    def reduce(*pieces):
        for k in pieces:
            for item in sums:
                item.reduce(k)

    def gather(k):
        for item in sums:
            item.gather(k)

    rows, width = tok_ref.shape
    shard = width // n
    span = heads * HD
    at = lax.axis_index("tp")
    barrier = pltpu.get_barrier_semaphore()
    for o in range(1, n):
        pl.semaphore_signal(
            barrier, inc=1, device_id={"tp": lax.rem(at + o, n)}, device_id_type=MESH
        )
    if cube:
        sums[0].signal(barrier)
    pl.semaphore_wait(barrier, n - 1 + (3 if cube else 0))
    if cube:
        rest.begin()
        og_ref[...] = lax.dot_general(
            mixed_ref[...], branch_ref[...], TN, preferred_element_type=F32
        ).astype(BF16)
        sums[1].begin()
        for part, ref in enumerate((dq_ref, dk_ref, dv_ref)):
            for h in range(heads):
                piece = ref[:, h * HD : (h + 1) * HD]
                if part < 2:
                    piece = (
                        piece * cos_ref[...] - pltpu.roll(piece, HD // 2, 1) * sin_ref[...]
                    )
                at_column = part * span + h * HD
                dproj_ref[:, at_column : at_column + HD] = piece.astype(BF16)
            in_ref[part * width : (part + 1) * width, :] = lax.dot_general(
                inner_ref[...], dproj_ref[:, part * span : (part + 1) * span], TN,
                preferred_element_type=F32,
            ).astype(BF16)
        sums[0].begin()
    block = 256
    count = rows // block

    def term(o, i):
        target = lax.rem(at + o, n)
        place = pl.ds(i * block, block)
        return pltpu.make_async_remote_copy(
            src_ref=part_ref.at[place, pl.ds(pl.multiple_of(target * shard, 128), shard)],
            dst_ref=land_ref.at[o - 1, place],
            send_sem=send.at[o - 1, i], recv_sem=recv.at[o - 1, i],
            device_id={"tp": target}, device_id_type=MESH,
        )

    def totals(o):
        return pltpu.make_async_remote_copy(
            src_ref=sums_ref, dst_ref=far_ref.at[o - 1],
            send_sem=ssend.at[o - 1], recv_sem=srecv.at[o - 1],
            device_id={"tp": lax.rem(at + o, n)}, device_id_type=MESH,
        )

    own = pl.ds(pl.multiple_of(at * shard, 128), shard)
    for i in range(count):
        place = pl.ds(i * block, block)
        total = None
        for part in range(3):
            piece = lax.dot_general(
                dproj_ref[place, part * span : (part + 1) * span], w_ref[part], NT,
                preferred_element_type=F32,
            )
            total = piece if total is None else total + piece
        part_ref[place, :] = total.astype(BF16)
        for o in range(1, n):
            term(o, i).start()
        normed = (tok_ref[place, :].astype(F32) - stat_ref[place, 0:1]) * stat_ref[place, 1:2]
        first = jnp.sum(total, axis=1, keepdims=True)
        second = jnp.sum(total * normed, axis=1, keepdims=True)
        lane = lax.broadcasted_iota(jnp.int32, (block, HD), 1)
        both = jnp.where(lane == 0, first, jnp.where(lane == 1, second, 0.0))
        sums_ref[:, i * block : (i + 1) * block] = both.T[:8]
    for o in range(1, n):
        totals(o).start()
    reduce(0, 1, 2, 3, 4, 5, 6, 7)
    gather(0)
    gather(1)
    total = sums_ref[...]
    for o in range(1, n):
        totals(o).wait_recv()
        total = total + far_ref[o - 1]
    mine_ref[...] = total
    for i in range(count):
        place = pl.ds(i * block, block)
        spread = jnp.concatenate(
            [mine_ref[:, i * block : (i + 1) * block], jnp.zeros((HD - 8, block), F32)], axis=0
        ).T / width
        total = part_ref[place, own].astype(F32)
        for o in range(1, n):
            term(o, i).wait_recv()
            total = total + land_ref[o - 1, place].astype(F32)
        inverse = stat_ref[place, 1:2]
        normed = (tok_ref[place, own].astype(F32) - stat_ref[place, 0:1]) * inverse
        out_ref[place, :] = branch_ref[place, own].astype(F32) + inverse * (
            total - spread[:, 0:1] - normed * spread[:, 1:2]
        )
    gather(2)
    for item in sums + ([rest] if cube else []):
        item.finish()
    for o in range(1, n):
        totals(o).wait_send()
        for i in range(count):
            term(o, i).wait_send()


def unproject(cube, operands, tok_full, stat, weight, heads, n):
    rows, width = tok_full.shape
    shard = width // n
    span = heads * HD
    vmem = pl.BlockSpec(memory_space=pltpu.VMEM)
    shapes = [(3 * width, span), (span, width)] if cube else []
    more_out, early, extra = [], [], []
    if cube:
        mid = operands[-1]
        more_out = [jax.ShapeDtypeStruct((high // 2, wide), BF16) for high, wide in shapes]
        more_out.append(jax.ShapeDtypeStruct((2 * mid.shape[0], mid.shape[1]), BF16))
        early = [pltpu.VMEM(shape, BF16) for shape in [(rows, 3 * span)] + shapes]
        for shape in shapes:
            extra += sum_scratch(shape)[1:4]
        extra += [pltpu.SemaphoreType.DMA((2,))] * 3
    return pl.pallas_call(
        functools.partial(unproject_kernel, heads, n, cube),
        in_specs=[vmem] * (len(operands) + 3),
        out_specs=[vmem] * (1 + len(shapes)) + [pl.BlockSpec(memory_space=pl.ANY)] * int(cube),
        out_shape=[jax.ShapeDtypeStruct((rows, shard), F32)] + more_out,
        scratch_shapes=early
        + [
            pltpu.VMEM((rows, width), BF16),
            pltpu.VMEM((8, rows), F32),
            pltpu.VMEM((n - 1, rows, shard), BF16),
            pltpu.VMEM((8, rows), F32),
            pltpu.VMEM((n - 1, 8, rows), F32),
            pltpu.SemaphoreType.DMA((n - 1, rows // 256)),
            pltpu.SemaphoreType.DMA((n - 1, rows // 256)),
            pltpu.SemaphoreType.DMA((n - 1,)),
            pltpu.SemaphoreType.DMA((n - 1,)),
        ]
        + extra,
        compiler_params=params(61, collective_id=4, has_side_effects=True),
        cost_estimate=cost(1e6, 1e6),
        name="unproject",
    )(*operands, tok_full, stat, weight)


def per_device(tokens, segment_ids, in_weight, out_weight, gate_up_weight, down_weight, cotangent):
    rows = tokens.shape[0]
    width = in_weight.shape[0]
    span = in_weight.shape[2]
    heads = span // HD
    hidden_local = down_weight.shape[0]
    me = lax.axis_index("ctx")
    tp_size = lax.axis_size("tp")
    cube = lax.axis_size("ctx") == CUBE

    def gather(local, axis=1):
        return lax.all_gather(local, "tp", axis=axis, tiled=True)

    places = me * rows + jnp.arange(rows, dtype=jnp.int32)
    cosine, sine = rope_tables(places)
    in_w = jnp.transpose(in_weight, (1, 0, 2))
    gu_w = jnp.transpose(
        gate_up_weight.reshape(width, 2, hidden_local // BLOCK, BLOCK), (0, 2, 1, 3)
    )
    gu_w = gu_w.reshape(width, 2 * hidden_local)

    all_seg = lax.all_gather(segment_ids, "ctx", axis=0, tiled=True)
    count = all_seg.shape[0]
    every = jnp.arange(count, dtype=jnp.int32)
    opens = jnp.concatenate([jnp.ones((1,), jnp.bool_), all_seg[1:] != all_seg[:-1]])
    all_begin = lax.cummax(jnp.where(opens, every, 0))
    blocks = all_begin.reshape(count // rows, rows)

    tok_full, gu_w, blocks, all_begin = lax.optimization_barrier(
        (gather(tokens), gu_w, blocks, all_begin)
    )
    key_info = jnp.stack(
        [me, blocks[me, 0] // rows, (blocks[me, rows - 1] + rows - 1) // rows]
    ).astype(jnp.int32)
    query_info = jnp.stack(
        [
            me,
            jnp.sum((blocks[:, 0] < (me + 1) * rows).astype(jnp.int32)) - 1,
            jnp.sum((blocks[:, rows - 1] <= me * rows).astype(jnp.int32)) - 1,
        ]
    ).astype(jnp.int32)
    begin = lax.dynamic_slice_in_dim(blocks, me, 1, 0)
    all_begin = all_begin[None, :]
    if cube:
        inner1, stat1, query, raw, mixed, lse, all_pairs, cot_full, out_part = attend_far(
            tok_full, in_w, cosine, sine, begin, cotangent, out_weight, heads, tp_size
        )
    else:
        inner1, stat1, query, pairs = project(tok_full, in_w, cosine, sine, heads)
        all_pairs = lax.all_gather(pairs, "ctx", axis=0, tiled=True)
        cot_full = gather(cotangent)
        raw, mixed, lse = attend(key_info, query, all_pairs, begin, heads)
        out_part = jnp.dot(mixed, out_weight, preferred_element_type=F32).astype(BF16)
    late_query, mixed = lax.optimization_barrier((query, mixed))
    all_query = lax.all_gather(late_query, "ctx", axis=0, tiled=True)
    inner2, resid1, stat2, grad_hidden = merge(
        out_part, tok_full, cot_full, down_weight, tp_size
    )

    hidden, grad_gu, down_grad, gu_grad = feed(inner2, cot_full, gu_w, grad_hidden, BLOCK)
    down_grad, gu_grad, all_query, grad_gu, hidden = lax.optimization_barrier(
        (down_grad, gu_grad, all_query, grad_gu, hidden)
    )
    if not cube:
        down_grad = lax.psum(down_grad, "ctx")
    gu_grad = lax.optimization_barrier(lax.psum(gu_grad, "ctx"))

    grad_part = lax.dot_general(grad_gu, gu_w, NT, preferred_element_type=F32).astype(BF16)
    branch_grad, branch, *mids = norm_back(
        grad_part, cot_full, resid1, stat2, hidden, down_weight, tp_size,
        [down_grad] if cube else [],
    )
    grad_mixed, delta = mixed_grad(branch_grad, out_weight, raw, lse, heads)
    if cube:
        dq, dk, dv, layer_out, mid = attend_back_far(
            grad_mixed, all_query, all_pairs, blocks, branch, mids[0], heads, tp_size
        )
    else:
        branch = lax.psum_scatter(branch, "tp", scatter_dimension=1, tiled=True)
        layer_out = branch
        all_grad = lax.all_gather(grad_mixed, "ctx", axis=0, tiled=True)
        dq = query_grad(key_info, query, grad_mixed, lse, delta, all_pairs, begin, heads)
        dk, dv = key_grad(query_info, pairs, all_query, all_grad, all_begin, heads)

    if cube:
        tokens_grad, *halves = unproject(
            True, [dq, dk, dv, cosine, sine, inner1, mixed, branch_grad, mid],
            tok_full, stat1, in_w, heads, tp_size,
        )
        swap = [(i, i + 1 - 2 * (i % 2)) for i in range(CUBE)]
        core = (me % 2)[None]
        far = [lax.ppermute(half, "ctx", swap) for half in halves]
        *far, gu_grad = lax.optimization_barrier((*far, weave(gu_grad, BLOCK)))
        in_grad, out_grad, down_grad = join(core, halves, far)
    else:
        out_grad = lax.dot_general(
            mixed, branch_grad, TN, preferred_element_type=F32
        ).astype(BF16)
        dproj, in_grad = unrotate(dq, dk, dv, cosine, sine, inner1, heads)
        in_grad, out_grad, down_grad, gu_grad = lax.optimization_barrier(
            (in_grad, out_grad, down_grad, gu_grad)
        )
        in_grad, out_grad = lax.psum((in_grad, out_grad), "ctx")
        (tokens_grad,) = unproject(
            False, [dproj, branch_grad], tok_full, stat1, in_w, heads, tp_size
        )
        in_grad, out_grad, down_grad = widen(in_grad), out_grad.astype(F32), widen(down_grad)
        gu_grad = weave(gu_grad, BLOCK)
    return (
        layer_out,
        tokens_grad,
        jnp.transpose(in_grad.reshape(3, width, span), (1, 0, 2)),
        out_grad,
        gu_grad,
        down_grad,
    )


def solution(mesh):
    placed = (
        P("ctx", "tp"),
        P("ctx"),
        P(None, None, "tp"),
        P("tp", None),
        P(None, None, "tp"),
        P("tp", None),
        P("ctx", "tp"),
    )
    return jax.shard_map(
        per_device,
        mesh=mesh,
        in_specs=placed,
        out_specs=(
            P("ctx", "tp"),
            P("ctx", "tp"),
            P(None, None, "tp"),
            P("tp", None),
            P(None, None, "tp"),
            P("tp", None),
        ),
        check_vma=False,
    )
```

```python
import functools

import jax
import jax.numpy as jnp
from jax import lax
from jax.experimental import pallas as pl
from jax.experimental.pallas import tpu as pltpu
from jax.sharding import PartitionSpec as P

HD = 128
EPS = 1e-05
NEG = -1e30
SCALE = HD ** (-0.5)
LOG2E = 1.4426950408889634
C2 = SCALE * LOG2E
F32 = jnp.float32
BF16 = jnp.bfloat16
NT = (((1,), (1,)), ((), ()))
TN = (((0,), (0,)), ((), ()))
MESH = pl.DeviceIdType.MESH
BLOCK = 512
SUB = 32


def params(mib, **more):
    return pltpu.CompilerParams(vmem_limit_bytes=mib << 20, **more)


def cost(flops, nbytes, trans=0):
    return pl.CostEstimate(flops=int(flops), bytes_accessed=int(nbytes), transcendentals=int(trans))


def rope_tables(places):
    half = HD // 2
    freq = 10000.0 ** (-jnp.arange(half, dtype=F32) * 2.0 / HD)
    angle = places.astype(F32)[:, None] * freq[None, :]
    cosine, sine = jnp.cos(angle), jnp.sin(angle)
    return jnp.concatenate([cosine, cosine], axis=1), jnp.concatenate([-sine, sine], axis=1)


def project_kernel(heads, tok_ref, w_ref, cos_ref, sin_ref, inner_ref, stat_ref, q_ref, kv_ref):
    x = tok_ref[...].astype(F32)
    center = x - jnp.mean(x, axis=1, keepdims=True)
    inverse = lax.rsqrt(jnp.mean(center * center, axis=1, keepdims=True) + EPS)
    inner = (center * inverse).astype(BF16)
    inner_ref[...] = inner
    stat_ref[...] = jnp.concatenate(
        [jnp.mean(x, axis=1, keepdims=True), inverse], axis=1
    )
    cosine, sine = cos_ref[...], sin_ref[...]
    span = heads * HD
    for part in range(3):
        out = jnp.dot(inner, w_ref[part], preferred_element_type=F32)
        if part == 2:
            kv_ref[:, span:] = out.astype(BF16)
            continue
        for h in range(heads):
            piece = out[:, h * HD : (h + 1) * HD]
            turned = (piece * cosine + pltpu.roll(piece, HD // 2, 1) * sine).astype(BF16)
            if part == 0:
                q_ref[:, h * HD : (h + 1) * HD] = turned
            else:
                kv_ref[:, h * HD : (h + 1) * HD] = turned


def project(tok_full, weight, cosine, sine, heads):
    rows, width = tok_full.shape
    span = heads * HD
    block = 256
    row = lambda n: pl.BlockSpec((block, n), lambda i: (i, 0))
    return pl.pallas_call(
        functools.partial(project_kernel, heads),
        grid=(rows // block,),
        in_specs=[
            row(width),
            pl.BlockSpec((3, width, span), lambda i: (0, 0, 0)),
            row(HD),
            row(HD),
        ],
        out_specs=[row(width), row(2), row(span), row(2 * span)],
        out_shape=[
            jax.ShapeDtypeStruct((rows, width), BF16),
            jax.ShapeDtypeStruct((rows, 2), F32),
            jax.ShapeDtypeStruct((rows, span), BF16),
            jax.ShapeDtypeStruct((rows, 2 * span), BF16),
        ],
        compiler_params=params(56),
        cost_estimate=cost(6 * rows * width * span, 6 * width * span + 6 * rows * width),
        name="project",
    )(tok_full, weight, cosine, sine)


def masked(scores, j, me, rows, begin):
    key_place = lax.broadcasted_iota(jnp.int32, scores.shape, 0) + j * rows
    query_place = lax.broadcasted_iota(jnp.int32, scores.shape, 1) + me * rows
    return jnp.where((key_place <= query_place) & (key_place >= begin), scores, NEG)


def attend_kernel(
    heads, info, q_ref, k_ref, v_ref, begin_ref, raw_ref, mixed_ref, lse_ref,
    high_ref, total_ref, acc_ref, s_ref,
):
    me, first, clear = info[0], info[1], info[2]
    j = pl.program_id(0)
    rows = q_ref.shape[0]

    @pl.when(j == 0)
    def _():
        high_ref[...] = jnp.full_like(high_ref, NEG)
        total_ref[...] = jnp.zeros_like(total_ref)
        acc_ref[...] = jnp.zeros_like(acc_ref)

    def block(hide):
        def score(h):
            hs = slice(h * HD, (h + 1) * HD)
            s = lax.dot_general(k_ref[:, hs], q_ref[:, hs], NT, preferred_element_type=F32)
            if hide:
                s = masked(s, j, me, rows, begin_ref[...])
            s_ref[h % 2] = s

        def spread(h):
            hs = slice(h * HD, (h + 1) * HD)
            s = s_ref[h % 2]
            old = high_ref[h : h + 1, :]
            new = jnp.maximum(old, jnp.max(s, axis=0, keepdims=True))
            high_ref[h : h + 1, :] = new
            p = jnp.exp2(s * C2 - new * C2)
            decay = jnp.exp2((old - new) * C2)
            total_ref[h : h + 1, :] = total_ref[h : h + 1, :] * decay + jnp.sum(
                p, axis=0, keepdims=True
            )
            acc_ref[h] = acc_ref[h] * decay + lax.dot_general(
                v_ref[:, hs], p.astype(BF16), TN, preferred_element_type=F32
            )

        score(0)
        for h in range(heads):
            if h + 1 < heads:
                score(h + 1)
            spread(h)

    @pl.when((j >= clear) & (j < me))
    def _():
        block(False)

    @pl.when(((j >= first) & (j < clear) & (j < me)) | (j == me))
    def _():
        block(True)

    @pl.when(j == me)
    def _():
        for h in range(heads):
            hs = slice(h * HD, (h + 1) * HD)
            out = (acc_ref[h] / total_ref[h : h + 1, :]).T
            raw_ref[:, hs] = out
            mixed_ref[:, hs] = out.astype(BF16)
        lse_ref[...] = high_ref[...] * C2 + jnp.log2(total_ref[...])


def attend(info, query, pairs, begin, heads):
    rows = query.shape[0]
    total = pairs.shape[0]
    span = heads * HD
    full = lambda shape: pl.BlockSpec(shape, lambda j, s: (0, 0))
    key = pl.BlockSpec((rows, span), lambda j, s: (jnp.clip(j, s[1], s[0]), 0))
    value = pl.BlockSpec((rows, span), lambda j, s: (jnp.clip(j, s[1], s[0]), 1))
    return pl.pallas_call(
        functools.partial(attend_kernel, heads),
        grid_spec=pltpu.PrefetchScalarGridSpec(
            num_scalar_prefetch=1,
            grid=(total // rows,),
            in_specs=[full((rows, span)), key, value, full((1, rows))],
            out_specs=[full((rows, span)), full((rows, span)), full((heads, rows))],
            scratch_shapes=[
                pltpu.VMEM((heads, rows), F32),
                pltpu.VMEM((heads, rows), F32),
                pltpu.VMEM((heads, HD, rows), F32),
                pltpu.VMEM((2, rows, rows), F32),
            ],
        ),
        out_shape=[
            jax.ShapeDtypeStruct((rows, span), F32),
            jax.ShapeDtypeStruct((rows, span), BF16),
            jax.ShapeDtypeStruct((heads, rows), F32),
        ],
        compiler_params=params(56),
        cost_estimate=cost(4 * rows * total * span, 4 * total * span, rows * total * heads),
        name="attend",
    )(info, query, pairs, pairs, begin)


CUBE = 8
CUBE_SENDS = 10


class Cube:
    def __init__(self, buf, send, recv):
        me = lax.axis_index("ctx")
        flip = (1 - 2 * (me % 2), 2 - 4 * ((me // 2) % 2), 4 - 8 * (me // 4))
        self.me, self.flip, self.buf, self.send, self.recv = me, flip, buf, send, recv
        self.rows = buf.shape[0] // CUBE

    def copy(self, n):
        core, x, y = self.flip
        half = self.rows // 2
        block, part, target = (
            (0, None, core),
            (0, 0, x), (0, 1, x), (0, 1, y), (0, 0, y),
            (x, 0, y), (y, 1, x),
            (x, None, core), (y, None, core), (x + y, None, core),
        )[n]
        start = (self.me + block) * self.rows
        size = self.rows
        if part is not None:
            start, size = start + part * half, half
        place = self.buf.at[pl.ds(pl.multiple_of(start, 16), size)]
        return pltpu.make_async_remote_copy(
            src_ref=place, dst_ref=place, send_sem=self.send.at[n], recv_sem=self.recv.at[n],
            device_id={"ctx": self.me + target}, device_id_type=MESH,
        )

    def arrived(self, n):
        self.copy(n).wait_recv()

    def start(self, *which):
        for n in which:
            self.copy(n).start()

    def signal(self, barrier):
        for target in self.flip:
            pl.semaphore_signal(
                barrier, inc=1, device_id={"ctx": self.me + target}, device_id_type=MESH
            )

    def block(self, step):
        core, x, y = self.flip
        on = lambda *steps: sum((step == n).astype(jnp.int32) for n in steps)
        return self.me + on(1, 4, 5, 7) * core + on(2, 4, 6, 7) * x + on(3, 5, 6, 7) * y

    def advance(self, step):
        @pl.when(step == 1)
        def _():
            self.arrived(0)

        @pl.when(step == 2)
        def _():
            self.arrived(1)
            self.start(5)
            self.arrived(3)
            self.start(6)
            self.arrived(2)
            self.start(7)

        @pl.when(step == 3)
        def _():
            self.arrived(4)
            self.start(8)

        @pl.when(step == 4)
        def _():
            self.arrived(7)

        @pl.when(step == 5)
        def _():
            self.arrived(8)

        @pl.when(step == 6)
        def _():
            self.arrived(5)
            self.arrived(6)
            self.start(9)

        @pl.when(step == 7)
        def _():
            self.arrived(9)

    def finish(self):
        for n in range(CUBE_SENDS):
            self.copy(n).wait_send()


SUM_SENDS = 9


class CubeSum:
    def __init__(self, own, near, land, send, recv, local, out=None, mid=None):
        me = lax.axis_index("ctx")
        core, x, y = me % 2, (me // 2) % 2, me // 4
        self.me, self.own, self.out, self.land, self.mid = me, own, out, land, mid
        self.near, self.send, self.recv, self.local = near, send, recv, local
        rows = own.shape[0]
        self.half, self.eighth, self.last = rows // 2, rows // 8, rows // 16
        second = rows // 4
        self.to = (1 - 2 * core, 2 - 4 * x, 4 - 8 * y)
        self.mine, self.other = core * self.half, (1 - core) * self.half
        self.offset = 0 if local is not None else self.mine
        self.keep1 = (x * self.eighth, second + y * self.eighth)
        self.give1 = ((1 - x) * self.eighth, second + (1 - y) * self.eighth)
        self.keep2 = (self.keep1[0] + y * self.last, self.keep1[1] + x * self.last)
        self.give2 = (self.keep1[0] + (1 - y) * self.last, self.keep1[1] + (1 - x) * self.last)

    def copy(self, n):
        core, x, y = self.to
        half, eighth, last, out, land = self.half, self.eighth, self.last, self.out, self.land
        source, start, size, target = (
            (self.own, self.other, half, core),
            (land, self.give1[0], eighth, x), (land, self.give1[1], eighth, y),
            (land, self.give2[0], last, y), (land, self.give2[1], last, x),
            (out, self.keep2[0], last, y), (out, self.keep2[1], last, x),
            (out, self.keep1[0], eighth, x), (out, self.keep1[1], eighth, y),
        )[n]
        src = source.at[pl.ds(pl.multiple_of(start, 16), size)]
        if n < 5:
            landing = (0, half, half + eighth, half + 2 * eighth, half + 2 * eighth + last)[n]
            dst = land.at[pl.ds(landing, size)]
        else:
            dst = src
        return pltpu.make_async_remote_copy(
            src_ref=src, dst_ref=dst, send_sem=self.send.at[n], recv_sem=self.recv.at[n],
            device_id={"ctx": self.me + target}, device_id_type=MESH,
        )

    def add(self, target, to, source, at, landed, size):
        step = size
        while step * self.own.shape[1] > 256 * 1024 and step % 32 == 0:
            step = step // 2

        def part(i, carry):
            def rows(begin):
                return pl.ds(pl.multiple_of(begin + i * step, 16), step)

            total = source[rows(at), :].astype(F32) + self.land[rows(landed), :].astype(F32)
            target[rows(to), :] = total.astype(BF16)
            return carry

        lax.fori_loop(0, size // step, part, 0)

    def read(self):
        rows = pl.ds(pl.multiple_of(self.mine, 16), self.half)
        return pltpu.make_async_copy(self.own.at[rows], self.near, self.local.at[0])

    def begin(self):
        self.copy(0).start()
        if self.local is not None:
            self.read().start()

    def reduce(self, k):
        half, eighth, last, land = self.half, self.eighth, self.last, self.land
        i = k % 2
        if k == 0:
            if self.local is not None:
                self.read().wait()
            self.copy(0).wait_recv()
        if k < 2:
            at = self.give1[i]
            self.add(land, at, self.near, self.offset + at, at, eighth)
            self.copy(1 + i).start()
        elif k < 4:
            at = self.keep1[i]
            self.add(land, at, self.near, self.offset + at, at, eighth)
        elif k < 6:
            self.copy(1 + i).wait_recv()
            landed = half + i * eighth - self.keep1[i]
            if self.out is None:
                at = self.keep1[i]
                self.add(self.mid, i * eighth, land, at, landed + at, eighth)
                return
            at = self.give2[i]
            self.add(land, at, land, at, landed + at, last)
            self.copy(3 + i).start()
            at = self.keep2[i]
            self.add(land, at, land, at, landed + at, last)
        else:
            self.copy(3 + i).wait_recv()
            at = self.keep2[i]
            self.add(self.out, at, land, at, half + 2 * eighth + i * last, last)

    def gather(self, k):
        for i in range(2):
            if k == 0:
                self.copy(5 + i).start()
            if k == 1:
                self.copy(5 + i).wait_recv()
                self.copy(7 + i).start()
            if k == 2:
                self.copy(7 + i).wait_recv()

    def finish(self):
        for n in range(3 if self.out is None else SUM_SENDS):
            self.copy(n).wait_send()

    def signal(self, barrier):
        for target in self.to:
            pl.semaphore_signal(
                barrier, inc=1, device_id={"ctx": self.me + target}, device_id_type=MESH
            )


class MidSum:
    def __init__(self, mid, land, out, send, recv):
        me = lax.axis_index("ctx")
        x, y = (me // 2) % 2, me // 4
        self.me, self.mid, self.land, self.out, self.send, self.recv = me, mid, land, out, send, recv
        self.eighth, self.last = mid.shape[0] // 2, mid.shape[0] // 4
        self.bit = (y, x)
        self.to = (4 - 8 * y, 2 - 4 * x)

    def copy(self, n):
        i = n % 2
        keep = i * self.eighth + self.bit[i] * self.last
        give = i * self.eighth + (1 - self.bit[i]) * self.last
        if n < 2:
            src = self.mid.at[pl.ds(pl.multiple_of(give, 16), self.last)]
            dst = self.land.at[pl.ds(i * self.last, self.last)]
        else:
            src = dst = self.out.at[pl.ds(pl.multiple_of(keep, 16), self.last)]
        return pltpu.make_async_remote_copy(
            src_ref=src, dst_ref=dst, send_sem=self.send.at[n], recv_sem=self.recv.at[n],
            device_id={"ctx": self.me + self.to[i]}, device_id_type=MESH,
        )

    def begin(self):
        for i in range(2):
            self.copy(i).start()

    def turn(self):
        for i in range(2):
            self.copy(i).wait_recv()
            keep = i * self.eighth + self.bit[i] * self.last
            rows = pl.ds(pl.multiple_of(keep, 16), self.last)
            landed = self.land[i * self.last : (i + 1) * self.last, :]
            self.out[rows, :] = (
                self.mid[rows, :].astype(F32) + landed.astype(F32)
            ).astype(BF16)
            self.copy(2 + i).start()

    def finish(self):
        for i in range(2):
            self.copy(2 + i).wait_recv()
        for n in range(4):
            self.copy(n).wait_send()


class LastGather:
    def __init__(self, mid, out, send, recv, local):
        me = lax.axis_index("ctx")
        x, y = (me // 2) % 2, me // 4
        self.me, self.mid, self.out = me, mid, out
        self.send, self.recv, self.local = send, recv, local
        self.eighth = mid.shape[0] // 2
        self.start_at = (x * self.eighth, (2 + y) * self.eighth)
        self.to = (2 - 4 * x, 4 - 8 * y)

    def ends(self, i):
        src = self.mid.at[pl.ds(i * self.eighth, self.eighth)]
        return src, self.out.at[pl.ds(pl.multiple_of(self.start_at[i], 16), self.eighth)]

    def copy(self, i):
        src, dst = self.ends(i)
        return pltpu.make_async_remote_copy(
            src_ref=src, dst_ref=dst, send_sem=self.send.at[i], recv_sem=self.recv.at[i],
            device_id={"ctx": self.me + self.to[i]}, device_id_type=MESH,
        )

    def keep(self, i):
        src, dst = self.ends(i)
        return pltpu.make_async_copy(src, dst, self.local.at[i])

    def begin(self):
        for i in range(2):
            self.copy(i).start()
            self.keep(i).start()

    def finish(self):
        for i in range(2):
            self.copy(i).wait()
            self.keep(i).wait()


def sum_scratch(shape):
    return [
        pltpu.VMEM((shape[0] // 2, shape[1]), BF16),
        pltpu.VMEM((shape[0] // 2 + 3 * (shape[0] // 8), shape[1]), BF16),
        pltpu.SemaphoreType.DMA((SUM_SENDS,)),
        pltpu.SemaphoreType.DMA((SUM_SENDS,)),
        pltpu.SemaphoreType.DMA((1,)),
    ]


def join_kernel(count, core_ref, *refs):
    for own_ref, far_ref, out_ref in zip(refs[:count], refs[count : 2 * count], refs[2 * count :]):
        @pl.when(pl.program_id(0) == 0)
        def _():
            out_ref[...] = own_ref[...].astype(F32)

        @pl.when(pl.program_id(0) == 1)
        def _():
            out_ref[...] = far_ref[...].astype(F32)


def join(core, own, far):
    steps = 4
    block = lambda half, at: pl.BlockSpec((half.shape[0] // steps, half.shape[1]), at)
    first = lambda h, b, s: (jnp.where(h == 0, b, steps - 1), 0)
    second = lambda h, b, s: (jnp.where(h == 0, 0, b), 0)
    target = lambda h, b, s: (jnp.where(h == 0, s[0], 1 - s[0]) * steps + b, 0)
    size = sum(half.shape[0] * half.shape[1] for half in own)
    return pl.pallas_call(
        functools.partial(join_kernel, len(own)),
        grid_spec=pltpu.PrefetchScalarGridSpec(
            num_scalar_prefetch=1,
            grid=(2, steps),
            in_specs=[block(half, first) for half in own] + [block(half, second) for half in own],
            out_specs=[block(half, target) for half in own],
        ),
        out_shape=[
            jax.ShapeDtypeStruct((2 * half.shape[0], half.shape[1]), F32) for half in own
        ],
        compiler_params=params(56),
        cost_estimate=cost(2 * size, 12 * size),
        name="join",
    )(core, *own, *far)


def hidden_scores(scores, key_block, query_block, rows, begin):
    key_place = lax.broadcasted_iota(jnp.int32, scores.shape, 0) + key_block * rows
    query_place = lax.broadcasted_iota(jnp.int32, scores.shape, 1) + query_block * rows
    return jnp.where((key_place <= query_place) & (key_place >= begin), scores, NEG)


FAR_STEPS = 8
FAR_SENDS = 17


def attend_far_kernel(
    heads, n, tok_ref, in_ref, cos_ref, sin_ref, begin_ref, cot_ref, w_ref,
    inner_ref, stat_ref, raw_ref, mixed_ref, lse_ref, keep_ref, full_ref, part_ref,
    pair_ref, q_ref, high_ref, total_ref, acc_ref, s_ref,
    guest_ref, guest_high, guest_total, guest_acc, guest_out, guest_stat, back_out, back_stat,
    send, recv, zsend, zrecv,
):
    rows = q_ref.shape[0]
    half = rows // 2
    span = heads * HD
    shard = cot_ref.shape[1]
    at = lax.axis_index("tp")
    me = lax.axis_index("ctx")
    core, x, y = me % 2, (me // 2) % 2, me // 4
    to_core, to_x, to_y = 1 - 2 * core, 2 - 4 * x, 4 - 8 * y
    diagonal = me + to_x + to_y
    barrier = pltpu.get_barrier_semaphore()
    for target in (me + to_core, me + to_x, me + to_y, diagonal):
        pl.semaphore_signal(barrier, inc=1, device_id={"ctx": target}, device_id_type=MESH)

    @pl.when(at > 0)
    def _():
        pl.semaphore_signal(barrier, inc=1, device_id={"tp": at - 1}, device_id_type=MESH)

    @pl.when(at < n - 1)
    def _():
        pl.semaphore_signal(barrier, inc=1, device_id={"tp": at + 1}, device_id_type=MESH)

    def block_rows(block):
        return pl.ds(pl.multiple_of(block * rows, 16), rows)

    def copy(k):
        if k < 14:
            block, part, parts, target = (
                (me, 0, 1, to_core),
                (me, 0, 2, to_x), (me, 1, 2, to_x),
                (me, 0, 4, to_y), (me, 1, 4, to_y), (me, 2, 4, to_y), (me, 3, 4, to_y),
                (me + to_x, 0, 1, to_core), (me + to_y, 0, 1, to_core),
                (me + to_y, 0, 4, to_x), (me + to_y, 1, 4, to_x),
                (me + to_y, 2, 4, to_x), (me + to_y, 3, 4, to_x),
                (diagonal, 0, 1, to_core),
            )[k]
            size = rows // parts
            src = dst = pair_ref.at[pl.ds(pl.multiple_of(block * rows + part * size, 16), size)]
        else:
            src, dst = (
                (q_ref, guest_ref), (guest_out, back_out), (guest_stat, back_stat)
            )[k - 14]
            target = to_x + to_y
        return pltpu.make_async_remote_copy(
            src_ref=src, dst_ref=dst, send_sem=send.at[k], recv_sem=recv.at[k],
            device_id={"ctx": me + target}, device_id_type=MESH,
        )

    def on_chip(*which):
        return sum((me // 2 == chip).astype(jnp.int32) for chip in which) > 0

    def project(rows_at, part):
        out = jnp.dot(inner_ref[rows_at, :], in_ref[part], preferred_element_type=F32)
        if part == 2:
            return out.astype(BF16)
        cosine, sine = cos_ref[rows_at, :], sin_ref[rows_at, :]
        pieces = []
        for h in range(heads):
            piece = out[:, h * HD : (h + 1) * HD]
            pieces.append((piece * cosine + pltpu.roll(piece, HD // 2, 1) * sine).astype(BF16))
        return jnp.concatenate(pieces, axis=1)

    def own_pairs(part):
        here = slice(part * half, (part + 1) * half)
        value = tok_ref[here, :].astype(F32)
        mean = jnp.mean(value, axis=1, keepdims=True)
        center = value - mean
        inverse = lax.rsqrt(jnp.mean(center * center, axis=1, keepdims=True) + EPS)
        stat_ref[here, :] = jnp.concatenate([mean, inverse], axis=1)
        inner_ref[here, :] = (center * inverse).astype(BF16)
        place = pl.ds(pl.multiple_of(me * rows + part * half, 16), half)
        pair_ref[place, :span] = project(here, 1)
        pair_ref[place, span:] = project(here, 2)

    own_pairs(0)
    full_ref[:, pl.ds(pl.multiple_of(at * shard, 128), shard)] = cot_ref[...]
    pl.semaphore_wait(barrier, jnp.where((at > 0) & (at < n - 1), 6, 5))

    @pl.when(y == 0)
    def _():
        copy(3).start()
        copy(4).start()

    @pl.when(x == 0)
    def _():
        copy(1).start()

    own_pairs(1)

    @pl.when(y == 0)
    def _():
        copy(5).start()
        copy(6).start()

    @pl.when(x == 0)
    def _():
        copy(2).start()

    copy(0).start()
    q_ref[...] = project(slice(0, rows), 0)

    @pl.when(on_chip(3))
    def _():
        copy(14).start()

    keep_ref[:, : 2 * span] = pair_ref[block_rows(me), :]
    keep_ref[:, 2 * span :] = q_ref[...]

    def pass_on(right, s, k):
        place = full_ref.at[:, pl.ds(pl.multiple_of(s * shard, 128), shard)]
        which = (1 if right else 0, k)
        return pltpu.make_async_remote_copy(
            src_ref=place, dst_ref=place, send_sem=zsend.at[which], recv_sem=zrecv.at[which],
            device_id={"tp": at + 1 if right else at - 1}, device_id_type=MESH,
        )

    def line_step(k):
        @pl.when(at >= k)
        def _():
            if k > 0:
                pass_on(True, at - k, k - 1).wait_recv()

            @pl.when(at < n - 1)
            def _():
                pass_on(True, at - k, k).start()

        @pl.when(at + k < n)
        def _():
            if k > 0:
                pass_on(False, at + k, k - 1).wait_recv()

            @pl.when(at > 0)
            def _():
                pass_on(False, at + k, k).start()

    def clear(high, total, acc):
        high[...] = jnp.full_like(high, NEG)
        total[...] = jnp.zeros_like(total)
        acc[...] = jnp.zeros_like(acc)

    def attend_block(key_block, queries, query_block, high, total, acc):
        place = block_rows(key_block)
        begin = begin_ref[pl.ds(query_block, 1), :]

        def score(h):
            hs = slice(h * HD, (h + 1) * HD)
            s = lax.dot_general(
                pair_ref[place, hs], queries[:, hs], NT, preferred_element_type=F32
            )
            s_ref[h % 2] = hidden_scores(s, key_block, query_block, rows, begin)

        def spread(h):
            s = s_ref[h % 2]
            old = high[h : h + 1, :]
            new = jnp.maximum(old, jnp.max(s, axis=0, keepdims=True))
            high[h : h + 1, :] = new
            p = jnp.exp2(s * C2 - new * C2)
            decay = jnp.exp2((old - new) * C2)
            total[h : h + 1, :] = total[h : h + 1, :] * decay + jnp.sum(p, axis=0, keepdims=True)
            acc[h] = acc[h] * decay + lax.dot_general(
                pair_ref[place, span + h * HD : span + (h + 1) * HD], p.astype(BF16), TN,
                preferred_element_type=F32,
            )

        score(0)
        for h in range(heads):
            if h + 1 < heads:
                score(h + 1)
            spread(h)

    def guest():
        clear(guest_high, guest_total, guest_acc)
        copy(14).wait_recv()

        def turn(k, carry):
            attend_block(
                me + k * to_core, guest_ref, diagonal, guest_high, guest_total, guest_acc
            )
            return carry

        lax.fori_loop(0, 2, turn, 0)
        for h in range(heads):
            guest_out[h * HD : (h + 1) * HD, :] = (
                guest_acc[h] / guest_total[h : h + 1, :]
            ).astype(BF16)
        guest_stat[:heads, :] = guest_high[...]
        guest_stat[heads:, :] = guest_total[...]
        copy(15).start()
        copy(16).start()

    clear(high_ref, total_ref, acc_ref)

    def turn(step, carry):
        for k in range(n):
            @pl.when(step == (min(k * 2, FAR_STEPS - n + k) if n <= FAR_STEPS else k))
            def _():
                line_step(k)

        @pl.when(step == 1)
        def _():
            copy(0).wait_recv()

        @pl.when((step == 2) & on_chip(0))
        def _():
            guest()

        @pl.when((step == 2) & on_chip(3))
        def _():
            for k in range(4):
                copy(3 + k).wait_recv()
                copy(9 + k).start()

        @pl.when((step == 2) & (x == 1))
        def _():
            copy(1).wait_recv()
            copy(2).wait_recv()
            copy(7).start()

        @pl.when((step == 3) & on_chip(2))
        def _():
            for k in range(4):
                copy(3 + k).wait_recv()

        @pl.when((step == 3) & (y == 1))
        def _():
            copy(8).start()

        @pl.when((step == 4) & (x == 1))
        def _():
            copy(7).wait_recv()

        @pl.when((step == 5) & (y == 1))
        def _():
            copy(8).wait_recv()

        @pl.when((step == 6) & on_chip(2))
        def _():
            for k in range(4):
                copy(9 + k).wait_recv()
            copy(13).start()

        @pl.when((step == 7) & on_chip(2))
        def _():
            copy(13).wait_recv()

        on = lambda *steps: sum((step == k).astype(jnp.int32) for k in steps)
        block = (
            me + on(1, 4, 5, 7) * to_core + on(2, 4, 6, 7) * to_x + on(3, 5, 6, 7) * to_y
        )
        here = on(0, 1) + on(2, 4) * x + on(3, 5) * y + on(6, 7) * y * (1 - x)

        @pl.when((block <= me) & (here > 0))
        def _():
            attend_block(block, q_ref, me, high_ref, total_ref, acc_ref)

        return carry

    lax.fori_loop(0, FAR_STEPS, turn, 0)

    @pl.when(on_chip(3))
    def _():
        copy(15).wait_recv()
        copy(16).wait_recv()
        for h in range(heads):
            old, other = high_ref[h : h + 1, :], back_stat[h : h + 1, :]
            new = jnp.maximum(old, other)
            high_ref[h : h + 1, :] = new
            decay = jnp.exp2((old - new) * C2)
            weight = jnp.exp2((other - new) * C2) * back_stat[heads + h : heads + h + 1, :]
            total_ref[h : h + 1, :] = total_ref[h : h + 1, :] * decay + weight
            acc_ref[h] = acc_ref[h] * decay + weight * back_out[
                h * HD : (h + 1) * HD, :
            ].astype(F32)

    for h in range(heads):
        hs = slice(h * HD, (h + 1) * HD)
        out = (acc_ref[h] / total_ref[h : h + 1, :]).T
        raw_ref[:, hs] = out
        mixed_ref[:, hs] = out.astype(BF16)
    part_ref[...] = jnp.dot(
        mixed_ref[...], w_ref[...], preferred_element_type=F32
    ).astype(BF16)
    lse_ref[...] = high_ref[...] * C2 + jnp.log2(total_ref[...])
    for senders, which in (
        (me >= 0, (0,)), (x == 0, (1, 2)), (y == 0, (3, 4, 5, 6)), (x == 1, (7,)), (y == 1, (8,)),
        (on_chip(3), (9, 10, 11, 12, 14)), (on_chip(2), (13,)), (on_chip(0), (15, 16)),
    ):
        @pl.when(senders)
        def _():
            for k in which:
                copy(k).wait_send()

    for k in range(n):
        @pl.when((at >= k) & (at < n - 1))
        def _():
            pass_on(True, at - k, k).wait_send()

        @pl.when((at + k < n) & (at > 0))
        def _():
            pass_on(False, at + k, k).wait_send()


def attend_far(tok_full, in_weight, cosine, sine, begin, cot, weight, heads, n):
    rows, width = tok_full.shape
    span = heads * HD
    vmem = pl.BlockSpec(memory_space=pltpu.VMEM)
    state = [
        pltpu.VMEM((heads, rows), F32),
        pltpu.VMEM((heads, rows), F32),
        pltpu.VMEM((heads, HD, rows), F32),
    ]
    answer = [pltpu.VMEM((span, rows), BF16), pltpu.VMEM((2 * heads, rows), F32)]
    return pl.pallas_call(
        functools.partial(attend_far_kernel, heads, n),
        in_specs=[vmem] * 7,
        out_specs=[vmem] * 8,
        out_shape=[
            jax.ShapeDtypeStruct((rows, width), BF16),
            jax.ShapeDtypeStruct((rows, 2), F32),
            jax.ShapeDtypeStruct((rows, span), F32),
            jax.ShapeDtypeStruct((rows, span), BF16),
            jax.ShapeDtypeStruct((heads, rows), F32),
            jax.ShapeDtypeStruct((rows, 3 * span), BF16),
            jax.ShapeDtypeStruct((rows, n * cot.shape[1]), BF16),
            jax.ShapeDtypeStruct((rows, width), BF16),
        ],
        scratch_shapes=[
            pltpu.VMEM((CUBE * rows, 2 * span), BF16),
            pltpu.VMEM((rows, span), BF16),
            *state,
            pltpu.VMEM((2, rows, rows), F32),
            pltpu.VMEM((rows, span), BF16),
            *state,
            *answer,
            *answer,
            pltpu.SemaphoreType.DMA((FAR_SENDS,)),
            pltpu.SemaphoreType.DMA((FAR_SENDS,)),
            pltpu.SemaphoreType.DMA((2, n)),
            pltpu.SemaphoreType.DMA((2, n)),
        ],
        compiler_params=params(60, collective_id=2, has_side_effects=True),
        cost_estimate=cost(1e6, 1e6),
        name="attend_far",
    )(tok_full, in_weight, cosine, sine, begin, cot, weight)


def attend_back_far_kernel(
    heads, n, g_ref, kept_ref, begin_ref, part_ref, mid_ref,
    dq_ref, dk_ref, dv_ref, layer_ref, next_ref,
    all_ref, acc_ref, rows_ref, s_ref, p_ref, land_ref, pair_ref, q_ref,
    send, recv, zsend, zrecv, read_sem, mid_land, msend, mrecv,
):
    rows = g_ref.shape[0]
    span = heads * HD
    shard = layer_ref.shape[1]
    at = lax.axis_index("tp")
    cube = Cube(all_ref, send, recv)
    middle = MidSum(mid_ref, mid_land, next_ref, msend, mrecv)
    me = cube.me
    barrier = pltpu.get_barrier_semaphore()
    cube.signal(barrier)
    for o in range(1, n):
        pl.semaphore_signal(
            barrier, inc=1, device_id={"tp": lax.rem(at + o, n)}, device_id_type=MESH
        )

    def read(step, keys):
        place = pl.ds(pl.multiple_of(cube.block(step) * rows, 16), rows)
        near, columns = (pair_ref, (0, 2 * span)) if keys else (q_ref, (2 * span, span))
        return pltpu.make_async_copy(
            kept_ref.at[place, pl.ds(*columns)], near.at[place],
            read_sem.at[0 if keys else 1, step],
        )

    def read_all(step, carry):
        block = cube.block(step)

        @pl.when(block <= me)
        def _():
            read(step, True).start()

        @pl.when(block >= me)
        def _():
            read(step, False).start()

        return carry

    lax.fori_loop(0, CUBE, read_all, 0)
    all_ref[pl.ds(pl.multiple_of(me * rows, 16), rows), :] = g_ref[...]
    acc_ref[...] = jnp.zeros_like(acc_ref)
    dk_ref[...] = jnp.zeros_like(dk_ref)
    dv_ref[...] = jnp.zeros_like(dv_ref)
    pl.semaphore_wait(barrier, 3 + n - 1)

    def term(o):
        target = lax.rem(at + o, n)
        return pltpu.make_async_remote_copy(
            src_ref=part_ref.at[:, pl.ds(pl.multiple_of(target * shard, 128), shard)],
            dst_ref=land_ref.at[o - 1],
            send_sem=zsend.at[o - 1], recv_sem=zrecv.at[o - 1],
            device_id={"tp": target}, device_id_type=MESH,
        )

    own = pl.ds(pl.multiple_of(me * rows, 16), rows)

    cube.start(0, 1, 3, 2, 4)

    def turn(step, carry):
        cube.advance(step)

        @pl.when(step == 0)
        def _():
            for o in range(1, n):
                term(o).start()
            middle.begin()

        @pl.when(step == 3)
        def _():
            middle.turn()

        block = cube.block(step)
        place = pl.ds(pl.multiple_of(block * rows, 16), rows)

        @pl.when(block <= me)
        def _():
            read(step, True).wait()

        @pl.when(block >= me)
        def _():
            read(step, False).wait()

        def scores(h, key_block, key_place, query_block, query_place):
            hs = slice(h * HD, (h + 1) * HD)
            vs = slice(span + h * HD, span + (h + 1) * HD)
            s = lax.dot_general(
                pair_ref[key_place, hs], q_ref[query_place, hs], NT, preferred_element_type=F32
            )
            begin = begin_ref[pl.ds(query_block, 1), :]
            s_ref[h % 2] = hidden_scores(s, key_block, query_block, rows, begin)
            p_ref[h % 2] = lax.dot_general(
                pair_ref[key_place, vs], all_ref[query_place, hs], NT, preferred_element_type=F32
            )

        def read_rows(query_place):
            coded = all_ref[query_place, span:].astype(F32).T
            for k in range(2 * heads):
                rows_ref[k : k + 1, :] = (
                    coded[3 * k : 3 * k + 1]
                    + coded[3 * k + 1 : 3 * k + 2]
                    + coded[3 * k + 2 : 3 * k + 3]
                )

        def weights(h):
            p = jnp.exp2(s_ref[h % 2] * C2 - rows_ref[h : h + 1, :])
            ds = p * (p_ref[h % 2] - rows_ref[heads + h : heads + h + 1, :])
            return p.astype(BF16), ds.astype(BF16)

        @pl.when(block <= me)
        def _():
            read_rows(own)
            scores(0, block, place, me, own)
            for h in range(heads):
                if h + 1 < heads:
                    scores(h + 1, block, place, me, own)
                _, ds = weights(h)
                acc_ref[h] = acc_ref[h] + lax.dot_general(
                    pair_ref[place, h * HD : (h + 1) * HD], ds, TN, preferred_element_type=F32
                )

        @pl.when(block >= me)
        def _():
            read_rows(place)
            scores(0, me, own, block, place)
            for h in range(heads):
                hs = slice(h * HD, (h + 1) * HD)
                if h + 1 < heads:
                    scores(h + 1, me, own, block, place)
                p, ds = weights(h)
                dv_ref[:, hs] += jnp.dot(p, all_ref[place, hs], preferred_element_type=F32)
                dk_ref[:, hs] += jnp.dot(ds, q_ref[place, hs], preferred_element_type=F32)

        return carry

    lax.fori_loop(0, CUBE, turn, 0)
    for h in range(heads):
        dq_ref[:, h * HD : (h + 1) * HD] = (acc_ref[h] * SCALE).T
    dk_ref[...] = dk_ref[...] * SCALE
    total = part_ref[:, pl.ds(pl.multiple_of(at * shard, 128), shard)].astype(F32)
    for o in range(1, n):
        term(o).wait_recv()
        total = total + land_ref[o - 1].astype(F32)
    layer_ref[...] = total.astype(BF16)
    middle.finish()
    cube.finish()
    for o in range(1, n):
        term(o).wait_send()


def attend_back_far(grad, kept, all_begin, part, mid, heads, n):
    rows = grad.shape[0]
    span = heads * HD
    shard = part.shape[1] // n
    vmem = pl.BlockSpec(memory_space=pltpu.VMEM)
    wide = jax.ShapeDtypeStruct((rows, span), F32)
    return pl.pallas_call(
        functools.partial(attend_back_far_kernel, heads, n),
        in_specs=[vmem, pl.BlockSpec(memory_space=pl.ANY)] + [vmem] * 3,
        out_specs=[vmem] * 5,
        out_shape=[wide, wide, wide, jax.ShapeDtypeStruct((rows, shard), BF16)]
        + [jax.ShapeDtypeStruct(mid.shape, BF16)],
        scratch_shapes=[
            pltpu.VMEM((CUBE * rows, span + HD), BF16),
            pltpu.VMEM((heads, HD, rows), F32),
            pltpu.VMEM((2 * heads, rows), F32),
            pltpu.VMEM((2, rows, rows), F32),
            pltpu.VMEM((2, rows, rows), F32),
            pltpu.VMEM((n - 1, rows, shard), BF16),
            pltpu.VMEM((CUBE * rows, 2 * span), BF16),
            pltpu.VMEM((CUBE * rows, span), BF16),
            pltpu.SemaphoreType.DMA((CUBE_SENDS,)),
            pltpu.SemaphoreType.DMA((CUBE_SENDS,)),
            pltpu.SemaphoreType.DMA((n - 1,)),
            pltpu.SemaphoreType.DMA((n - 1,)),
            pltpu.SemaphoreType.DMA((2, CUBE)),
            pltpu.VMEM((mid.shape[0] // 2, mid.shape[1]), BF16),
            pltpu.SemaphoreType.DMA((4,)),
            pltpu.SemaphoreType.DMA((4,)),
        ],
        compiler_params=params(62, collective_id=3, has_side_effects=True),
        cost_estimate=cost(1e6, 1e6),
        name="attend_back_far",
    )(grad, kept, all_begin, part, mid)


def query_grad_kernel(
    heads, info, q_ref, do_ref, lse_ref, delta_ref, k_ref, v_ref, begin_ref,
    dq_ref, acc_ref, s_ref, g_ref,
):
    me, first, clear = info[0], info[1], info[2]
    j = pl.program_id(0)
    rows = q_ref.shape[0]

    @pl.when(j == 0)
    def _():
        acc_ref[...] = jnp.zeros_like(acc_ref)

    def block(hide):
        def score(h):
            hs = slice(h * HD, (h + 1) * HD)
            s = lax.dot_general(k_ref[:, hs], q_ref[:, hs], NT, preferred_element_type=F32)
            if hide:
                s = masked(s, j, me, rows, begin_ref[...])
            s_ref[h % 2] = s
            g_ref[h % 2] = lax.dot_general(
                v_ref[:, hs], do_ref[:, hs], NT, preferred_element_type=F32
            )

        def spread(h):
            hs = slice(h * HD, (h + 1) * HD)
            p = jnp.exp2(s_ref[h % 2] * C2 - lse_ref[h : h + 1, :])
            ds = (p * (g_ref[h % 2] - delta_ref[h : h + 1, :])).astype(BF16)
            acc_ref[h] = acc_ref[h] + lax.dot_general(
                k_ref[:, hs], ds, TN, preferred_element_type=F32
            )

        score(0)
        for h in range(heads):
            if h + 1 < heads:
                score(h + 1)
            spread(h)

    @pl.when((j >= clear) & (j < me))
    def _():
        block(False)

    @pl.when(((j >= first) & (j < clear) & (j < me)) | (j == me))
    def _():
        block(True)

    @pl.when(j == me)
    def _():
        for h in range(heads):
            dq_ref[:, h * HD : (h + 1) * HD] = (acc_ref[h] * SCALE).T


def query_grad(info, query, grad_mixed, lse, delta, pairs, begin, heads):
    rows = query.shape[0]
    total = pairs.shape[0]
    span = heads * HD
    full = lambda shape: pl.BlockSpec(shape, lambda j, s: (0, 0))
    key = pl.BlockSpec((rows, span), lambda j, s: (jnp.clip(j, s[1], s[0]), 0))
    value = pl.BlockSpec((rows, span), lambda j, s: (jnp.clip(j, s[1], s[0]), 1))
    wide = full((rows, span))
    thin = full((heads, rows))
    return pl.pallas_call(
        functools.partial(query_grad_kernel, heads),
        grid_spec=pltpu.PrefetchScalarGridSpec(
            num_scalar_prefetch=1,
            grid=(total // rows,),
            in_specs=[wide, wide, thin, thin, key, value, full((1, rows))],
            out_specs=wide,
            scratch_shapes=[
                pltpu.VMEM((heads, HD, rows), F32),
                pltpu.VMEM((2, rows, rows), F32),
                pltpu.VMEM((2, rows, rows), F32),
            ],
        ),
        out_shape=jax.ShapeDtypeStruct((rows, span), F32),
        compiler_params=params(58),
        cost_estimate=cost(6 * rows * total * span, 4 * total * span, rows * total * heads),
        name="query_grad",
    )(info, query, grad_mixed, lse, delta, pairs, pairs, begin)


def key_grad_kernel(
    heads, info, k_ref, v_ref, q_ref, g_ref, begin_ref, dk_ref, dv_ref,
    rows_ref, s_ref, p_ref,
):
    me, last, clear = info[0], info[1], info[2]
    j = pl.program_id(0)
    rows = k_ref.shape[0]
    span = heads * HD

    @pl.when(j == me)
    def _():
        dk_ref[...] = jnp.zeros_like(dk_ref)
        dv_ref[...] = jnp.zeros_like(dv_ref)

    def block(hide):
        coded = g_ref[:, span:].astype(F32).T
        for n in range(2 * heads):
            rows_ref[n : n + 1, :] = (
                coded[3 * n : 3 * n + 1] + coded[3 * n + 1 : 3 * n + 2] + coded[3 * n + 2 : 3 * n + 3]
            )

        def score(h):
            hs = slice(h * HD, (h + 1) * HD)
            s = lax.dot_general(k_ref[:, hs], q_ref[:, hs], NT, preferred_element_type=F32)
            if hide:
                key_place = lax.broadcasted_iota(jnp.int32, s.shape, 0) + me * rows
                query_place = lax.broadcasted_iota(jnp.int32, s.shape, 1) + j * rows
                s = jnp.where(
                    (key_place <= query_place) & (key_place >= begin_ref[...]), s, NEG
                )
            s_ref[h % 2] = s
            p_ref[h % 2] = lax.dot_general(
                v_ref[:, hs], g_ref[:, hs], NT, preferred_element_type=F32
            )

        def spread(h):
            hs = slice(h * HD, (h + 1) * HD)
            p = jnp.exp2(s_ref[h % 2] * C2 - rows_ref[h : h + 1, :])
            ds = (p * (p_ref[h % 2] - rows_ref[heads + h : heads + h + 1, :])).astype(BF16)
            dv_ref[:, hs] += jnp.dot(p.astype(BF16), g_ref[:, hs], preferred_element_type=F32)
            dk_ref[:, hs] += jnp.dot(ds, q_ref[:, hs], preferred_element_type=F32)

        score(0)
        for h in range(heads):
            if h + 1 < heads:
                score(h + 1)
            spread(h)

    @pl.when((j > me) & (j <= clear))
    def _():
        block(False)

    @pl.when((j == me) | ((j > me) & (j > clear) & (j <= last)))
    def _():
        block(True)

    @pl.when(j == pl.num_programs(0) - 1)
    def _():
        dk_ref[...] = dk_ref[...] * SCALE


def key_grad(info, pairs, all_query, all_grad, all_begin, heads):
    rows = pairs.shape[0]
    total = all_query.shape[0]
    span = heads * HD
    full = lambda shape, at=0: pl.BlockSpec(shape, lambda j, s: (0, at))
    near = lambda j, s: (jnp.clip(j, s[0], s[1]), 0)
    wide = full((rows, span))
    return pl.pallas_call(
        functools.partial(key_grad_kernel, heads),
        grid_spec=pltpu.PrefetchScalarGridSpec(
            num_scalar_prefetch=1,
            grid=(total // rows,),
            in_specs=[
                wide, full((rows, span), 1),
                pl.BlockSpec((rows, span), near),
                pl.BlockSpec((rows, span + HD), near),
                pl.BlockSpec((1, rows), lambda j, s: (0, jnp.clip(j, s[0], s[1]))),
            ],
            out_specs=[wide, wide],
            scratch_shapes=[
                pltpu.VMEM((2 * heads, rows), F32),
                pltpu.VMEM((2, rows, rows), F32),
                pltpu.VMEM((2, rows, rows), F32),
            ],
        ),
        out_shape=[jax.ShapeDtypeStruct((rows, span), F32)] * 2,
        compiler_params=params(58),
        cost_estimate=cost(8 * rows * total * span, 4 * total * span, rows * total * heads),
        name="key_grad",
    )(info, pairs, pairs, all_query, all_grad, all_begin)


def mixed_grad_kernel(heads, branch_ref, w_ref, raw_ref, lse_ref, out_ref, delta_ref):
    span = heads * HD
    low = lax.dot_general(
        branch_ref[...], w_ref[...], NT, preferred_element_type=F32
    ).astype(BF16)
    out_ref[:, :span] = low
    count = low.shape[0]
    both = low.astype(F32) * raw_ref[...]
    for h in range(heads):
        delta_ref[h : h + 1, :] = jnp.sum(both[:, h * HD : (h + 1) * HD].T, axis=0, keepdims=True)
    lines = []
    for n in range(2 * heads):
        value = lse_ref[n : n + 1, :] if n < heads else delta_ref[n - heads : n - heads + 1, :]
        for _ in range(3):
            piece = value.astype(BF16).astype(F32)
            lines.append(piece)
            value = value - piece
    lines.append(jnp.zeros((HD - len(lines), count), F32))
    out_ref[:, span:] = jnp.concatenate(lines, axis=0).T.astype(BF16)


def mixed_grad(branch, weight, raw, lse, heads):
    rows, width = branch.shape
    span = heads * HD
    block = 256
    row = lambda n: pl.BlockSpec((block, n), lambda i: (i, 0))
    line = pl.BlockSpec((heads, block), lambda i: (0, i))
    return pl.pallas_call(
        functools.partial(mixed_grad_kernel, heads),
        grid=(rows // block,),
        in_specs=[row(width), pl.BlockSpec((span, width), lambda i: (0, 0)), row(span), line],
        out_specs=[row(span + HD), line],
        out_shape=[
            jax.ShapeDtypeStruct((rows, span + HD), BF16),
            jax.ShapeDtypeStruct((heads, rows), F32),
        ],
        compiler_params=params(56),
        cost_estimate=cost(2 * rows * width * span, 2 * width * span + 4 * rows * width),
        name="mixed_grad",
    )(branch, weight, raw, lse)


def feed_kernel(
    inner_ref, cot_ref, w_ref, grad_ref, hidden_ref, dgu_ref, down_grad_ref, gu_grad_ref
):
    block = grad_ref.shape[1]
    both = jnp.dot(inner_ref[...], w_ref[...], preferred_element_type=F32)
    grad = grad_ref[...].astype(F32)
    gate, up = both[:, :block], both[:, block:]
    sigma = 1.0 / (1.0 + jnp.exp(-gate))
    active = gate * sigma
    hidden_ref[...] = (active * up).astype(BF16)
    dgu_ref[:, :block] = (grad * up * sigma * (1.0 + gate * (1.0 - sigma))).astype(BF16)
    dgu_ref[:, block:] = (grad * active).astype(BF16)
    down_grad_ref[...] = lax.dot_general(
        hidden_ref[...], cot_ref[...], TN, preferred_element_type=F32
    ).astype(BF16)
    gu_grad_ref[...] = lax.dot_general(
        inner_ref[...], dgu_ref[...], TN, preferred_element_type=F32
    ).astype(BF16)


def feed(inner, cot, weight, grad, block):
    rows, width = inner.shape
    units = grad.shape[1]
    whole = pl.BlockSpec((rows, width), lambda j: (0, 0))
    column = lambda high, wide: pl.BlockSpec((high, wide), lambda j: (0, j))
    line = pl.BlockSpec((block, width), lambda j: (j, 0))
    return pl.pallas_call(
        feed_kernel,
        grid=(units // block,),
        in_specs=[whole, whole, column(width, 2 * block), column(rows, block)],
        out_specs=[column(rows, block), column(rows, 2 * block), line, column(width, 2 * block)],
        out_shape=[
            jax.ShapeDtypeStruct((rows, units), BF16),
            jax.ShapeDtypeStruct((rows, 2 * units), BF16),
            jax.ShapeDtypeStruct((units, width), BF16),
            jax.ShapeDtypeStruct((width, 2 * units), BF16),
        ],
        compiler_params=params(60),
        cost_estimate=cost(
            12 * rows * width * units, 12 * width * units + 4 * rows * width, rows * units
        ),
        name="feed",
    )(inner, cot, weight, grad)


def weave_kernel(block, sum_ref, out_ref):
    for j in range(sum_ref.shape[1] // (2 * block)):
        for k in range(2):
            at = (2 * j + k) * block
            out_ref[:, k, j * block : (j + 1) * block] = sum_ref[:, at : at + block].astype(F32)


def weave(summed, block):
    width, both = summed.shape
    rows = 256
    return pl.pallas_call(
        functools.partial(weave_kernel, block),
        grid=(width // rows,),
        in_specs=[pl.BlockSpec((rows, both), lambda i: (i, 0))],
        out_specs=pl.BlockSpec((rows, 2, both // 2), lambda i: (i, 0, 0)),
        out_shape=jax.ShapeDtypeStruct((width, 2, both // 2), F32),
        compiler_params=params(56),
        cost_estimate=cost(width * both, 6 * width * both),
        name="weave",
    )(summed)


def widen_kernel(in_ref, out_ref):
    out_ref[...] = in_ref[...].astype(F32)


def widen(summed):
    high, wide = summed.shape
    block = pl.BlockSpec((512, wide), lambda i: (i, 0))
    return pl.pallas_call(
        widen_kernel,
        grid=(high // 512,),
        in_specs=[block],
        out_specs=block,
        out_shape=jax.ShapeDtypeStruct((high, wide), F32),
        compiler_params=params(56),
        cost_estimate=cost(high * wide, 6 * high * wide),
        name="widen",
    )(summed)


def line_barrier(at, n, cube=None):
    barrier = pltpu.get_barrier_semaphore()
    if cube is not None:
        cube.signal(barrier)

    @pl.when(at > 0)
    def _():
        pl.semaphore_signal(barrier, inc=1, device_id={"tp": at - 1}, device_id_type=MESH)

    @pl.when(at < n - 1)
    def _():
        pl.semaphore_signal(barrier, inc=1, device_id={"tp": at + 1}, device_id_type=MESH)

    near = jnp.where((at > 0) & (at < n - 1), 2, 1)
    pl.semaphore_wait(barrier, near + (0 if cube is None else 3))


def sum_rows(n, sub, part_ref, out_ref, row_fn, from_left, from_right, send, recv, aside={}):
    at = lax.axis_index("tp")
    chunks = part_ref.shape[0] // sub
    middle = (n // 2 - 1, n // 2)

    def link(kind, right, src, dst, c):
        which = (kind * 2 + (1 if right else 0), c)
        return pltpu.make_async_remote_copy(
            src_ref=src.at[pl.ds(c * sub, sub)],
            dst_ref=dst.at[pl.ds(c * sub, sub)],
            send_sem=send.at[which],
            recv_sem=recv.at[which],
            device_id={"tp": at + 1 if right else at - 1},
            device_id_type=MESH,
        )

    def came(right):
        return from_left if right else from_right

    def first(right, c):
        return link(0, right, part_ref, came(right), c)

    def onward(right, c):
        return link(0, right, came(right), came(right), c)

    def hand(right, c):
        return link(1, right, out_ref, out_ref, c)

    def reduce_step(c):
        owner = middle[c % 2]
        rows = slice(c * sub, (c + 1) * sub)
        for right in (True, False):
            edge = 0 if right else n - 1
            held = came(right)

            @pl.when(((at < owner) if right else (at > owner)) & (at != edge))
            def _():
                copy = onward(right, c)
                copy.wait_recv()
                held[rows, :] = (
                    held[rows, :].astype(F32) + part_ref[rows, :].astype(F32)
                ).astype(BF16)
                copy.start()

    def final_step(c):
        owner = middle[c % 2]
        rows = slice(c * sub, (c + 1) * sub)

        @pl.when(at == owner)
        def _():
            total = part_ref[rows, :].astype(F32)
            onward(True, c).wait_recv()
            total = total + from_left[rows, :].astype(F32)
            onward(False, c).wait_recv()
            total = total + from_right[rows, :].astype(F32)
            row_fn(total, rows)
            hand(True, c).start()
            hand(False, c).start()

    def hand_step(c):
        owner = middle[c % 2]
        for right in (True, False):
            edge = n - 1 if right else 0

            @pl.when((at > owner) if right else (at < owner))
            def _():
                copy = hand(right, c)
                copy.wait_recv()

                @pl.when(at != edge)
                def _():
                    copy.start()

    for c in range(chunks):
        @pl.when(at == 0)
        def _():
            first(True, c).start()

        @pl.when(at == n - 1)
        def _():
            first(False, c).start()

    for c in range(chunks + 4):
        for piece in aside.get(c, ()):
            piece()
        if c < chunks:
            reduce_step(c)
        if 2 <= c < chunks + 2:
            final_step(c - 2)
        if c >= 4:
            hand_step(c - 4)
    for c in range(chunks):
        owner = middle[c % 2]

        @pl.when(at < owner)
        def _():
            first(True, c).wait_send()

        @pl.when(at > owner)
        def _():
            first(False, c).wait_send()

        @pl.when((at >= owner) & (at < n - 1))
        def _():
            hand(True, c).wait_send()

        @pl.when((at <= owner) & (at > 0))
        def _():
            hand(False, c).wait_send()


def merge_kernel(
    n, sub, part_ref, tok_ref, far_cot, far_down, inner_ref, resid_out, stat_ref, hidden_ref,
    from_left, from_right, send, recv, cot_ref, down_ref, resid_ref, read_sem, keep_sem,
):
    reads = (
        pltpu.make_async_copy(far_cot, cot_ref, read_sem.at[0]),
        pltpu.make_async_copy(far_down, down_ref, read_sem.at[1]),
    )
    for read in reads:
        read.start()
    line_barrier(lax.axis_index("tp"), n)
    stat_ref[...] = jnp.zeros_like(stat_ref)

    def keep(rows):
        slot = rows.start // (2 * sub)
        held = resid_ref.at[pl.ds(slot * sub, sub)]
        return pltpu.make_async_copy(
            held, resid_out.at[pl.ds(rows.start, sub)], keep_sem.at[slot]
        )

    def row_fn(total, rows):
        x = tok_ref[rows, :].astype(F32) + total
        mean = jnp.mean(x, axis=1, keepdims=True)
        center = x - mean
        inverse = lax.rsqrt(jnp.mean(center * center, axis=1, keepdims=True) + EPS)
        slot = rows.start // (2 * sub)
        resid_ref[slot * sub : (slot + 1) * sub, :] = x
        keep(rows).start()
        stat_ref[rows, :] = jnp.concatenate([mean, inverse], axis=1)
        inner_ref[rows, :] = (center * inverse).astype(BF16)

    def piece(at):
        if at == 0:
            for read in reads:
                read.wait()
        hidden_ref[:, at : at + 256] = lax.dot_general(
            cot_ref[...], down_ref[at : at + 256, :], NT, preferred_element_type=F32
        ).astype(BF16)

    aside = {}
    for k in range(down_ref.shape[0] // 256):
        aside[1 + 2 * k] = (functools.partial(piece, k * 256),)
    sum_rows(n, sub, part_ref, inner_ref, row_fn, from_left, from_right, send, recv, aside)
    for c in range(part_ref.shape[0] // sub):
        @pl.when(lax.axis_index("tp") == n // 2 - 1 + c % 2)
        def _():
            keep(slice(c * sub, (c + 1) * sub)).wait()


def merge(part, tok_full, cot_full, down, n):
    rows, width = part.shape
    sub = SUB
    vmem = pl.BlockSpec(memory_space=pltpu.VMEM)
    far = pl.BlockSpec(memory_space=pl.ANY)
    return pl.pallas_call(
        functools.partial(merge_kernel, n, sub),
        in_specs=[vmem, vmem, far, far],
        out_specs=[vmem, far, vmem, vmem],
        out_shape=[
            jax.ShapeDtypeStruct((rows, width), BF16),
            jax.ShapeDtypeStruct((rows, width), F32),
            jax.ShapeDtypeStruct((rows, 2), F32),
            jax.ShapeDtypeStruct((rows, down.shape[0]), BF16),
        ],
        scratch_shapes=[pltpu.VMEM((rows, width), BF16)] * 2
        + [pltpu.SemaphoreType.DMA((4, rows // sub))] * 2
        + [
            pltpu.VMEM((rows, width), BF16),
            pltpu.VMEM(down.shape, BF16),
            pltpu.VMEM((rows // 2, width), F32),
            pltpu.SemaphoreType.DMA((2,)),
            pltpu.SemaphoreType.DMA((rows // (2 * sub),)),
        ],
        compiler_params=params(56, collective_id=5, has_side_effects=True),
        cost_estimate=cost(1e6, 1e6),
        name="merge",
    )(part, tok_full, cot_full, down)


def norm_back_kernel(
    n, sub, cube, part_ref, cot_ref, stat_ref, *refs
):
    total = None
    far, refs = refs[:3], refs[3:]
    if cube:
        own, out_ref, layer_ref, mid, from_left, from_right, send, recv = refs[:8]
        resid_ref, hidden_ref, down_ref, read_sem = refs[8:12]
        total = CubeSum(own, *refs[12:17], mid=mid)
    else:
        out_ref, layer_ref, from_left, from_right, send, recv = refs[:6]
        resid_ref, hidden_ref, down_ref, read_sem = refs[6:10]
    reads = [
        pltpu.make_async_copy(source, held, read_sem.at[k])
        for k, (source, held) in enumerate(zip(far, (resid_ref, hidden_ref, down_ref)))
    ]
    for read in reads:
        read.start()
    at = lax.axis_index("tp")
    line_barrier(lax.axis_index("tp"), n, total)
    aside = {}

    def piece(start):
        if start == 0:
            for read in reads:
                read.wait()
        cols = slice(start, start + 256)
        row = lax.broadcasted_iota(jnp.int32, (part_ref.shape[0], 256), 0)
        owned = (row // sub) % 2 == at - (n // 2 - 1)
        layer_ref[:, cols] = (
            jnp.where(owned, resid_ref[:, cols], 0.0)
            + jnp.dot(hidden_ref[...], down_ref[:, cols], preferred_element_type=F32)
        ).astype(BF16)

    for k in range(down_ref.shape[1] // 256):
        aside[1 + 2 * k] = (functools.partial(piece, k * 256),)
    if cube:
        total.begin()
        for k, c in enumerate((6, 8, 10, 12)):
            aside[c] = (functools.partial(total.reduce, k),)

    def row_fn(summed, rows):
        inverse = stat_ref[rows, 1:2]
        normed = (resid_ref[rows, :] - stat_ref[rows, 0:1]) * inverse
        mean = jnp.mean(summed, axis=1, keepdims=True)
        inner = jnp.mean(summed * normed, axis=1, keepdims=True)
        out = cot_ref[rows, :].astype(F32) + inverse * (summed - mean - normed * inner)
        out_ref[rows, :] = out.astype(BF16)

    sum_rows(n, sub, part_ref, out_ref, row_fn, from_left, from_right, send, recv, aside)
    if cube:
        total.reduce(4)
        total.reduce(5)
        total.finish()


def norm_back(part, cot, resid, stat, hidden, down, n, grads):
    rows, width = part.shape
    sub = SUB
    vmem = pl.BlockSpec(memory_space=pltpu.VMEM)
    far = pl.BlockSpec(memory_space=pl.ANY)
    extra = []
    for grad in grads:
        extra += sum_scratch(grad.shape)
    return pl.pallas_call(
        functools.partial(norm_back_kernel, n, sub, len(grads) > 0),
        in_specs=[vmem] * 3 + [far] * (3 + len(grads)),
        out_specs=[vmem] * (2 + len(grads)),
        out_shape=[jax.ShapeDtypeStruct((rows, width), BF16)] * 2
        + [jax.ShapeDtypeStruct((grad.shape[0] // 4, grad.shape[1]), BF16) for grad in grads],
        scratch_shapes=[pltpu.VMEM((rows, width), BF16)] * 2
        + [pltpu.SemaphoreType.DMA((4, rows // sub))] * 2
        + [
            pltpu.VMEM(resid.shape, F32),
            pltpu.VMEM(hidden.shape, BF16),
            pltpu.VMEM(down.shape, BF16),
            pltpu.SemaphoreType.DMA((3,)),
        ]
        + extra,
        compiler_params=params(60, collective_id=1, has_side_effects=True),
        cost_estimate=cost(1e6, 1e6),
        name="norm_back",
    )(part, cot, stat, resid, hidden, down, *grads)


def unrotate_kernel(
    heads, dq_ref, dk_ref, dv_ref, cos_ref, sin_ref, inner_ref, dproj_ref, grad_ref
):
    def back(ref):
        for h in range(heads):
            hs = slice(h * HD, (h + 1) * HD)
            piece = ref[:, hs]
            dproj_ref[:, hs] = (
                piece * cos_ref[...] - pltpu.roll(piece, HD // 2, 1) * sin_ref[...]
            ).astype(BF16)

    part = pl.program_id(0)

    @pl.when(part == 0)
    def _():
        back(dq_ref)

    @pl.when(part == 1)
    def _():
        back(dk_ref)

    @pl.when(part == 2)
    def _():
        dproj_ref[...] = dv_ref[...].astype(BF16)

    grad_ref[...] = lax.dot_general(
        inner_ref[...], dproj_ref[...], TN, preferred_element_type=F32
    ).astype(BF16)


def unrotate(dq, dk, dv, cosine, sine, inner, heads):
    rows, span = dq.shape
    width = inner.shape[1]
    whole = lambda n: pl.BlockSpec((rows, n), lambda i: (0, 0))
    return pl.pallas_call(
        functools.partial(unrotate_kernel, heads),
        grid=(3,),
        in_specs=[whole(span)] * 3 + [whole(HD)] * 2 + [whole(width)],
        out_specs=[
            pl.BlockSpec((rows, span), lambda i: (0, i)),
            pl.BlockSpec((width, span), lambda i: (i, 0)),
        ],
        out_shape=[
            jax.ShapeDtypeStruct((rows, 3 * span), BF16),
            jax.ShapeDtypeStruct((3 * width, span), BF16),
        ],
        compiler_params=params(56),
        cost_estimate=cost(6 * rows * span * width, 12 * rows * span + 6 * width * span),
        name="unrotate",
    )(dq, dk, dv, cosine, sine, inner)


def unproject_kernel(heads, n, cube, *refs):
    sums, rest = [], None
    if cube:
        dq_ref, dk_ref, dv_ref, cos_ref, sin_ref, inner_ref, mixed_ref = refs[:7]
        branch_ref, mid_ref, tok_ref, stat_ref, w_ref = refs[7:12]
        out_ref, in_out, og_out, down_out, dproj_ref, in_ref, og_ref = refs[12:19]
        part_ref, mine_ref, land_ref, sums_ref, far_ref, send, recv, ssend, srecv = refs[19:28]
        for own, out, at in ((in_ref, in_out, 28), (og_ref, og_out, 31)):
            sums.append(CubeSum(own, own, *refs[at : at + 3], None, out=out))
        rest = LastGather(mid_ref, down_out, *refs[34:37])
    else:
        dproj_ref, branch_ref, tok_ref, stat_ref, w_ref, out_ref = refs[:6]
        part_ref, mine_ref, land_ref, sums_ref, far_ref, send, recv, ssend, srecv = refs[6:15]

    def reduce(*pieces):
        for k in pieces:
            for item in sums:
                item.reduce(k)

    def gather(k):
        for item in sums:
            item.gather(k)

    rows, width = tok_ref.shape
    shard = width // n
    span = heads * HD
    at = lax.axis_index("tp")
    barrier = pltpu.get_barrier_semaphore()
    for o in range(1, n):
        pl.semaphore_signal(
            barrier, inc=1, device_id={"tp": lax.rem(at + o, n)}, device_id_type=MESH
        )
    if cube:
        sums[0].signal(barrier)
    pl.semaphore_wait(barrier, n - 1 + (3 if cube else 0))
    if cube:
        rest.begin()
        og_ref[...] = lax.dot_general(
            mixed_ref[...], branch_ref[...], TN, preferred_element_type=F32
        ).astype(BF16)
        sums[1].begin()
        for part, ref in enumerate((dq_ref, dk_ref, dv_ref)):
            for h in range(heads):
                piece = ref[:, h * HD : (h + 1) * HD]
                if part < 2:
                    piece = (
                        piece * cos_ref[...] - pltpu.roll(piece, HD // 2, 1) * sin_ref[...]
                    )
                at_column = part * span + h * HD
                dproj_ref[:, at_column : at_column + HD] = piece.astype(BF16)
            in_ref[part * width : (part + 1) * width, :] = lax.dot_general(
                inner_ref[...], dproj_ref[:, part * span : (part + 1) * span], TN,
                preferred_element_type=F32,
            ).astype(BF16)
        sums[0].begin()
    block = 256
    count = rows // block

    def term(o, i):
        target = lax.rem(at + o, n)
        place = pl.ds(i * block, block)
        return pltpu.make_async_remote_copy(
            src_ref=part_ref.at[place, pl.ds(pl.multiple_of(target * shard, 128), shard)],
            dst_ref=land_ref.at[o - 1, place],
            send_sem=send.at[o - 1, i], recv_sem=recv.at[o - 1, i],
            device_id={"tp": target}, device_id_type=MESH,
        )

    def totals(o):
        return pltpu.make_async_remote_copy(
            src_ref=sums_ref, dst_ref=far_ref.at[o - 1],
            send_sem=ssend.at[o - 1], recv_sem=srecv.at[o - 1],
            device_id={"tp": lax.rem(at + o, n)}, device_id_type=MESH,
        )

    own = pl.ds(pl.multiple_of(at * shard, 128), shard)
    for i in range(count):
        place = pl.ds(i * block, block)
        total = None
        for part in range(3):
            piece = lax.dot_general(
                dproj_ref[place, part * span : (part + 1) * span], w_ref[part], NT,
                preferred_element_type=F32,
            )
            total = piece if total is None else total + piece
        part_ref[place, :] = total.astype(BF16)
        for o in range(1, n):
            term(o, i).start()
        normed = (tok_ref[place, :].astype(F32) - stat_ref[place, 0:1]) * stat_ref[place, 1:2]
        first = jnp.sum(total, axis=1, keepdims=True)
        second = jnp.sum(total * normed, axis=1, keepdims=True)
        lane = lax.broadcasted_iota(jnp.int32, (block, HD), 1)
        both = jnp.where(lane == 0, first, jnp.where(lane == 1, second, 0.0))
        sums_ref[:, i * block : (i + 1) * block] = both.T[:8]
    for o in range(1, n):
        totals(o).start()
    reduce(0, 1, 2, 3, 4, 5, 6, 7)
    gather(0)
    gather(1)
    total = sums_ref[...]
    for o in range(1, n):
        totals(o).wait_recv()
        total = total + far_ref[o - 1]
    mine_ref[...] = total
    for i in range(count):
        place = pl.ds(i * block, block)
        spread = jnp.concatenate(
            [mine_ref[:, i * block : (i + 1) * block], jnp.zeros((HD - 8, block), F32)], axis=0
        ).T / width
        total = part_ref[place, own].astype(F32)
        for o in range(1, n):
            term(o, i).wait_recv()
            total = total + land_ref[o - 1, place].astype(F32)
        inverse = stat_ref[place, 1:2]
        normed = (tok_ref[place, own].astype(F32) - stat_ref[place, 0:1]) * inverse
        out_ref[place, :] = branch_ref[place, own].astype(F32) + inverse * (
            total - spread[:, 0:1] - normed * spread[:, 1:2]
        )
    gather(2)
    for item in sums + ([rest] if cube else []):
        item.finish()
    for o in range(1, n):
        totals(o).wait_send()
        for i in range(count):
            term(o, i).wait_send()


def unproject(cube, operands, tok_full, stat, weight, heads, n):
    rows, width = tok_full.shape
    shard = width // n
    span = heads * HD
    vmem = pl.BlockSpec(memory_space=pltpu.VMEM)
    shapes = [(3 * width, span), (span, width)] if cube else []
    more_out, early, extra = [], [], []
    if cube:
        mid = operands[-1]
        more_out = [jax.ShapeDtypeStruct((high // 2, wide), BF16) for high, wide in shapes]
        more_out.append(jax.ShapeDtypeStruct((2 * mid.shape[0], mid.shape[1]), BF16))
        early = [pltpu.VMEM(shape, BF16) for shape in [(rows, 3 * span)] + shapes]
        for shape in shapes:
            extra += sum_scratch(shape)[1:4]
        extra += [pltpu.SemaphoreType.DMA((2,))] * 3
    return pl.pallas_call(
        functools.partial(unproject_kernel, heads, n, cube),
        in_specs=[vmem] * (len(operands) + 3),
        out_specs=[vmem] * (1 + len(shapes)) + [pl.BlockSpec(memory_space=pl.ANY)] * int(cube),
        out_shape=[jax.ShapeDtypeStruct((rows, shard), F32)] + more_out,
        scratch_shapes=early
        + [
            pltpu.VMEM((rows, width), BF16),
            pltpu.VMEM((8, rows), F32),
            pltpu.VMEM((n - 1, rows, shard), BF16),
            pltpu.VMEM((8, rows), F32),
            pltpu.VMEM((n - 1, 8, rows), F32),
            pltpu.SemaphoreType.DMA((n - 1, rows // 256)),
            pltpu.SemaphoreType.DMA((n - 1, rows // 256)),
            pltpu.SemaphoreType.DMA((n - 1,)),
            pltpu.SemaphoreType.DMA((n - 1,)),
        ]
        + extra,
        compiler_params=params(61, collective_id=4, has_side_effects=True),
        cost_estimate=cost(1e6, 1e6),
        name="unproject",
    )(*operands, tok_full, stat, weight)


def per_device(tokens, segment_ids, in_weight, out_weight, gate_up_weight, down_weight, cotangent):
    rows = tokens.shape[0]
    width = in_weight.shape[0]
    span = in_weight.shape[2]
    heads = span // HD
    hidden_local = down_weight.shape[0]
    me = lax.axis_index("ctx")
    tp_size = lax.axis_size("tp")
    cube = lax.axis_size("ctx") == CUBE

    def gather(local, axis=1):
        return lax.all_gather(local, "tp", axis=axis, tiled=True)

    places = me * rows + jnp.arange(rows, dtype=jnp.int32)
    cosine, sine = rope_tables(places)
    in_w = jnp.transpose(in_weight, (1, 0, 2))
    gu_w = jnp.transpose(
        gate_up_weight.reshape(width, 2, hidden_local // BLOCK, BLOCK), (0, 2, 1, 3)
    )
    gu_w = gu_w.reshape(width, 2 * hidden_local)

    all_seg = lax.all_gather(segment_ids, "ctx", axis=0, tiled=True)
    count = all_seg.shape[0]
    every = jnp.arange(count, dtype=jnp.int32)
    opens = jnp.concatenate([jnp.ones((1,), jnp.bool_), all_seg[1:] != all_seg[:-1]])
    all_begin = lax.cummax(jnp.where(opens, every, 0))
    blocks = all_begin.reshape(count // rows, rows)

    tok_full, gu_w, blocks, all_begin = lax.optimization_barrier(
        (gather(tokens), gu_w, blocks, all_begin)
    )
    key_info = jnp.stack(
        [me, blocks[me, 0] // rows, (blocks[me, rows - 1] + rows - 1) // rows]
    ).astype(jnp.int32)
    query_info = jnp.stack(
        [
            me,
            jnp.sum((blocks[:, 0] < (me + 1) * rows).astype(jnp.int32)) - 1,
            jnp.sum((blocks[:, rows - 1] <= me * rows).astype(jnp.int32)) - 1,
        ]
    ).astype(jnp.int32)
    begin = lax.dynamic_slice_in_dim(blocks, me, 1, 0)
    all_begin = all_begin[None, :]
    if cube:
        inner1, stat1, raw, mixed, lse, kept, cot_full, out_part = attend_far(
            tok_full, in_w, cosine, sine, blocks, cotangent, out_weight, heads, tp_size
        )
        kept = lax.all_gather(kept, "ctx", axis=0, tiled=True)
    else:
        inner1, stat1, query, pairs = project(tok_full, in_w, cosine, sine, heads)
        all_pairs = lax.all_gather(pairs, "ctx", axis=0, tiled=True)
        cot_full = gather(cotangent)
        raw, mixed, lse = attend(key_info, query, all_pairs, begin, heads)
        out_part = jnp.dot(mixed, out_weight, preferred_element_type=F32).astype(BF16)
        late_query, mixed = lax.optimization_barrier((query, mixed))
        kept = lax.all_gather(late_query, "ctx", axis=0, tiled=True)
    inner2, resid1, stat2, grad_hidden = merge(
        out_part, tok_full, cot_full, down_weight, tp_size
    )

    hidden, grad_gu, down_grad, gu_grad = feed(inner2, cot_full, gu_w, grad_hidden, BLOCK)
    down_grad, gu_grad, kept, grad_gu, hidden = lax.optimization_barrier(
        (down_grad, gu_grad, kept, grad_gu, hidden)
    )
    if not cube:
        down_grad = lax.psum(down_grad, "ctx")
    gu_grad = lax.optimization_barrier(lax.psum(gu_grad, "ctx"))

    grad_part = lax.dot_general(grad_gu, gu_w, NT, preferred_element_type=F32).astype(BF16)
    branch_grad, branch, *mids = norm_back(
        grad_part, cot_full, resid1, stat2, hidden, down_weight, tp_size,
        [down_grad] if cube else [],
    )
    grad_mixed, delta = mixed_grad(branch_grad, out_weight, raw, lse, heads)
    if cube:
        dq, dk, dv, layer_out, mid = attend_back_far(
            grad_mixed, kept, blocks, branch, mids[0], heads, tp_size
        )
    else:
        branch = lax.psum_scatter(branch, "tp", scatter_dimension=1, tiled=True)
        layer_out = branch
        all_grad = lax.all_gather(grad_mixed, "ctx", axis=0, tiled=True)
        dq = query_grad(key_info, query, grad_mixed, lse, delta, all_pairs, begin, heads)
        dk, dv = key_grad(query_info, pairs, kept, all_grad, all_begin, heads)

    if cube:
        tokens_grad, *halves = unproject(
            True, [dq, dk, dv, cosine, sine, inner1, mixed, branch_grad, mid],
            tok_full, stat1, in_w, heads, tp_size,
        )
        swap = [(i, i + 1 - 2 * (i % 2)) for i in range(CUBE)]
        core = (me % 2)[None]
        far = [lax.ppermute(half, "ctx", swap) for half in halves]
        *far, gu_grad = lax.optimization_barrier((*far, weave(gu_grad, BLOCK)))
        in_grad, out_grad, down_grad = join(core, halves, far)
    else:
        out_grad = lax.dot_general(
            mixed, branch_grad, TN, preferred_element_type=F32
        ).astype(BF16)
        dproj, in_grad = unrotate(dq, dk, dv, cosine, sine, inner1, heads)
        in_grad, out_grad, down_grad, gu_grad = lax.optimization_barrier(
            (in_grad, out_grad, down_grad, gu_grad)
        )
        in_grad, out_grad = lax.psum((in_grad, out_grad), "ctx")
        (tokens_grad,) = unproject(
            False, [dproj, branch_grad], tok_full, stat1, in_w, heads, tp_size
        )
        in_grad, out_grad, down_grad = widen(in_grad), out_grad.astype(F32), widen(down_grad)
        gu_grad = weave(gu_grad, BLOCK)
    return (
        layer_out,
        tokens_grad,
        jnp.transpose(in_grad.reshape(3, width, span), (1, 0, 2)),
        out_grad,
        gu_grad,
        down_grad,
    )


def solution(mesh):
    placed = (
        P("ctx", "tp"),
        P("ctx"),
        P(None, None, "tp"),
        P("tp", None),
        P(None, None, "tp"),
        P("tp", None),
        P("ctx", "tp"),
    )
    return jax.shard_map(
        per_device,
        mesh=mesh,
        in_specs=placed,
        out_specs=(
            P("ctx", "tp"),
            P("ctx", "tp"),
            P(None, None, "tp"),
            P("tp", None),
            P(None, None, "tp"),
            P("tp", None),
        ),
        check_vma=False,
    )
```

```python
import functools

import jax
import jax.numpy as jnp
from jax import lax
from jax.experimental import pallas as pl
from jax.experimental.pallas import tpu as pltpu
from jax.sharding import PartitionSpec as P

HD = 128
EPS = 1e-05
NEG = -1e30
SCALE = HD ** (-0.5)
LOG2E = 1.4426950408889634
C2 = SCALE * LOG2E
F32 = jnp.float32
BF16 = jnp.bfloat16
NT = (((1,), (1,)), ((), ()))
TN = (((0,), (0,)), ((), ()))
MESH = pl.DeviceIdType.MESH
BLOCK = 512
SUB = 32


def params(mib, **more):
    return pltpu.CompilerParams(vmem_limit_bytes=mib << 20, **more)


def cost(flops, nbytes, trans=0):
    return pl.CostEstimate(flops=int(flops), bytes_accessed=int(nbytes), transcendentals=int(trans))


def rope_tables(places):
    half = HD // 2
    freq = 10000.0 ** (-jnp.arange(half, dtype=F32) * 2.0 / HD)
    angle = places.astype(F32)[:, None] * freq[None, :]
    cosine, sine = jnp.cos(angle), jnp.sin(angle)
    return jnp.concatenate([cosine, cosine], axis=1), jnp.concatenate([-sine, sine], axis=1)


def project_kernel(heads, tok_ref, w_ref, cos_ref, sin_ref, inner_ref, stat_ref, q_ref, kv_ref):
    x = tok_ref[...].astype(F32)
    center = x - jnp.mean(x, axis=1, keepdims=True)
    inverse = lax.rsqrt(jnp.mean(center * center, axis=1, keepdims=True) + EPS)
    inner = (center * inverse).astype(BF16)
    inner_ref[...] = inner
    stat_ref[...] = jnp.concatenate(
        [jnp.mean(x, axis=1, keepdims=True), inverse], axis=1
    )
    cosine, sine = cos_ref[...], sin_ref[...]
    span = heads * HD
    for part in range(3):
        out = jnp.dot(inner, w_ref[part], preferred_element_type=F32)
        if part == 2:
            kv_ref[:, span:] = out.astype(BF16)
            continue
        for h in range(heads):
            piece = out[:, h * HD : (h + 1) * HD]
            turned = (piece * cosine + pltpu.roll(piece, HD // 2, 1) * sine).astype(BF16)
            if part == 0:
                q_ref[:, h * HD : (h + 1) * HD] = turned
            else:
                kv_ref[:, h * HD : (h + 1) * HD] = turned


def project(tok_full, weight, cosine, sine, heads):
    rows, width = tok_full.shape
    span = heads * HD
    block = 256
    row = lambda n: pl.BlockSpec((block, n), lambda i: (i, 0))
    return pl.pallas_call(
        functools.partial(project_kernel, heads),
        grid=(rows // block,),
        in_specs=[
            row(width),
            pl.BlockSpec((3, width, span), lambda i: (0, 0, 0)),
            row(HD),
            row(HD),
        ],
        out_specs=[row(width), row(2), row(span), row(2 * span)],
        out_shape=[
            jax.ShapeDtypeStruct((rows, width), BF16),
            jax.ShapeDtypeStruct((rows, 2), F32),
            jax.ShapeDtypeStruct((rows, span), BF16),
            jax.ShapeDtypeStruct((rows, 2 * span), BF16),
        ],
        compiler_params=params(56),
        cost_estimate=cost(6 * rows * width * span, 6 * width * span + 6 * rows * width),
        name="project",
    )(tok_full, weight, cosine, sine)


def masked(scores, j, me, rows, begin):
    key_place = lax.broadcasted_iota(jnp.int32, scores.shape, 0) + j * rows
    query_place = lax.broadcasted_iota(jnp.int32, scores.shape, 1) + me * rows
    return jnp.where((key_place <= query_place) & (key_place >= begin), scores, NEG)


def attend_kernel(
    heads, info, q_ref, k_ref, v_ref, begin_ref, raw_ref, mixed_ref, lse_ref,
    high_ref, total_ref, acc_ref, s_ref,
):
    me, first, clear = info[0], info[1], info[2]
    j = pl.program_id(0)
    rows = q_ref.shape[0]

    @pl.when(j == 0)
    def _():
        high_ref[...] = jnp.full_like(high_ref, NEG)
        total_ref[...] = jnp.zeros_like(total_ref)
        acc_ref[...] = jnp.zeros_like(acc_ref)

    def block(hide):
        def score(h):
            hs = slice(h * HD, (h + 1) * HD)
            s = lax.dot_general(k_ref[:, hs], q_ref[:, hs], NT, preferred_element_type=F32)
            if hide:
                s = masked(s, j, me, rows, begin_ref[...])
            s_ref[h % 2] = s

        def spread(h):
            hs = slice(h * HD, (h + 1) * HD)
            s = s_ref[h % 2]
            old = high_ref[h : h + 1, :]
            new = jnp.maximum(old, jnp.max(s, axis=0, keepdims=True))
            high_ref[h : h + 1, :] = new
            p = jnp.exp2(s * C2 - new * C2)
            decay = jnp.exp2((old - new) * C2)
            total_ref[h : h + 1, :] = total_ref[h : h + 1, :] * decay + jnp.sum(
                p, axis=0, keepdims=True
            )
            acc_ref[h] = acc_ref[h] * decay + lax.dot_general(
                v_ref[:, hs], p.astype(BF16), TN, preferred_element_type=F32
            )

        score(0)
        for h in range(heads):
            if h + 1 < heads:
                score(h + 1)
            spread(h)

    @pl.when((j >= clear) & (j < me))
    def _():
        block(False)

    @pl.when(((j >= first) & (j < clear) & (j < me)) | (j == me))
    def _():
        block(True)

    @pl.when(j == me)
    def _():
        for h in range(heads):
            hs = slice(h * HD, (h + 1) * HD)
            out = (acc_ref[h] / total_ref[h : h + 1, :]).T
            raw_ref[:, hs] = out
            mixed_ref[:, hs] = out.astype(BF16)
        lse_ref[...] = high_ref[...] * C2 + jnp.log2(total_ref[...])


def attend(info, query, pairs, begin, heads):
    rows = query.shape[0]
    total = pairs.shape[0]
    span = heads * HD
    full = lambda shape: pl.BlockSpec(shape, lambda j, s: (0, 0))
    key = pl.BlockSpec((rows, span), lambda j, s: (jnp.clip(j, s[1], s[0]), 0))
    value = pl.BlockSpec((rows, span), lambda j, s: (jnp.clip(j, s[1], s[0]), 1))
    return pl.pallas_call(
        functools.partial(attend_kernel, heads),
        grid_spec=pltpu.PrefetchScalarGridSpec(
            num_scalar_prefetch=1,
            grid=(total // rows,),
            in_specs=[full((rows, span)), key, value, full((1, rows))],
            out_specs=[full((rows, span)), full((rows, span)), full((heads, rows))],
            scratch_shapes=[
                pltpu.VMEM((heads, rows), F32),
                pltpu.VMEM((heads, rows), F32),
                pltpu.VMEM((heads, HD, rows), F32),
                pltpu.VMEM((2, rows, rows), F32),
            ],
        ),
        out_shape=[
            jax.ShapeDtypeStruct((rows, span), F32),
            jax.ShapeDtypeStruct((rows, span), BF16),
            jax.ShapeDtypeStruct((heads, rows), F32),
        ],
        compiler_params=params(56),
        cost_estimate=cost(4 * rows * total * span, 4 * total * span, rows * total * heads),
        name="attend",
    )(info, query, pairs, pairs, begin)


CUBE = 8
CUBE_SENDS = 10


class Cube:
    def __init__(self, buf, send, recv):
        me = lax.axis_index("ctx")
        flip = (1 - 2 * (me % 2), 2 - 4 * ((me // 2) % 2), 4 - 8 * (me // 4))
        self.me, self.flip, self.buf, self.send, self.recv = me, flip, buf, send, recv
        self.rows = buf.shape[0] // CUBE

    def copy(self, n):
        core, x, y = self.flip
        half = self.rows // 2
        block, part, target = (
            (0, None, core),
            (0, 0, x), (0, 1, x), (0, 1, y), (0, 0, y),
            (x, 0, y), (y, 1, x),
            (x, None, core), (y, None, core), (x + y, None, core),
        )[n]
        start = (self.me + block) * self.rows
        size = self.rows
        if part is not None:
            start, size = start + part * half, half
        place = self.buf.at[pl.ds(pl.multiple_of(start, 16), size)]
        return pltpu.make_async_remote_copy(
            src_ref=place, dst_ref=place, send_sem=self.send.at[n], recv_sem=self.recv.at[n],
            device_id={"ctx": self.me + target}, device_id_type=MESH,
        )

    def arrived(self, n):
        self.copy(n).wait_recv()

    def start(self, *which):
        for n in which:
            self.copy(n).start()

    def signal(self, barrier):
        for target in self.flip:
            pl.semaphore_signal(
                barrier, inc=1, device_id={"ctx": self.me + target}, device_id_type=MESH
            )

    def block(self, step):
        core, x, y = self.flip
        on = lambda *steps: sum((step == n).astype(jnp.int32) for n in steps)
        return self.me + on(1, 4, 5, 7) * core + on(2, 4, 6, 7) * x + on(3, 5, 6, 7) * y

    def advance(self, step):
        @pl.when(step == 1)
        def _():
            self.arrived(0)

        @pl.when(step == 2)
        def _():
            self.arrived(1)
            self.start(5)
            self.arrived(3)
            self.start(6)
            self.arrived(2)
            self.start(7)

        @pl.when(step == 3)
        def _():
            self.arrived(4)
            self.start(8)

        @pl.when(step == 4)
        def _():
            self.arrived(7)

        @pl.when(step == 5)
        def _():
            self.arrived(8)

        @pl.when(step == 6)
        def _():
            self.arrived(5)
            self.arrived(6)
            self.start(9)

        @pl.when(step == 7)
        def _():
            self.arrived(9)

    def finish(self):
        for n in range(CUBE_SENDS):
            self.copy(n).wait_send()


SUM_SENDS = 9


class CubeSum:
    def __init__(self, own, near, land, send, recv, local, out=None, mid=None):
        me = lax.axis_index("ctx")
        core, x, y = me % 2, (me // 2) % 2, me // 4
        self.me, self.own, self.out, self.land, self.mid = me, own, out, land, mid
        self.near, self.send, self.recv, self.local = near, send, recv, local
        rows = own.shape[0]
        self.half, self.eighth, self.last = rows // 2, rows // 8, rows // 16
        second = rows // 4
        self.to = (1 - 2 * core, 2 - 4 * x, 4 - 8 * y)
        self.mine, self.other = core * self.half, (1 - core) * self.half
        self.offset = 0 if local is not None else self.mine
        self.keep1 = (x * self.eighth, second + y * self.eighth)
        self.give1 = ((1 - x) * self.eighth, second + (1 - y) * self.eighth)
        self.keep2 = (self.keep1[0] + y * self.last, self.keep1[1] + x * self.last)
        self.give2 = (self.keep1[0] + (1 - y) * self.last, self.keep1[1] + (1 - x) * self.last)

    def copy(self, n):
        core, x, y = self.to
        half, eighth, last, out, land = self.half, self.eighth, self.last, self.out, self.land
        source, start, size, target = (
            (self.own, self.other, half, core),
            (land, self.give1[0], eighth, x), (land, self.give1[1], eighth, y),
            (land, self.give2[0], last, y), (land, self.give2[1], last, x),
            (out, self.keep2[0], last, y), (out, self.keep2[1], last, x),
            (out, self.keep1[0], eighth, x), (out, self.keep1[1], eighth, y),
        )[n]
        src = source.at[pl.ds(pl.multiple_of(start, 16), size)]
        if n < 5:
            landing = (0, half, half + eighth, half + 2 * eighth, half + 2 * eighth + last)[n]
            dst = land.at[pl.ds(landing, size)]
        else:
            dst = src
        return pltpu.make_async_remote_copy(
            src_ref=src, dst_ref=dst, send_sem=self.send.at[n], recv_sem=self.recv.at[n],
            device_id={"ctx": self.me + target}, device_id_type=MESH,
        )

    def add(self, target, to, source, at, landed, size):
        step = size
        while step * self.own.shape[1] > 256 * 1024 and step % 32 == 0:
            step = step // 2

        def part(i, carry):
            def rows(begin):
                return pl.ds(pl.multiple_of(begin + i * step, 16), step)

            total = source[rows(at), :].astype(F32) + self.land[rows(landed), :].astype(F32)
            target[rows(to), :] = total.astype(BF16)
            return carry

        lax.fori_loop(0, size // step, part, 0)

    def read(self):
        rows = pl.ds(pl.multiple_of(self.mine, 16), self.half)
        return pltpu.make_async_copy(self.own.at[rows], self.near, self.local.at[0])

    def begin(self):
        self.copy(0).start()
        if self.local is not None:
            self.read().start()

    def reduce(self, k):
        half, eighth, last, land = self.half, self.eighth, self.last, self.land
        i = k % 2
        if k == 0:
            if self.local is not None:
                self.read().wait()
            self.copy(0).wait_recv()
        if k < 2:
            at = self.give1[i]
            self.add(land, at, self.near, self.offset + at, at, eighth)
            self.copy(1 + i).start()
        elif k < 4:
            at = self.keep1[i]
            self.add(land, at, self.near, self.offset + at, at, eighth)
        elif k < 6:
            self.copy(1 + i).wait_recv()
            landed = half + i * eighth - self.keep1[i]
            if self.out is None:
                at = self.keep1[i]
                self.add(self.mid, i * eighth, land, at, landed + at, eighth)
                return
            at = self.give2[i]
            self.add(land, at, land, at, landed + at, last)
            self.copy(3 + i).start()
            at = self.keep2[i]
            self.add(land, at, land, at, landed + at, last)
        else:
            self.copy(3 + i).wait_recv()
            at = self.keep2[i]
            self.add(self.out, at, land, at, half + 2 * eighth + i * last, last)

    def gather(self, k):
        for i in range(2):
            if k == 0:
                self.copy(5 + i).start()
            if k == 1:
                self.copy(5 + i).wait_recv()
                self.copy(7 + i).start()
            if k == 2:
                self.copy(7 + i).wait_recv()

    def finish(self):
        for n in range(3 if self.out is None else SUM_SENDS):
            self.copy(n).wait_send()

    def signal(self, barrier):
        for target in self.to:
            pl.semaphore_signal(
                barrier, inc=1, device_id={"ctx": self.me + target}, device_id_type=MESH
            )


class MidSum:
    def __init__(self, mid, land, out, send, recv):
        me = lax.axis_index("ctx")
        x, y = (me // 2) % 2, me // 4
        self.me, self.mid, self.land, self.out, self.send, self.recv = me, mid, land, out, send, recv
        self.eighth, self.last = mid.shape[0] // 2, mid.shape[0] // 4
        self.bit = (y, x)
        self.to = (4 - 8 * y, 2 - 4 * x)

    def copy(self, n):
        i = n % 2
        keep = i * self.eighth + self.bit[i] * self.last
        give = i * self.eighth + (1 - self.bit[i]) * self.last
        if n < 2:
            src = self.mid.at[pl.ds(pl.multiple_of(give, 16), self.last)]
            dst = self.land.at[pl.ds(i * self.last, self.last)]
        else:
            src = dst = self.out.at[pl.ds(pl.multiple_of(keep, 16), self.last)]
        return pltpu.make_async_remote_copy(
            src_ref=src, dst_ref=dst, send_sem=self.send.at[n], recv_sem=self.recv.at[n],
            device_id={"ctx": self.me + self.to[i]}, device_id_type=MESH,
        )

    def begin(self):
        for i in range(2):
            self.copy(i).start()

    def turn(self):
        for i in range(2):
            self.copy(i).wait_recv()
            keep = i * self.eighth + self.bit[i] * self.last
            rows = pl.ds(pl.multiple_of(keep, 16), self.last)
            landed = self.land[i * self.last : (i + 1) * self.last, :]
            self.out[rows, :] = (
                self.mid[rows, :].astype(F32) + landed.astype(F32)
            ).astype(BF16)
            self.copy(2 + i).start()

    def finish(self):
        for i in range(2):
            self.copy(2 + i).wait_recv()
        for n in range(4):
            self.copy(n).wait_send()


class LastGather:
    def __init__(self, mid, out, send, recv, local):
        me = lax.axis_index("ctx")
        x, y = (me // 2) % 2, me // 4
        self.me, self.mid, self.out = me, mid, out
        self.send, self.recv, self.local = send, recv, local
        self.eighth = mid.shape[0] // 2
        self.start_at = (x * self.eighth, (2 + y) * self.eighth)
        self.to = (2 - 4 * x, 4 - 8 * y)

    def ends(self, i):
        src = self.mid.at[pl.ds(i * self.eighth, self.eighth)]
        return src, self.out.at[pl.ds(pl.multiple_of(self.start_at[i], 16), self.eighth)]

    def copy(self, i):
        src, dst = self.ends(i)
        return pltpu.make_async_remote_copy(
            src_ref=src, dst_ref=dst, send_sem=self.send.at[i], recv_sem=self.recv.at[i],
            device_id={"ctx": self.me + self.to[i]}, device_id_type=MESH,
        )

    def keep(self, i):
        src, dst = self.ends(i)
        return pltpu.make_async_copy(src, dst, self.local.at[i])

    def begin(self):
        for i in range(2):
            self.copy(i).start()
            self.keep(i).start()

    def finish(self):
        for i in range(2):
            self.copy(i).wait()
            self.keep(i).wait()


def sum_scratch(shape):
    return [
        pltpu.VMEM((shape[0] // 2, shape[1]), BF16),
        pltpu.VMEM((shape[0] // 2 + 3 * (shape[0] // 8), shape[1]), BF16),
        pltpu.SemaphoreType.DMA((SUM_SENDS,)),
        pltpu.SemaphoreType.DMA((SUM_SENDS,)),
        pltpu.SemaphoreType.DMA((1,)),
    ]


def join_kernel(count, core_ref, *refs):
    for own_ref, far_ref, out_ref in zip(refs[:count], refs[count : 2 * count], refs[2 * count :]):
        @pl.when(pl.program_id(0) == 0)
        def _():
            out_ref[...] = own_ref[...].astype(F32)

        @pl.when(pl.program_id(0) == 1)
        def _():
            out_ref[...] = far_ref[...].astype(F32)


def join(core, own, far):
    steps = 4
    block = lambda half, at: pl.BlockSpec((half.shape[0] // steps, half.shape[1]), at)
    first = lambda h, b, s: (jnp.where(h == 0, b, steps - 1), 0)
    second = lambda h, b, s: (jnp.where(h == 0, 0, b), 0)
    target = lambda h, b, s: (jnp.where(h == 0, s[0], 1 - s[0]) * steps + b, 0)
    size = sum(half.shape[0] * half.shape[1] for half in own)
    return pl.pallas_call(
        functools.partial(join_kernel, len(own)),
        grid_spec=pltpu.PrefetchScalarGridSpec(
            num_scalar_prefetch=1,
            grid=(2, steps),
            in_specs=[block(half, first) for half in own] + [block(half, second) for half in own],
            out_specs=[block(half, target) for half in own],
        ),
        out_shape=[
            jax.ShapeDtypeStruct((2 * half.shape[0], half.shape[1]), F32) for half in own
        ],
        compiler_params=params(56),
        cost_estimate=cost(2 * size, 12 * size),
        name="join",
    )(core, *own, *far)


def hidden_scores(scores, key_block, query_block, rows, begin):
    key_place = lax.broadcasted_iota(jnp.int32, scores.shape, 0) + key_block * rows
    query_place = lax.broadcasted_iota(jnp.int32, scores.shape, 1) + query_block * rows
    return jnp.where((key_place <= query_place) & (key_place >= begin), scores, NEG)


FAR_STEPS = 8
FAR_SENDS = 17


def attend_far_kernel(
    heads, n, tok_ref, in_ref, cos_ref, sin_ref, begin_ref, cot_ref, w_ref,
    inner_ref, stat_ref, raw_ref, mixed_ref, lse_ref, keep_ref, full_ref, part_ref,
    pair_ref, q_ref, high_ref, total_ref, acc_ref, s_ref,
    guest_ref, guest_high, guest_total, guest_acc, guest_out, guest_stat, back_out, back_stat,
    send, recv, zsend, zrecv,
):
    rows = q_ref.shape[0]
    half = rows // 2
    span = heads * HD
    shard = cot_ref.shape[1]
    at = lax.axis_index("tp")
    me = lax.axis_index("ctx")
    core, x, y = me % 2, (me // 2) % 2, me // 4
    to_core, to_x, to_y = 1 - 2 * core, 2 - 4 * x, 4 - 8 * y
    diagonal = me + to_x + to_y
    barrier = pltpu.get_barrier_semaphore()
    for target in (me + to_core, me + to_x, me + to_y, diagonal):
        pl.semaphore_signal(barrier, inc=1, device_id={"ctx": target}, device_id_type=MESH)

    @pl.when(at > 0)
    def _():
        pl.semaphore_signal(barrier, inc=1, device_id={"tp": at - 1}, device_id_type=MESH)

    @pl.when(at < n - 1)
    def _():
        pl.semaphore_signal(barrier, inc=1, device_id={"tp": at + 1}, device_id_type=MESH)

    def block_rows(block):
        return pl.ds(pl.multiple_of(block * rows, 16), rows)

    def copy(k):
        if k < 14:
            block, part, parts, target = (
                (me, 0, 1, to_core),
                (me, 0, 2, to_x), (me, 1, 2, to_x),
                (me, 0, 4, to_y), (me, 1, 4, to_y), (me, 2, 4, to_y), (me, 3, 4, to_y),
                (me + to_x, 0, 1, to_core), (me + to_y, 0, 1, to_core),
                (me + to_y, 0, 4, to_x), (me + to_y, 1, 4, to_x),
                (me + to_y, 2, 4, to_x), (me + to_y, 3, 4, to_x),
                (diagonal, 0, 1, to_core),
            )[k]
            size = rows // parts
            src = dst = pair_ref.at[pl.ds(pl.multiple_of(block * rows + part * size, 16), size)]
        else:
            src, dst = (
                (q_ref, guest_ref), (guest_out, back_out), (guest_stat, back_stat)
            )[k - 14]
            target = to_x + to_y
        return pltpu.make_async_remote_copy(
            src_ref=src, dst_ref=dst, send_sem=send.at[k], recv_sem=recv.at[k],
            device_id={"ctx": me + target}, device_id_type=MESH,
        )

    def on_chip(*which):
        return sum((me // 2 == chip).astype(jnp.int32) for chip in which) > 0

    def project(rows_at, part):
        out = jnp.dot(inner_ref[rows_at, :], in_ref[part], preferred_element_type=F32)
        if part == 2:
            return out.astype(BF16)
        cosine, sine = cos_ref[rows_at, :], sin_ref[rows_at, :]
        pieces = []
        for h in range(heads):
            piece = out[:, h * HD : (h + 1) * HD]
            pieces.append((piece * cosine + pltpu.roll(piece, HD // 2, 1) * sine).astype(BF16))
        return jnp.concatenate(pieces, axis=1)

    def own_pairs(part):
        here = slice(part * half, (part + 1) * half)
        value = tok_ref[here, :].astype(F32)
        mean = jnp.mean(value, axis=1, keepdims=True)
        center = value - mean
        inverse = lax.rsqrt(jnp.mean(center * center, axis=1, keepdims=True) + EPS)
        stat_ref[here, :] = jnp.concatenate([mean, inverse], axis=1)
        inner_ref[here, :] = (center * inverse).astype(BF16)
        place = pl.ds(pl.multiple_of(me * rows + part * half, 16), half)
        pair_ref[place, :span] = project(here, 1)
        pair_ref[place, span:] = project(here, 2)

    own_pairs(0)
    full_ref[:, pl.ds(pl.multiple_of(at * shard, 128), shard)] = cot_ref[...]
    pl.semaphore_wait(barrier, jnp.where((at > 0) & (at < n - 1), 6, 5))

    @pl.when(y == 0)
    def _():
        copy(3).start()
        copy(4).start()

    @pl.when(x == 0)
    def _():
        copy(1).start()

    own_pairs(1)

    @pl.when(y == 0)
    def _():
        copy(5).start()
        copy(6).start()

    @pl.when(x == 0)
    def _():
        copy(2).start()

    copy(0).start()
    q_ref[...] = project(slice(0, rows), 0)

    @pl.when(on_chip(3))
    def _():
        copy(14).start()

    keep_ref[:, : 2 * span] = pair_ref[block_rows(me), :]
    keep_ref[:, 2 * span :] = q_ref[...]

    def pass_on(right, s, k):
        place = full_ref.at[:, pl.ds(pl.multiple_of(s * shard, 128), shard)]
        which = (1 if right else 0, k)
        return pltpu.make_async_remote_copy(
            src_ref=place, dst_ref=place, send_sem=zsend.at[which], recv_sem=zrecv.at[which],
            device_id={"tp": at + 1 if right else at - 1}, device_id_type=MESH,
        )

    def line_step(k):
        @pl.when(at >= k)
        def _():
            if k > 0:
                pass_on(True, at - k, k - 1).wait_recv()

            @pl.when(at < n - 1)
            def _():
                pass_on(True, at - k, k).start()

        @pl.when(at + k < n)
        def _():
            if k > 0:
                pass_on(False, at + k, k - 1).wait_recv()

            @pl.when(at > 0)
            def _():
                pass_on(False, at + k, k).start()

    def clear(high, total, acc):
        high[...] = jnp.full_like(high, NEG)
        total[...] = jnp.zeros_like(total)
        acc[...] = jnp.zeros_like(acc)

    def attend_block(key_block, queries, query_block, high, total, acc):
        place = block_rows(key_block)
        begin = begin_ref[pl.ds(query_block, 1), :]

        def score(h):
            hs = slice(h * HD, (h + 1) * HD)
            s = lax.dot_general(
                pair_ref[place, hs], queries[:, hs], NT, preferred_element_type=F32
            )
            s_ref[h % 2] = hidden_scores(s, key_block, query_block, rows, begin)

        def spread(h):
            s = s_ref[h % 2]
            old = high[h : h + 1, :]
            new = jnp.maximum(old, jnp.max(s, axis=0, keepdims=True))
            high[h : h + 1, :] = new
            p = jnp.exp2(s * C2 - new * C2)
            decay = jnp.exp2((old - new) * C2)
            total[h : h + 1, :] = total[h : h + 1, :] * decay + jnp.sum(p, axis=0, keepdims=True)
            acc[h] = acc[h] * decay + lax.dot_general(
                pair_ref[place, span + h * HD : span + (h + 1) * HD], p.astype(BF16), TN,
                preferred_element_type=F32,
            )

        score(0)
        for h in range(heads):
            if h + 1 < heads:
                score(h + 1)
            spread(h)

    def guest():
        clear(guest_high, guest_total, guest_acc)
        copy(14).wait_recv()

        def turn(k, carry):
            attend_block(
                me + k * to_core, guest_ref, diagonal, guest_high, guest_total, guest_acc
            )
            return carry

        lax.fori_loop(0, 2, turn, 0)
        for h in range(heads):
            guest_out[h * HD : (h + 1) * HD, :] = (
                guest_acc[h] / guest_total[h : h + 1, :]
            ).astype(BF16)
        guest_stat[:heads, :] = guest_high[...]
        guest_stat[heads:, :] = guest_total[...]
        copy(15).start()
        copy(16).start()

    clear(high_ref, total_ref, acc_ref)

    def turn(step, carry):
        for k in range(n):
            @pl.when(step == (min(k * 2, FAR_STEPS - n + k) if n <= FAR_STEPS else k))
            def _():
                line_step(k)

        @pl.when(step == 1)
        def _():
            copy(0).wait_recv()

        @pl.when((step == 2) & on_chip(0))
        def _():
            guest()

        @pl.when((step == 2) & on_chip(3))
        def _():
            for k in range(4):
                copy(3 + k).wait_recv()
                copy(9 + k).start()

        @pl.when((step == 2) & (x == 1))
        def _():
            copy(1).wait_recv()
            copy(2).wait_recv()
            copy(7).start()

        @pl.when((step == 3) & on_chip(2))
        def _():
            for k in range(4):
                copy(3 + k).wait_recv()

        @pl.when((step == 3) & (y == 1))
        def _():
            copy(8).start()

        @pl.when((step == 4) & (x == 1))
        def _():
            copy(7).wait_recv()

        @pl.when((step == 5) & (y == 1))
        def _():
            copy(8).wait_recv()

        @pl.when((step == 6) & on_chip(2))
        def _():
            for k in range(4):
                copy(9 + k).wait_recv()
            copy(13).start()

        @pl.when((step == 7) & on_chip(2))
        def _():
            copy(13).wait_recv()

        on = lambda *steps: sum((step == k).astype(jnp.int32) for k in steps)
        block = (
            me + on(1, 4, 5, 7) * to_core + on(2, 4, 6, 7) * to_x + on(3, 5, 6, 7) * to_y
        )
        here = on(0, 1) + on(2, 4) * x + on(3, 5) * y + on(6, 7) * y * (1 - x)

        @pl.when((block <= me) & (here > 0))
        def _():
            attend_block(block, q_ref, me, high_ref, total_ref, acc_ref)

        return carry

    lax.fori_loop(0, FAR_STEPS, turn, 0)

    @pl.when(on_chip(3))
    def _():
        copy(15).wait_recv()
        copy(16).wait_recv()
        for h in range(heads):
            old, other = high_ref[h : h + 1, :], back_stat[h : h + 1, :]
            new = jnp.maximum(old, other)
            high_ref[h : h + 1, :] = new
            decay = jnp.exp2((old - new) * C2)
            weight = jnp.exp2((other - new) * C2) * back_stat[heads + h : heads + h + 1, :]
            total_ref[h : h + 1, :] = total_ref[h : h + 1, :] * decay + weight
            acc_ref[h] = acc_ref[h] * decay + weight * back_out[
                h * HD : (h + 1) * HD, :
            ].astype(F32)

    for h in range(heads):
        hs = slice(h * HD, (h + 1) * HD)
        out = (acc_ref[h] / total_ref[h : h + 1, :]).T
        raw_ref[:, hs] = out
        mixed_ref[:, hs] = out.astype(BF16)
    part_ref[...] = jnp.dot(
        mixed_ref[...], w_ref[...], preferred_element_type=F32
    ).astype(BF16)
    lse_ref[...] = high_ref[...] * C2 + jnp.log2(total_ref[...])
    for senders, which in (
        (me >= 0, (0,)), (x == 0, (1, 2)), (y == 0, (3, 4, 5, 6)), (x == 1, (7,)), (y == 1, (8,)),
        (on_chip(3), (9, 10, 11, 12, 14)), (on_chip(2), (13,)), (on_chip(0), (15, 16)),
    ):
        @pl.when(senders)
        def _():
            for k in which:
                copy(k).wait_send()

    for k in range(n):
        @pl.when((at >= k) & (at < n - 1))
        def _():
            pass_on(True, at - k, k).wait_send()

        @pl.when((at + k < n) & (at > 0))
        def _():
            pass_on(False, at + k, k).wait_send()


def attend_far(tok_full, in_weight, cosine, sine, begin, cot, weight, heads, n):
    rows, width = tok_full.shape
    span = heads * HD
    vmem = pl.BlockSpec(memory_space=pltpu.VMEM)
    state = [
        pltpu.VMEM((heads, rows), F32),
        pltpu.VMEM((heads, rows), F32),
        pltpu.VMEM((heads, HD, rows), F32),
    ]
    answer = [pltpu.VMEM((span, rows), BF16), pltpu.VMEM((2 * heads, rows), F32)]
    return pl.pallas_call(
        functools.partial(attend_far_kernel, heads, n),
        in_specs=[vmem] * 7,
        out_specs=[vmem] * 8,
        out_shape=[
            jax.ShapeDtypeStruct((rows, width), BF16),
            jax.ShapeDtypeStruct((rows, 2), F32),
            jax.ShapeDtypeStruct((rows, span), F32),
            jax.ShapeDtypeStruct((rows, span), BF16),
            jax.ShapeDtypeStruct((heads, rows), F32),
            jax.ShapeDtypeStruct((rows, 3 * span), BF16),
            jax.ShapeDtypeStruct((rows, n * cot.shape[1]), BF16),
            jax.ShapeDtypeStruct((rows, width), BF16),
        ],
        scratch_shapes=[
            pltpu.VMEM((CUBE * rows, 2 * span), BF16),
            pltpu.VMEM((rows, span), BF16),
            *state,
            pltpu.VMEM((2, rows, rows), F32),
            pltpu.VMEM((rows, span), BF16),
            *state,
            *answer,
            *answer,
            pltpu.SemaphoreType.DMA((FAR_SENDS,)),
            pltpu.SemaphoreType.DMA((FAR_SENDS,)),
            pltpu.SemaphoreType.DMA((2, n)),
            pltpu.SemaphoreType.DMA((2, n)),
        ],
        compiler_params=params(60, collective_id=2, has_side_effects=True),
        cost_estimate=cost(1e6, 1e6),
        name="attend_far",
    )(tok_full, in_weight, cosine, sine, begin, cot, weight)


def attend_back_far_kernel(
    heads, n, g_ref, kept_ref, begin_ref, part_ref, mid_ref,
    dq_ref, dk_ref, dv_ref, layer_ref, next_ref,
    all_ref, acc_ref, rows_ref, s_ref, p_ref, land_ref, pair_ref, q_ref,
    send, recv, zsend, zrecv, read_sem, mid_land, msend, mrecv,
):
    rows = g_ref.shape[0]
    span = heads * HD
    shard = layer_ref.shape[1]
    at = lax.axis_index("tp")
    cube = Cube(all_ref, send, recv)
    middle = MidSum(mid_ref, mid_land, next_ref, msend, mrecv)
    me = cube.me
    barrier = pltpu.get_barrier_semaphore()
    cube.signal(barrier)
    for o in range(1, n):
        pl.semaphore_signal(
            barrier, inc=1, device_id={"tp": lax.rem(at + o, n)}, device_id_type=MESH
        )

    def read(step, keys):
        place = pl.ds(pl.multiple_of(cube.block(step) * rows, 16), rows)
        near, columns = (pair_ref, (0, 2 * span)) if keys else (q_ref, (2 * span, span))
        return pltpu.make_async_copy(
            kept_ref.at[place, pl.ds(*columns)], near.at[place],
            read_sem.at[0 if keys else 1, step],
        )

    def read_all(step, carry):
        block = cube.block(step)

        @pl.when(block <= me)
        def _():
            read(step, True).start()

        @pl.when(block >= me)
        def _():
            read(step, False).start()

        return carry

    lax.fori_loop(0, CUBE, read_all, 0)
    all_ref[pl.ds(pl.multiple_of(me * rows, 16), rows), :] = g_ref[...]
    acc_ref[...] = jnp.zeros_like(acc_ref)
    dk_ref[...] = jnp.zeros_like(dk_ref)
    dv_ref[...] = jnp.zeros_like(dv_ref)
    pl.semaphore_wait(barrier, 3 + n - 1)

    def term(o):
        target = lax.rem(at + o, n)
        return pltpu.make_async_remote_copy(
            src_ref=part_ref.at[:, pl.ds(pl.multiple_of(target * shard, 128), shard)],
            dst_ref=land_ref.at[o - 1],
            send_sem=zsend.at[o - 1], recv_sem=zrecv.at[o - 1],
            device_id={"tp": target}, device_id_type=MESH,
        )

    own = pl.ds(pl.multiple_of(me * rows, 16), rows)

    cube.start(0, 1, 3, 2, 4)

    def turn(step, carry):
        cube.advance(step)

        @pl.when(step == 0)
        def _():
            for o in range(1, n):
                term(o).start()
            middle.begin()

        @pl.when(step == 3)
        def _():
            middle.turn()

        block = cube.block(step)
        place = pl.ds(pl.multiple_of(block * rows, 16), rows)

        @pl.when(block <= me)
        def _():
            read(step, True).wait()

        @pl.when(block >= me)
        def _():
            read(step, False).wait()

        def scores(h, key_block, key_place, query_block, query_place):
            hs = slice(h * HD, (h + 1) * HD)
            vs = slice(span + h * HD, span + (h + 1) * HD)
            s = lax.dot_general(
                pair_ref[key_place, hs], q_ref[query_place, hs], NT, preferred_element_type=F32
            )
            begin = begin_ref[pl.ds(query_block, 1), :]
            s_ref[h % 2] = hidden_scores(s, key_block, query_block, rows, begin)
            p_ref[h % 2] = lax.dot_general(
                pair_ref[key_place, vs], all_ref[query_place, hs], NT, preferred_element_type=F32
            )

        def read_rows(query_place):
            coded = all_ref[query_place, span:].astype(F32).T
            for k in range(2 * heads):
                rows_ref[k : k + 1, :] = (
                    coded[3 * k : 3 * k + 1]
                    + coded[3 * k + 1 : 3 * k + 2]
                    + coded[3 * k + 2 : 3 * k + 3]
                )

        def weights(h):
            p = jnp.exp2(s_ref[h % 2] * C2 - rows_ref[h : h + 1, :])
            ds = p * (p_ref[h % 2] - rows_ref[heads + h : heads + h + 1, :])
            return p.astype(BF16), ds.astype(BF16)

        @pl.when(block <= me)
        def _():
            read_rows(own)
            scores(0, block, place, me, own)
            for h in range(heads):
                if h + 1 < heads:
                    scores(h + 1, block, place, me, own)
                _, ds = weights(h)
                acc_ref[h] = acc_ref[h] + lax.dot_general(
                    pair_ref[place, h * HD : (h + 1) * HD], ds, TN, preferred_element_type=F32
                )

        @pl.when(block >= me)
        def _():
            read_rows(place)
            scores(0, me, own, block, place)
            for h in range(heads):
                hs = slice(h * HD, (h + 1) * HD)
                if h + 1 < heads:
                    scores(h + 1, me, own, block, place)
                p, ds = weights(h)
                dv_ref[:, hs] += jnp.dot(p, all_ref[place, hs], preferred_element_type=F32)
                dk_ref[:, hs] += jnp.dot(ds, q_ref[place, hs], preferred_element_type=F32)

        return carry

    lax.fori_loop(0, CUBE, turn, 0)
    for h in range(heads):
        dq_ref[:, h * HD : (h + 1) * HD] = (acc_ref[h] * SCALE).T
    dk_ref[...] = dk_ref[...] * SCALE
    total = part_ref[:, pl.ds(pl.multiple_of(at * shard, 128), shard)].astype(F32)
    for o in range(1, n):
        term(o).wait_recv()
        total = total + land_ref[o - 1].astype(F32)
    layer_ref[...] = total.astype(BF16)
    middle.finish()
    cube.finish()
    for o in range(1, n):
        term(o).wait_send()


def attend_back_far(grad, kept, all_begin, part, mid, heads, n):
    rows = grad.shape[0]
    span = heads * HD
    shard = part.shape[1] // n
    vmem = pl.BlockSpec(memory_space=pltpu.VMEM)
    wide = jax.ShapeDtypeStruct((rows, span), F32)
    return pl.pallas_call(
        functools.partial(attend_back_far_kernel, heads, n),
        in_specs=[vmem, pl.BlockSpec(memory_space=pl.ANY)] + [vmem] * 3,
        out_specs=[vmem] * 5,
        out_shape=[wide, wide, wide, jax.ShapeDtypeStruct((rows, shard), BF16)]
        + [jax.ShapeDtypeStruct(mid.shape, BF16)],
        scratch_shapes=[
            pltpu.VMEM((CUBE * rows, span + HD), BF16),
            pltpu.VMEM((heads, HD, rows), F32),
            pltpu.VMEM((2 * heads, rows), F32),
            pltpu.VMEM((2, rows, rows), F32),
            pltpu.VMEM((2, rows, rows), F32),
            pltpu.VMEM((n - 1, rows, shard), BF16),
            pltpu.VMEM((CUBE * rows, 2 * span), BF16),
            pltpu.VMEM((CUBE * rows, span), BF16),
            pltpu.SemaphoreType.DMA((CUBE_SENDS,)),
            pltpu.SemaphoreType.DMA((CUBE_SENDS,)),
            pltpu.SemaphoreType.DMA((n - 1,)),
            pltpu.SemaphoreType.DMA((n - 1,)),
            pltpu.SemaphoreType.DMA((2, CUBE)),
            pltpu.VMEM((mid.shape[0] // 2, mid.shape[1]), BF16),
            pltpu.SemaphoreType.DMA((4,)),
            pltpu.SemaphoreType.DMA((4,)),
        ],
        compiler_params=params(62, collective_id=3, has_side_effects=True),
        cost_estimate=cost(1e6, 1e6),
        name="attend_back_far",
    )(grad, kept, all_begin, part, mid)


def query_grad_kernel(
    heads, info, q_ref, do_ref, lse_ref, delta_ref, k_ref, v_ref, begin_ref,
    dq_ref, acc_ref, s_ref, g_ref,
):
    me, first, clear = info[0], info[1], info[2]
    j = pl.program_id(0)
    rows = q_ref.shape[0]

    @pl.when(j == 0)
    def _():
        acc_ref[...] = jnp.zeros_like(acc_ref)

    def block(hide):
        def score(h):
            hs = slice(h * HD, (h + 1) * HD)
            s = lax.dot_general(k_ref[:, hs], q_ref[:, hs], NT, preferred_element_type=F32)
            if hide:
                s = masked(s, j, me, rows, begin_ref[...])
            s_ref[h % 2] = s
            g_ref[h % 2] = lax.dot_general(
                v_ref[:, hs], do_ref[:, hs], NT, preferred_element_type=F32
            )

        def spread(h):
            hs = slice(h * HD, (h + 1) * HD)
            p = jnp.exp2(s_ref[h % 2] * C2 - lse_ref[h : h + 1, :])
            ds = (p * (g_ref[h % 2] - delta_ref[h : h + 1, :])).astype(BF16)
            acc_ref[h] = acc_ref[h] + lax.dot_general(
                k_ref[:, hs], ds, TN, preferred_element_type=F32
            )

        score(0)
        for h in range(heads):
            if h + 1 < heads:
                score(h + 1)
            spread(h)

    @pl.when((j >= clear) & (j < me))
    def _():
        block(False)

    @pl.when(((j >= first) & (j < clear) & (j < me)) | (j == me))
    def _():
        block(True)

    @pl.when(j == me)
    def _():
        for h in range(heads):
            dq_ref[:, h * HD : (h + 1) * HD] = (acc_ref[h] * SCALE).T


def query_grad(info, query, grad_mixed, lse, delta, pairs, begin, heads):
    rows = query.shape[0]
    total = pairs.shape[0]
    span = heads * HD
    full = lambda shape: pl.BlockSpec(shape, lambda j, s: (0, 0))
    key = pl.BlockSpec((rows, span), lambda j, s: (jnp.clip(j, s[1], s[0]), 0))
    value = pl.BlockSpec((rows, span), lambda j, s: (jnp.clip(j, s[1], s[0]), 1))
    wide = full((rows, span))
    thin = full((heads, rows))
    return pl.pallas_call(
        functools.partial(query_grad_kernel, heads),
        grid_spec=pltpu.PrefetchScalarGridSpec(
            num_scalar_prefetch=1,
            grid=(total // rows,),
            in_specs=[wide, wide, thin, thin, key, value, full((1, rows))],
            out_specs=wide,
            scratch_shapes=[
                pltpu.VMEM((heads, HD, rows), F32),
                pltpu.VMEM((2, rows, rows), F32),
                pltpu.VMEM((2, rows, rows), F32),
            ],
        ),
        out_shape=jax.ShapeDtypeStruct((rows, span), F32),
        compiler_params=params(58),
        cost_estimate=cost(6 * rows * total * span, 4 * total * span, rows * total * heads),
        name="query_grad",
    )(info, query, grad_mixed, lse, delta, pairs, pairs, begin)


def key_grad_kernel(
    heads, info, k_ref, v_ref, q_ref, g_ref, begin_ref, dk_ref, dv_ref,
    rows_ref, s_ref, p_ref,
):
    me, last, clear = info[0], info[1], info[2]
    j = pl.program_id(0)
    rows = k_ref.shape[0]
    span = heads * HD

    @pl.when(j == me)
    def _():
        dk_ref[...] = jnp.zeros_like(dk_ref)
        dv_ref[...] = jnp.zeros_like(dv_ref)

    def block(hide):
        coded = g_ref[:, span:].astype(F32).T
        for n in range(2 * heads):
            rows_ref[n : n + 1, :] = (
                coded[3 * n : 3 * n + 1] + coded[3 * n + 1 : 3 * n + 2] + coded[3 * n + 2 : 3 * n + 3]
            )

        def score(h):
            hs = slice(h * HD, (h + 1) * HD)
            s = lax.dot_general(k_ref[:, hs], q_ref[:, hs], NT, preferred_element_type=F32)
            if hide:
                key_place = lax.broadcasted_iota(jnp.int32, s.shape, 0) + me * rows
                query_place = lax.broadcasted_iota(jnp.int32, s.shape, 1) + j * rows
                s = jnp.where(
                    (key_place <= query_place) & (key_place >= begin_ref[...]), s, NEG
                )
            s_ref[h % 2] = s
            p_ref[h % 2] = lax.dot_general(
                v_ref[:, hs], g_ref[:, hs], NT, preferred_element_type=F32
            )

        def spread(h):
            hs = slice(h * HD, (h + 1) * HD)
            p = jnp.exp2(s_ref[h % 2] * C2 - rows_ref[h : h + 1, :])
            ds = (p * (p_ref[h % 2] - rows_ref[heads + h : heads + h + 1, :])).astype(BF16)
            dv_ref[:, hs] += jnp.dot(p.astype(BF16), g_ref[:, hs], preferred_element_type=F32)
            dk_ref[:, hs] += jnp.dot(ds, q_ref[:, hs], preferred_element_type=F32)

        score(0)
        for h in range(heads):
            if h + 1 < heads:
                score(h + 1)
            spread(h)

    @pl.when((j > me) & (j <= clear))
    def _():
        block(False)

    @pl.when((j == me) | ((j > me) & (j > clear) & (j <= last)))
    def _():
        block(True)

    @pl.when(j == pl.num_programs(0) - 1)
    def _():
        dk_ref[...] = dk_ref[...] * SCALE


def key_grad(info, pairs, all_query, all_grad, all_begin, heads):
    rows = pairs.shape[0]
    total = all_query.shape[0]
    span = heads * HD
    full = lambda shape, at=0: pl.BlockSpec(shape, lambda j, s: (0, at))
    near = lambda j, s: (jnp.clip(j, s[0], s[1]), 0)
    wide = full((rows, span))
    return pl.pallas_call(
        functools.partial(key_grad_kernel, heads),
        grid_spec=pltpu.PrefetchScalarGridSpec(
            num_scalar_prefetch=1,
            grid=(total // rows,),
            in_specs=[
                wide, full((rows, span), 1),
                pl.BlockSpec((rows, span), near),
                pl.BlockSpec((rows, span + HD), near),
                pl.BlockSpec((1, rows), lambda j, s: (0, jnp.clip(j, s[0], s[1]))),
            ],
            out_specs=[wide, wide],
            scratch_shapes=[
                pltpu.VMEM((2 * heads, rows), F32),
                pltpu.VMEM((2, rows, rows), F32),
                pltpu.VMEM((2, rows, rows), F32),
            ],
        ),
        out_shape=[jax.ShapeDtypeStruct((rows, span), F32)] * 2,
        compiler_params=params(58),
        cost_estimate=cost(8 * rows * total * span, 4 * total * span, rows * total * heads),
        name="key_grad",
    )(info, pairs, pairs, all_query, all_grad, all_begin)


def mixed_grad_kernel(heads, branch_ref, w_ref, raw_ref, lse_ref, out_ref, delta_ref):
    span = heads * HD
    low = lax.dot_general(
        branch_ref[...], w_ref[...], NT, preferred_element_type=F32
    ).astype(BF16)
    out_ref[:, :span] = low
    count = low.shape[0]
    both = low.astype(F32) * raw_ref[...]
    for h in range(heads):
        delta_ref[h : h + 1, :] = jnp.sum(both[:, h * HD : (h + 1) * HD].T, axis=0, keepdims=True)
    lines = []
    for n in range(2 * heads):
        value = lse_ref[n : n + 1, :] if n < heads else delta_ref[n - heads : n - heads + 1, :]
        for _ in range(3):
            piece = value.astype(BF16).astype(F32)
            lines.append(piece)
            value = value - piece
    lines.append(jnp.zeros((HD - len(lines), count), F32))
    out_ref[:, span:] = jnp.concatenate(lines, axis=0).T.astype(BF16)


def mixed_grad(branch, weight, raw, lse, heads):
    rows, width = branch.shape
    span = heads * HD
    block = 256
    row = lambda n: pl.BlockSpec((block, n), lambda i: (i, 0))
    line = pl.BlockSpec((heads, block), lambda i: (0, i))
    return pl.pallas_call(
        functools.partial(mixed_grad_kernel, heads),
        grid=(rows // block,),
        in_specs=[row(width), pl.BlockSpec((span, width), lambda i: (0, 0)), row(span), line],
        out_specs=[row(span + HD), line],
        out_shape=[
            jax.ShapeDtypeStruct((rows, span + HD), BF16),
            jax.ShapeDtypeStruct((heads, rows), F32),
        ],
        compiler_params=params(56),
        cost_estimate=cost(2 * rows * width * span, 2 * width * span + 4 * rows * width),
        name="mixed_grad",
    )(branch, weight, raw, lse)


def feed_kernel(
    inner_ref, cot_ref, w_ref, grad_ref, hidden_ref, dgu_ref, down_grad_ref, gu_grad_ref
):
    block = grad_ref.shape[1]
    both = jnp.dot(inner_ref[...], w_ref[...], preferred_element_type=F32)
    grad = grad_ref[...].astype(F32)
    gate, up = both[:, :block], both[:, block:]
    sigma = 1.0 / (1.0 + jnp.exp(-gate))
    active = gate * sigma
    hidden_ref[...] = (active * up).astype(BF16)
    dgu_ref[:, :block] = (grad * up * sigma * (1.0 + gate * (1.0 - sigma))).astype(BF16)
    dgu_ref[:, block:] = (grad * active).astype(BF16)
    down_grad_ref[...] = lax.dot_general(
        hidden_ref[...], cot_ref[...], TN, preferred_element_type=F32
    ).astype(BF16)
    gu_grad_ref[...] = lax.dot_general(
        inner_ref[...], dgu_ref[...], TN, preferred_element_type=F32
    ).astype(BF16)


def feed(inner, cot, weight, grad, block):
    rows, width = inner.shape
    units = grad.shape[1]
    whole = pl.BlockSpec((rows, width), lambda j: (0, 0))
    column = lambda high, wide: pl.BlockSpec((high, wide), lambda j: (0, j))
    line = pl.BlockSpec((block, width), lambda j: (j, 0))
    return pl.pallas_call(
        feed_kernel,
        grid=(units // block,),
        in_specs=[whole, whole, column(width, 2 * block), column(rows, block)],
        out_specs=[column(rows, block), column(rows, 2 * block), line, column(width, 2 * block)],
        out_shape=[
            jax.ShapeDtypeStruct((rows, units), BF16),
            jax.ShapeDtypeStruct((rows, 2 * units), BF16),
            jax.ShapeDtypeStruct((units, width), BF16),
            jax.ShapeDtypeStruct((width, 2 * units), BF16),
        ],
        compiler_params=params(60),
        cost_estimate=cost(
            12 * rows * width * units, 12 * width * units + 4 * rows * width, rows * units
        ),
        name="feed",
    )(inner, cot, weight, grad)


def weave_kernel(block, sum_ref, out_ref):
    for j in range(sum_ref.shape[1] // (2 * block)):
        for k in range(2):
            at = (2 * j + k) * block
            out_ref[:, k, j * block : (j + 1) * block] = sum_ref[:, at : at + block].astype(F32)


def weave(summed, block):
    width, both = summed.shape
    rows = 256
    return pl.pallas_call(
        functools.partial(weave_kernel, block),
        grid=(width // rows,),
        in_specs=[pl.BlockSpec((rows, both), lambda i: (i, 0))],
        out_specs=pl.BlockSpec((rows, 2, both // 2), lambda i: (i, 0, 0)),
        out_shape=jax.ShapeDtypeStruct((width, 2, both // 2), F32),
        compiler_params=params(56),
        cost_estimate=cost(width * both, 6 * width * both),
        name="weave",
    )(summed)


def widen_kernel(in_ref, out_ref):
    out_ref[...] = in_ref[...].astype(F32)


def widen(summed):
    high, wide = summed.shape
    block = pl.BlockSpec((512, wide), lambda i: (i, 0))
    return pl.pallas_call(
        widen_kernel,
        grid=(high // 512,),
        in_specs=[block],
        out_specs=block,
        out_shape=jax.ShapeDtypeStruct((high, wide), F32),
        compiler_params=params(56),
        cost_estimate=cost(high * wide, 6 * high * wide),
        name="widen",
    )(summed)


def line_barrier(at, n, cube=None):
    barrier = pltpu.get_barrier_semaphore()
    if cube is not None:
        cube.signal(barrier)

    @pl.when(at > 0)
    def _():
        pl.semaphore_signal(barrier, inc=1, device_id={"tp": at - 1}, device_id_type=MESH)

    @pl.when(at < n - 1)
    def _():
        pl.semaphore_signal(barrier, inc=1, device_id={"tp": at + 1}, device_id_type=MESH)

    near = jnp.where((at > 0) & (at < n - 1), 2, 1)
    pl.semaphore_wait(barrier, near + (0 if cube is None else 3))


def sum_rows(n, sub, part_ref, out_ref, row_fn, from_left, from_right, send, recv, aside={}):
    at = lax.axis_index("tp")
    chunks = part_ref.shape[0] // sub
    middle = (n // 2 - 1, n // 2)

    def link(kind, right, src, dst, c):
        which = (kind * 2 + (1 if right else 0), c)
        return pltpu.make_async_remote_copy(
            src_ref=src.at[pl.ds(c * sub, sub)],
            dst_ref=dst.at[pl.ds(c * sub, sub)],
            send_sem=send.at[which],
            recv_sem=recv.at[which],
            device_id={"tp": at + 1 if right else at - 1},
            device_id_type=MESH,
        )

    def came(right):
        return from_left if right else from_right

    def first(right, c):
        return link(0, right, part_ref, came(right), c)

    def onward(right, c):
        return link(0, right, came(right), came(right), c)

    def hand(right, c):
        return link(1, right, out_ref, out_ref, c)

    def reduce_step(c):
        owner = middle[c % 2]
        rows = slice(c * sub, (c + 1) * sub)
        for right in (True, False):
            edge = 0 if right else n - 1
            held = came(right)

            @pl.when(((at < owner) if right else (at > owner)) & (at != edge))
            def _():
                copy = onward(right, c)
                copy.wait_recv()
                held[rows, :] = (
                    held[rows, :].astype(F32) + part_ref[rows, :].astype(F32)
                ).astype(BF16)
                copy.start()

    def final_step(c):
        owner = middle[c % 2]
        rows = slice(c * sub, (c + 1) * sub)

        @pl.when(at == owner)
        def _():
            total = part_ref[rows, :].astype(F32)
            onward(True, c).wait_recv()
            total = total + from_left[rows, :].astype(F32)
            onward(False, c).wait_recv()
            total = total + from_right[rows, :].astype(F32)
            row_fn(total, rows)
            hand(True, c).start()
            hand(False, c).start()

    def hand_step(c):
        owner = middle[c % 2]
        for right in (True, False):
            edge = n - 1 if right else 0

            @pl.when((at > owner) if right else (at < owner))
            def _():
                copy = hand(right, c)
                copy.wait_recv()

                @pl.when(at != edge)
                def _():
                    copy.start()

    for c in range(chunks):
        @pl.when(at == 0)
        def _():
            first(True, c).start()

        @pl.when(at == n - 1)
        def _():
            first(False, c).start()

    for c in range(chunks + 4):
        for piece in aside.get(c, ()):
            piece()
        if c < chunks:
            reduce_step(c)
        if 2 <= c < chunks + 2:
            final_step(c - 2)
        if c >= 4:
            hand_step(c - 4)
    for c in range(chunks):
        owner = middle[c % 2]

        @pl.when(at < owner)
        def _():
            first(True, c).wait_send()

        @pl.when(at > owner)
        def _():
            first(False, c).wait_send()

        @pl.when((at >= owner) & (at < n - 1))
        def _():
            hand(True, c).wait_send()

        @pl.when((at <= owner) & (at > 0))
        def _():
            hand(False, c).wait_send()


def merge_kernel(
    n, sub, part_ref, tok_ref, far_cot, far_down, inner_ref, resid_out, stat_ref, hidden_ref,
    from_left, from_right, send, recv, cot_ref, down_ref, resid_ref, read_sem, keep_sem,
):
    reads = (
        pltpu.make_async_copy(far_cot, cot_ref, read_sem.at[0]),
        pltpu.make_async_copy(far_down, down_ref, read_sem.at[1]),
    )
    for read in reads:
        read.start()
    line_barrier(lax.axis_index("tp"), n)
    stat_ref[...] = jnp.zeros_like(stat_ref)

    def keep(rows):
        slot = rows.start // (2 * sub)
        held = resid_ref.at[pl.ds(slot * sub, sub)]
        return pltpu.make_async_copy(
            held, resid_out.at[pl.ds(rows.start, sub)], keep_sem.at[slot]
        )

    def row_fn(total, rows):
        x = tok_ref[rows, :].astype(F32) + total
        mean = jnp.mean(x, axis=1, keepdims=True)
        center = x - mean
        inverse = lax.rsqrt(jnp.mean(center * center, axis=1, keepdims=True) + EPS)
        slot = rows.start // (2 * sub)
        resid_ref[slot * sub : (slot + 1) * sub, :] = x
        keep(rows).start()
        stat_ref[rows, :] = jnp.concatenate([mean, inverse], axis=1)
        inner_ref[rows, :] = (center * inverse).astype(BF16)

    def piece(at):
        if at == 0:
            for read in reads:
                read.wait()
        hidden_ref[:, at : at + 256] = lax.dot_general(
            cot_ref[...], down_ref[at : at + 256, :], NT, preferred_element_type=F32
        ).astype(BF16)

    aside = {}
    for k in range(down_ref.shape[0] // 256):
        aside[1 + 2 * k] = (functools.partial(piece, k * 256),)
    sum_rows(n, sub, part_ref, inner_ref, row_fn, from_left, from_right, send, recv, aside)
    for c in range(part_ref.shape[0] // sub):
        @pl.when(lax.axis_index("tp") == n // 2 - 1 + c % 2)
        def _():
            keep(slice(c * sub, (c + 1) * sub)).wait()


def merge(part, tok_full, cot_full, down, n):
    rows, width = part.shape
    sub = SUB
    vmem = pl.BlockSpec(memory_space=pltpu.VMEM)
    far = pl.BlockSpec(memory_space=pl.ANY)
    return pl.pallas_call(
        functools.partial(merge_kernel, n, sub),
        in_specs=[vmem, vmem, far, far],
        out_specs=[vmem, far, vmem, vmem],
        out_shape=[
            jax.ShapeDtypeStruct((rows, width), BF16),
            jax.ShapeDtypeStruct((rows, width), F32),
            jax.ShapeDtypeStruct((rows, 2), F32),
            jax.ShapeDtypeStruct((rows, down.shape[0]), BF16),
        ],
        scratch_shapes=[pltpu.VMEM((rows, width), BF16)] * 2
        + [pltpu.SemaphoreType.DMA((4, rows // sub))] * 2
        + [
            pltpu.VMEM((rows, width), BF16),
            pltpu.VMEM(down.shape, BF16),
            pltpu.VMEM((rows // 2, width), F32),
            pltpu.SemaphoreType.DMA((2,)),
            pltpu.SemaphoreType.DMA((rows // (2 * sub),)),
        ],
        compiler_params=params(56, collective_id=5, has_side_effects=True),
        cost_estimate=cost(1e6, 1e6),
        name="merge",
    )(part, tok_full, cot_full, down)


def norm_back_kernel(
    n, sub, cube, part_ref, cot_ref, stat_ref, *refs
):
    total = None
    far, refs = refs[:3], refs[3:]
    if cube:
        own, out_ref, layer_ref, mid, from_left, from_right, send, recv = refs[:8]
        resid_ref, hidden_ref, down_ref, read_sem = refs[8:12]
        total = CubeSum(own, *refs[12:17], mid=mid)
    else:
        out_ref, layer_ref, from_left, from_right, send, recv = refs[:6]
        resid_ref, hidden_ref, down_ref, read_sem = refs[6:10]
    reads = [
        pltpu.make_async_copy(source, held, read_sem.at[k])
        for k, (source, held) in enumerate(zip(far, (resid_ref, hidden_ref, down_ref)))
    ]
    for read in reads:
        read.start()
    at = lax.axis_index("tp")
    line_barrier(lax.axis_index("tp"), n, total)
    aside = {}

    def piece(start):
        if start == 0:
            for read in reads:
                read.wait()
        cols = slice(start, start + 256)
        row = lax.broadcasted_iota(jnp.int32, (part_ref.shape[0], 256), 0)
        owned = (row // sub) % 2 == at - (n // 2 - 1)
        layer_ref[:, cols] = (
            jnp.where(owned, resid_ref[:, cols], 0.0)
            + jnp.dot(hidden_ref[...], down_ref[:, cols], preferred_element_type=F32)
        ).astype(BF16)

    for k in range(down_ref.shape[1] // 256):
        aside[1 + 2 * k] = (functools.partial(piece, k * 256),)
    if cube:
        total.begin()
        for k, c in enumerate((14, 16, 18, 20)):
            aside[c] = (functools.partial(total.reduce, k),)

    def row_fn(summed, rows):
        inverse = stat_ref[rows, 1:2]
        normed = (resid_ref[rows, :] - stat_ref[rows, 0:1]) * inverse
        mean = jnp.mean(summed, axis=1, keepdims=True)
        inner = jnp.mean(summed * normed, axis=1, keepdims=True)
        out = cot_ref[rows, :].astype(F32) + inverse * (summed - mean - normed * inner)
        out_ref[rows, :] = out.astype(BF16)

    sum_rows(n, sub, part_ref, out_ref, row_fn, from_left, from_right, send, recv, aside)
    if cube:
        total.reduce(4)
        total.reduce(5)
        total.finish()


def norm_back(part, cot, resid, stat, hidden, down, n, grads):
    rows, width = part.shape
    sub = SUB
    vmem = pl.BlockSpec(memory_space=pltpu.VMEM)
    far = pl.BlockSpec(memory_space=pl.ANY)
    extra = []
    for grad in grads:
        extra += sum_scratch(grad.shape)
    return pl.pallas_call(
        functools.partial(norm_back_kernel, n, sub, len(grads) > 0),
        in_specs=[vmem] * 3 + [far] * (3 + len(grads)),
        out_specs=[vmem] * (2 + len(grads)),
        out_shape=[jax.ShapeDtypeStruct((rows, width), BF16)] * 2
        + [jax.ShapeDtypeStruct((grad.shape[0] // 4, grad.shape[1]), BF16) for grad in grads],
        scratch_shapes=[pltpu.VMEM((rows, width), BF16)] * 2
        + [pltpu.SemaphoreType.DMA((4, rows // sub))] * 2
        + [
            pltpu.VMEM(resid.shape, F32),
            pltpu.VMEM(hidden.shape, BF16),
            pltpu.VMEM(down.shape, BF16),
            pltpu.SemaphoreType.DMA((3,)),
        ]
        + extra,
        compiler_params=params(60, collective_id=1, has_side_effects=True),
        cost_estimate=cost(1e6, 1e6),
        name="norm_back",
    )(part, cot, stat, resid, hidden, down, *grads)


def unrotate_kernel(
    heads, dq_ref, dk_ref, dv_ref, cos_ref, sin_ref, inner_ref, dproj_ref, grad_ref
):
    def back(ref):
        for h in range(heads):
            hs = slice(h * HD, (h + 1) * HD)
            piece = ref[:, hs]
            dproj_ref[:, hs] = (
                piece * cos_ref[...] - pltpu.roll(piece, HD // 2, 1) * sin_ref[...]
            ).astype(BF16)

    part = pl.program_id(0)

    @pl.when(part == 0)
    def _():
        back(dq_ref)

    @pl.when(part == 1)
    def _():
        back(dk_ref)

    @pl.when(part == 2)
    def _():
        dproj_ref[...] = dv_ref[...].astype(BF16)

    grad_ref[...] = lax.dot_general(
        inner_ref[...], dproj_ref[...], TN, preferred_element_type=F32
    ).astype(BF16)


def unrotate(dq, dk, dv, cosine, sine, inner, heads):
    rows, span = dq.shape
    width = inner.shape[1]
    whole = lambda n: pl.BlockSpec((rows, n), lambda i: (0, 0))
    return pl.pallas_call(
        functools.partial(unrotate_kernel, heads),
        grid=(3,),
        in_specs=[whole(span)] * 3 + [whole(HD)] * 2 + [whole(width)],
        out_specs=[
            pl.BlockSpec((rows, span), lambda i: (0, i)),
            pl.BlockSpec((width, span), lambda i: (i, 0)),
        ],
        out_shape=[
            jax.ShapeDtypeStruct((rows, 3 * span), BF16),
            jax.ShapeDtypeStruct((3 * width, span), BF16),
        ],
        compiler_params=params(56),
        cost_estimate=cost(6 * rows * span * width, 12 * rows * span + 6 * width * span),
        name="unrotate",
    )(dq, dk, dv, cosine, sine, inner)


def unproject_kernel(heads, n, cube, *refs):
    sums, rest = [], None
    if cube:
        dq_ref, dk_ref, dv_ref, cos_ref, sin_ref, inner_ref, mixed_ref = refs[:7]
        branch_ref, mid_ref, tok_ref, stat_ref, w_ref = refs[7:12]
        out_ref, in_out, og_out, down_out, dproj_ref, in_ref, og_ref = refs[12:19]
        part_ref, mine_ref, land_ref, sums_ref, far_ref, send, recv, ssend, srecv = refs[19:28]
        for own, out, at in ((in_ref, in_out, 28), (og_ref, og_out, 31)):
            sums.append(CubeSum(own, own, *refs[at : at + 3], None, out=out))
        rest = LastGather(mid_ref, down_out, *refs[34:37])
    else:
        dproj_ref, branch_ref, tok_ref, stat_ref, w_ref, out_ref = refs[:6]
        part_ref, mine_ref, land_ref, sums_ref, far_ref, send, recv, ssend, srecv = refs[6:15]

    def reduce(*pieces):
        for k in pieces:
            for item in sums:
                item.reduce(k)

    def gather(k):
        for item in sums:
            item.gather(k)

    rows, width = tok_ref.shape
    shard = width // n
    span = heads * HD
    at = lax.axis_index("tp")
    barrier = pltpu.get_barrier_semaphore()
    for o in range(1, n):
        pl.semaphore_signal(
            barrier, inc=1, device_id={"tp": lax.rem(at + o, n)}, device_id_type=MESH
        )
    if cube:
        sums[0].signal(barrier)
    pl.semaphore_wait(barrier, n - 1 + (3 if cube else 0))
    if cube:
        og_ref[...] = lax.dot_general(
            mixed_ref[...], branch_ref[...], TN, preferred_element_type=F32
        ).astype(BF16)
        sums[1].begin()
        for part, ref in enumerate((dq_ref, dk_ref, dv_ref)):
            for h in range(heads):
                piece = ref[:, h * HD : (h + 1) * HD]
                if part < 2:
                    piece = (
                        piece * cos_ref[...] - pltpu.roll(piece, HD // 2, 1) * sin_ref[...]
                    )
                at_column = part * span + h * HD
                dproj_ref[:, at_column : at_column + HD] = piece.astype(BF16)
            in_ref[part * width : (part + 1) * width, :] = lax.dot_general(
                inner_ref[...], dproj_ref[:, part * span : (part + 1) * span], TN,
                preferred_element_type=F32,
            ).astype(BF16)
        sums[0].begin()
    block = 256
    count = rows // block

    def term(o, i):
        target = lax.rem(at + o, n)
        place = pl.ds(i * block, block)
        return pltpu.make_async_remote_copy(
            src_ref=part_ref.at[place, pl.ds(pl.multiple_of(target * shard, 128), shard)],
            dst_ref=land_ref.at[o - 1, place],
            send_sem=send.at[o - 1, i], recv_sem=recv.at[o - 1, i],
            device_id={"tp": target}, device_id_type=MESH,
        )

    def totals(o):
        return pltpu.make_async_remote_copy(
            src_ref=sums_ref, dst_ref=far_ref.at[o - 1],
            send_sem=ssend.at[o - 1], recv_sem=srecv.at[o - 1],
            device_id={"tp": lax.rem(at + o, n)}, device_id_type=MESH,
        )

    own = pl.ds(pl.multiple_of(at * shard, 128), shard)
    for i in range(count):
        place = pl.ds(i * block, block)
        total = None
        for part in range(3):
            piece = lax.dot_general(
                dproj_ref[place, part * span : (part + 1) * span], w_ref[part], NT,
                preferred_element_type=F32,
            )
            total = piece if total is None else total + piece
        part_ref[place, :] = total.astype(BF16)
        for o in range(1, n):
            term(o, i).start()
        normed = (tok_ref[place, :].astype(F32) - stat_ref[place, 0:1]) * stat_ref[place, 1:2]
        first = jnp.sum(total, axis=1, keepdims=True)
        second = jnp.sum(total * normed, axis=1, keepdims=True)
        lane = lax.broadcasted_iota(jnp.int32, (block, HD), 1)
        both = jnp.where(lane == 0, first, jnp.where(lane == 1, second, 0.0))
        sums_ref[:, i * block : (i + 1) * block] = both.T[:8]
    for o in range(1, n):
        totals(o).start()
    reduce(0, 1, 2, 3, 4, 5)
    if cube:
        rest.begin()
    reduce(6, 7)
    gather(0)
    gather(1)
    total = sums_ref[...]
    for o in range(1, n):
        totals(o).wait_recv()
        total = total + far_ref[o - 1]
    mine_ref[...] = total
    for i in range(count):
        place = pl.ds(i * block, block)
        spread = jnp.concatenate(
            [mine_ref[:, i * block : (i + 1) * block], jnp.zeros((HD - 8, block), F32)], axis=0
        ).T / width
        total = part_ref[place, own].astype(F32)
        for o in range(1, n):
            term(o, i).wait_recv()
            total = total + land_ref[o - 1, place].astype(F32)
        inverse = stat_ref[place, 1:2]
        normed = (tok_ref[place, own].astype(F32) - stat_ref[place, 0:1]) * inverse
        out_ref[place, :] = branch_ref[place, own].astype(F32) + inverse * (
            total - spread[:, 0:1] - normed * spread[:, 1:2]
        )
    gather(2)
    for item in sums + ([rest] if cube else []):
        item.finish()
    for o in range(1, n):
        totals(o).wait_send()
        for i in range(count):
            term(o, i).wait_send()


def unproject(cube, operands, tok_full, stat, weight, heads, n):
    rows, width = tok_full.shape
    shard = width // n
    span = heads * HD
    vmem = pl.BlockSpec(memory_space=pltpu.VMEM)
    shapes = [(3 * width, span), (span, width)] if cube else []
    more_out, early, extra = [], [], []
    if cube:
        mid = operands[-1]
        more_out = [jax.ShapeDtypeStruct((high // 2, wide), BF16) for high, wide in shapes]
        more_out.append(jax.ShapeDtypeStruct((2 * mid.shape[0], mid.shape[1]), BF16))
        early = [pltpu.VMEM(shape, BF16) for shape in [(rows, 3 * span)] + shapes]
        for shape in shapes:
            extra += sum_scratch(shape)[1:4]
        extra += [pltpu.SemaphoreType.DMA((2,))] * 3
    return pl.pallas_call(
        functools.partial(unproject_kernel, heads, n, cube),
        in_specs=[vmem] * (len(operands) + 3),
        out_specs=[vmem] * (1 + len(shapes)) + [pl.BlockSpec(memory_space=pl.ANY)] * int(cube),
        out_shape=[jax.ShapeDtypeStruct((rows, shard), F32)] + more_out,
        scratch_shapes=early
        + [
            pltpu.VMEM((rows, width), BF16),
            pltpu.VMEM((8, rows), F32),
            pltpu.VMEM((n - 1, rows, shard), BF16),
            pltpu.VMEM((8, rows), F32),
            pltpu.VMEM((n - 1, 8, rows), F32),
            pltpu.SemaphoreType.DMA((n - 1, rows // 256)),
            pltpu.SemaphoreType.DMA((n - 1, rows // 256)),
            pltpu.SemaphoreType.DMA((n - 1,)),
            pltpu.SemaphoreType.DMA((n - 1,)),
        ]
        + extra,
        compiler_params=params(61, collective_id=4, has_side_effects=True),
        cost_estimate=cost(1e6, 1e6),
        name="unproject",
    )(*operands, tok_full, stat, weight)


def per_device(tokens, segment_ids, in_weight, out_weight, gate_up_weight, down_weight, cotangent):
    rows = tokens.shape[0]
    width = in_weight.shape[0]
    span = in_weight.shape[2]
    heads = span // HD
    hidden_local = down_weight.shape[0]
    me = lax.axis_index("ctx")
    tp_size = lax.axis_size("tp")
    cube = lax.axis_size("ctx") == CUBE

    def gather(local, axis=1):
        return lax.all_gather(local, "tp", axis=axis, tiled=True)

    places = me * rows + jnp.arange(rows, dtype=jnp.int32)
    cosine, sine = rope_tables(places)
    in_w = jnp.transpose(in_weight, (1, 0, 2))
    gu_w = jnp.transpose(
        gate_up_weight.reshape(width, 2, hidden_local // BLOCK, BLOCK), (0, 2, 1, 3)
    )
    gu_w = gu_w.reshape(width, 2 * hidden_local)

    all_seg = lax.all_gather(segment_ids, "ctx", axis=0, tiled=True)
    count = all_seg.shape[0]
    every = jnp.arange(count, dtype=jnp.int32)
    opens = jnp.concatenate([jnp.ones((1,), jnp.bool_), all_seg[1:] != all_seg[:-1]])
    all_begin = lax.cummax(jnp.where(opens, every, 0))
    blocks = all_begin.reshape(count // rows, rows)

    tok_full, gu_w, blocks, all_begin = lax.optimization_barrier(
        (gather(tokens), gu_w, blocks, all_begin)
    )
    key_info = jnp.stack(
        [me, blocks[me, 0] // rows, (blocks[me, rows - 1] + rows - 1) // rows]
    ).astype(jnp.int32)
    query_info = jnp.stack(
        [
            me,
            jnp.sum((blocks[:, 0] < (me + 1) * rows).astype(jnp.int32)) - 1,
            jnp.sum((blocks[:, rows - 1] <= me * rows).astype(jnp.int32)) - 1,
        ]
    ).astype(jnp.int32)
    begin = lax.dynamic_slice_in_dim(blocks, me, 1, 0)
    all_begin = all_begin[None, :]
    if cube:
        inner1, stat1, raw, mixed, lse, kept, cot_full, out_part = attend_far(
            tok_full, in_w, cosine, sine, blocks, cotangent, out_weight, heads, tp_size
        )
        kept = lax.all_gather(kept, "ctx", axis=0, tiled=True)
    else:
        inner1, stat1, query, pairs = project(tok_full, in_w, cosine, sine, heads)
        all_pairs = lax.all_gather(pairs, "ctx", axis=0, tiled=True)
        cot_full = gather(cotangent)
        raw, mixed, lse = attend(key_info, query, all_pairs, begin, heads)
        out_part = jnp.dot(mixed, out_weight, preferred_element_type=F32).astype(BF16)
        late_query, mixed = lax.optimization_barrier((query, mixed))
        kept = lax.all_gather(late_query, "ctx", axis=0, tiled=True)
    inner2, resid1, stat2, grad_hidden = merge(
        out_part, tok_full, cot_full, down_weight, tp_size
    )

    hidden, grad_gu, down_grad, gu_grad = feed(inner2, cot_full, gu_w, grad_hidden, BLOCK)
    down_grad, gu_grad, kept, grad_gu, hidden = lax.optimization_barrier(
        (down_grad, gu_grad, kept, grad_gu, hidden)
    )
    if not cube:
        down_grad = lax.psum(down_grad, "ctx")
    gu_grad = lax.optimization_barrier(lax.psum(gu_grad, "ctx"))

    grad_part = lax.dot_general(grad_gu, gu_w, NT, preferred_element_type=F32).astype(BF16)
    branch_grad, branch, *mids = norm_back(
        grad_part, cot_full, resid1, stat2, hidden, down_weight, tp_size,
        [down_grad] if cube else [],
    )
    grad_mixed, delta = mixed_grad(branch_grad, out_weight, raw, lse, heads)
    if cube:
        dq, dk, dv, layer_out, mid = attend_back_far(
            grad_mixed, kept, blocks, branch, mids[0], heads, tp_size
        )
    else:
        branch = lax.psum_scatter(branch, "tp", scatter_dimension=1, tiled=True)
        layer_out = branch
        all_grad = lax.all_gather(grad_mixed, "ctx", axis=0, tiled=True)
        dq = query_grad(key_info, query, grad_mixed, lse, delta, all_pairs, begin, heads)
        dk, dv = key_grad(query_info, pairs, kept, all_grad, all_begin, heads)

    if cube:
        tokens_grad, *halves = unproject(
            True, [dq, dk, dv, cosine, sine, inner1, mixed, branch_grad, mid],
            tok_full, stat1, in_w, heads, tp_size,
        )
        swap = [(i, i + 1 - 2 * (i % 2)) for i in range(CUBE)]
        core = (me % 2)[None]
        far = [lax.ppermute(half, "ctx", swap) for half in halves]
        *far, gu_grad = lax.optimization_barrier((*far, weave(gu_grad, BLOCK)))
        in_grad, out_grad, down_grad = join(core, halves, far)
    else:
        out_grad = lax.dot_general(
            mixed, branch_grad, TN, preferred_element_type=F32
        ).astype(BF16)
        dproj, in_grad = unrotate(dq, dk, dv, cosine, sine, inner1, heads)
        in_grad, out_grad, down_grad, gu_grad = lax.optimization_barrier(
            (in_grad, out_grad, down_grad, gu_grad)
        )
        in_grad, out_grad = lax.psum((in_grad, out_grad), "ctx")
        (tokens_grad,) = unproject(
            False, [dproj, branch_grad], tok_full, stat1, in_w, heads, tp_size
        )
        in_grad, out_grad, down_grad = widen(in_grad), out_grad.astype(F32), widen(down_grad)
        gu_grad = weave(gu_grad, BLOCK)
    return (
        layer_out,
        tokens_grad,
        jnp.transpose(in_grad.reshape(3, width, span), (1, 0, 2)),
        out_grad,
        gu_grad,
        down_grad,
    )


def solution(mesh):
    placed = (
        P("ctx", "tp"),
        P("ctx"),
        P(None, None, "tp"),
        P("tp", None),
        P(None, None, "tp"),
        P("tp", None),
        P("ctx", "tp"),
    )
    return jax.shard_map(
        per_device,
        mesh=mesh,
        in_specs=placed,
        out_specs=(
            P("ctx", "tp"),
            P("ctx", "tp"),
            P(None, None, "tp"),
            P("tp", None),
            P(None, None, "tp"),
            P("tp", None),
        ),
        check_vma=False,
    )
```

```python
import functools

import jax
import jax.numpy as jnp
from jax import lax
from jax.experimental import pallas as pl
from jax.experimental.pallas import tpu as pltpu
from jax.sharding import PartitionSpec as P

HD = 128
EPS = 1e-05
NEG = -1e30
SCALE = HD ** (-0.5)
LOG2E = 1.4426950408889634
C2 = SCALE * LOG2E
F32 = jnp.float32
BF16 = jnp.bfloat16
NT = (((1,), (1,)), ((), ()))
TN = (((0,), (0,)), ((), ()))
MESH = pl.DeviceIdType.MESH
BLOCK = 512
SUB = 32


def params(mib, **more):
    return pltpu.CompilerParams(vmem_limit_bytes=mib << 20, **more)


def cost(flops, nbytes, trans=0):
    return pl.CostEstimate(flops=int(flops), bytes_accessed=int(nbytes), transcendentals=int(trans))


def rope_tables(places):
    half = HD // 2
    freq = 10000.0 ** (-jnp.arange(half, dtype=F32) * 2.0 / HD)
    angle = places.astype(F32)[:, None] * freq[None, :]
    cosine, sine = jnp.cos(angle), jnp.sin(angle)
    return jnp.concatenate([cosine, cosine], axis=1), jnp.concatenate([-sine, sine], axis=1)


def project_kernel(heads, tok_ref, w_ref, cos_ref, sin_ref, inner_ref, stat_ref, q_ref, kv_ref):
    x = tok_ref[...].astype(F32)
    center = x - jnp.mean(x, axis=1, keepdims=True)
    inverse = lax.rsqrt(jnp.mean(center * center, axis=1, keepdims=True) + EPS)
    inner = (center * inverse).astype(BF16)
    inner_ref[...] = inner
    stat_ref[...] = jnp.concatenate(
        [jnp.mean(x, axis=1, keepdims=True), inverse], axis=1
    )
    cosine, sine = cos_ref[...], sin_ref[...]
    span = heads * HD
    for part in range(3):
        out = jnp.dot(inner, w_ref[part], preferred_element_type=F32)
        if part == 2:
            kv_ref[:, span:] = out.astype(BF16)
            continue
        for h in range(heads):
            piece = out[:, h * HD : (h + 1) * HD]
            turned = (piece * cosine + pltpu.roll(piece, HD // 2, 1) * sine).astype(BF16)
            if part == 0:
                q_ref[:, h * HD : (h + 1) * HD] = turned
            else:
                kv_ref[:, h * HD : (h + 1) * HD] = turned


def project(tok_full, weight, cosine, sine, heads):
    rows, width = tok_full.shape
    span = heads * HD
    block = 256
    row = lambda n: pl.BlockSpec((block, n), lambda i: (i, 0))
    return pl.pallas_call(
        functools.partial(project_kernel, heads),
        grid=(rows // block,),
        in_specs=[
            row(width),
            pl.BlockSpec((3, width, span), lambda i: (0, 0, 0)),
            row(HD),
            row(HD),
        ],
        out_specs=[row(width), row(2), row(span), row(2 * span)],
        out_shape=[
            jax.ShapeDtypeStruct((rows, width), BF16),
            jax.ShapeDtypeStruct((rows, 2), F32),
            jax.ShapeDtypeStruct((rows, span), BF16),
            jax.ShapeDtypeStruct((rows, 2 * span), BF16),
        ],
        compiler_params=params(56),
        cost_estimate=cost(6 * rows * width * span, 6 * width * span + 6 * rows * width),
        name="project",
    )(tok_full, weight, cosine, sine)


def masked(scores, j, me, rows, begin):
    key_place = lax.broadcasted_iota(jnp.int32, scores.shape, 0) + j * rows
    query_place = lax.broadcasted_iota(jnp.int32, scores.shape, 1) + me * rows
    return jnp.where((key_place <= query_place) & (key_place >= begin), scores, NEG)


def attend_kernel(
    heads, info, q_ref, k_ref, v_ref, begin_ref, raw_ref, mixed_ref, lse_ref,
    high_ref, total_ref, acc_ref, s_ref,
):
    me, first, clear = info[0], info[1], info[2]
    j = pl.program_id(0)
    rows = q_ref.shape[0]

    @pl.when(j == 0)
    def _():
        high_ref[...] = jnp.full_like(high_ref, NEG)
        total_ref[...] = jnp.zeros_like(total_ref)
        acc_ref[...] = jnp.zeros_like(acc_ref)

    def block(hide):
        def score(h):
            hs = slice(h * HD, (h + 1) * HD)
            s = lax.dot_general(k_ref[:, hs], q_ref[:, hs], NT, preferred_element_type=F32)
            if hide:
                s = masked(s, j, me, rows, begin_ref[...])
            s_ref[h % 2] = s

        def spread(h):
            hs = slice(h * HD, (h + 1) * HD)
            s = s_ref[h % 2]
            old = high_ref[h : h + 1, :]
            new = jnp.maximum(old, jnp.max(s, axis=0, keepdims=True))
            high_ref[h : h + 1, :] = new
            p = jnp.exp2(s * C2 - new * C2)
            decay = jnp.exp2((old - new) * C2)
            total_ref[h : h + 1, :] = total_ref[h : h + 1, :] * decay + jnp.sum(
                p, axis=0, keepdims=True
            )
            acc_ref[h] = acc_ref[h] * decay + lax.dot_general(
                v_ref[:, hs], p.astype(BF16), TN, preferred_element_type=F32
            )

        score(0)
        for h in range(heads):
            if h + 1 < heads:
                score(h + 1)
            spread(h)

    @pl.when((j >= clear) & (j < me))
    def _():
        block(False)

    @pl.when(((j >= first) & (j < clear) & (j < me)) | (j == me))
    def _():
        block(True)

    @pl.when(j == me)
    def _():
        for h in range(heads):
            hs = slice(h * HD, (h + 1) * HD)
            out = (acc_ref[h] / total_ref[h : h + 1, :]).T
            raw_ref[:, hs] = out
            mixed_ref[:, hs] = out.astype(BF16)
        lse_ref[...] = high_ref[...] * C2 + jnp.log2(total_ref[...])


def attend(info, query, pairs, begin, heads):
    rows = query.shape[0]
    total = pairs.shape[0]
    span = heads * HD
    full = lambda shape: pl.BlockSpec(shape, lambda j, s: (0, 0))
    key = pl.BlockSpec((rows, span), lambda j, s: (jnp.clip(j, s[1], s[0]), 0))
    value = pl.BlockSpec((rows, span), lambda j, s: (jnp.clip(j, s[1], s[0]), 1))
    return pl.pallas_call(
        functools.partial(attend_kernel, heads),
        grid_spec=pltpu.PrefetchScalarGridSpec(
            num_scalar_prefetch=1,
            grid=(total // rows,),
            in_specs=[full((rows, span)), key, value, full((1, rows))],
            out_specs=[full((rows, span)), full((rows, span)), full((heads, rows))],
            scratch_shapes=[
                pltpu.VMEM((heads, rows), F32),
                pltpu.VMEM((heads, rows), F32),
                pltpu.VMEM((heads, HD, rows), F32),
                pltpu.VMEM((2, rows, rows), F32),
            ],
        ),
        out_shape=[
            jax.ShapeDtypeStruct((rows, span), F32),
            jax.ShapeDtypeStruct((rows, span), BF16),
            jax.ShapeDtypeStruct((heads, rows), F32),
        ],
        compiler_params=params(56),
        cost_estimate=cost(4 * rows * total * span, 4 * total * span, rows * total * heads),
        name="attend",
    )(info, query, pairs, pairs, begin)


CUBE = 8
CUBE_SENDS = 10


class Cube:
    def __init__(self, buf, send, recv):
        me = lax.axis_index("ctx")
        flip = (1 - 2 * (me % 2), 2 - 4 * ((me // 2) % 2), 4 - 8 * (me // 4))
        self.me, self.flip, self.buf, self.send, self.recv = me, flip, buf, send, recv
        self.rows = buf.shape[0] // CUBE

    def copy(self, n):
        core, x, y = self.flip
        half = self.rows // 2
        block, part, target = (
            (0, None, core),
            (0, 0, x), (0, 1, x), (0, 1, y), (0, 0, y),
            (x, 0, y), (y, 1, x),
            (x, None, core), (y, None, core), (x + y, None, core),
        )[n]
        start = (self.me + block) * self.rows
        size = self.rows
        if part is not None:
            start, size = start + part * half, half
        place = self.buf.at[pl.ds(pl.multiple_of(start, 16), size)]
        return pltpu.make_async_remote_copy(
            src_ref=place, dst_ref=place, send_sem=self.send.at[n], recv_sem=self.recv.at[n],
            device_id={"ctx": self.me + target}, device_id_type=MESH,
        )

    def arrived(self, n):
        self.copy(n).wait_recv()

    def start(self, *which):
        for n in which:
            self.copy(n).start()

    def signal(self, barrier):
        for target in self.flip:
            pl.semaphore_signal(
                barrier, inc=1, device_id={"ctx": self.me + target}, device_id_type=MESH
            )

    def block(self, step):
        core, x, y = self.flip
        on = lambda *steps: sum((step == n).astype(jnp.int32) for n in steps)
        return self.me + on(1, 4, 5, 7) * core + on(2, 4, 6, 7) * x + on(3, 5, 6, 7) * y

    def advance(self, step):
        @pl.when(step == 1)
        def _():
            self.arrived(0)

        @pl.when(step == 2)
        def _():
            self.arrived(1)
            self.start(5)
            self.arrived(3)
            self.start(6)
            self.arrived(2)
            self.start(7)

        @pl.when(step == 3)
        def _():
            self.arrived(4)
            self.start(8)

        @pl.when(step == 4)
        def _():
            self.arrived(7)

        @pl.when(step == 5)
        def _():
            self.arrived(8)

        @pl.when(step == 6)
        def _():
            self.arrived(5)
            self.arrived(6)
            self.start(9)

        @pl.when(step == 7)
        def _():
            self.arrived(9)

    def finish(self):
        for n in range(CUBE_SENDS):
            self.copy(n).wait_send()


SUM_SENDS = 9


class CubeSum:
    def __init__(self, own, near, land, send, recv, local, out=None, mid=None):
        me = lax.axis_index("ctx")
        core, x, y = me % 2, (me // 2) % 2, me // 4
        self.me, self.own, self.out, self.land, self.mid = me, own, out, land, mid
        self.near, self.send, self.recv, self.local = near, send, recv, local
        rows = own.shape[0]
        self.half, self.eighth, self.last = rows // 2, rows // 8, rows // 16
        second = rows // 4
        self.to = (1 - 2 * core, 2 - 4 * x, 4 - 8 * y)
        self.mine, self.other = core * self.half, (1 - core) * self.half
        self.offset = 0 if local is not None else self.mine
        self.keep1 = (x * self.eighth, second + y * self.eighth)
        self.give1 = ((1 - x) * self.eighth, second + (1 - y) * self.eighth)
        self.keep2 = (self.keep1[0] + y * self.last, self.keep1[1] + x * self.last)
        self.give2 = (self.keep1[0] + (1 - y) * self.last, self.keep1[1] + (1 - x) * self.last)

    def copy(self, n):
        core, x, y = self.to
        half, eighth, last, out, land = self.half, self.eighth, self.last, self.out, self.land
        source, start, size, target = (
            (self.own, self.other, half, core),
            (land, self.give1[0], eighth, x), (land, self.give1[1], eighth, y),
            (land, self.give2[0], last, y), (land, self.give2[1], last, x),
            (out, self.keep2[0], last, y), (out, self.keep2[1], last, x),
            (out, self.keep1[0], eighth, x), (out, self.keep1[1], eighth, y),
        )[n]
        src = source.at[pl.ds(pl.multiple_of(start, 16), size)]
        if n < 5:
            landing = (0, half, half + eighth, half + 2 * eighth, half + 2 * eighth + last)[n]
            dst = land.at[pl.ds(landing, size)]
        else:
            dst = src
        return pltpu.make_async_remote_copy(
            src_ref=src, dst_ref=dst, send_sem=self.send.at[n], recv_sem=self.recv.at[n],
            device_id={"ctx": self.me + target}, device_id_type=MESH,
        )

    def add(self, target, to, source, at, landed, size):
        step = size
        while step * self.own.shape[1] > 256 * 1024 and step % 32 == 0:
            step = step // 2

        def part(i, carry):
            def rows(begin):
                return pl.ds(pl.multiple_of(begin + i * step, 16), step)

            total = source[rows(at), :].astype(F32) + self.land[rows(landed), :].astype(F32)
            target[rows(to), :] = total.astype(BF16)
            return carry

        lax.fori_loop(0, size // step, part, 0)

    def read(self):
        rows = pl.ds(pl.multiple_of(self.mine, 16), self.half)
        return pltpu.make_async_copy(self.own.at[rows], self.near, self.local.at[0])

    def begin(self):
        self.copy(0).start()
        if self.local is not None:
            self.read().start()

    def reduce(self, k):
        half, eighth, last, land = self.half, self.eighth, self.last, self.land
        i = k % 2
        if k == 0:
            if self.local is not None:
                self.read().wait()
            self.copy(0).wait_recv()
        if k < 2:
            at = self.give1[i]
            self.add(land, at, self.near, self.offset + at, at, eighth)
            self.copy(1 + i).start()
        elif k < 4:
            at = self.keep1[i]
            self.add(land, at, self.near, self.offset + at, at, eighth)
        elif k < 6:
            self.copy(1 + i).wait_recv()
            landed = half + i * eighth - self.keep1[i]
            if self.out is None:
                at = self.keep1[i]
                self.add(self.mid, i * eighth, land, at, landed + at, eighth)
                return
            at = self.give2[i]
            self.add(land, at, land, at, landed + at, last)
            self.copy(3 + i).start()
            at = self.keep2[i]
            self.add(land, at, land, at, landed + at, last)
        else:
            self.copy(3 + i).wait_recv()
            at = self.keep2[i]
            self.add(self.out, at, land, at, half + 2 * eighth + i * last, last)

    def gather(self, k):
        for i in range(2):
            if k == 0:
                self.copy(5 + i).start()
            if k == 1:
                self.copy(5 + i).wait_recv()
                self.copy(7 + i).start()
            if k == 2:
                self.copy(7 + i).wait_recv()

    def finish(self):
        for n in range(3 if self.out is None else SUM_SENDS):
            self.copy(n).wait_send()

    def signal(self, barrier):
        for target in self.to:
            pl.semaphore_signal(
                barrier, inc=1, device_id={"ctx": self.me + target}, device_id_type=MESH
            )


class MidSum:
    def __init__(self, mid, land, out, send, recv):
        me = lax.axis_index("ctx")
        x, y = (me // 2) % 2, me // 4
        self.me, self.mid, self.land, self.out, self.send, self.recv = me, mid, land, out, send, recv
        self.eighth, self.last = mid.shape[0] // 2, mid.shape[0] // 4
        self.bit = (y, x)
        self.to = (4 - 8 * y, 2 - 4 * x)

    def copy(self, n):
        i = n % 2
        keep = i * self.eighth + self.bit[i] * self.last
        give = i * self.eighth + (1 - self.bit[i]) * self.last
        if n < 2:
            src = self.mid.at[pl.ds(pl.multiple_of(give, 16), self.last)]
            dst = self.land.at[pl.ds(i * self.last, self.last)]
        else:
            src = dst = self.out.at[pl.ds(pl.multiple_of(keep, 16), self.last)]
        return pltpu.make_async_remote_copy(
            src_ref=src, dst_ref=dst, send_sem=self.send.at[n], recv_sem=self.recv.at[n],
            device_id={"ctx": self.me + self.to[i]}, device_id_type=MESH,
        )

    def begin(self):
        for i in range(2):
            self.copy(i).start()

    def turn(self):
        for i in range(2):
            self.copy(i).wait_recv()
            keep = i * self.eighth + self.bit[i] * self.last
            rows = pl.ds(pl.multiple_of(keep, 16), self.last)
            landed = self.land[i * self.last : (i + 1) * self.last, :]
            self.out[rows, :] = (
                self.mid[rows, :].astype(F32) + landed.astype(F32)
            ).astype(BF16)
            self.copy(2 + i).start()

    def finish(self):
        for i in range(2):
            self.copy(2 + i).wait_recv()
        for n in range(4):
            self.copy(n).wait_send()


class LastGather:
    def __init__(self, mid, out, send, recv, local):
        me = lax.axis_index("ctx")
        x, y = (me // 2) % 2, me // 4
        self.me, self.mid, self.out = me, mid, out
        self.send, self.recv, self.local = send, recv, local
        self.eighth = mid.shape[0] // 2
        self.start_at = (x * self.eighth, (2 + y) * self.eighth)
        self.to = (2 - 4 * x, 4 - 8 * y)

    def ends(self, i):
        src = self.mid.at[pl.ds(i * self.eighth, self.eighth)]
        return src, self.out.at[pl.ds(pl.multiple_of(self.start_at[i], 16), self.eighth)]

    def copy(self, i):
        src, dst = self.ends(i)
        return pltpu.make_async_remote_copy(
            src_ref=src, dst_ref=dst, send_sem=self.send.at[i], recv_sem=self.recv.at[i],
            device_id={"ctx": self.me + self.to[i]}, device_id_type=MESH,
        )

    def keep(self, i):
        src, dst = self.ends(i)
        return pltpu.make_async_copy(src, dst, self.local.at[i])

    def begin(self):
        for i in range(2):
            self.copy(i).start()
            self.keep(i).start()

    def finish(self):
        for i in range(2):
            self.copy(i).wait()
            self.keep(i).wait()


def sum_scratch(shape):
    return [
        pltpu.VMEM((shape[0] // 2, shape[1]), BF16),
        pltpu.VMEM((shape[0] // 2 + 3 * (shape[0] // 8), shape[1]), BF16),
        pltpu.SemaphoreType.DMA((SUM_SENDS,)),
        pltpu.SemaphoreType.DMA((SUM_SENDS,)),
        pltpu.SemaphoreType.DMA((1,)),
    ]


def join_kernel(count, core_ref, *refs):
    for own_ref, far_ref, out_ref in zip(refs[:count], refs[count : 2 * count], refs[2 * count :]):
        @pl.when(pl.program_id(0) == 0)
        def _():
            out_ref[...] = own_ref[...].astype(F32)

        @pl.when(pl.program_id(0) == 1)
        def _():
            out_ref[...] = far_ref[...].astype(F32)


def join(core, own, far):
    steps = 4
    block = lambda half, at: pl.BlockSpec((half.shape[0] // steps, half.shape[1]), at)
    first = lambda h, b, s: (jnp.where(h == 0, b, steps - 1), 0)
    second = lambda h, b, s: (jnp.where(h == 0, 0, b), 0)
    target = lambda h, b, s: (jnp.where(h == 0, s[0], 1 - s[0]) * steps + b, 0)
    size = sum(half.shape[0] * half.shape[1] for half in own)
    return pl.pallas_call(
        functools.partial(join_kernel, len(own)),
        grid_spec=pltpu.PrefetchScalarGridSpec(
            num_scalar_prefetch=1,
            grid=(2, steps),
            in_specs=[block(half, first) for half in own] + [block(half, second) for half in own],
            out_specs=[block(half, target) for half in own],
        ),
        out_shape=[
            jax.ShapeDtypeStruct((2 * half.shape[0], half.shape[1]), F32) for half in own
        ],
        compiler_params=params(56),
        cost_estimate=cost(2 * size, 12 * size),
        name="join",
    )(core, *own, *far)


def hidden_scores(scores, key_block, query_block, rows, begin):
    key_place = lax.broadcasted_iota(jnp.int32, scores.shape, 0) + key_block * rows
    query_place = lax.broadcasted_iota(jnp.int32, scores.shape, 1) + query_block * rows
    return jnp.where((key_place <= query_place) & (key_place >= begin), scores, NEG)


FAR_STEPS = 8
FAR_SENDS = 17


def attend_far_kernel(
    heads, n, tok_ref, in_ref, cos_ref, sin_ref, begin_ref, cot_ref, w_ref,
    inner_ref, stat_ref, raw_ref, mixed_ref, lse_ref, keep_ref, full_ref, part_ref,
    pair_ref, q_ref, high_ref, total_ref, acc_ref, s_ref,
    guest_ref, guest_high, guest_total, guest_acc, guest_out, guest_stat, back_out, back_stat,
    send, recv, zsend, zrecv,
):
    rows = q_ref.shape[0]
    half = rows // 2
    span = heads * HD
    shard = cot_ref.shape[1]
    at = lax.axis_index("tp")
    me = lax.axis_index("ctx")
    core, x, y = me % 2, (me // 2) % 2, me // 4
    to_core, to_x, to_y = 1 - 2 * core, 2 - 4 * x, 4 - 8 * y
    diagonal = me + to_x + to_y
    barrier = pltpu.get_barrier_semaphore()
    for target in (me + to_core, me + to_x, me + to_y, diagonal):
        pl.semaphore_signal(barrier, inc=1, device_id={"ctx": target}, device_id_type=MESH)

    @pl.when(at > 0)
    def _():
        pl.semaphore_signal(barrier, inc=1, device_id={"tp": at - 1}, device_id_type=MESH)

    @pl.when(at < n - 1)
    def _():
        pl.semaphore_signal(barrier, inc=1, device_id={"tp": at + 1}, device_id_type=MESH)

    def block_rows(block):
        return pl.ds(pl.multiple_of(block * rows, 16), rows)

    def copy(k):
        if k < 14:
            block, part, parts, target = (
                (me, 0, 1, to_core),
                (me, 0, 2, to_x), (me, 1, 2, to_x),
                (me, 0, 4, to_y), (me, 1, 4, to_y), (me, 2, 4, to_y), (me, 3, 4, to_y),
                (me + to_x, 0, 1, to_core), (me + to_y, 0, 1, to_core),
                (me + to_y, 0, 4, to_x), (me + to_y, 1, 4, to_x),
                (me + to_y, 2, 4, to_x), (me + to_y, 3, 4, to_x),
                (diagonal, 0, 1, to_core),
            )[k]
            size = rows // parts
            src = dst = pair_ref.at[pl.ds(pl.multiple_of(block * rows + part * size, 16), size)]
        else:
            src, dst = (
                (q_ref, guest_ref), (guest_out, back_out), (guest_stat, back_stat)
            )[k - 14]
            target = to_x + to_y
        return pltpu.make_async_remote_copy(
            src_ref=src, dst_ref=dst, send_sem=send.at[k], recv_sem=recv.at[k],
            device_id={"ctx": me + target}, device_id_type=MESH,
        )

    def on_chip(*which):
        return sum((me // 2 == chip).astype(jnp.int32) for chip in which) > 0

    def project(rows_at, part):
        out = jnp.dot(inner_ref[rows_at, :], in_ref[part], preferred_element_type=F32)
        if part == 2:
            return out.astype(BF16)
        cosine, sine = cos_ref[rows_at, :], sin_ref[rows_at, :]
        pieces = []
        for h in range(heads):
            piece = out[:, h * HD : (h + 1) * HD]
            pieces.append((piece * cosine + pltpu.roll(piece, HD // 2, 1) * sine).astype(BF16))
        return jnp.concatenate(pieces, axis=1)

    def own_pairs(part):
        here = slice(part * half, (part + 1) * half)
        value = tok_ref[here, :].astype(F32)
        mean = jnp.mean(value, axis=1, keepdims=True)
        center = value - mean
        inverse = lax.rsqrt(jnp.mean(center * center, axis=1, keepdims=True) + EPS)
        stat_ref[here, :] = jnp.concatenate([mean, inverse], axis=1)
        inner_ref[here, :] = (center * inverse).astype(BF16)
        place = pl.ds(pl.multiple_of(me * rows + part * half, 16), half)
        pair_ref[place, :span] = project(here, 1)
        pair_ref[place, span:] = project(here, 2)

    own_pairs(0)
    full_ref[:, pl.ds(pl.multiple_of(at * shard, 128), shard)] = cot_ref[...]
    pl.semaphore_wait(barrier, jnp.where((at > 0) & (at < n - 1), 6, 5))

    @pl.when(y == 0)
    def _():
        copy(3).start()
        copy(4).start()

    @pl.when(x == 0)
    def _():
        copy(1).start()

    own_pairs(1)

    @pl.when(y == 0)
    def _():
        copy(5).start()
        copy(6).start()

    @pl.when(x == 0)
    def _():
        copy(2).start()

    copy(0).start()
    q_ref[...] = project(slice(0, rows), 0)

    @pl.when(on_chip(3))
    def _():
        copy(14).start()

    keep_ref[:, : 2 * span] = pair_ref[block_rows(me), :]
    keep_ref[:, 2 * span :] = q_ref[...]

    def pass_on(right, s, k):
        place = full_ref.at[:, pl.ds(pl.multiple_of(s * shard, 128), shard)]
        which = (1 if right else 0, k)
        return pltpu.make_async_remote_copy(
            src_ref=place, dst_ref=place, send_sem=zsend.at[which], recv_sem=zrecv.at[which],
            device_id={"tp": at + 1 if right else at - 1}, device_id_type=MESH,
        )

    def line_step(k):
        @pl.when(at >= k)
        def _():
            if k > 0:
                pass_on(True, at - k, k - 1).wait_recv()

            @pl.when(at < n - 1)
            def _():
                pass_on(True, at - k, k).start()

        @pl.when(at + k < n)
        def _():
            if k > 0:
                pass_on(False, at + k, k - 1).wait_recv()

            @pl.when(at > 0)
            def _():
                pass_on(False, at + k, k).start()

    def clear(high, total, acc):
        high[...] = jnp.full_like(high, NEG)
        total[...] = jnp.zeros_like(total)
        acc[...] = jnp.zeros_like(acc)

    def attend_block(key_block, queries, query_block, high, total, acc):
        place = block_rows(key_block)
        begin = begin_ref[pl.ds(query_block, 1), :]

        def score(h):
            hs = slice(h * HD, (h + 1) * HD)
            s = lax.dot_general(
                pair_ref[place, hs], queries[:, hs], NT, preferred_element_type=F32
            )
            s_ref[h % 2] = hidden_scores(s, key_block, query_block, rows, begin)

        def spread(h):
            s = s_ref[h % 2]
            old = high[h : h + 1, :]
            new = jnp.maximum(old, jnp.max(s, axis=0, keepdims=True))
            high[h : h + 1, :] = new
            p = jnp.exp2(s * C2 - new * C2)
            decay = jnp.exp2((old - new) * C2)
            total[h : h + 1, :] = total[h : h + 1, :] * decay + jnp.sum(p, axis=0, keepdims=True)
            acc[h] = acc[h] * decay + lax.dot_general(
                pair_ref[place, span + h * HD : span + (h + 1) * HD], p.astype(BF16), TN,
                preferred_element_type=F32,
            )

        score(0)
        for h in range(heads):
            if h + 1 < heads:
                score(h + 1)
            spread(h)

    def guest():
        clear(guest_high, guest_total, guest_acc)
        copy(14).wait_recv()

        def turn(k, carry):
            attend_block(
                me + k * to_core, guest_ref, diagonal, guest_high, guest_total, guest_acc
            )
            return carry

        lax.fori_loop(0, 2, turn, 0)
        for h in range(heads):
            guest_out[h * HD : (h + 1) * HD, :] = (
                guest_acc[h] / guest_total[h : h + 1, :]
            ).astype(BF16)
        guest_stat[:heads, :] = guest_high[...]
        guest_stat[heads:, :] = guest_total[...]
        copy(15).start()
        copy(16).start()

    clear(high_ref, total_ref, acc_ref)

    def turn(step, carry):
        for k in range(n):
            @pl.when(step == (min(k * 2, FAR_STEPS - n + k) if n <= FAR_STEPS else k))
            def _():
                line_step(k)

        @pl.when(step == 1)
        def _():
            copy(0).wait_recv()

        @pl.when((step == 2) & on_chip(0))
        def _():
            guest()

        @pl.when((step == 2) & on_chip(3))
        def _():
            for k in range(4):
                copy(3 + k).wait_recv()
                copy(9 + k).start()

        @pl.when((step == 2) & (x == 1))
        def _():
            copy(1).wait_recv()
            copy(2).wait_recv()
            copy(7).start()

        @pl.when((step == 3) & on_chip(2))
        def _():
            for k in range(4):
                copy(3 + k).wait_recv()

        @pl.when((step == 3) & (y == 1))
        def _():
            copy(8).start()

        @pl.when((step == 4) & (x == 1))
        def _():
            copy(7).wait_recv()

        @pl.when((step == 5) & (y == 1))
        def _():
            copy(8).wait_recv()

        @pl.when((step == 6) & on_chip(2))
        def _():
            for k in range(4):
                copy(9 + k).wait_recv()
            copy(13).start()

        @pl.when((step == 7) & on_chip(2))
        def _():
            copy(13).wait_recv()

        on = lambda *steps: sum((step == k).astype(jnp.int32) for k in steps)
        block = (
            me + on(1, 4, 5, 7) * to_core + on(2, 4, 6, 7) * to_x + on(3, 5, 6, 7) * to_y
        )
        here = on(0, 1) + on(2, 4) * x + on(3, 5) * y + on(6, 7) * y * (1 - x)

        @pl.when((block <= me) & (here > 0))
        def _():
            attend_block(block, q_ref, me, high_ref, total_ref, acc_ref)

        return carry

    lax.fori_loop(0, FAR_STEPS, turn, 0)

    @pl.when(on_chip(3))
    def _():
        copy(15).wait_recv()
        copy(16).wait_recv()
        for h in range(heads):
            old, other = high_ref[h : h + 1, :], back_stat[h : h + 1, :]
            new = jnp.maximum(old, other)
            high_ref[h : h + 1, :] = new
            decay = jnp.exp2((old - new) * C2)
            weight = jnp.exp2((other - new) * C2) * back_stat[heads + h : heads + h + 1, :]
            total_ref[h : h + 1, :] = total_ref[h : h + 1, :] * decay + weight
            acc_ref[h] = acc_ref[h] * decay + weight * back_out[
                h * HD : (h + 1) * HD, :
            ].astype(F32)

    for h in range(heads):
        hs = slice(h * HD, (h + 1) * HD)
        out = (acc_ref[h] / total_ref[h : h + 1, :]).T
        raw_ref[:, hs] = out
        mixed_ref[:, hs] = out.astype(BF16)
    part_ref[...] = jnp.dot(
        mixed_ref[...], w_ref[...], preferred_element_type=F32
    ).astype(BF16)
    lse_ref[...] = high_ref[...] * C2 + jnp.log2(total_ref[...])
    for senders, which in (
        (me >= 0, (0,)), (x == 0, (1, 2)), (y == 0, (3, 4, 5, 6)), (x == 1, (7,)), (y == 1, (8,)),
        (on_chip(3), (9, 10, 11, 12, 14)), (on_chip(2), (13,)), (on_chip(0), (15, 16)),
    ):
        @pl.when(senders)
        def _():
            for k in which:
                copy(k).wait_send()

    for k in range(n):
        @pl.when((at >= k) & (at < n - 1))
        def _():
            pass_on(True, at - k, k).wait_send()

        @pl.when((at + k < n) & (at > 0))
        def _():
            pass_on(False, at + k, k).wait_send()


def attend_far(tok_full, in_weight, cosine, sine, begin, cot, weight, heads, n):
    rows, width = tok_full.shape
    span = heads * HD
    vmem = pl.BlockSpec(memory_space=pltpu.VMEM)
    state = [
        pltpu.VMEM((heads, rows), F32),
        pltpu.VMEM((heads, rows), F32),
        pltpu.VMEM((heads, HD, rows), F32),
    ]
    answer = [pltpu.VMEM((span, rows), BF16), pltpu.VMEM((2 * heads, rows), F32)]
    return pl.pallas_call(
        functools.partial(attend_far_kernel, heads, n),
        in_specs=[vmem] * 7,
        out_specs=[vmem] * 8,
        out_shape=[
            jax.ShapeDtypeStruct((rows, width), BF16),
            jax.ShapeDtypeStruct((rows, 2), F32),
            jax.ShapeDtypeStruct((rows, span), F32),
            jax.ShapeDtypeStruct((rows, span), BF16),
            jax.ShapeDtypeStruct((heads, rows), F32),
            jax.ShapeDtypeStruct((rows, 3 * span), BF16),
            jax.ShapeDtypeStruct((rows, n * cot.shape[1]), BF16),
            jax.ShapeDtypeStruct((rows, width), BF16),
        ],
        scratch_shapes=[
            pltpu.VMEM((CUBE * rows, 2 * span), BF16),
            pltpu.VMEM((rows, span), BF16),
            *state,
            pltpu.VMEM((2, rows, rows), F32),
            pltpu.VMEM((rows, span), BF16),
            *state,
            *answer,
            *answer,
            pltpu.SemaphoreType.DMA((FAR_SENDS,)),
            pltpu.SemaphoreType.DMA((FAR_SENDS,)),
            pltpu.SemaphoreType.DMA((2, n)),
            pltpu.SemaphoreType.DMA((2, n)),
        ],
        compiler_params=params(60, collective_id=2, has_side_effects=True),
        cost_estimate=cost(1e6, 1e6),
        name="attend_far",
    )(tok_full, in_weight, cosine, sine, begin, cot, weight)


def attend_back_far_kernel(
    heads, n, g_ref, kept_ref, begin_ref, part_ref, mid_ref,
    dq_ref, dk_ref, dv_ref, layer_ref, next_ref,
    all_ref, acc_ref, rows_ref, s_ref, p_ref, land_ref, pair_ref, q_ref,
    send, recv, zsend, zrecv, read_sem, mid_land, msend, mrecv,
):
    rows = g_ref.shape[0]
    span = heads * HD
    shard = layer_ref.shape[1]
    at = lax.axis_index("tp")
    cube = Cube(all_ref, send, recv)
    middle = MidSum(mid_ref, mid_land, next_ref, msend, mrecv)
    me = cube.me
    barrier = pltpu.get_barrier_semaphore()
    cube.signal(barrier)
    for o in range(1, n):
        pl.semaphore_signal(
            barrier, inc=1, device_id={"tp": lax.rem(at + o, n)}, device_id_type=MESH
        )

    def read(step, keys):
        place = pl.ds(pl.multiple_of(cube.block(step) * rows, 16), rows)
        near, columns = (pair_ref, (0, 2 * span)) if keys else (q_ref, (2 * span, span))
        return pltpu.make_async_copy(
            kept_ref.at[place, pl.ds(*columns)], near.at[place],
            read_sem.at[0 if keys else 1, step],
        )

    def read_all(step, carry):
        block = cube.block(step)

        @pl.when(block <= me)
        def _():
            read(step, True).start()

        @pl.when(block >= me)
        def _():
            read(step, False).start()

        return carry

    lax.fori_loop(0, CUBE, read_all, 0)
    all_ref[pl.ds(pl.multiple_of(me * rows, 16), rows), :] = g_ref[...]
    acc_ref[...] = jnp.zeros_like(acc_ref)
    dk_ref[...] = jnp.zeros_like(dk_ref)
    dv_ref[...] = jnp.zeros_like(dv_ref)
    pl.semaphore_wait(barrier, 3 + n - 1)

    def term(o):
        target = lax.rem(at + o, n)
        return pltpu.make_async_remote_copy(
            src_ref=part_ref.at[:, pl.ds(pl.multiple_of(target * shard, 128), shard)],
            dst_ref=land_ref.at[o - 1],
            send_sem=zsend.at[o - 1], recv_sem=zrecv.at[o - 1],
            device_id={"tp": target}, device_id_type=MESH,
        )

    own = pl.ds(pl.multiple_of(me * rows, 16), rows)

    cube.start(0, 1, 3, 2, 4)

    def turn(step, carry):
        cube.advance(step)

        @pl.when(step == 0)
        def _():
            for o in range(1, n):
                term(o).start()
            middle.begin()

        @pl.when(step == 3)
        def _():
            middle.turn()

        block = cube.block(step)
        place = pl.ds(pl.multiple_of(block * rows, 16), rows)

        @pl.when(block <= me)
        def _():
            read(step, True).wait()

        @pl.when(block >= me)
        def _():
            read(step, False).wait()

        def scores(h, key_block, key_place, query_block, query_place):
            hs = slice(h * HD, (h + 1) * HD)
            vs = slice(span + h * HD, span + (h + 1) * HD)
            s = lax.dot_general(
                pair_ref[key_place, hs], q_ref[query_place, hs], NT, preferred_element_type=F32
            )
            begin = begin_ref[pl.ds(query_block, 1), :]
            s_ref[h % 2] = hidden_scores(s, key_block, query_block, rows, begin)
            p_ref[h % 2] = lax.dot_general(
                pair_ref[key_place, vs], all_ref[query_place, hs], NT, preferred_element_type=F32
            )

        def read_rows(query_place):
            coded = all_ref[query_place, span:].astype(F32).T
            for k in range(2 * heads):
                rows_ref[k : k + 1, :] = (
                    coded[3 * k : 3 * k + 1]
                    + coded[3 * k + 1 : 3 * k + 2]
                    + coded[3 * k + 2 : 3 * k + 3]
                )

        def weights(h):
            p = jnp.exp2(s_ref[h % 2] * C2 - rows_ref[h : h + 1, :])
            ds = p * (p_ref[h % 2] - rows_ref[heads + h : heads + h + 1, :])
            return p.astype(BF16), ds.astype(BF16)

        @pl.when(block <= me)
        def _():
            read_rows(own)
            scores(0, block, place, me, own)
            for h in range(heads):
                if h + 1 < heads:
                    scores(h + 1, block, place, me, own)
                _, ds = weights(h)
                acc_ref[h] = acc_ref[h] + lax.dot_general(
                    pair_ref[place, h * HD : (h + 1) * HD], ds, TN, preferred_element_type=F32
                )

        @pl.when(block >= me)
        def _():
            read_rows(place)
            scores(0, me, own, block, place)
            for h in range(heads):
                hs = slice(h * HD, (h + 1) * HD)
                if h + 1 < heads:
                    scores(h + 1, me, own, block, place)
                p, ds = weights(h)
                dv_ref[:, hs] += jnp.dot(p, all_ref[place, hs], preferred_element_type=F32)
                dk_ref[:, hs] += jnp.dot(ds, q_ref[place, hs], preferred_element_type=F32)

        return carry

    lax.fori_loop(0, CUBE, turn, 0)
    for h in range(heads):
        dq_ref[:, h * HD : (h + 1) * HD] = (acc_ref[h] * SCALE).T
    dk_ref[...] = dk_ref[...] * SCALE
    total = part_ref[:, pl.ds(pl.multiple_of(at * shard, 128), shard)].astype(F32)
    for o in range(1, n):
        term(o).wait_recv()
        total = total + land_ref[o - 1].astype(F32)
    layer_ref[...] = total.astype(BF16)
    middle.finish()
    cube.finish()
    for o in range(1, n):
        term(o).wait_send()


def attend_back_far(grad, kept, all_begin, part, mid, heads, n):
    rows = grad.shape[0]
    span = heads * HD
    shard = part.shape[1] // n
    vmem = pl.BlockSpec(memory_space=pltpu.VMEM)
    wide = jax.ShapeDtypeStruct((rows, span), F32)
    return pl.pallas_call(
        functools.partial(attend_back_far_kernel, heads, n),
        in_specs=[vmem, pl.BlockSpec(memory_space=pl.ANY)] + [vmem] * 3,
        out_specs=[vmem] * 5,
        out_shape=[wide, wide, wide, jax.ShapeDtypeStruct((rows, shard), BF16)]
        + [jax.ShapeDtypeStruct(mid.shape, BF16)],
        scratch_shapes=[
            pltpu.VMEM((CUBE * rows, span + HD), BF16),
            pltpu.VMEM((heads, HD, rows), F32),
            pltpu.VMEM((2 * heads, rows), F32),
            pltpu.VMEM((2, rows, rows), F32),
            pltpu.VMEM((2, rows, rows), F32),
            pltpu.VMEM((n - 1, rows, shard), BF16),
            pltpu.VMEM((CUBE * rows, 2 * span), BF16),
            pltpu.VMEM((CUBE * rows, span), BF16),
            pltpu.SemaphoreType.DMA((CUBE_SENDS,)),
            pltpu.SemaphoreType.DMA((CUBE_SENDS,)),
            pltpu.SemaphoreType.DMA((n - 1,)),
            pltpu.SemaphoreType.DMA((n - 1,)),
            pltpu.SemaphoreType.DMA((2, CUBE)),
            pltpu.VMEM((mid.shape[0] // 2, mid.shape[1]), BF16),
            pltpu.SemaphoreType.DMA((4,)),
            pltpu.SemaphoreType.DMA((4,)),
        ],
        compiler_params=params(62, collective_id=3, has_side_effects=True),
        cost_estimate=cost(1e6, 1e6),
        name="attend_back_far",
    )(grad, kept, all_begin, part, mid)


def query_grad_kernel(
    heads, info, q_ref, do_ref, lse_ref, delta_ref, k_ref, v_ref, begin_ref,
    dq_ref, acc_ref, s_ref, g_ref,
):
    me, first, clear = info[0], info[1], info[2]
    j = pl.program_id(0)
    rows = q_ref.shape[0]

    @pl.when(j == 0)
    def _():
        acc_ref[...] = jnp.zeros_like(acc_ref)

    def block(hide):
        def score(h):
            hs = slice(h * HD, (h + 1) * HD)
            s = lax.dot_general(k_ref[:, hs], q_ref[:, hs], NT, preferred_element_type=F32)
            if hide:
                s = masked(s, j, me, rows, begin_ref[...])
            s_ref[h % 2] = s
            g_ref[h % 2] = lax.dot_general(
                v_ref[:, hs], do_ref[:, hs], NT, preferred_element_type=F32
            )

        def spread(h):
            hs = slice(h * HD, (h + 1) * HD)
            p = jnp.exp2(s_ref[h % 2] * C2 - lse_ref[h : h + 1, :])
            ds = (p * (g_ref[h % 2] - delta_ref[h : h + 1, :])).astype(BF16)
            acc_ref[h] = acc_ref[h] + lax.dot_general(
                k_ref[:, hs], ds, TN, preferred_element_type=F32
            )

        score(0)
        for h in range(heads):
            if h + 1 < heads:
                score(h + 1)
            spread(h)

    @pl.when((j >= clear) & (j < me))
    def _():
        block(False)

    @pl.when(((j >= first) & (j < clear) & (j < me)) | (j == me))
    def _():
        block(True)

    @pl.when(j == me)
    def _():
        for h in range(heads):
            dq_ref[:, h * HD : (h + 1) * HD] = (acc_ref[h] * SCALE).T


def query_grad(info, query, grad_mixed, lse, delta, pairs, begin, heads):
    rows = query.shape[0]
    total = pairs.shape[0]
    span = heads * HD
    full = lambda shape: pl.BlockSpec(shape, lambda j, s: (0, 0))
    key = pl.BlockSpec((rows, span), lambda j, s: (jnp.clip(j, s[1], s[0]), 0))
    value = pl.BlockSpec((rows, span), lambda j, s: (jnp.clip(j, s[1], s[0]), 1))
    wide = full((rows, span))
    thin = full((heads, rows))
    return pl.pallas_call(
        functools.partial(query_grad_kernel, heads),
        grid_spec=pltpu.PrefetchScalarGridSpec(
            num_scalar_prefetch=1,
            grid=(total // rows,),
            in_specs=[wide, wide, thin, thin, key, value, full((1, rows))],
            out_specs=wide,
            scratch_shapes=[
                pltpu.VMEM((heads, HD, rows), F32),
                pltpu.VMEM((2, rows, rows), F32),
                pltpu.VMEM((2, rows, rows), F32),
            ],
        ),
        out_shape=jax.ShapeDtypeStruct((rows, span), F32),
        compiler_params=params(58),
        cost_estimate=cost(6 * rows * total * span, 4 * total * span, rows * total * heads),
        name="query_grad",
    )(info, query, grad_mixed, lse, delta, pairs, pairs, begin)


def key_grad_kernel(
    heads, info, k_ref, v_ref, q_ref, g_ref, begin_ref, dk_ref, dv_ref,
    rows_ref, s_ref, p_ref,
):
    me, last, clear = info[0], info[1], info[2]
    j = pl.program_id(0)
    rows = k_ref.shape[0]
    span = heads * HD

    @pl.when(j == me)
    def _():
        dk_ref[...] = jnp.zeros_like(dk_ref)
        dv_ref[...] = jnp.zeros_like(dv_ref)

    def block(hide):
        coded = g_ref[:, span:].astype(F32).T
        for n in range(2 * heads):
            rows_ref[n : n + 1, :] = (
                coded[3 * n : 3 * n + 1] + coded[3 * n + 1 : 3 * n + 2] + coded[3 * n + 2 : 3 * n + 3]
            )

        def score(h):
            hs = slice(h * HD, (h + 1) * HD)
            s = lax.dot_general(k_ref[:, hs], q_ref[:, hs], NT, preferred_element_type=F32)
            if hide:
                key_place = lax.broadcasted_iota(jnp.int32, s.shape, 0) + me * rows
                query_place = lax.broadcasted_iota(jnp.int32, s.shape, 1) + j * rows
                s = jnp.where(
                    (key_place <= query_place) & (key_place >= begin_ref[...]), s, NEG
                )
            s_ref[h % 2] = s
            p_ref[h % 2] = lax.dot_general(
                v_ref[:, hs], g_ref[:, hs], NT, preferred_element_type=F32
            )

        def spread(h):
            hs = slice(h * HD, (h + 1) * HD)
            p = jnp.exp2(s_ref[h % 2] * C2 - rows_ref[h : h + 1, :])
            ds = (p * (p_ref[h % 2] - rows_ref[heads + h : heads + h + 1, :])).astype(BF16)
            dv_ref[:, hs] += jnp.dot(p.astype(BF16), g_ref[:, hs], preferred_element_type=F32)
            dk_ref[:, hs] += jnp.dot(ds, q_ref[:, hs], preferred_element_type=F32)

        score(0)
        for h in range(heads):
            if h + 1 < heads:
                score(h + 1)
            spread(h)

    @pl.when((j > me) & (j <= clear))
    def _():
        block(False)

    @pl.when((j == me) | ((j > me) & (j > clear) & (j <= last)))
    def _():
        block(True)

    @pl.when(j == pl.num_programs(0) - 1)
    def _():
        dk_ref[...] = dk_ref[...] * SCALE


def key_grad(info, pairs, all_query, all_grad, all_begin, heads):
    rows = pairs.shape[0]
    total = all_query.shape[0]
    span = heads * HD
    full = lambda shape, at=0: pl.BlockSpec(shape, lambda j, s: (0, at))
    near = lambda j, s: (jnp.clip(j, s[0], s[1]), 0)
    wide = full((rows, span))
    return pl.pallas_call(
        functools.partial(key_grad_kernel, heads),
        grid_spec=pltpu.PrefetchScalarGridSpec(
            num_scalar_prefetch=1,
            grid=(total // rows,),
            in_specs=[
                wide, full((rows, span), 1),
                pl.BlockSpec((rows, span), near),
                pl.BlockSpec((rows, span + HD), near),
                pl.BlockSpec((1, rows), lambda j, s: (0, jnp.clip(j, s[0], s[1]))),
            ],
            out_specs=[wide, wide],
            scratch_shapes=[
                pltpu.VMEM((2 * heads, rows), F32),
                pltpu.VMEM((2, rows, rows), F32),
                pltpu.VMEM((2, rows, rows), F32),
            ],
        ),
        out_shape=[jax.ShapeDtypeStruct((rows, span), F32)] * 2,
        compiler_params=params(58),
        cost_estimate=cost(8 * rows * total * span, 4 * total * span, rows * total * heads),
        name="key_grad",
    )(info, pairs, pairs, all_query, all_grad, all_begin)


def mixed_grad_kernel(heads, branch_ref, w_ref, raw_ref, lse_ref, out_ref, delta_ref):
    span = heads * HD
    low = lax.dot_general(
        branch_ref[...], w_ref[...], NT, preferred_element_type=F32
    ).astype(BF16)
    out_ref[:, :span] = low
    count = low.shape[0]
    both = low.astype(F32) * raw_ref[...]
    for h in range(heads):
        delta_ref[h : h + 1, :] = jnp.sum(both[:, h * HD : (h + 1) * HD].T, axis=0, keepdims=True)
    lines = []
    for n in range(2 * heads):
        value = lse_ref[n : n + 1, :] if n < heads else delta_ref[n - heads : n - heads + 1, :]
        for _ in range(3):
            piece = value.astype(BF16).astype(F32)
            lines.append(piece)
            value = value - piece
    lines.append(jnp.zeros((HD - len(lines), count), F32))
    out_ref[:, span:] = jnp.concatenate(lines, axis=0).T.astype(BF16)


def mixed_grad(branch, weight, raw, lse, heads):
    rows, width = branch.shape
    span = heads * HD
    block = 256
    row = lambda n: pl.BlockSpec((block, n), lambda i: (i, 0))
    line = pl.BlockSpec((heads, block), lambda i: (0, i))
    return pl.pallas_call(
        functools.partial(mixed_grad_kernel, heads),
        grid=(rows // block,),
        in_specs=[row(width), pl.BlockSpec((span, width), lambda i: (0, 0)), row(span), line],
        out_specs=[row(span + HD), line],
        out_shape=[
            jax.ShapeDtypeStruct((rows, span + HD), BF16),
            jax.ShapeDtypeStruct((heads, rows), F32),
        ],
        compiler_params=params(56),
        cost_estimate=cost(2 * rows * width * span, 2 * width * span + 4 * rows * width),
        name="mixed_grad",
    )(branch, weight, raw, lse)


def feed_kernel(
    inner_ref, cot_ref, w_ref, grad_ref, hidden_ref, dgu_ref, down_grad_ref, gu_grad_ref
):
    block = grad_ref.shape[1]
    both = jnp.dot(inner_ref[...], w_ref[...], preferred_element_type=F32)
    grad = grad_ref[...].astype(F32)
    gate, up = both[:, :block], both[:, block:]
    sigma = 1.0 / (1.0 + jnp.exp(-gate))
    active = gate * sigma
    hidden_ref[...] = (active * up).astype(BF16)
    dgu_ref[:, :block] = (grad * up * sigma * (1.0 + gate * (1.0 - sigma))).astype(BF16)
    dgu_ref[:, block:] = (grad * active).astype(BF16)
    down_grad_ref[...] = lax.dot_general(
        hidden_ref[...], cot_ref[...], TN, preferred_element_type=F32
    ).astype(BF16)
    gu_grad_ref[...] = lax.dot_general(
        inner_ref[...], dgu_ref[...], TN, preferred_element_type=F32
    ).astype(BF16)


def feed(inner, cot, weight, grad, block):
    rows, width = inner.shape
    units = grad.shape[1]
    whole = pl.BlockSpec((rows, width), lambda j: (0, 0))
    column = lambda high, wide: pl.BlockSpec((high, wide), lambda j: (0, j))
    line = pl.BlockSpec((block, width), lambda j: (j, 0))
    return pl.pallas_call(
        feed_kernel,
        grid=(units // block,),
        in_specs=[whole, whole, column(width, 2 * block), column(rows, block)],
        out_specs=[column(rows, block), column(rows, 2 * block), line, column(width, 2 * block)],
        out_shape=[
            jax.ShapeDtypeStruct((rows, units), BF16),
            jax.ShapeDtypeStruct((rows, 2 * units), BF16),
            jax.ShapeDtypeStruct((units, width), BF16),
            jax.ShapeDtypeStruct((width, 2 * units), BF16),
        ],
        compiler_params=params(60),
        cost_estimate=cost(
            12 * rows * width * units, 12 * width * units + 4 * rows * width, rows * units
        ),
        name="feed",
    )(inner, cot, weight, grad)


def weave_kernel(block, sum_ref, out_ref):
    for j in range(sum_ref.shape[1] // (2 * block)):
        for k in range(2):
            at = (2 * j + k) * block
            out_ref[:, k, j * block : (j + 1) * block] = sum_ref[:, at : at + block].astype(F32)


def weave(summed, block):
    width, both = summed.shape
    rows = 256
    return pl.pallas_call(
        functools.partial(weave_kernel, block),
        grid=(width // rows,),
        in_specs=[pl.BlockSpec((rows, both), lambda i: (i, 0))],
        out_specs=pl.BlockSpec((rows, 2, both // 2), lambda i: (i, 0, 0)),
        out_shape=jax.ShapeDtypeStruct((width, 2, both // 2), F32),
        compiler_params=params(56),
        cost_estimate=cost(width * both, 6 * width * both),
        name="weave",
    )(summed)


def widen_kernel(in_ref, out_ref):
    out_ref[...] = in_ref[...].astype(F32)


def widen(summed):
    high, wide = summed.shape
    block = pl.BlockSpec((512, wide), lambda i: (i, 0))
    return pl.pallas_call(
        widen_kernel,
        grid=(high // 512,),
        in_specs=[block],
        out_specs=block,
        out_shape=jax.ShapeDtypeStruct((high, wide), F32),
        compiler_params=params(56),
        cost_estimate=cost(high * wide, 6 * high * wide),
        name="widen",
    )(summed)


def line_barrier(at, n, cube=None):
    barrier = pltpu.get_barrier_semaphore()
    if cube is not None:
        cube.signal(barrier)

    @pl.when(at > 0)
    def _():
        pl.semaphore_signal(barrier, inc=1, device_id={"tp": at - 1}, device_id_type=MESH)

    @pl.when(at < n - 1)
    def _():
        pl.semaphore_signal(barrier, inc=1, device_id={"tp": at + 1}, device_id_type=MESH)

    near = jnp.where((at > 0) & (at < n - 1), 2, 1)
    pl.semaphore_wait(barrier, near + (0 if cube is None else 3))


def sum_rows(n, sub, part_ref, out_ref, row_fn, from_left, from_right, send, recv, aside={}):
    at = lax.axis_index("tp")
    chunks = part_ref.shape[0] // sub
    middle = (n // 2 - 1, n // 2)

    def link(kind, right, src, dst, c):
        which = (kind * 2 + (1 if right else 0), c)
        return pltpu.make_async_remote_copy(
            src_ref=src.at[pl.ds(c * sub, sub)],
            dst_ref=dst.at[pl.ds(c * sub, sub)],
            send_sem=send.at[which],
            recv_sem=recv.at[which],
            device_id={"tp": at + 1 if right else at - 1},
            device_id_type=MESH,
        )

    def came(right):
        return from_left if right else from_right

    def first(right, c):
        return link(0, right, part_ref, came(right), c)

    def onward(right, c):
        return link(0, right, came(right), came(right), c)

    def hand(right, c):
        return link(1, right, out_ref, out_ref, c)

    def reduce_step(c):
        owner = middle[c % 2]
        rows = slice(c * sub, (c + 1) * sub)
        for right in (True, False):
            edge = 0 if right else n - 1
            held = came(right)

            @pl.when(((at < owner) if right else (at > owner)) & (at != edge))
            def _():
                copy = onward(right, c)
                copy.wait_recv()
                held[rows, :] = (
                    held[rows, :].astype(F32) + part_ref[rows, :].astype(F32)
                ).astype(BF16)
                copy.start()

    def final_step(c):
        owner = middle[c % 2]
        rows = slice(c * sub, (c + 1) * sub)

        @pl.when(at == owner)
        def _():
            total = part_ref[rows, :].astype(F32)
            onward(True, c).wait_recv()
            total = total + from_left[rows, :].astype(F32)
            onward(False, c).wait_recv()
            total = total + from_right[rows, :].astype(F32)
            row_fn(total, rows)
            hand(True, c).start()
            hand(False, c).start()

    def hand_step(c):
        owner = middle[c % 2]
        for right in (True, False):
            edge = n - 1 if right else 0

            @pl.when((at > owner) if right else (at < owner))
            def _():
                copy = hand(right, c)
                copy.wait_recv()

                @pl.when(at != edge)
                def _():
                    copy.start()

    for c in range(chunks):
        @pl.when(at == 0)
        def _():
            first(True, c).start()

        @pl.when(at == n - 1)
        def _():
            first(False, c).start()

    for c in range(chunks + 4):
        for piece in aside.get(c, ()):
            piece()
        if c < chunks:
            reduce_step(c)
        if 2 <= c < chunks + 2:
            final_step(c - 2)
        if c >= 4:
            hand_step(c - 4)
    for c in range(chunks):
        owner = middle[c % 2]

        @pl.when(at < owner)
        def _():
            first(True, c).wait_send()

        @pl.when(at > owner)
        def _():
            first(False, c).wait_send()

        @pl.when((at >= owner) & (at < n - 1))
        def _():
            hand(True, c).wait_send()

        @pl.when((at <= owner) & (at > 0))
        def _():
            hand(False, c).wait_send()


def merge_kernel(
    n, sub, part_ref, tok_ref, far_cot, far_down, inner_ref, resid_out, stat_ref, hidden_ref,
    from_left, from_right, send, recv, cot_ref, down_ref, resid_ref, read_sem, keep_sem,
):
    reads = (
        pltpu.make_async_copy(far_cot, cot_ref, read_sem.at[0]),
        pltpu.make_async_copy(far_down, down_ref, read_sem.at[1]),
    )
    for read in reads:
        read.start()
    line_barrier(lax.axis_index("tp"), n)
    stat_ref[...] = jnp.zeros_like(stat_ref)

    def keep(rows):
        slot = rows.start // (2 * sub)
        held = resid_ref.at[pl.ds(slot * sub, sub)]
        return pltpu.make_async_copy(
            held, resid_out.at[pl.ds(rows.start, sub)], keep_sem.at[slot]
        )

    def row_fn(total, rows):
        x = tok_ref[rows, :].astype(F32) + total
        mean = jnp.mean(x, axis=1, keepdims=True)
        center = x - mean
        inverse = lax.rsqrt(jnp.mean(center * center, axis=1, keepdims=True) + EPS)
        slot = rows.start // (2 * sub)
        resid_ref[slot * sub : (slot + 1) * sub, :] = x
        keep(rows).start()
        stat_ref[rows, :] = jnp.concatenate([mean, inverse], axis=1)
        inner_ref[rows, :] = (center * inverse).astype(BF16)

    def piece(at):
        if at == 0:
            for read in reads:
                read.wait()
        hidden_ref[:, at : at + 256] = lax.dot_general(
            cot_ref[...], down_ref[at : at + 256, :], NT, preferred_element_type=F32
        ).astype(BF16)

    aside = {}
    for k in range(down_ref.shape[0] // 256):
        aside[1 + 2 * k] = (functools.partial(piece, k * 256),)
    sum_rows(n, sub, part_ref, inner_ref, row_fn, from_left, from_right, send, recv, aside)
    for c in range(part_ref.shape[0] // sub):
        @pl.when(lax.axis_index("tp") == n // 2 - 1 + c % 2)
        def _():
            keep(slice(c * sub, (c + 1) * sub)).wait()


def merge(part, tok_full, cot_full, down, n):
    rows, width = part.shape
    sub = SUB
    vmem = pl.BlockSpec(memory_space=pltpu.VMEM)
    far = pl.BlockSpec(memory_space=pl.ANY)
    return pl.pallas_call(
        functools.partial(merge_kernel, n, sub),
        in_specs=[vmem, vmem, far, far],
        out_specs=[vmem, far, vmem, vmem],
        out_shape=[
            jax.ShapeDtypeStruct((rows, width), BF16),
            jax.ShapeDtypeStruct((rows, width), F32),
            jax.ShapeDtypeStruct((rows, 2), F32),
            jax.ShapeDtypeStruct((rows, down.shape[0]), BF16),
        ],
        scratch_shapes=[pltpu.VMEM((rows, width), BF16)] * 2
        + [pltpu.SemaphoreType.DMA((4, rows // sub))] * 2
        + [
            pltpu.VMEM((rows, width), BF16),
            pltpu.VMEM(down.shape, BF16),
            pltpu.VMEM((rows // 2, width), F32),
            pltpu.SemaphoreType.DMA((2,)),
            pltpu.SemaphoreType.DMA((rows // (2 * sub),)),
        ],
        compiler_params=params(56, collective_id=5, has_side_effects=True),
        cost_estimate=cost(1e6, 1e6),
        name="merge",
    )(part, tok_full, cot_full, down)


def norm_back_kernel(
    n, sub, cube, part_ref, cot_ref, stat_ref, *refs
):
    total = None
    far, refs = refs[:3], refs[3:]
    if cube:
        own, out_ref, layer_ref, mid, from_left, from_right, send, recv = refs[:8]
        resid_ref, hidden_ref, down_ref, read_sem = refs[8:12]
        total = CubeSum(own, *refs[12:17], mid=mid)
    else:
        out_ref, layer_ref, from_left, from_right, send, recv = refs[:6]
        resid_ref, hidden_ref, down_ref, read_sem = refs[6:10]
    reads = [
        pltpu.make_async_copy(source, held, read_sem.at[k])
        for k, (source, held) in enumerate(zip(far, (resid_ref, hidden_ref, down_ref)))
    ]
    for read in reads:
        read.start()
    at = lax.axis_index("tp")
    line_barrier(lax.axis_index("tp"), n, total)
    aside = {}

    def piece(start):
        if start == 0:
            for read in reads:
                read.wait()
        cols = slice(start, start + 256)
        row = lax.broadcasted_iota(jnp.int32, (part_ref.shape[0], 256), 0)
        owned = (row // sub) % 2 == at - (n // 2 - 1)
        layer_ref[:, cols] = (
            jnp.where(owned, resid_ref[:, cols], 0.0)
            + jnp.dot(hidden_ref[...], down_ref[:, cols], preferred_element_type=F32)
        ).astype(BF16)

    for k in range(down_ref.shape[1] // 256):
        aside[1 + 2 * k] = (functools.partial(piece, k * 256),)
    if cube:
        total.begin()
        for k, c in enumerate((14, 16, 18, 20)):
            aside[c] = (functools.partial(total.reduce, k),)

    def row_fn(summed, rows):
        inverse = stat_ref[rows, 1:2]
        normed = (resid_ref[rows, :] - stat_ref[rows, 0:1]) * inverse
        mean = jnp.mean(summed, axis=1, keepdims=True)
        inner = jnp.mean(summed * normed, axis=1, keepdims=True)
        out = cot_ref[rows, :].astype(F32) + inverse * (summed - mean - normed * inner)
        out_ref[rows, :] = out.astype(BF16)

    sum_rows(n, sub, part_ref, out_ref, row_fn, from_left, from_right, send, recv, aside)
    if cube:
        total.reduce(4)
        total.reduce(5)
        total.finish()


def norm_back(part, cot, resid, stat, hidden, down, n, grads):
    rows, width = part.shape
    sub = SUB
    vmem = pl.BlockSpec(memory_space=pltpu.VMEM)
    far = pl.BlockSpec(memory_space=pl.ANY)
    extra = []
    for grad in grads:
        extra += sum_scratch(grad.shape)
    return pl.pallas_call(
        functools.partial(norm_back_kernel, n, sub, len(grads) > 0),
        in_specs=[vmem] * 3 + [far] * (3 + len(grads)),
        out_specs=[vmem] * (2 + len(grads)),
        out_shape=[jax.ShapeDtypeStruct((rows, width), BF16)] * 2
        + [jax.ShapeDtypeStruct((grad.shape[0] // 4, grad.shape[1]), BF16) for grad in grads],
        scratch_shapes=[pltpu.VMEM((rows, width), BF16)] * 2
        + [pltpu.SemaphoreType.DMA((4, rows // sub))] * 2
        + [
            pltpu.VMEM(resid.shape, F32),
            pltpu.VMEM(hidden.shape, BF16),
            pltpu.VMEM(down.shape, BF16),
            pltpu.SemaphoreType.DMA((3,)),
        ]
        + extra,
        compiler_params=params(60, collective_id=1, has_side_effects=True),
        cost_estimate=cost(1e6, 1e6),
        name="norm_back",
    )(part, cot, stat, resid, hidden, down, *grads)


def unrotate_kernel(
    heads, dq_ref, dk_ref, dv_ref, cos_ref, sin_ref, inner_ref, dproj_ref, grad_ref
):
    def back(ref):
        for h in range(heads):
            hs = slice(h * HD, (h + 1) * HD)
            piece = ref[:, hs]
            dproj_ref[:, hs] = (
                piece * cos_ref[...] - pltpu.roll(piece, HD // 2, 1) * sin_ref[...]
            ).astype(BF16)

    part = pl.program_id(0)

    @pl.when(part == 0)
    def _():
        back(dq_ref)

    @pl.when(part == 1)
    def _():
        back(dk_ref)

    @pl.when(part == 2)
    def _():
        dproj_ref[...] = dv_ref[...].astype(BF16)

    grad_ref[...] = lax.dot_general(
        inner_ref[...], dproj_ref[...], TN, preferred_element_type=F32
    ).astype(BF16)


def unrotate(dq, dk, dv, cosine, sine, inner, heads):
    rows, span = dq.shape
    width = inner.shape[1]
    whole = lambda n: pl.BlockSpec((rows, n), lambda i: (0, 0))
    return pl.pallas_call(
        functools.partial(unrotate_kernel, heads),
        grid=(3,),
        in_specs=[whole(span)] * 3 + [whole(HD)] * 2 + [whole(width)],
        out_specs=[
            pl.BlockSpec((rows, span), lambda i: (0, i)),
            pl.BlockSpec((width, span), lambda i: (i, 0)),
        ],
        out_shape=[
            jax.ShapeDtypeStruct((rows, 3 * span), BF16),
            jax.ShapeDtypeStruct((3 * width, span), BF16),
        ],
        compiler_params=params(56),
        cost_estimate=cost(6 * rows * span * width, 12 * rows * span + 6 * width * span),
        name="unrotate",
    )(dq, dk, dv, cosine, sine, inner)


def unproject_kernel(heads, n, cube, *refs):
    sums, rest = [], None
    if cube:
        dq_ref, dk_ref, dv_ref, cos_ref, sin_ref, inner_ref, mixed_ref = refs[:7]
        branch_ref, mid_ref, far_tok, stat_ref, far_w = refs[7:12]
        out_ref, in_out, og_out, down_out, dproj_ref, in_ref, og_ref = refs[12:19]
        part_ref, mine_ref, land_ref, sums_ref, far_ref, send, recv, ssend, srecv = refs[19:28]
        for own, out, at in ((in_ref, in_out, 28), (og_ref, og_out, 31)):
            sums.append(CubeSum(own, own, *refs[at : at + 3], None, out=out))
        rest = LastGather(mid_ref, down_out, *refs[34:37])
    else:
        dproj_ref, branch_ref, far_tok, stat_ref, far_w, out_ref = refs[:6]
        part_ref, mine_ref, land_ref, sums_ref, far_ref, send, recv, ssend, srecv = refs[6:15]

    tok_ref, w_ref, read_sem = refs[-3:]
    reads = (
        pltpu.make_async_copy(far_tok, tok_ref, read_sem.at[0]),
        pltpu.make_async_copy(far_w, w_ref, read_sem.at[1]),
    )
    for read in reads:
        read.start()

    def reduce(*pieces):
        for k in pieces:
            for item in sums:
                item.reduce(k)

    def gather(k):
        for item in sums:
            item.gather(k)

    rows, width = tok_ref.shape
    shard = width // n
    span = heads * HD
    at = lax.axis_index("tp")
    barrier = pltpu.get_barrier_semaphore()
    for o in range(1, n):
        pl.semaphore_signal(
            barrier, inc=1, device_id={"tp": lax.rem(at + o, n)}, device_id_type=MESH
        )
    if cube:
        sums[0].signal(barrier)
    pl.semaphore_wait(barrier, n - 1 + (3 if cube else 0))
    if cube:
        og_ref[...] = lax.dot_general(
            mixed_ref[...], branch_ref[...], TN, preferred_element_type=F32
        ).astype(BF16)
        sums[1].begin()
        for part, ref in enumerate((dq_ref, dk_ref, dv_ref)):
            for h in range(heads):
                piece = ref[:, h * HD : (h + 1) * HD]
                if part < 2:
                    piece = (
                        piece * cos_ref[...] - pltpu.roll(piece, HD // 2, 1) * sin_ref[...]
                    )
                at_column = part * span + h * HD
                dproj_ref[:, at_column : at_column + HD] = piece.astype(BF16)
            in_ref[part * width : (part + 1) * width, :] = lax.dot_general(
                inner_ref[...], dproj_ref[:, part * span : (part + 1) * span], TN,
                preferred_element_type=F32,
            ).astype(BF16)
        sums[0].begin()
    block = 256
    count = rows // block

    def term(o, i):
        target = lax.rem(at + o, n)
        place = pl.ds(i * block, block)
        return pltpu.make_async_remote_copy(
            src_ref=part_ref.at[place, pl.ds(pl.multiple_of(target * shard, 128), shard)],
            dst_ref=land_ref.at[o - 1, place],
            send_sem=send.at[o - 1, i], recv_sem=recv.at[o - 1, i],
            device_id={"tp": target}, device_id_type=MESH,
        )

    def totals(o):
        return pltpu.make_async_remote_copy(
            src_ref=sums_ref, dst_ref=far_ref.at[o - 1],
            send_sem=ssend.at[o - 1], recv_sem=srecv.at[o - 1],
            device_id={"tp": lax.rem(at + o, n)}, device_id_type=MESH,
        )

    own = pl.ds(pl.multiple_of(at * shard, 128), shard)
    for read in reads:
        read.wait()
    for i in range(count):
        place = pl.ds(i * block, block)
        total = None
        for part in range(3):
            piece = lax.dot_general(
                dproj_ref[place, part * span : (part + 1) * span], w_ref[part], NT,
                preferred_element_type=F32,
            )
            total = piece if total is None else total + piece
        part_ref[place, :] = total.astype(BF16)
        for o in range(1, n):
            term(o, i).start()
        normed = (tok_ref[place, :].astype(F32) - stat_ref[place, 0:1]) * stat_ref[place, 1:2]
        first = jnp.sum(total, axis=1, keepdims=True)
        second = jnp.sum(total * normed, axis=1, keepdims=True)
        lane = lax.broadcasted_iota(jnp.int32, (block, HD), 1)
        both = jnp.where(lane == 0, first, jnp.where(lane == 1, second, 0.0))
        sums_ref[:, i * block : (i + 1) * block] = both.T[:8]
    for o in range(1, n):
        totals(o).start()
    reduce(0, 1, 2, 3, 4, 5)
    if cube:
        rest.begin()
    reduce(6, 7)
    gather(0)
    gather(1)
    total = sums_ref[...]
    for o in range(1, n):
        totals(o).wait_recv()
        total = total + far_ref[o - 1]
    mine_ref[...] = total
    for i in range(count):
        place = pl.ds(i * block, block)
        spread = jnp.concatenate(
            [mine_ref[:, i * block : (i + 1) * block], jnp.zeros((HD - 8, block), F32)], axis=0
        ).T / width
        total = part_ref[place, own].astype(F32)
        for o in range(1, n):
            term(o, i).wait_recv()
            total = total + land_ref[o - 1, place].astype(F32)
        inverse = stat_ref[place, 1:2]
        normed = (tok_ref[place, own].astype(F32) - stat_ref[place, 0:1]) * inverse
        out_ref[place, :] = branch_ref[place, own].astype(F32) + inverse * (
            total - spread[:, 0:1] - normed * spread[:, 1:2]
        )
    gather(2)
    for item in sums + ([rest] if cube else []):
        item.finish()
    for o in range(1, n):
        totals(o).wait_send()
        for i in range(count):
            term(o, i).wait_send()


def unproject(cube, operands, tok_full, stat, weight, heads, n):
    rows, width = tok_full.shape
    shard = width // n
    span = heads * HD
    far = pl.BlockSpec(memory_space=pl.ANY)
    vmem = pl.BlockSpec(memory_space=pltpu.VMEM)
    shapes = [(3 * width, span), (span, width)] if cube else []
    more_out, early, extra = [], [], []
    if cube:
        mid = operands[-1]
        more_out = [jax.ShapeDtypeStruct((high // 2, wide), BF16) for high, wide in shapes]
        more_out.append(jax.ShapeDtypeStruct((2 * mid.shape[0], mid.shape[1]), BF16))
        early = [pltpu.VMEM(shape, BF16) for shape in [(rows, 3 * span)] + shapes]
        for shape in shapes:
            extra += sum_scratch(shape)[1:4]
        extra += [pltpu.SemaphoreType.DMA((2,))] * 3
    return pl.pallas_call(
        functools.partial(unproject_kernel, heads, n, cube),
        in_specs=[vmem] * (len(operands) - int(cube)) + [far] * int(cube) + [far, vmem, far],
        out_specs=[vmem] * (1 + len(shapes)) + [pl.BlockSpec(memory_space=pl.ANY)] * int(cube),
        out_shape=[jax.ShapeDtypeStruct((rows, shard), F32)] + more_out,
        scratch_shapes=early
        + [
            pltpu.VMEM((rows, width), BF16),
            pltpu.VMEM((8, rows), F32),
            pltpu.VMEM((n - 1, rows, shard), BF16),
            pltpu.VMEM((8, rows), F32),
            pltpu.VMEM((n - 1, 8, rows), F32),
            pltpu.SemaphoreType.DMA((n - 1, rows // 256)),
            pltpu.SemaphoreType.DMA((n - 1, rows // 256)),
            pltpu.SemaphoreType.DMA((n - 1,)),
            pltpu.SemaphoreType.DMA((n - 1,)),
        ]
        + extra
        + [
            pltpu.VMEM((rows, width), BF16),
            pltpu.VMEM(weight.shape, BF16),
            pltpu.SemaphoreType.DMA((2,)),
        ],
        compiler_params=params(61, collective_id=4, has_side_effects=True),
        cost_estimate=cost(1e6, 1e6),
        name="unproject",
    )(*operands, tok_full, stat, weight)


def per_device(tokens, segment_ids, in_weight, out_weight, gate_up_weight, down_weight, cotangent):
    rows = tokens.shape[0]
    width = in_weight.shape[0]
    span = in_weight.shape[2]
    heads = span // HD
    hidden_local = down_weight.shape[0]
    me = lax.axis_index("ctx")
    tp_size = lax.axis_size("tp")
    cube = lax.axis_size("ctx") == CUBE

    def gather(local, axis=1):
        return lax.all_gather(local, "tp", axis=axis, tiled=True)

    places = me * rows + jnp.arange(rows, dtype=jnp.int32)
    cosine, sine = rope_tables(places)
    in_w = jnp.transpose(in_weight, (1, 0, 2))
    gu_w = jnp.transpose(
        gate_up_weight.reshape(width, 2, hidden_local // BLOCK, BLOCK), (0, 2, 1, 3)
    )
    gu_w = gu_w.reshape(width, 2 * hidden_local)

    all_seg = lax.all_gather(segment_ids, "ctx", axis=0, tiled=True)
    count = all_seg.shape[0]
    every = jnp.arange(count, dtype=jnp.int32)
    opens = jnp.concatenate([jnp.ones((1,), jnp.bool_), all_seg[1:] != all_seg[:-1]])
    all_begin = lax.cummax(jnp.where(opens, every, 0))
    blocks = all_begin.reshape(count // rows, rows)

    tok_full, gu_w, blocks, all_begin = lax.optimization_barrier(
        (gather(tokens), gu_w, blocks, all_begin)
    )
    key_info = jnp.stack(
        [me, blocks[me, 0] // rows, (blocks[me, rows - 1] + rows - 1) // rows]
    ).astype(jnp.int32)
    query_info = jnp.stack(
        [
            me,
            jnp.sum((blocks[:, 0] < (me + 1) * rows).astype(jnp.int32)) - 1,
            jnp.sum((blocks[:, rows - 1] <= me * rows).astype(jnp.int32)) - 1,
        ]
    ).astype(jnp.int32)
    begin = lax.dynamic_slice_in_dim(blocks, me, 1, 0)
    all_begin = all_begin[None, :]
    if cube:
        inner1, stat1, raw, mixed, lse, kept, cot_full, out_part = attend_far(
            tok_full, in_w, cosine, sine, blocks, cotangent, out_weight, heads, tp_size
        )
        kept = lax.all_gather(kept, "ctx", axis=0, tiled=True)
    else:
        inner1, stat1, query, pairs = project(tok_full, in_w, cosine, sine, heads)
        all_pairs = lax.all_gather(pairs, "ctx", axis=0, tiled=True)
        cot_full = gather(cotangent)
        raw, mixed, lse = attend(key_info, query, all_pairs, begin, heads)
        out_part = jnp.dot(mixed, out_weight, preferred_element_type=F32).astype(BF16)
        late_query, mixed = lax.optimization_barrier((query, mixed))
        kept = lax.all_gather(late_query, "ctx", axis=0, tiled=True)
    inner2, resid1, stat2, grad_hidden = merge(
        out_part, tok_full, cot_full, down_weight, tp_size
    )

    hidden, grad_gu, down_grad, gu_grad = feed(inner2, cot_full, gu_w, grad_hidden, BLOCK)
    down_grad, gu_grad, kept, grad_gu, hidden = lax.optimization_barrier(
        (down_grad, gu_grad, kept, grad_gu, hidden)
    )
    if not cube:
        down_grad = lax.psum(down_grad, "ctx")
    gu_grad = lax.optimization_barrier(lax.psum(gu_grad, "ctx"))

    grad_part = lax.dot_general(grad_gu, gu_w, NT, preferred_element_type=F32).astype(BF16)
    branch_grad, branch, *mids = norm_back(
        grad_part, cot_full, resid1, stat2, hidden, down_weight, tp_size,
        [down_grad] if cube else [],
    )
    grad_mixed, delta = mixed_grad(branch_grad, out_weight, raw, lse, heads)
    if cube:
        dq, dk, dv, layer_out, mid = attend_back_far(
            grad_mixed, kept, blocks, branch, mids[0], heads, tp_size
        )
    else:
        branch = lax.psum_scatter(branch, "tp", scatter_dimension=1, tiled=True)
        layer_out = branch
        all_grad = lax.all_gather(grad_mixed, "ctx", axis=0, tiled=True)
        dq = query_grad(key_info, query, grad_mixed, lse, delta, all_pairs, begin, heads)
        dk, dv = key_grad(query_info, pairs, kept, all_grad, all_begin, heads)

    if cube:
        tokens_grad, *halves = unproject(
            True, [dq, dk, dv, cosine, sine, inner1, mixed, branch_grad, mid],
            tok_full, stat1, in_w, heads, tp_size,
        )
        swap = [(i, i + 1 - 2 * (i % 2)) for i in range(CUBE)]
        core = (me % 2)[None]
        far = [lax.ppermute(half, "ctx", swap) for half in halves]
        *far, gu_grad = lax.optimization_barrier((*far, weave(gu_grad, BLOCK)))
        in_grad, out_grad, down_grad = join(core, halves, far)
    else:
        out_grad = lax.dot_general(
            mixed, branch_grad, TN, preferred_element_type=F32
        ).astype(BF16)
        dproj, in_grad = unrotate(dq, dk, dv, cosine, sine, inner1, heads)
        in_grad, out_grad, down_grad, gu_grad = lax.optimization_barrier(
            (in_grad, out_grad, down_grad, gu_grad)
        )
        in_grad, out_grad = lax.psum((in_grad, out_grad), "ctx")
        (tokens_grad,) = unproject(
            False, [dproj, branch_grad], tok_full, stat1, in_w, heads, tp_size
        )
        in_grad, out_grad, down_grad = widen(in_grad), out_grad.astype(F32), widen(down_grad)
        gu_grad = weave(gu_grad, BLOCK)
    return (
        layer_out,
        tokens_grad,
        jnp.transpose(in_grad.reshape(3, width, span), (1, 0, 2)),
        out_grad,
        gu_grad,
        down_grad,
    )


def solution(mesh):
    placed = (
        P("ctx", "tp"),
        P("ctx"),
        P(None, None, "tp"),
        P("tp", None),
        P(None, None, "tp"),
        P("tp", None),
        P("ctx", "tp"),
    )
    return jax.shard_map(
        per_device,
        mesh=mesh,
        in_specs=placed,
        out_specs=(
            P("ctx", "tp"),
            P("ctx", "tp"),
            P(None, None, "tp"),
            P("tp", None),
            P(None, None, "tp"),
            P("tp", None),
        ),
        check_vma=False,
    )
```
